32 devices in a mesh: dp: 16 (over z, y, x), mp: 2 (over core).
Axes of the slice: x: 2, y: 2, z: 4, core: 2. Of those that a mesh axis runs over, the one named last changes fastest.
Arguments:
- acoustic: bfloat16 [4096, 512], P('dp'), may hold values from -6 to 6
- memory: bfloat16 [32768, 512], P('dp'), may hold values from -6 to 6
- embedding: bfloat16 [8404, 512], replicated, may hold values from -6 to 6
- w_query: bfloat16 [512, 512], P(None, 'mp'), may hold values from -0.25 to 0.25
- w_key: bfloat16 [512, 512], P(None, 'mp'), may hold values from -0.25 to 0.25
- w_value: bfloat16 [512, 512], P(None, 'mp'), may hold values from -0.25 to 0.25
- w_out: bfloat16 [512, 512], P('mp'), may hold values from -2 to 2
- w_in: bfloat16 [512, 2048], P(None, 'mp'), may hold values from -0.25 to 0.25
- w_back: bfloat16 [2048, 512], P('mp'), may hold values from -0.1875 to 0.1875
- w_vocab: bfloat16 [512, 8404], P(None, 'mp'), may hold values from -0.25 to 0.25
- gain_one: float32 [512], replicated, may hold values from 0.5 to 1.5
- bias_one: float32 [512], replicated, may hold values from -3 to 3
- gain_two: float32 [512], replicated, may hold values from 0.5 to 1.5
- bias_two: float32 [512], replicated, may hold values from -3 to 3
- fsmn_kernel: float32 [11, 512], replicated, may hold values from -1.75 to 1.75
- rate_table: float32 [2, 512], replicated, may hold values from -3 to 3
- token_lengths: int32 [32], P('dp'), may hold values from 1 to 128, 3072 in all
- memory_lengths: int32 [32], P('dp'), may hold values from 1 to 1024, 24576 in all
- rate_groups: int32 [32], P('dp'), may hold values from 0 to 1
- glance_mask: int32 [4096], P('dp'), may hold values 0 or 1
- targets: int32 [4096], P('dp'), may hold values from 0 to 8403
Outputs:
- token_loss: float32 [4096], P('dp')
- grad_acoustic: float32 [4096, 512], P('dp')
- grad_memory: float32 [32768, 512], P('dp', 'mp')
- grad_embedding: float32 [8404, 512], P(None, 'dp')
- grad_query: float32 [512, 512], P('dp', 'mp')
- grad_key: float32 [512, 512], P('dp', 'mp')
- grad_value: float32 [512, 512], P('dp', 'mp')
- grad_out: float32 [512, 512], P('mp', 'dp')
- grad_in: float32 [512, 2048], P('dp', 'mp')
- grad_back: float32 [2048, 512], P('mp', 'dp')
- grad_vocab: float32 [512, 8404], P('dp', 'mp')
- grad_gain_one: float32 [512], P('dp')
- grad_bias_one: float32 [512], P('dp')
- grad_gain_two: float32 [512], P('dp')
- grad_bias_two: float32 [512], P('dp')
- grad_kernel: float32 [11, 512], P(None, 'dp')
- grad_rate: float32 [2, 512], replicated
The draws below stay inside these ranges and needn't reach their ends.
Inputs may be any that keep to these rules, and one draw needn't show every extreme that they name: Utterance u occupies the first token_lengths[u] of its 128 token slots. Utterance u occupies the first memory_lengths[u] of its 1024 frame slots.
All inputs are finite; a program needn't handle non-finite values. No bound on the sum of `token_lengths` or of `memory_lengths` or of `glance_mask` on one device may be relied on, other than what follows from the above.
Results may differ from the reference program's by a relative error of at most 0.025.
Values sent between devices are 32-bit elements; how exact they have to be, the bound alone decides.
A program may use at most 192 MiB of HBM per device.

```python
import math
import jax
import jax.numpy as jnp
import numpy as np
from jax import lax

D = 512
HEADS = 4
HD = 128
FF = 2048
KER = 11
V = 8404
UTT = 2
LTOK = 128
LMEM = 1024
UTTS = 32
TOKENS = 4096
MEM = 32768
N_DP = 16


def plant(array, rng, smallest, high):
    longest = array.shape.index(max(array.shape))
    spots = []
    for shift in (0, 1):
        where = [jax.random.randint(jax.random.fold_in(rng, axis), (), 0, length) for axis, length in enumerate(array.shape)]
        where[longest] = (where[longest] + shift) % array.shape[longest]
        spots.append(tuple(where))
    return array.at[spots[0]].set(smallest).at[spots[1]].set(high)


def block_scale(stream_key, dims, shards, low, high):
    factor_of = 1.0
    for dim, blocks in shards:
        heights = jax.random.uniform(jax.random.fold_in(jax.random.fold_in(stream_key, 6), dim), (blocks,), jnp.float32, low / len(shards), high / len(shards))
        factor_of = factor_of * jnp.repeat(jnp.exp(heights), dims[dim] // blocks).reshape((-1,) + (1,) * (len(dims) - 1 - dim))
    return factor_of


def rank_bounds(amount, lean):
    portions = [(1 << 20) // math.isqrt(rank ** lean) + 1 for rank in range(1, amount + 1)]
    scale = 1 + sum(portions) // (1 << 30)
    return np.cumsum(np.array([max(1, weight // scale) for weight in portions]))


def ranked_ids(stream_key, extent, amount, skew):
    listing = rank_bounds(amount, skew)
    lot = jax.random.randint(jax.random.fold_in(stream_key, 1), extent, 0, int(listing[amount - 1]))
    standing = jnp.searchsorted(jnp.asarray(listing, jnp.int32), lot, side="right")
    return jax.random.permutation(jax.random.fold_in(stream_key, 2), amount)[standing].astype(jnp.int32)


def length_profile(number_of, total, bound, skew):
    portions = [(1 << 20) // math.isqrt(grade ** skew) + 1 for grade in range(2, number_of + 1)]
    surplus, given = total - bound - (number_of - 1), [1] * (number_of - 1)
    while surplus > 0:
        candidates = [i for i in range(number_of - 1) if given[i] < bound]
        mass, remaining = sum([portions[i] for i in candidates]), surplus
        for i in candidates:
            addition = min(bound - given[i], max(1, remaining * portions[i] // mass), surplus)
            given[i] = given[i] + addition
            surplus = surplus - addition
    return np.array([bound] + given)


def ragged(stream_key, number_of, total, reach, lean):
    if number_of == 2:
        one = jax.random.randint(stream_key, (), max(1, total - reach), min(reach, total - 1) + 1)
        return jnp.stack([one, total - one])
    tallies = jnp.asarray(length_profile(number_of, total, reach, lean), jnp.int32)
    pairs = (number_of - 1) // 2
    donor, sink = tallies[1:1 + 2 * pairs:2], tallies[2:2 + 2 * pairs:2]
    margin = jnp.minimum(donor - 1, reach - sink)
    passed = jax.random.randint(jax.random.fold_in(stream_key, 1), (pairs,), 0, 1 << 20) % (margin + 1)
    tallies = tallies.at[1:1 + 2 * pairs:2].set(donor - passed).at[2:2 + 2 * pairs:2].set(sink + passed)
    return tallies[jax.random.permutation(jax.random.fold_in(stream_key, 2), number_of)]


def noise(key, extent, scale, most, split=(), dtype=jnp.bfloat16):
    result = scale * jax.random.normal(key, extent, jnp.float32)
    if split:
        result = result * block_scale(key, extent, split, -0.22, 0.18)
    return jnp.clip(result, -most, most).astype(dtype)


def setup_inputs(seed: int = 0) -> dict:
    key_of = jax.random.split(jax.random.key(seed), 22)
    return {
        "acoustic": noise(key_of[0], (TOKENS, D), 1.0, 6.0, ((0, 16),)),
        "memory": noise(key_of[1], (MEM, D), 1.0, 6.0, ((0, 16),)),
        "embedding": noise(key_of[2], (V, D), 1.0, 6.0),
        "w_query": noise(key_of[3], (D, D), D ** -0.5, 0.25, ((1, 2),)),
        "w_key": noise(key_of[4], (D, D), D ** -0.5, 0.25, ((1, 2),)),
        "w_value": noise(key_of[5], (D, D), D ** -0.5, 0.25, ((1, 2),)),
        "w_out": noise(key_of[6], (D, D), (max(1, 16 * D // LMEM)) ** -0.5, 2.0, ((0, 2),)),
        "w_in": noise(key_of[7], (D, FF), D ** -0.5, 0.25, ((1, 2),)),
        "w_back": noise(key_of[8], (FF, D), (FF // 2) ** -0.5, 0.1875, ((0, 2),)),
        "w_vocab": noise(key_of[9], (D, V), D ** -0.5, 0.25, ((1, 2),)),
        "gain_one": jnp.clip(1.0 + 0.1 * jax.random.normal(key_of[10], (D,), jnp.float32), 0.5, 1.5),
        "bias_one": noise(key_of[11], (D,), 0.3, 3.0, (), jnp.float32),
        "gain_two": jnp.clip(1.0 + 0.1 * jax.random.normal(key_of[12], (D,), jnp.float32), 0.5, 1.5),
        "bias_two": noise(key_of[13], (D,), 0.3, 3.0, (), jnp.float32),
        "fsmn_kernel": noise(key_of[14], (KER, D), KER ** -0.5, 1.75, (), jnp.float32),
        "rate_table": noise(key_of[15], (2, D), 0.5, 3.0, (), jnp.float32),
        "token_lengths": ragged(key_of[16], UTTS, UTTS * LTOK * 3 // 4, LTOK, 1).astype(jnp.int32),
        "memory_lengths": ragged(key_of[17], UTTS, UTTS * LMEM * 3 // 4, LMEM, 1).astype(jnp.int32),
        "rate_groups": plant(jax.random.randint(key_of[18], (UTTS,), 0, 2), jax.random.fold_in(key_of[18], 1), 0, 1).astype(jnp.int32),
        "glance_mask": plant((jax.random.randint(key_of[19], (TOKENS,), 0, 2) < 1).astype(jnp.int32), jax.random.fold_in(key_of[19], 1), 0, 1),
        "targets": plant(ranked_ids(key_of[20], (TOKENS,), V, 2), jax.random.fold_in(key_of[20], 3), 0, V - 1).astype(jnp.int32),
    }


PRECISE = lax.Precision.HIGHEST
EPSILON = 1e-05

@jax.custom_vjp
def low(v):
    return lax.optimization_barrier(v.astype(jnp.bfloat16)).astype(jnp.float32)

@jax.custom_vjp
def low_back(v):
    return v

def low_keep(v):
    return (low(v), None)

def low_pass(kept, grad):
    return (grad,)

def back_keep(v):
    return (v, None)

def back_low(kept, grad):
    return (low(grad),)
low.defvjp(low_keep, low_pass)
low_back.defvjp(back_keep, back_low)

def rounded_both(value):
    return low(low_back(value))

def product_high(left_side, right_side):
    return jnp.dot(left_side, right_side, precision=PRECISE, preferred_element_type=jnp.float32)

def norm_rows(row_values, gain_vector, bias_vector):
    average = lax.optimization_barrier(jnp.mean(row_values, axis=-1, keepdims=True))
    centred = row_values - average
    variance = lax.optimization_barrier(jnp.mean(centred * centred, axis=-1, keepdims=True))
    return centred * lax.rsqrt(variance + EPSILON) * gain_vector + bias_vector

def memory_block(activations, kernel, valid_mask):
    half_width = kernel.shape[0] // 2
    token_slots = activations.shape[1]
    padded = jnp.pad(activations * valid_mask, ((0, 0), (half_width, half_width), (0, 0)))
    summed = jnp.zeros_like(activations)
    for position in range(kernel.shape[0]):
        summed = summed + kernel[position] * padded[:, position:position + token_slots]
    return summed * valid_mask

def decoder(weights, stream_in, memory_rows, group_ids, valid_tok, valid_mem, target_ids):
    w_query, w_key, w_value, w_out, w_in, w_back, w_vocab, gain_one, bias_one, gain_two, bias_two, kernel, rate_table = weights
    utterances = valid_tok.shape[0]
    token_slots = valid_tok.shape[1]
    frames = valid_mem.shape[1]
    model_width = stream_in.shape[1]
    score_scale = 1.0 / math.sqrt(HD)
    norm_one = norm_rows(stream_in, gain_one, bias_one)
    convolved = memory_block(norm_one.reshape(utterances, token_slots, model_width), kernel, valid_tok[:, :, None])
    stream_one = stream_in + convolved.reshape(-1, model_width)
    rate_rows = jnp.where(group_ids[:, None, None] == 1, rate_table[1], rate_table[0])
    mem_low = low((memory_rows.reshape(utterances, frames, model_width) + rate_rows).reshape(-1, model_width))
    key_rows = rounded_both(product_high(mem_low, w_key)).reshape(utterances, frames, HEADS, HD)
    value_rows = rounded_both(product_high(mem_low, w_value)).reshape(utterances, frames, HEADS, HD)
    query_rows = rounded_both(product_high(low(stream_one), w_query)).reshape(utterances, token_slots, HEADS, HD)
    scores = low_back(jnp.einsum('uthd,umhd->uhtm', query_rows, key_rows, precision=PRECISE) * score_scale)
    scores = jnp.where(valid_mem[:, None, None, :], scores, -1e+30)
    attention_probs = jax.nn.softmax(scores, axis=-1)
    mixed_heads = rounded_both(jnp.einsum('uhtm,umhd->uthd', low(attention_probs), value_rows, precision=PRECISE)).reshape(-1, HEADS * HD)
    stream_two = stream_one + low_back(product_high(mixed_heads, w_out))
    pre_activation = low_back(product_high(low(norm_rows(stream_two, gain_two, bias_two)), w_in))
    hidden = low(jax.nn.gelu(pre_activation, approximate=False))
    stream_three = stream_two + low_back(product_high(hidden, w_back))
    logits = low_back(product_high(low(stream_three), w_vocab))
    log_total = jax.nn.logsumexp(logits, axis=-1)
    picked = jnp.take_along_axis(logits, target_ids[:, None], axis=-1)[:, 0]
    return (log_total - picked) * valid_tok.reshape(-1)

def reference(acoustic, memory, embedding, w_query, w_key, w_value, w_out, w_in, w_back, w_vocab, gain_one, bias_one, gain_two, bias_two, fsmn_kernel, rate_table, token_lengths, memory_lengths, rate_groups, glance_mask, targets):
    weights = tuple((member.astype(jnp.float32) for member in (w_query, w_key, w_value, w_out, w_in, w_back, w_vocab, gain_one, bias_one, gain_two, bias_two, fsmn_kernel, rate_table)))
    table_wide = embedding.astype(jnp.float32)
    sliced = (acoustic.astype(jnp.float32).reshape(N_DP, UTT * LTOK, D), memory.astype(jnp.float32).reshape(N_DP, UTT * LMEM, D), token_lengths.reshape(N_DP, UTT), memory_lengths.reshape(N_DP, UTT), rate_groups.reshape(N_DP, UTT), glance_mask.reshape(N_DP, UTT * LTOK), targets.reshape(N_DP, UTT * LTOK))

    def group_step(running, pieces):
        acoustic_rows, memory_rows, token_count, frame_count, group_ids, glance_ids, target_ids = pieces
        valid_tok = (jnp.arange(LTOK)[None, :] < token_count[:, None]).astype(jnp.float32)
        valid_mem = jnp.arange(LMEM)[None, :] < frame_count[:, None]
        first_loss = decoder(weights, acoustic_rows, memory_rows, group_ids, valid_tok, valid_mem, target_ids)
        blend_weight = glance_ids.astype(jnp.float32) * valid_tok.reshape(-1) * jax.nn.sigmoid(first_loss - math.log(V))

        def second_pass(weights_in, acoustic_in, memory_in, table_in):
            taken = table_in[target_ids]
            stream = acoustic_in + blend_weight[:, None] * (taken - acoustic_in)
            return decoder(weights_in, stream, memory_in, group_ids, valid_tok, valid_mem, target_ids)
        token_loss, pullback = jax.vjp(second_pass, weights, acoustic_rows, memory_rows, table_wide)
        gradients = pullback(jnp.ones_like(token_loss))
        updated = (jax.tree.map(jnp.add, running[0], gradients[0]), running[1] + gradients[3])
        return (updated, (token_loss, gradients[1], gradients[2]))
    start = (tuple((jnp.zeros_like(member) for member in weights)), jnp.zeros_like(table_wide))
    totals, stacked = lax.scan(group_step, start, sliced)
    grad_weights, grad_table = totals
    token_loss, grad_acoustic, grad_memory = stacked
    return (token_loss.reshape(-1), grad_acoustic.reshape(-1, D), grad_memory.reshape(-1, D), grad_table, grad_weights[0], grad_weights[1], grad_weights[2], grad_weights[3], grad_weights[4], grad_weights[5], grad_weights[6], grad_weights[7], grad_weights[8], grad_weights[9], grad_weights[10], grad_weights[11], grad_weights[12])
```

```python
from functools import partial
import math

import jax
import jax.numpy as jnp
from jax import lax
from jax.experimental import pallas as pl
from jax.experimental.pallas import tpu as pltpu
from jax.sharding import PartitionSpec as P

MESH = pl.DeviceIdType.MESH
VMEM = pl.BlockSpec(memory_space=pltpu.VMEM)

HD = 128
V = 8404


EPSILON = 1e-05


def other_core():
    return {"mp": 1 - lax.axis_index("mp")}


def greet_other_core():
    barrier = pltpu.get_barrier_semaphore()
    pl.semaphore_signal(barrier, inc=1, device_id=other_core(), device_id_type=MESH)
    pl.semaphore_wait(barrier, 1)


def pair_add_kernel(mine, total, arrived, send_sem, recv_sem):
    greet_other_core()
    copy = pltpu.make_async_remote_copy(
        src_ref=mine, dst_ref=arrived, send_sem=send_sem, recv_sem=recv_sem,
        device_id=other_core(), device_id_type=MESH,
    )
    copy.start()
    copy.wait()
    total[...] = mine[...] + arrived[...]


def pair_get_kernel(mine, theirs, arrived, send_sem, recv_sem):
    greet_other_core()
    copy = pltpu.make_async_remote_copy(
        src_ref=mine, dst_ref=arrived, send_sem=send_sem, recv_sem=recv_sem,
        device_id=other_core(), device_id_type=MESH,
    )
    copy.start()
    copy.wait()
    theirs[...] = arrived[...]


def pair_half_kernel(mine, total, arrived, send_sem, recv_sem):
    greet_other_core()
    width = total.shape[1]
    core = lax.axis_index("mp")
    copy = pltpu.make_async_remote_copy(
        src_ref=mine.at[:, pl.ds(pl.multiple_of((1 - core) * width, 128), width)],
        dst_ref=arrived, send_sem=send_sem, recv_sem=recv_sem,
        device_id=other_core(), device_id_type=MESH,
    )
    copy.start()
    copy.wait()
    total[...] = mine[:, pl.ds(pl.multiple_of(core * width, 128), width)] + arrived[...]


def pair_call(kernel, mine, shape, collective_id):
    out = jax.ShapeDtypeStruct(shape, jnp.float32)
    return pl.pallas_call(
        kernel,
        out_shape=out,
        in_specs=[VMEM],
        out_specs=VMEM,
        scratch_shapes=[
            pltpu.VMEM(shape, jnp.float32),
            pltpu.SemaphoreType.DMA,
            pltpu.SemaphoreType.DMA,
        ],
        compiler_params=pltpu.CompilerParams(
            collective_id=collective_id, has_side_effects=True, vmem_limit_bytes=32 << 20
        ),
    )(mine)


def pair_add(mine):
    return pair_call(pair_add_kernel, mine, mine.shape, 1)


def pair_get(mine):
    return pair_call(pair_get_kernel, mine, mine.shape, 2)


def pair_half(mine):
    return pair_call(pair_half_kernel, mine, (mine.shape[0], mine.shape[1] // 2), 3)


def scatter_sum_kernel(bits, low_bits, chunks, shared_rows, n_in, *refs):
    ins, small = refs[:n_in], refs[n_in]
    outs, small_out = refs[n_in + 1 : 2 * n_in + 1], refs[2 * n_in + 1]
    scratch = refs[2 * n_in + 2 :]
    steps = len(bits)
    n_chunks = len(chunks)
    arrived = [scratch[c * steps : (c + 1) * steps] for c in range(n_chunks)]
    small_arrived, small_sent, send_sem, recv_sem, small_send, small_recv = scratch[n_chunks * steps :]
    me, core = lax.axis_index("dp"), lax.axis_index("mp")
    bit_of = {b: lax.rem(me // (1 << b), 2) for b in low_bits + bits}
    peer_of = {b: {"dp": me + (1 - 2 * bit_of[b]) * (1 << b)} for b in low_bits + bits}

    barrier = pltpu.get_barrier_semaphore()
    for b in low_bits + bits:
        pl.semaphore_signal(barrier, inc=1, device_id=peer_of[b], device_id_type=MESH)
    pl.semaphore_signal(barrier, inc=1, device_id=other_core(), device_id_type=MESH)
    pl.semaphore_wait(barrier, len(low_bits) + steps + 1)

    def pick(c, step, half):
        source, start, width, order = chunks[c]
        rest = sorted([b for b in bits if b not in order[:step]], reverse=True)
        where = tuple(half if b == order[step] else slice(None) for b in rest)
        if step == 0:
            return ins[source], where + (slice(None), pl.ds(start, width))
        return arrived[c][step - 1], where + (slice(None), slice(None))

    def send(c, step):
        b = chunks[c][3][step]
        ref, where = pick(c, step, 1 - bit_of[b])
        copy = pltpu.make_async_remote_copy(
            src_ref=ref.at[where], dst_ref=arrived[c][step],
            send_sem=send_sem.at[c, step], recv_sem=recv_sem.at[c, step],
            device_id=peer_of[b], device_id_type=MESH,
        )
        copy.start()
        return copy

    def take(c, step, copy):
        b = chunks[c][3][step]
        ref, where = pick(c, step, bit_of[b])
        copy.wait_recv()
        got = arrived[c][step]
        if step == steps - 1:
            source, start, width, _ = chunks[c]
            outs[source][:, pl.ds(start, width)] = got[...] + ref[where]
        else:
            got[...] = got[...] + ref[where]

    small_peers = [peer_of[b] for b in low_bits + bits] + [other_core()]
    small_sent[0] = small[...]

    def small_send_step(step):
        copy = pltpu.make_async_remote_copy(
            src_ref=small_sent.at[step], dst_ref=small_arrived.at[step],
            send_sem=small_send.at[step], recv_sem=small_recv.at[step],
            device_id=small_peers[step], device_id_type=MESH,
        )
        copy.start()
        return copy

    def small_take(step, copy):
        copy.wait_recv()
        if step + 1 < len(small_peers):
            small_sent[step + 1] = small_sent[step] + small_arrived[step]
        else:
            small_out[...] = small_sent[step]
            rows = small_out.shape[0] - shared_rows
            small_out[pl.ds(shared_rows, rows)] = (
                small_sent[step, pl.ds(shared_rows, rows)]
                + small_arrived[step, pl.ds(shared_rows, rows)]
            )

    started = []
    small_copy = small_send_step(0)
    small_step = 0
    started.append(small_copy)
    flying = {}
    for c in range(n_chunks):
        flying[c] = send(c, 0)
        started.append(flying[c])
    for wave in range(n_chunks + 2 * (steps - 1)):
        for step in reversed(range(steps)):
            c = wave - 2 * step
            if not 0 <= c < n_chunks:
                continue
            take(c, step, flying[c])
            if step + 1 < steps:
                flying[c] = send(c, step + 1)
                started.append(flying[c])
        if small_step < len(small_peers):
            small_take(small_step, small_copy)
            small_step += 1
            if small_step < len(small_peers):
                small_copy = small_send_step(small_step)
                started.append(small_copy)
    for copy in started:
        copy.wait_send()


def scatter_sum(parts, small, shared_rows, n_dp):
    nbits = n_dp.bit_length() - 1
    rows = parts[0].shape[0]
    steps = nbits
    while rows >> steps < 8:
        steps -= 1
    low_bits, bits = list(range(nbits - steps)), list(range(nbits - steps, nbits))
    block = rows >> steps
    shaped = [p.reshape((2,) * steps + (block, p.shape[1])) for p in parts]
    forward = bits
    swapped = [bits[1], bits[0]] + bits[2:]
    chunks = []
    for i, p in enumerate(parts):
        width = p.shape[1]
        pieces = max(1, width // 1024)
        edges = [width // 128 * k // pieces * 128 for k in range(pieces)] + [width]
        for k in range(pieces):
            chunks.append((i, edges[k], edges[k + 1] - edges[k], [forward, swapped][len(chunks) % 2]))
    scratch = []
    for _, _, width, _ in chunks:
        for step in range(steps):
            scratch.append(pltpu.VMEM((2,) * (steps - 1 - step) + (block, width), jnp.float32))
    n_small = nbits + 1
    scratch += [
        pltpu.VMEM((n_small,) + small.shape, jnp.float32),
        pltpu.VMEM((n_small,) + small.shape, jnp.float32),
        pltpu.SemaphoreType.DMA((len(chunks), steps)),
        pltpu.SemaphoreType.DMA((len(chunks), steps)),
        pltpu.SemaphoreType.DMA((n_small,)),
        pltpu.SemaphoreType.DMA((n_small,)),
    ]
    out = pl.pallas_call(
        partial(scatter_sum_kernel, bits, low_bits, chunks, shared_rows, len(parts)),
        out_shape=[jax.ShapeDtypeStruct((block, p.shape[1]), jnp.float32) for p in parts]
        + [jax.ShapeDtypeStruct(small.shape, jnp.float32)],
        in_specs=[VMEM] * (len(parts) + 1),
        out_specs=[VMEM] * (len(parts) + 1),
        scratch_shapes=scratch,
        compiler_params=pltpu.CompilerParams(
            collective_id=4, has_side_effects=True, vmem_limit_bytes=56 << 20
        ),
    )(*shaped, small)
    summed, small_sum = list(out[:-1]), out[-1]
    if low_bits:
        size = 1 << len(low_bits)
        groups = [list(range(g * size, (g + 1) * size)) for g in range(n_dp // size)]
        summed = [
            lax.psum_scatter(s, "dp", scatter_dimension=0, axis_index_groups=groups, tiled=True)
            for s in summed
        ]
    return summed, small_sum


def norm_rows(row_values, gain_vector, bias_vector):
    average = jnp.mean(row_values, axis=-1, keepdims=True)
    centred = row_values - average
    variance = jnp.mean(centred * centred, axis=-1, keepdims=True)
    return centred * lax.rsqrt(variance + EPSILON) * gain_vector + bias_vector


def memory_block(activations, kernel, valid_mask):
    half_width = kernel.shape[0] // 2
    token_slots = activations.shape[1]
    padded = jnp.pad(activations * valid_mask, ((0, 0), (half_width, half_width), (0, 0)))
    summed = jnp.zeros_like(activations)
    for position in range(kernel.shape[0]):
        summed = summed + kernel[position] * padded[:, position : position + token_slots]
    return summed * valid_mask


def product(left_side, right_side):
    return jnp.dot(left_side, right_side, preferred_element_type=jnp.float32)


def product_left(left_side, right_side):
    return lax.dot_general(
        left_side, right_side, (((0,), (0,)), ((), ())), preferred_element_type=jnp.float32
    )


def product_right(left_side, right_side):
    return lax.dot_general(
        left_side, right_side, (((1,), (1,)), ((), ())), preferred_element_type=jnp.float32
    )


def logit_stats(logits, target_ids, offset):
    vocab_ids = offset + lax.broadcasted_iota(jnp.int32, logits.shape, 1)
    onehot = (vocab_ids == target_ids[:, None]).astype(jnp.float32)
    picked = jnp.sum(onehot * logits, axis=1)
    local_top = jnp.max(logits, axis=1)
    local_sum = jnp.sum(jnp.exp(logits - local_top[:, None]), axis=1)
    zeros = jnp.zeros_like(local_top)
    theirs = pair_get(jnp.stack([local_top, local_sum, picked] + [zeros] * 5))
    top_value = jnp.maximum(local_top, theirs[0])
    denominator = local_sum * jnp.exp(local_top - top_value) + theirs[1] * jnp.exp(
        theirs[0] - top_value
    )
    return (top_value + jnp.log(denominator), picked + theirs[2], onehot)


def attention_scores(query_rows, key_rows, valid_mem, score_scale):
    scores = (
        jnp.einsum("uthd,umhd->uhtm", query_rows, key_rows, preferred_element_type=jnp.float32)
        * score_scale
    )
    return jnp.where(valid_mem[:, None, None, :], scores, -1e30)


def per_device(
    acoustic,
    memory,
    embedding,
    w_query,
    w_key,
    w_value,
    w_out,
    w_in,
    w_back,
    w_vocab,
    gain_one,
    bias_one,
    gain_two,
    bias_two,
    fsmn_kernel,
    rate_table,
    token_lengths,
    memory_lengths,
    rate_groups,
    glance_mask,
    targets,
):
    all_targets = lax.all_gather(targets, "dp", tiled=True)
    utterances = token_lengths.shape[0]
    tok_rows, model_width = acoustic.shape
    token_slots = tok_rows // utterances
    frames = memory.shape[0] // utterances
    heads_here = w_query.shape[1] // HD
    offset = lax.axis_index("mp") * w_vocab.shape[1]
    score_scale = 1.0 / math.sqrt(HD)
    valid_tok = (
        lax.broadcasted_iota(jnp.int32, (utterances, token_slots), 1) < token_lengths[:, None]
    ).astype(jnp.float32)
    valid_mem = lax.broadcasted_iota(jnp.int32, (utterances, frames), 1) < memory_lengths[:, None]
    valid_rows = valid_tok.reshape(tok_rows)
    rate_rows = jnp.where(rate_groups[:, None, None] == 1, rate_table[1], rate_table[0])
    mem_low = (
        (memory.astype(jnp.float32).reshape(utterances, frames, model_width) + rate_rows)
        .astype(jnp.bfloat16)
        .reshape(utterances * frames, model_width)
    )
    key_rows = (
        product(mem_low, w_key).astype(jnp.bfloat16).reshape(utterances, frames, heads_here, HD)
    )
    value_rows = (
        product(mem_low, w_value).astype(jnp.bfloat16).reshape(utterances, frames, heads_here, HD)
    )

    def conv_rows(activations, kernel):
        shaped = activations.reshape(utterances, token_slots, model_width)
        return memory_block(shaped, kernel, valid_tok[:, :, None]).reshape(tok_rows, model_width)

    def decoder_pass(stream_in):
        norm_one, back_one = jax.vjp(norm_rows, stream_in, gain_one, bias_one)
        convolved, back_conv = jax.vjp(conv_rows, norm_one, fsmn_kernel)
        stream_one = stream_in + convolved
        stream_low = stream_one.astype(jnp.bfloat16)
        query_rows = (
            product(stream_low, w_query)
            .astype(jnp.bfloat16)
            .reshape(utterances, token_slots, heads_here, HD)
        )
        scores = attention_scores(query_rows, key_rows, valid_mem, score_scale)
        score_top = jnp.max(scores, axis=-1, keepdims=True)
        raised = jnp.exp(scores - score_top)
        score_sum = jnp.sum(raised, axis=-1, keepdims=True)
        probs_low = (raised / score_sum).astype(jnp.bfloat16)
        mixed_heads = (
            jnp.einsum("uhtm,umhd->uthd", probs_low, value_rows, preferred_element_type=jnp.float32)
            .astype(jnp.bfloat16)
            .reshape(tok_rows, heads_here * HD)
        )
        stream_two = stream_one + pair_add(product(mixed_heads, w_out))
        norm_two, back_two = jax.vjp(norm_rows, stream_two, gain_two, bias_two)
        norm_low = norm_two.astype(jnp.bfloat16)
        activated, back_act = jax.vjp(
            partial(jax.nn.gelu, approximate=False), product(norm_low, w_in)
        )
        hidden = activated.astype(jnp.bfloat16)
        stream_three = stream_two + pair_add(product(hidden, w_back))
        top_low = stream_three.astype(jnp.bfloat16)
        logits = product(top_low, w_vocab)
        log_total, picked, onehot = logit_stats(logits, targets, offset)
        token_loss = (log_total - picked) * valid_rows
        saved_state = (
            back_one,
            back_conv,
            stream_low,
            query_rows,
            score_top + jnp.log(score_sum),
            mixed_heads,
            back_two,
            norm_low,
            back_act,
            hidden,
            top_low,
            logits,
            log_total,
            onehot,
        )
        return (token_loss, saved_state)

    acoustic_wide = acoustic.astype(jnp.float32)
    first_loss, unused = decoder_pass(acoustic_wide)
    blend_weight = (
        glance_mask.astype(jnp.float32) * valid_rows * jax.nn.sigmoid(first_loss - math.log(V))
    )
    rows_taken = embedding[targets].astype(jnp.float32)
    stream_in = acoustic_wide + blend_weight[:, None] * (rows_taken - acoustic_wide)
    token_loss, saved_state = decoder_pass(stream_in)
    (
        back_one,
        back_conv,
        stream_low,
        query_rows,
        score_log,
        mixed_heads,
        back_two,
        norm_low,
        back_act,
        hidden,
        top_low,
        logits,
        log_total,
        onehot,
    ) = saved_state
    grad_logits = ((jnp.exp(logits - log_total[:, None]) - onehot) * valid_rows[:, None]).astype(
        jnp.bfloat16
    )
    vocab_here = grad_logits.shape[1]
    grad_vocab = product_left(
        top_low, jnp.pad(grad_logits, ((0, 0), (0, -vocab_here % 128)))
    )
    grad_three = pair_add(product_right(grad_logits, w_vocab))
    grad_branch = grad_three.astype(jnp.bfloat16)
    grad_back = product_left(grad_branch, hidden)
    grad_pre = back_act(product_right(grad_branch, w_back))[0].astype(jnp.bfloat16)
    grad_in = product_left(norm_low, grad_pre)
    grad_norm_two = pair_add(product_right(grad_pre, w_in))
    grad_two_norm, grad_gain_two, grad_bias_two = back_two(grad_norm_two)
    grad_two = grad_three + grad_two_norm
    grad_attended = grad_two.astype(jnp.bfloat16)
    grad_out = product_left(grad_attended, mixed_heads)
    grad_mixed = (
        product_right(grad_attended, w_out)
        .astype(jnp.bfloat16)
        .reshape(utterances, token_slots, heads_here, HD)
    )
    scores = attention_scores(query_rows, key_rows, valid_mem, score_scale)
    attention_probs = jnp.exp(scores - score_log)
    probs_low = attention_probs.astype(jnp.bfloat16)
    grad_probs = jnp.einsum(
        "uthd,umhd->uhtm", grad_mixed, value_rows, preferred_element_type=jnp.float32
    )
    grad_values = (
        jnp.einsum("uhtm,uthd->umhd", probs_low, grad_mixed, preferred_element_type=jnp.float32)
        .astype(jnp.bfloat16)
        .reshape(utterances * frames, heads_here * HD)
    )
    grad_scores = (
        attention_probs
        * (grad_probs - jnp.sum(attention_probs * grad_probs, axis=-1, keepdims=True))
    ).astype(jnp.bfloat16)
    grad_queries = (
        (
            jnp.einsum("uhtm,umhd->uthd", grad_scores, key_rows, preferred_element_type=jnp.float32)
            * score_scale
        )
        .astype(jnp.bfloat16)
        .reshape(tok_rows, heads_here * HD)
    )
    grad_keys = (
        (
            jnp.einsum(
                "uhtm,uthd->umhd", grad_scores, query_rows, preferred_element_type=jnp.float32
            )
            * score_scale
        )
        .astype(jnp.bfloat16)
        .reshape(utterances * frames, heads_here * HD)
    )
    grad_query = product_left(stream_low, grad_queries)
    grad_one = grad_two + pair_add(product_right(grad_queries, w_query))
    grad_key = product_left(mem_low, grad_keys)
    grad_value = product_left(mem_low, grad_values)
    grad_mem_part = product_right(grad_keys, w_key) + product_right(grad_values, w_value)
    grad_memory = pair_half(grad_mem_part)
    utterance_sums = jnp.sum(grad_mem_part.reshape(utterances, frames, model_width), axis=1)
    group_one = (rate_groups == 1).astype(jnp.float32)[:, None]
    rate_part = jnp.stack(
        [
            jnp.sum((1.0 - group_one) * utterance_sums, axis=0),
            jnp.sum(group_one * utterance_sums, axis=0),
        ]
    )
    grad_norm_one, grad_kernel = back_conv(grad_one)
    grad_zero_norm, grad_gain_one, grad_bias_one = back_one(grad_norm_one)
    grad_zero = grad_one + grad_zero_norm
    grad_acoustic = grad_zero - blend_weight[:, None] * grad_zero
    table_terms = blend_weight[:, None] * grad_zero
    group_size = lax.axis_size("dp")
    arrived_rows = lax.all_to_all(table_terms, "dp", split_axis=1, concat_axis=0, tiled=True)
    grad_embedding = jax.ops.segment_sum(
        arrived_rows, all_targets, num_segments=embedding.shape[0]
    )
    grad_kernel = jnp.pad(grad_kernel, ((0, 12 - grad_kernel.shape[0]), (0, 0)))
    small = jnp.concatenate(
        [
            grad_kernel,
            grad_gain_one[None],
            grad_bias_one[None],
            grad_gain_two[None],
            grad_bias_two[None],
            rate_part,
            jnp.zeros((6, model_width), jnp.float32),
        ]
    )
    (grad_vocab, grad_in, grad_back, grad_query, grad_key, grad_value, grad_out), small = scatter_sum(
        [grad_vocab, grad_in, grad_back, grad_query, grad_key, grad_value, grad_out],
        small,
        16,
        group_size,
    )
    grad_vocab = grad_vocab[:, :vocab_here]
    grad_back, grad_out = grad_back.T, grad_out.T
    grad_rate = small[16:18]
    own = model_width // group_size
    small = lax.dynamic_slice_in_dim(small, lax.axis_index("dp") * own, own, axis=1)
    grad_kernel = small[: fsmn_kernel.shape[0]]
    grad_gain_one, grad_bias_one, grad_gain_two, grad_bias_two = (small[12 + i] for i in range(4))
    return (
        token_loss,
        grad_acoustic,
        grad_memory,
        grad_embedding,
        grad_query,
        grad_key,
        grad_value,
        grad_out,
        grad_in,
        grad_back,
        grad_vocab,
        grad_gain_one,
        grad_bias_one,
        grad_gain_two,
        grad_bias_two,
        grad_kernel,
        grad_rate,
    )


def solution(mesh):
    return jax.shard_map(
        per_device,
        mesh=mesh,
        in_specs=(
            P("dp", None),
            P("dp", None),
            P(),
            P(None, "mp"),
            P(None, "mp"),
            P(None, "mp"),
            P("mp", None),
            P(None, "mp"),
            P("mp", None),
            P(None, "mp"),
            P(),
            P(),
            P(),
            P(),
            P(),
            P(),
            P("dp"),
            P("dp"),
            P("dp"),
            P("dp"),
            P("dp"),
        ),
        out_specs=(
            P("dp"),
            P("dp", None),
            P("dp", "mp"),
            P(None, "dp"),
            P("dp", "mp"),
            P("dp", "mp"),
            P("dp", "mp"),
            P("mp", "dp"),
            P("dp", "mp"),
            P("mp", "dp"),
            P("dp", "mp"),
            P("dp"),
            P("dp"),
            P("dp"),
            P("dp"),
            P(None, "dp"),
            P(),
        ),
        check_vma=False,
    )
```

```python
from functools import partial
import math

import jax
import jax.numpy as jnp
from jax import lax
from jax.experimental import pallas as pl
from jax.experimental.pallas import tpu as pltpu
from jax.sharding import PartitionSpec as P

HD = 128
V = 8404
EPSILON = 1e-05
MESH = pl.DeviceIdType.MESH
VMEM = pl.BlockSpec(memory_space=pltpu.VMEM)
SMEM = pl.BlockSpec(memory_space=pltpu.SMEM)
ANY = pl.BlockSpec(memory_space=pl.ANY)
F32, BF16 = jnp.float32, jnp.bfloat16
NEG = -1e30


def other_core():
    return {"mp": 1 - lax.axis_index("mp")}


def dot_nn(a, b):
    return lax.dot_general(a, b, (((1,), (0,)), ((), ())), preferred_element_type=F32)


def dot_nt(a, b):
    return lax.dot_general(a, b, (((1,), (1,)), ((), ())), preferred_element_type=F32)


def dot_tn(a, b):
    return lax.dot_general(a, b, (((0,), (0,)), ((), ())), preferred_element_type=F32)


def normalise(rows):
    average = jnp.mean(rows, axis=-1, keepdims=True)
    centred = rows - average
    variance = jnp.mean(centred * centred, axis=-1, keepdims=True)
    scale = lax.rsqrt(variance + EPSILON)
    return centred * scale, scale


def normalise_back(grad_hat, hat, scale):
    first = jnp.mean(grad_hat, axis=-1, keepdims=True)
    second = jnp.mean(grad_hat * hat, axis=-1, keepdims=True)
    return scale * (grad_hat - first - hat * second)


def to_rows(columns):
    lane = lax.broadcasted_iota(jnp.int32, (columns[0].shape[0], 128), 1)
    tile = jnp.zeros(lane.shape, F32)
    for i, column in enumerate(columns):
        tile = jnp.where(lane == i, column, tile)
    return tile.T[:8]


def to_columns(rows):
    return jnp.concatenate([rows] * 16, axis=0).T


def decoder_kernel(
    vocab_here,
    half_cols,
    acoustic,
    taken,
    memory,
    w_query_hbm,
    w_key_hbm,
    w_value_hbm,
    w_out_hbm,
    w_in_hbm,
    w_back_hbm,
    w_vocab_hbm,
    w_tail_hbm,
    gain_one,
    bias_one,
    gain_two,
    bias_two,
    kernel_rows,
    rate_table,
    token_lengths,
    memory_lengths,
    rate_groups,
    glance,
    targets,
    loss_out,
    acoustic_out,
    memory_out,
    terms_out,
    small_out,
    vocab_out,
    in_out,
    back_out,
    query_out,
    out_out,
    kv_out,
    w_query,
    w_kv,
    w_out,
    w_in,
    w_back,
    w_vocab,
    mem_low,
    kv,
    padded,
    stream_in,
    stream_one,
    stream_two,
    stream_three,
    one_low,
    queries,
    probs,
    mixed,
    norm_low,
    hidden,
    gelu_slope,
    top,
    logits,
    grad_logits,
    part3,
    arrived3,
    grad_three,
    grad_two,
    branch_low,
    grad_pre,
    att_low,
    grad_queries,
    grad_kv,
    mem_part,
    mem_arrived,
    meta,
    stats,
    stats_arrived,
    sent,
    arrived,
    gathered,
    load_sem,
    swap_send,
    swap_recv,
):
    utterances, slots = targets.shape
    width = acoustic.shape[1]
    frames = memory.shape[0] // utterances
    heads = w_query_hbm.shape[1] // HD
    tokens = utterances * slots
    me, core = lax.axis_index("dp"), lax.axis_index("mp")
    side = lax.rem(me, 2)
    sibling = {"mp": 1 - core}
    pair = {"dp": me + 1 - 2 * side}
    cross = {"dp": me + 1 - 2 * side, "mp": 1 - core}
    score_scale = 1.0 / math.sqrt(HD)

    loads = []

    def load(source, target):
        copy = pltpu.make_async_copy(source, target, load_sem.at[len(loads)])
        copy.start()
        loads.append(copy)
        return copy

    load_memory = load(memory, mem_low)
    half = heads * HD
    load_kv = [
        load(w_key_hbm, w_kv.at[:, pl.ds(0, half)]),
        load(w_value_hbm, w_kv.at[:, pl.ds(half, half)]),
    ]
    load_query = load(w_query_hbm, w_query)
    load_out = load(w_out_hbm, w_out)
    load_in = load(w_in_hbm, w_in)
    load_back = load(w_back_hbm, w_back)
    main = w_vocab.shape[1] - w_tail_hbm.shape[1]
    load_vocab = [
        load(w_vocab_hbm.at[:, pl.ds(0, main)], w_vocab.at[:, pl.ds(0, main)]),
        load(w_tail_hbm, w_vocab.at[:, pl.ds(main, w_tail_hbm.shape[1])]),
    ]

    barrier = pltpu.get_barrier_semaphore()
    for device in (sibling, pair, cross):
        pl.semaphore_signal(barrier, inc=1, device_id=device, device_id_type=MESH)
    pl.semaphore_wait(barrier, 3)

    swaps = []

    def swap(source, target, device):
        k = len(swaps)
        copy = pltpu.make_async_remote_copy(
            src_ref=source,
            dst_ref=target,
            send_sem=swap_send.at[k],
            recv_sem=swap_recv.at[k],
            device_id=device,
            device_id_type=MESH,
        )
        copy.start()
        swaps.append(copy)
        return copy

    lane = lax.broadcasted_iota(jnp.int32, (1, slots), 1)
    row_of = lax.broadcasted_iota(jnp.int32, (8, slots), 0)
    for u in range(utterances):
        target_row = targets[pl.ds(u, 1), :].astype(F32)
        glance_row = glance[pl.ds(u, 1), :].astype(F32)
        valid_row = (lane < token_lengths[u]).astype(F32)
        meta[0, :, pl.ds(u * slots, slots)] = jnp.where(
            row_of == 0, target_row, jnp.where(row_of == 1, valid_row, glance_row)
        )
    meta_swap = swap(meta.at[0], meta.at[1], pair)
    own_columns = to_columns(meta[0])
    own_target = own_columns[:, 0:1]
    own_valid = own_columns[:, 1:2]
    own_glance = own_columns[:, 2:3]

    def rows(u):
        return pl.ds(u * slots, slots)

    gain_1, bias_1, gain_2, bias_2 = gain_one[...], bias_one[...], gain_two[...], bias_two[...]

    load_memory.wait()
    for copy in load_kv:
        copy.wait()
    step_rows = 256

    def kv_step(i, carry):
        at = pl.ds(pl.multiple_of(i * step_rows, step_rows), step_rows)
        group = jnp.zeros((1, width), jnp.int32) + rate_groups[i // (frames // step_rows)]
        rate_row = jnp.where(group == 1, rate_table[pl.ds(1, 1), :], rate_table[pl.ds(0, 1), :])
        low = (mem_low[at, :].astype(F32) + rate_row).astype(BF16)
        mem_low[at, :] = low
        kv[at, :] = dot_nn(low, w_kv[...]).astype(BF16)
        return carry

    lax.fori_loop(0, utterances * frames // step_rows, kv_step, 0)

    edge = jnp.zeros((8, width), F32)
    for u in range(utterances):
        padded[u, pl.ds(0, 8), :] = edge
        padded[u, pl.ds(8 + slots, 8), :] = edge

    load_query.wait()
    load_out.wait()

    def key_of(u, h):
        return kv[pl.ds(u * frames, frames), pl.ds(h * HD, HD)]

    def value_of(u, h):
        return kv[pl.ds(u * frames, frames), pl.ds(half + h * HD, HD)]

    frame_lane = lax.broadcasted_iota(jnp.int32, (1, frames), 1)

    def local_targets(target_column):
        local = target_column.astype(jnp.int32) - core * vocab_here
        return jnp.where((local >= 0) & (local < vocab_here), local, -1)

    def vocab_tile(tile, first, col, target, top_m, picked):
        ids = col + lax.broadcasted_iota(jnp.int32, (1, 128), 1)
        tile = jnp.where(ids < vocab_here, tile, NEG)
        logits[first] = tile
        return jnp.maximum(top_m, tile), picked + jnp.where(ids == target, tile, 0.0)

    def vocab_stats(top_rows, target, base, wide, narrow, first):
        start = (jnp.full((tokens, 128), NEG, F32), jnp.zeros((tokens, 128), F32))

        def step(j, carry):
            col = pl.multiple_of(base + j * 256, 128)
            product = dot_nn(top_rows(), w_vocab[:, pl.ds(col, 256)])
            carry = vocab_tile(product[:, :128], first + 2 * j, col, target, *carry)
            return vocab_tile(product[:, 128:], first + 2 * j + 1, col + 128, target, *carry)

        top_m, picked = lax.fori_loop(0, wide, step, start)
        if narrow:
            col = pl.multiple_of(base + wide * 256, 128)
            product = dot_nn(top_rows(), w_vocab[:, pl.ds(col, 128)])
            top_m, picked = vocab_tile(product, first + 2 * wide, col, target, top_m, picked)
        top_row = jnp.max(top_m, axis=1, keepdims=True)

        def add(j, total):
            return total + jnp.exp(logits[first + j] - top_row)

        total = lax.fori_loop(0, 2 * wide + narrow, add, jnp.zeros((tokens, 128), F32))
        return (
            top_row,
            jnp.sum(total, axis=1, keepdims=True),
            jnp.sum(picked, axis=1, keepdims=True),
        )

    def join(blocks):
        top_value = blocks[0][0:1]
        for b in blocks[1:]:
            top_value = jnp.maximum(top_value, b[0:1])
        total, picked = 0.0, 0.0
        for b in blocks:
            total = total + b[1:2] * jnp.exp(b[0:1] - top_value)
            picked = picked + b[2:3]
        return top_value + jnp.log(total), picked

    def forward(second):
        copies = []
        for u in range(utterances):
            at = rows(u)
            valid = own_valid[u * slots : (u + 1) * slots]
            hat, _ = normalise(stream_in[at, :])
            padded[u, pl.ds(8, slots), :] = (hat * gain_1 + bias_1) * valid
            for j in range(width // 128):
                cols = pl.ds(j * 128, 128)
                total = jnp.zeros((slots, 128), F32)
                for k in range(kernel_rows.shape[0]):
                    shift = 8 + k - kernel_rows.shape[0] // 2
                    total = total + kernel_rows[pl.ds(k, 1), cols] * padded[u, pl.ds(shift, slots), cols]
                stream_one[at, cols] = stream_in[at, cols] + total * valid
            low = stream_one[at, :].astype(BF16)
            one_low[at, :] = low
            queries[at, :] = dot_nn(low, w_query[...]).astype(BF16)
            frame_ok = frame_lane < memory_lengths[u]
            for h in range(heads):
                cols = pl.ds(h * HD, HD)
                scores = dot_nt(queries[at, cols], key_of(u, h)) * score_scale
                scores = jnp.where(frame_ok, scores, NEG)
                raised = jnp.exp(scores - jnp.max(scores, axis=-1, keepdims=True))
                prob = raised / jnp.sum(raised, axis=-1, keepdims=True)
                if second:
                    probs[u, h] = prob
                mixed[at, cols] = dot_nn(prob.astype(BF16), value_of(u, h)).astype(BF16)
            sent[u] = dot_nn(mixed[at, :], w_out[...])
            copies.append(swap(sent.at[u], arrived.at[u], sibling))
        if not second:
            load_in.wait()
            load_back.wait()
        ff_copies = []
        for u in range(utterances):
            at = rows(u)
            copies[u].wait()
            two = stream_one[at, :] + (sent[u] + arrived[u])
            stream_two[at, :] = two
            hat, _ = normalise(two)
            low = (hat * gain_2 + bias_2).astype(BF16)
            norm_low[at, :] = low
            pre = dot_nn(low, w_in[...])
            phi = 0.5 * (1.0 + lax.erf(pre * math.sqrt(0.5)))
            hidden[at, :] = (pre * phi).astype(BF16)
            if second:
                gelu_slope[at, :] = phi + pre * (
                    jnp.exp(-0.5 * pre * pre) * (1.0 / math.sqrt(2.0 * math.pi))
                )
            sent[utterances + u] = dot_nn(hidden[at, :], w_back[...])
            ff_copies.append(swap(sent.at[utterances + u], arrived.at[utterances + u], sibling))
        for u in range(utterances):
            at = rows(u)
            ff_copies[u].wait()
            three = stream_two[at, :] + (sent[utterances + u] + arrived[utterances + u])
            stream_three[u] = three
            top[0, at, :] = three.astype(BF16)

    stream_in[...] = acoustic[...].astype(F32)
    forward(False)
    for copy in load_vocab:
        copy.wait()
    first = vocab_stats(lambda: top[0], local_targets(own_target), 0, w_vocab.shape[1] // 256, 0, 0)
    stats[0, :, pl.ds(0, tokens)] = to_rows(first)
    first_swap = swap(stats.at[0, :, pl.ds(0, tokens)], stats_arrived.at[0, :, pl.ds(0, tokens)], sibling)
    wide_acoustic = acoustic[...].astype(F32)
    difference = taken[...].astype(F32) - wide_acoustic
    first_swap.wait()
    log_total, picked = join([stats[0, :, :tokens], stats_arrived[0, :, :tokens]])
    first_loss = (log_total - picked) * meta[0, 1:2, :]
    blend_row = meta[0, 2:3, :] * meta[0, 1:2, :] / (1.0 + jnp.exp(math.log(V) - first_loss))
    blend = to_columns(jnp.concatenate([blend_row] * 8, axis=0))[:, 0:1]
    stream_in[...] = wide_acoustic + blend * difference

    forward(True)
    token_swap = swap(stream_three.at[core], gathered.at[0], pair)
    base = side * half_cols
    wide, narrow = half_cols // 256, half_cols % 256 // 128
    per_group = 2 * wide + narrow
    meta_swap.wait()
    pair_columns = to_columns(meta[1])
    group_target = [local_targets(own_target), local_targets(pair_columns[:, 0:1])]
    group_valid = [own_valid, pair_columns[:, 1:2]]
    own_stats = vocab_stats(lambda: top[0], group_target[0], base, wide, narrow, 0)
    stats[1, :, pl.ds(0, tokens)] = to_rows(own_stats)
    token_swap.wait()
    share_swap = swap(gathered.at[0], gathered.at[1], sibling)
    at_core = pl.ds(pl.multiple_of(core * slots, slots), slots)
    at_other = pl.ds(pl.multiple_of((1 - core) * slots, slots), slots)
    top[1, at_core, :] = gathered[0].astype(BF16)
    share_swap.wait()
    top[1, at_other, :] = gathered[1].astype(BF16)
    pair_stats = vocab_stats(lambda: top[1], group_target[1], base, wide, narrow, per_group)
    stats[1, :, pl.ds(tokens, tokens)] = to_rows(pair_stats)
    stat_swaps = [
        swap(stats.at[1], stats_arrived.at[1], sibling),
        swap(stats.at[1], stats_arrived.at[2], pair),
        swap(stats.at[1], stats_arrived.at[3], cross),
    ]
    for copy in stat_swaps:
        copy.wait()

    def group_blocks(g):
        mine, theirs = pl.ds(g * tokens, tokens), pl.ds((1 - g) * tokens, tokens)
        return [
            stats[1, :, mine],
            stats_arrived[1, :, mine],
            stats_arrived[2, :, theirs],
            stats_arrived[3, :, theirs],
        ]

    log_totals = []
    for g in range(2):
        log_total, picked = join(group_blocks(g))
        log_totals.append(to_columns(jnp.concatenate([log_total] * 8, axis=0))[:, 0:1])
        if g == 0:
            loss = (log_total - picked) * meta[0, 1:2, :]
            for u in range(utterances):
                loss_out[pl.ds(u, 1), :] = loss[:, u * slots : (u + 1) * slots]

    for g in (1, 0):
        log_column, valid, target = log_totals[g], group_valid[g], group_target[g]

        def slope(j, carry):
            col = pl.multiple_of(j * 128, 128)
            ids = base + col + lax.broadcasted_iota(jnp.int32, (1, 128), 1)
            onehot = jnp.where(ids == target, 1.0, 0.0)
            grad = (jnp.exp(logits[g * per_group + j] - log_column) - onehot) * valid
            grad_logits[pl.ds(g * tokens, tokens), pl.ds(col, 128)] = grad.astype(BF16)
            return carry

        lax.fori_loop(0, per_group, slope, 0)
        part = dot_nt(
            grad_logits[pl.ds(g * tokens, tokens), :],
            w_vocab[:, pl.ds(pl.multiple_of(base, 128), half_cols)],
        )
        for u in range(utterances):
            part3[u, g] = part[u * slots : (u + 1) * slots]
    three_swap = swap(part3.at[1 - core], arrived3, sibling)
    top_all = jnp.concatenate([top[0], top[1]], axis=0)

    def vocab_grad(col, cols):
        vocab_out[:, pl.ds(col, cols)] = dot_tn(top_all, grad_logits[:, pl.ds(col, cols)])

    for j in range(wide):
        vocab_grad(j * 256, 256)
        if j == 0:
            three_swap.wait()
            sent[0] = part3[core, 1] + arrived3[1]
            pair_swap = swap(sent.at[0], arrived.at[0], pair)
    if narrow:
        vocab_grad(wide * 256, 128)
    pair_swap.wait()
    grad_three[core] = (part3[core, 0] + arrived3[0]) + arrived[0]
    share_three = swap(grad_three.at[core], arrived.at[1], sibling)
    share_three.wait()
    grad_three[1 - core] = arrived[1]

    copies = []
    for u in range(utterances):
        at = rows(u)
        low = grad_three[u].astype(BF16)
        branch_low[at, :] = low
        pre = (dot_nt(low, w_back[...]) * gelu_slope[at, :]).astype(BF16)
        grad_pre[at, :] = pre
        sent[utterances + u] = dot_nt(pre, w_in[...])
        copies.append(swap(sent.at[utterances + u], arrived.at[utterances + u], sibling))
    back_out[...] = dot_tn(branch_low[...], hidden[...])
    in_out[...] = dot_tn(norm_low[...], grad_pre[...])

    one_copies = []
    gain_2_total, bias_2_total = 0.0, 0.0
    for u in range(utterances):
        at = rows(u)
        copies[u].wait()
        grad_norm = sent[utterances + u] + arrived[utterances + u]
        hat, scale = normalise(stream_two[at, :])
        gain_2_total = gain_2_total + jnp.sum(grad_norm * hat, axis=0, keepdims=True)
        bias_2_total = bias_2_total + jnp.sum(grad_norm, axis=0, keepdims=True)
        two = grad_three[u] + normalise_back(grad_norm * gain_2, hat, scale)
        grad_two[at, :] = two
        low = two.astype(BF16)
        att_low[at, :] = low
        grad_mixed = dot_nt(low, w_out[...]).astype(BF16)
        for h in range(heads):
            cols = pl.ds(h * HD, HD)
            grad_head = grad_mixed[:, h * HD : (h + 1) * HD]
            prob = probs[u, h]
            grad_prob = dot_nt(grad_head, value_of(u, h))
            grad_kv[pl.ds(u * frames, frames), pl.ds(half + h * HD, HD)] = dot_tn(
                prob.astype(BF16), grad_head
            ).astype(BF16)
            inner = jnp.sum(prob * grad_prob, axis=-1, keepdims=True)
            grad_score = (prob * (grad_prob - inner)).astype(BF16)
            grad_queries[at, cols] = (dot_nn(grad_score, key_of(u, h)) * score_scale).astype(BF16)
            grad_kv[pl.ds(u * frames, frames), cols] = (
                dot_tn(grad_score, queries[at, cols]) * score_scale
            ).astype(BF16)
        sent[u] = dot_nt(grad_queries[at, :], w_query[...])
        one_copies.append(swap(sent.at[u], arrived.at[u], sibling))
    out_out[...] = dot_tn(att_low[...], mixed[...])
    query_out[...] = dot_tn(one_low[...], grad_queries[...])

    mem_copies = []
    for u in range(utterances):
        total = jnp.zeros((1, width), F32)
        for i in range(frames // step_rows):
            at = pl.ds(u * frames + i * step_rows, step_rows)
            part = dot_nt(grad_kv[at, :], w_kv[...])
            mem_part[0, at, :] = part[:, : width // 2]
            mem_part[1, at, :] = part[:, width // 2 :]
            total = total + jnp.sum(part, axis=0, keepdims=True)
        at = pl.ds(u * frames, frames)
        mem_copies.append(swap(mem_part.at[1 - core, at, :], mem_arrived.at[at, :], sibling))
        group = jnp.zeros((1, width), jnp.int32) + rate_groups[u]
        for r in range(2):
            share = jnp.where((group == 1) == (r == 1), total, 0.0)
            if u == 0:
                small_out[pl.ds(16 + r, 1), :] = share
            else:
                small_out[pl.ds(16 + r, 1), :] = small_out[pl.ds(16 + r, 1), :] + share
        product = dot_tn(mem_low[at, :], grad_kv[at, :])
        kv_out[...] = product if u == 0 else kv_out[...] + product

    gain_1_total, bias_1_total = 0.0, 0.0
    for u in range(utterances):
        at = rows(u)
        valid = own_valid[u * slots : (u + 1) * slots]
        one_copies[u].wait()
        one = grad_two[at, :] + (sent[u] + arrived[u])
        grad_two[at, :] = one
        masked = one * valid
        for k in range(kernel_rows.shape[0]):
            shift = 8 + k - kernel_rows.shape[0] // 2
            row = jnp.sum(masked * padded[u, pl.ds(shift, slots), :], axis=0, keepdims=True)
            if u == 0:
                small_out[pl.ds(k, 1), :] = row
            else:
                small_out[pl.ds(k, 1), :] = small_out[pl.ds(k, 1), :] + row
        padded[u, pl.ds(8, slots), :] = masked
        for j in range(width // 128):
            cols = pl.ds(j * 128, 128)
            total = jnp.zeros((slots, 128), F32)
            for k in range(kernel_rows.shape[0]):
                shift = 8 - k + kernel_rows.shape[0] // 2
                total = total + kernel_rows[pl.ds(k, 1), cols] * padded[u, pl.ds(shift, slots), cols]
            stream_one[at, cols] = total * valid
        grad_norm = stream_one[at, :]
        hat, scale = normalise(stream_in[at, :])
        gain_1_total = gain_1_total + jnp.sum(grad_norm * hat, axis=0, keepdims=True)
        bias_1_total = bias_1_total + jnp.sum(grad_norm, axis=0, keepdims=True)
        zero = grad_two[at, :] + normalise_back(grad_norm * gain_1, hat, scale)
        terms = blend[u * slots : (u + 1) * slots] * zero
        terms_out[at, :] = terms
        acoustic_out[at, :] = zero - terms
    small_out[pl.ds(11, 1), :] = jnp.zeros((1, width), F32)
    for i, row in enumerate((gain_1_total, bias_1_total, gain_2_total, bias_2_total)):
        small_out[pl.ds(12 + i, 1), :] = row
    small_out[pl.ds(18, 6), :] = jnp.zeros((6, width), F32)
    for u in range(utterances):
        at = pl.ds(u * frames, frames)
        mem_copies[u].wait()
        memory_out[at, :] = mem_part[core, at, :] + mem_arrived[at, :]


def decoder_call(
    acoustic, taken, memory, w_query, w_key, w_value, w_out, w_in, w_back, w_vocab, norms,
    fsmn_kernel, rate_table, token_lengths, memory_lengths, rate_groups, glance, targets,
):
    utterances = token_lengths.shape[0]
    tokens, width = acoustic.shape
    slots = tokens // utterances
    mem_rows = memory.shape[0]
    frames = mem_rows // utterances
    half = w_query.shape[1]
    heads = half // HD
    units = w_in.shape[1]
    vocab_here = w_vocab.shape[1]
    half_cols = (vocab_here + 255) // 256 * 128
    main = vocab_here // 128 * 128
    w_tail = jnp.pad(w_vocab[:, main:], ((0, 0), (0, 2 * half_cols - vocab_here)))
    f32 = lambda *shape: jax.ShapeDtypeStruct(shape, F32)
    out_shape = [
        f32(utterances, slots),
        f32(tokens, width),
        f32(mem_rows, width // 2),
        f32(tokens, width),
        f32(24, width),
        f32(width, half_cols),
        f32(width, units),
        f32(width, units),
        f32(width, half),
        f32(width, half),
        f32(width, 2 * half),
    ]
    v32 = lambda *shape: pltpu.VMEM(shape, F32)
    v16 = lambda *shape: pltpu.VMEM(shape, BF16)
    scratch = [
        v16(width, half),
        v16(width, 2 * half),
        v16(half, width),
        v16(width, units),
        v16(units, width),
        v16(width, 2 * half_cols),
        v16(mem_rows, width),
        v16(mem_rows, 2 * half),
        v32(utterances, slots + 16, width),
        v32(tokens, width),
        v32(tokens, width),
        v32(tokens, width),
        v32(utterances, slots, width),
        v16(tokens, width),
        v16(tokens, half),
        v32(utterances, heads, slots, frames),
        v16(tokens, half),
        v16(tokens, width),
        v16(tokens, units),
        v32(tokens, units),
        v16(2, tokens, width),
        v32(2 * half_cols // 128, tokens, 128),
        v16(2 * tokens, half_cols),
        v32(utterances, 2, slots, width),
        v32(2, slots, width),
        v32(utterances, slots, width),
        v32(tokens, width),
        v16(tokens, width),
        v16(tokens, units),
        v16(tokens, width),
        v16(tokens, half),
        v16(mem_rows, 2 * half),
        v32(2, mem_rows, width // 2),
        v32(mem_rows, width // 2),
        v32(2, 8, tokens),
        v32(2, 8, 2 * tokens),
        v32(4, 8, 2 * tokens),
        v32(2 * utterances, slots, width),
        v32(2 * utterances, slots, width),
        v32(2, slots, width),
        pltpu.SemaphoreType.DMA((16,)),
        pltpu.SemaphoreType.DMA((32,)),
        pltpu.SemaphoreType.DMA((32,)),
    ]
    return pl.pallas_call(
        partial(decoder_kernel, vocab_here, half_cols),
        out_shape=out_shape,
        in_specs=[VMEM] * 2 + [ANY] * 9 + [VMEM] * 6 + [SMEM] * 3 + [VMEM] * 2,
        out_specs=[VMEM] * len(out_shape),
        scratch_shapes=scratch,
        compiler_params=pltpu.CompilerParams(
            collective_id=1, has_side_effects=True, vmem_limit_bytes=62 << 20
        ),
    )(
        acoustic, taken, memory, w_query, w_key, w_value, w_out, w_in, w_back, w_vocab, w_tail,
        *[n[None] for n in norms], fsmn_kernel, rate_table,
        token_lengths, memory_lengths, rate_groups,
        glance.reshape(utterances, slots), targets.reshape(utterances, slots),
    )


def scatter_sum_kernel(bits, low_bits, chunks, shared_rows, n_in, *refs):
    ins, small = refs[:n_in], refs[n_in]
    outs, small_out = refs[n_in + 1 : 2 * n_in + 1], refs[2 * n_in + 1]
    scratch = list(refs[2 * n_in + 2 :])
    n_chunks = len(chunks)
    arrived = []
    for _, _, _, order in chunks:
        arrived.append([scratch.pop(0) for _ in order])
    small_arrived, small_sent, send_sem, recv_sem, small_send, small_recv = scratch
    me = lax.axis_index("dp")
    bit_of = {b: lax.rem(me // (1 << b), 2) for b in low_bits + bits}
    peer_of = {b: {"dp": me + (1 - 2 * bit_of[b]) * (1 << b)} for b in low_bits + bits}
    trade = not low_bits

    barrier = pltpu.get_barrier_semaphore()
    for b in low_bits + bits:
        pl.semaphore_signal(barrier, inc=1, device_id=peer_of[b], device_id_type=MESH)
    pl.semaphore_signal(barrier, inc=1, device_id=other_core(), device_id_type=MESH)
    pl.semaphore_wait(barrier, len(low_bits) + len(bits) + 1)

    def pick(c, step, half):
        source, start, width, order = chunks[c]
        rest = sorted([b for b in bits if b not in order[:step]], reverse=True)
        where = tuple(half if b == order[step] else slice(None) for b in rest)
        if step == 0:
            return ins[source], where + (slice(None), pl.ds(start, width))
        return arrived[c][step - 1], where + (slice(None), slice(None))

    def send(c, step):
        b = chunks[c][3][step]
        ref, where = pick(c, step, 1 - bit_of[b])
        copy = pltpu.make_async_remote_copy(
            src_ref=ref.at[where],
            dst_ref=arrived[c][step],
            send_sem=send_sem.at[c, step],
            recv_sem=recv_sem.at[c, step],
            device_id=peer_of[b],
            device_id_type=MESH,
        )
        copy.start()
        return copy

    def take(c, step, copy):
        source, start, width, order = chunks[c]
        ref, where = pick(c, step, bit_of[order[step]])
        copy.wait_recv()
        got = arrived[c][step]
        cols = pl.ds(start, width)
        if source == 0 and trade and step == len(order) - 1:
            outs[0][bit_of[0], :, cols] = ref[where]
            outs[0][1 - bit_of[0], :, cols] = got[...]
        elif step == len(order) - 1:
            outs[source][:, cols] = got[...] + ref[where]
        else:
            got[...] = got[...] + ref[where]

    small_peers = [peer_of[b] for b in low_bits + bits] + [other_core()]
    small_sent[0] = small[...]

    def small_send_step(step):
        copy = pltpu.make_async_remote_copy(
            src_ref=small_sent.at[step],
            dst_ref=small_arrived.at[step],
            send_sem=small_send.at[step],
            recv_sem=small_recv.at[step],
            device_id=small_peers[step],
            device_id_type=MESH,
        )
        copy.start()
        return copy

    def small_take(step, copy):
        copy.wait_recv()
        if step + 1 < len(small_peers):
            small_sent[step + 1] = small_sent[step] + small_arrived[step]
        else:
            small_out[...] = small_sent[step]
            rows = small_out.shape[0] - shared_rows
            small_out[pl.ds(shared_rows, rows)] = (
                small_sent[step, pl.ds(shared_rows, rows)]
                + small_arrived[step, pl.ds(shared_rows, rows)]
            )

    started = []
    small_copy = small_send_step(0)
    small_step = 0
    started.append(small_copy)
    flying = {}
    for c in range(n_chunks):
        flying[c] = send(c, 0)
        started.append(flying[c])
    longest = max(len(order) for _, _, _, order in chunks)
    for wave in range(n_chunks + 2 * (longest - 1)):
        for step in reversed(range(longest)):
            c = wave - 2 * step
            if not 0 <= c < n_chunks or step >= len(chunks[c][3]):
                continue
            take(c, step, flying[c])
            if step + 1 < len(chunks[c][3]):
                flying[c] = send(c, step + 1)
                started.append(flying[c])
        if small_step < len(small_peers):
            small_take(small_step, small_copy)
            small_step += 1
            if small_step < len(small_peers):
                small_copy = small_send_step(small_step)
                started.append(small_copy)
    for copy in started:
        copy.wait_send()


def scatter_sum(parts, small, shared_rows, n_dp):
    nbits = n_dp.bit_length() - 1
    rows = parts[0].shape[0]
    steps = nbits
    while rows >> steps < 8:
        steps -= 1
    low_bits, bits = list(range(nbits - steps)), list(range(nbits - steps, nbits))
    block = rows >> steps
    shaped = [p.reshape((2,) * steps + (block, p.shape[1])) for p in parts]
    swapped = [bits[1], bits[0]] + bits[2:]
    chunks = []
    for i, p in enumerate(parts):
        width = p.shape[1]
        pieces = max(1, width // 512)
        edges = [width // 128 * k // pieces * 128 for k in range(pieces)] + [width]
        for k in range(pieces):
            order = [bits, swapped][len(chunks) % 2]
            if i == 0:
                order = [b for b in bits if b != 0]
                if k % 2:
                    order = order[1:] + order[:1]
                if not low_bits:
                    order = order + [0]
            chunks.append((i, edges[k], edges[k + 1] - edges[k], order))
    scratch = []
    for _, _, width, order in chunks:
        for step in range(len(order)):
            scratch.append(pltpu.VMEM((2,) * (len(bits) - 1 - step) + (block, width), F32))
    n_small = nbits + 1
    scratch += [
        pltpu.VMEM((n_small,) + small.shape, F32),
        pltpu.VMEM((n_small,) + small.shape, F32),
        pltpu.SemaphoreType.DMA((len(chunks), steps)),
        pltpu.SemaphoreType.DMA((len(chunks), steps)),
        pltpu.SemaphoreType.DMA((n_small,)),
        pltpu.SemaphoreType.DMA((n_small,)),
    ]
    out_shape = [jax.ShapeDtypeStruct((block, p.shape[1]), F32) for p in parts]
    if not low_bits:
        out_shape[0] = jax.ShapeDtypeStruct((2,) + out_shape[0].shape, F32)
    out = pl.pallas_call(
        partial(scatter_sum_kernel, bits, low_bits, chunks, shared_rows, len(parts)),
        out_shape=out_shape + [jax.ShapeDtypeStruct(small.shape, F32)],
        in_specs=[VMEM] * (len(parts) + 1),
        out_specs=[VMEM] * (len(parts) + 1),
        scratch_shapes=scratch,
        compiler_params=pltpu.CompilerParams(
            collective_id=4, has_side_effects=True, vmem_limit_bytes=56 << 20
        ),
    )(*shaped, small)
    summed, small_sum = list(out[:-1]), out[-1]
    if low_bits:
        size = 1 << len(low_bits)
        groups = [list(range(g * size, (g + 1) * size)) for g in range(n_dp // size)]
        first = lax.all_to_all(
            summed[0].reshape(2, block // 2, -1), "dp", 0, 0,
            axis_index_groups=[[2 * g, 2 * g + 1] for g in range(n_dp // 2)], tiled=True,
        )
        summed = [first] + [
            lax.psum_scatter(s, "dp", scatter_dimension=0, axis_index_groups=groups, tiled=True)
            for s in summed[1:]
        ]
    vocab = jnp.concatenate([summed[0][0], summed[0][1]], axis=1)
    return [vocab] + summed[1:], small_sum


def per_device(
    acoustic,
    memory,
    embedding,
    w_query,
    w_key,
    w_value,
    w_out,
    w_in,
    w_back,
    w_vocab,
    gain_one,
    bias_one,
    gain_two,
    bias_two,
    fsmn_kernel,
    rate_table,
    token_lengths,
    memory_lengths,
    rate_groups,
    glance_mask,
    targets,
):
    tok_rows, model_width = acoustic.shape
    half = w_query.shape[1]
    (
        token_loss, grad_acoustic, grad_memory, table_terms, small,
        grad_vocab, grad_in, grad_back, grad_query, grad_out, grad_kv,
    ) = decoder_call(
        acoustic, embedding[targets], memory, w_query, w_key, w_value, w_out, w_in, w_back, w_vocab,
        (gain_one, bias_one, gain_two, bias_two), fsmn_kernel, rate_table,
        token_lengths, memory_lengths, rate_groups, glance_mask, targets,
    )
    group_size = lax.axis_size("dp")
    id_columns = jnp.broadcast_to(targets.astype(F32)[:, None], (tok_rows, group_size))
    arrived_rows, arrived_ids = (
        lax.all_to_all(table_terms, "dp", split_axis=1, concat_axis=0, tiled=True),
        lax.all_to_all(id_columns, "dp", split_axis=1, concat_axis=0, tiled=True),
    )
    grad_embedding = jax.ops.segment_sum(
        arrived_rows, arrived_ids[:, 0].astype(jnp.int32), num_segments=embedding.shape[0]
    )
    (grad_vocab, grad_in, grad_back, grad_query, grad_out, grad_kv), small = scatter_sum(
        [grad_vocab, grad_in, grad_back, grad_query, grad_out, grad_kv], small, 16, group_size
    )
    own = model_width // group_size
    grad_rate = small[16:18]
    small = lax.dynamic_slice_in_dim(small, lax.axis_index("dp") * own, own, axis=1)
    return (
        token_loss.reshape(tok_rows),
        grad_acoustic,
        grad_memory,
        grad_embedding,
        grad_query,
        grad_kv[:, :half],
        grad_kv[:, half:],
        grad_out.T,
        grad_in,
        grad_back.T,
        grad_vocab[:, : w_vocab.shape[1]],
        small[12],
        small[13],
        small[14],
        small[15],
        small[: fsmn_kernel.shape[0]],
        grad_rate,
    )


def solution(mesh):
    return jax.shard_map(
        per_device,
        mesh=mesh,
        in_specs=(
            P("dp", None),
            P("dp", None),
            P(),
            P(None, "mp"),
            P(None, "mp"),
            P(None, "mp"),
            P("mp", None),
            P(None, "mp"),
            P("mp", None),
            P(None, "mp"),
            P(),
            P(),
            P(),
            P(),
            P(),
            P(),
            P("dp"),
            P("dp"),
            P("dp"),
            P("dp"),
            P("dp"),
        ),
        out_specs=(
            P("dp"),
            P("dp", None),
            P("dp", "mp"),
            P(None, "dp"),
            P("dp", "mp"),
            P("dp", "mp"),
            P("dp", "mp"),
            P("mp", "dp"),
            P("dp", "mp"),
            P("mp", "dp"),
            P("dp", "mp"),
            P("dp"),
            P("dp"),
            P("dp"),
            P("dp"),
            P(None, "dp"),
            P(),
        ),
        check_vma=False,
    )
```

```python
import math
from types import SimpleNamespace

import jax
import jax.numpy as jnp
from jax import lax
from jax.experimental import pallas as pl
from jax.experimental.pallas import tpu as pltpu
from jax.sharding import PartitionSpec as P

HD = 128
V = 8404
EPSILON = 1e-05
MESH = pl.DeviceIdType.MESH
VMEM = pl.BlockSpec(memory_space=pltpu.VMEM)
SMEM = pl.BlockSpec(memory_space=pltpu.SMEM)
ANY = pl.BlockSpec(memory_space=pl.ANY)
F32, BF16 = jnp.float32, jnp.bfloat16
NEG = -1e30


def other_core():
    return {"mp": 1 - lax.axis_index("mp")}


def dot_nn(a, b):
    return lax.dot_general(a, b, (((1,), (0,)), ((), ())), preferred_element_type=F32)


def dot_nt(a, b):
    return lax.dot_general(a, b, (((1,), (1,)), ((), ())), preferred_element_type=F32)


def dot_tn(a, b):
    return lax.dot_general(a, b, (((0,), (0,)), ((), ())), preferred_element_type=F32)


def normalise(rows):
    average = jnp.mean(rows, axis=-1, keepdims=True)
    centred = rows - average
    variance = jnp.mean(centred * centred, axis=-1, keepdims=True)
    scale = lax.rsqrt(variance + EPSILON)
    return centred * scale, scale


def normalise_back(grad_hat, hat, scale):
    first = jnp.mean(grad_hat, axis=-1, keepdims=True)
    second = jnp.mean(grad_hat * hat, axis=-1, keepdims=True)
    return scale * (grad_hat - first - hat * second)


def to_rows(columns):
    lane = lax.broadcasted_iota(jnp.int32, (columns[0].shape[0], 128), 1)
    tile = jnp.zeros(lane.shape, F32)
    for i, column in enumerate(columns):
        tile = jnp.where(lane == i, column, tile)
    return tile.T[:8]


def to_columns(rows):
    return jnp.concatenate([rows] * 16, axis=0).T


class Planner:
    RATE = 0.0425e6
    HOP = 1.5
    BACKLOG = 12.0

    def __init__(self):
        self.now = 0.0
        self.free = {}
        self.flying = []
        self.waiting = []
        self.started = []
        self.count = 0

    def launch(self, item, step):
        link, size = item.steps[step]
        begin = max(self.now, self.free.get(link, 0.0))
        self.free[link] = begin + size / self.RATE
        copy = item.send(step)
        self.started.append(copy)
        self.count += 1
        self.flying.append((self.free[link] + self.HOP, self.count, item, step, copy))

    def release(self):
        kept = []
        for item in self.waiting:
            link = item.steps[0][0]
            if self.free.get(link, 0.0) - self.now < self.BACKLOG:
                self.launch(item, 0)
            else:
                kept.append(item)
        self.waiting = kept

    def post(self, *items):
        self.waiting += items
        self.release()

    def run_until(self, time):
        while self.flying or self.waiting:
            if not self.flying:
                self.now = max(self.now, min(self.free[i.steps[0][0]] for i in self.waiting))
                self.release()
                continue
            first = min(self.flying, key=lambda f: f[:2])
            if first[0] > time:
                break
            self.flying.remove(first)
            self.now = max(self.now, first[0])
            _, _, item, step, copy = first
            item.take(step, copy)
            if step + 1 < len(item.steps):
                self.launch(item, step + 1)
            self.release()
        if time != math.inf:
            self.now = max(self.now, time)
        self.release()

    def finish(self):
        self.run_until(math.inf)
        for copy in self.started:
            copy.wait_send()


class Chunk:
    def __init__(self, steps, send, take):
        self.steps, self.send, self.take = steps, send, take


def decoder_kernel(
    names,
    vocab_here,
    half_cols,
    table_rows,
    n_dp,
    bits,
    low_bits,
    *refs,
):
    r = SimpleNamespace(**dict(zip(names, refs)))
    acoustic, memory, table, tails = r.acoustic, r.memory, r.table, r.tails
    targets, glance = r.targets, r.glance
    gain_1, bias_1 = r.gain_one[...], r.bias_one[...]
    gain_2, bias_2 = r.gain_two[...], r.bias_two[...]
    kernel_rows, rate_table = r.kernel_rows, r.rate_table
    token_lengths, memory_lengths, rate_groups = r.token_lengths, r.memory_lengths, r.rate_groups
    w_query, w_kv, w_out, w_in, w_back, w_vocab = r.w_query, r.w_kv, r.w_out, r.w_in, r.w_back, r.w_vocab
    mem_low, kv, padded, spare = r.mem_low, r.kv, r.padded, r.spare
    stream_in, stream_one, stream_two, stream_three = r.stream_in, r.stream_one, r.stream_two, r.stream_three
    one_low, queries, probs, mixed = r.one_low, r.queries, r.probs, r.mixed
    norm_low, hidden, gelu_slope, top = r.norm_low, r.hidden, r.gelu_slope, r.top
    logits, grad_logits, part3, arrived3 = r.logits, r.grad_logits, r.part3, r.arrived3
    grad_three, grad_two, branch_low = r.grad_three, r.grad_two, r.branch_low
    grad_pre, att_low, grad_queries = r.grad_pre, r.att_low, r.grad_queries
    mem_arrived, meta, stats, stats_arrived = r.mem_arrived, r.meta, r.stats, r.stats_arrived
    sent, arrived, gathered = r.sent, r.arrived, r.gathered
    small_sent, small_arrived = r.small_sent, r.small_arrived
    terms, term_blocks, term_arrived = grad_three, r.term_blocks, r.term_arrived
    onehot_lo, table_theirs, table_out = r.onehot_lo, r.table_theirs, r.table_out
    swap_send, swap_recv, load_sem = r.swap_send, r.swap_recv, r.load_sem

    utterances, slots = targets.shape
    width = acoustic.shape[1]
    frames = memory.shape[0] // utterances
    half = w_query.shape[1]
    heads = half // HD
    tokens = utterances * slots
    me, core = lax.axis_index("dp"), lax.axis_index("mp")
    side = lax.rem(me, 2)
    sibling = {"mp": 1 - core}
    pair = {"dp": me + 1 - 2 * side}
    cross = {"dp": me + 1 - 2 * side, "mp": 1 - core}
    bit_of = {b: lax.rem(me // (1 << b), 2) for b in low_bits + bits}
    peer_of = {b: {"dp": me + (1 - 2 * bit_of[b]) * (1 << b)} for b in low_bits + bits}
    score_scale = 1.0 / math.sqrt(HD)

    loads = []

    def load(source, target):
        copy = pltpu.make_async_copy(source, target, load_sem.at[len(loads)])
        copy.start()
        loads.append(copy)
        return copy

    load_memory = load(memory, mem_low)
    load_kv = [
        load(r.w_key_hbm, w_kv.at[:, pl.ds(0, half)]),
        load(r.w_value_hbm, w_kv.at[:, pl.ds(half, half)]),
    ]
    load_query = load(r.w_query_hbm, w_query)
    load_out = load(r.w_out_hbm, w_out)

    barrier = pltpu.get_barrier_semaphore()

    def greet(k, carry):
        pl.semaphore_signal(
            barrier, inc=1, device_id={"dp": lax.rem(me + k, n_dp)}, device_id_type=MESH
        )
        return carry

    lax.fori_loop(1, n_dp, greet, 0)
    for device in (sibling, cross):
        pl.semaphore_signal(barrier, inc=1, device_id=device, device_id_type=MESH)

    load_in = load(r.w_in_hbm, w_in)
    load_back = load(r.w_back_hbm, w_back)
    block = 1024
    per_core = table_rows // (2 * block)
    mains = 2 * per_core * block

    def load_table(k):
        at = pl.ds(pl.multiple_of((core * per_core + k) * block, block), block)
        return load(table.at[at, :], spare.at[pl.ds(k % 2 * block, block), :])

    table_loads = [load_table(0), load_table(1)]
    tail_rows = tails.shape[0] - 256
    main = w_vocab.shape[0] - tail_rows
    load_vocab = [
        load(r.w_vocab_hbm.at[pl.ds(0, main), :], w_vocab.at[pl.ds(0, main), :]),
        load(tails.at[pl.ds(0, tail_rows), :], w_vocab.at[pl.ds(main, tail_rows), :]),
    ]

    swaps = []

    def swap(source, target, device):
        k = len(swaps)
        copy = pltpu.make_async_remote_copy(
            src_ref=source,
            dst_ref=target,
            send_sem=swap_send.at[k],
            recv_sem=swap_recv.at[k],
            device_id=device,
            device_id_type=MESH,
        )
        copy.start()
        swaps.append(copy)
        return copy

    lane = lax.broadcasted_iota(jnp.int32, (1, slots), 1)
    row_of = lax.broadcasted_iota(jnp.int32, (8, slots), 0)
    for u in range(utterances):
        target_row = targets[pl.ds(u, 1), :].astype(F32)
        glance_row = glance[pl.ds(u, 1), :].astype(F32)
        valid_row = (lane < token_lengths[u]).astype(F32)
        meta[0, :, pl.ds(u * slots, slots)] = jnp.where(
            row_of == 0, target_row, jnp.where(row_of == 1, valid_row, glance_row)
        )
    own_columns = to_columns(meta[0])
    own_target = own_columns[:, 0:1]
    own_valid = own_columns[:, 1:2]

    def rows(u):
        return pl.ds(u * slots, slots)

    load_memory.wait()
    for copy in load_kv:
        copy.wait()
    step_rows = 256
    row_chunks = frames // step_rows

    def kv_step(i, carry):
        at = pl.ds(pl.multiple_of(i * step_rows, step_rows), step_rows)
        group = jnp.zeros((1, width), jnp.int32) + rate_groups[i // row_chunks]
        rate_row = jnp.where(group == 1, rate_table[pl.ds(1, 1), :], rate_table[pl.ds(0, 1), :])
        low = (mem_low[at, :].astype(F32) + rate_row).astype(BF16)
        mem_low[at, :] = low
        kv[at, :] = dot_nn(low, w_kv[...]).astype(BF16)
        return carry

    lax.fori_loop(0, utterances * row_chunks, kv_step, 0)

    edge = jnp.zeros((8, width), F32)
    for u in range(utterances):
        padded[u, pl.ds(0, 8), :] = edge
        padded[u, pl.ds(8 + slots, 8), :] = edge

    pl.semaphore_wait(barrier, n_dp + 1)
    meta_swap = swap(meta.at[0], meta.at[1], pair)
    load_query.wait()
    load_out.wait()

    def key_of(u, h):
        return kv[pl.ds(u * frames, frames), pl.ds(h * HD, HD)]

    def value_of(u, h):
        return kv[pl.ds(u * frames, frames), pl.ds(half + h * HD, HD)]

    frame_lane = lax.broadcasted_iota(jnp.int32, (1, frames), 1)

    def look_up(first_row, count, allowed, source):
        ids = first_row + lax.broadcasted_iota(jnp.int32, (1, count), 1)
        local = jnp.where(allowed, own_target.astype(jnp.int32), -1)
        onehot = jnp.where(ids == local, 1.0, 0.0).astype(BF16)
        return dot_nn(onehot, source)

    def look_up_block(k):
        table_loads[k].wait()
        part = look_up(
            (core * per_core + k) * block, block, True, spare[pl.ds(k % 2 * block, block), :]
        )
        for u in range(utterances):
            piece = part[u * slots : (u + 1) * slots]
            part3[0, u] = piece if k == 0 else part3[0, u] + piece
        if k + 2 < per_core:
            table_loads.append(load_table(k + 2))

    def look_up_rest():
        part = look_up(mains, 256, core == 0, tails[pl.ds(tail_rows, 256), :])
        for u in range(utterances):
            part3[0, u] = part3[0, u] + part[u * slots : (u + 1) * slots]

    def local_targets(target_column):
        local = target_column.astype(jnp.int32) - core * vocab_here
        return jnp.where((local >= 0) & (local < vocab_here), local, -1)

    def vocab_tile(tile, first, col, target, top_m, picked):
        ids = col + lax.broadcasted_iota(jnp.int32, (1, 128), 1)
        tile = jnp.where(ids < vocab_here, tile, NEG)
        logits[first] = tile
        return jnp.maximum(top_m, tile), picked + jnp.where(ids == target, tile, 0.0)

    def vocab_stats(g, target, base, wide, narrow, first):
        start = (jnp.full((tokens, 128), NEG, F32), jnp.zeros((tokens, 128), F32))

        def step(j, carry):
            col = pl.multiple_of(base + j * 256, 128)
            product = dot_nt(top[g], w_vocab[pl.ds(col, 256), :])
            carry = vocab_tile(product[:, :128], first + 2 * j, col, target, *carry)
            return vocab_tile(product[:, 128:], first + 2 * j + 1, col + 128, target, *carry)

        top_m, picked = lax.fori_loop(0, wide, step, start)
        if narrow:
            col = pl.multiple_of(base + wide * 256, 128)
            product = dot_nt(top[g], w_vocab[pl.ds(col, 128), :])
            top_m, picked = vocab_tile(product, first + 2 * wide, col, target, top_m, picked)
        top_row = jnp.max(top_m, axis=1, keepdims=True)

        def add(j, total):
            return total + jnp.exp(logits[first + j] - top_row)

        total = lax.fori_loop(0, 2 * wide + narrow, add, jnp.zeros((tokens, 128), F32))
        return (
            top_row,
            jnp.sum(total, axis=1, keepdims=True),
            jnp.sum(picked, axis=1, keepdims=True),
        )

    def join(blocks):
        top_value = blocks[0][0:1]
        for b in blocks[1:]:
            top_value = jnp.maximum(top_value, b[0:1])
        total, picked = 0.0, 0.0
        for b in blocks:
            total = total + b[1:2] * jnp.exp(b[0:1] - top_value)
            picked = picked + b[2:3]
        return top_value + jnp.log(total), picked

    def forward(second, beside_one=None, beside_two=None):
        copies = []
        for u in range(utterances):
            at = rows(u)
            valid = own_valid[u * slots : (u + 1) * slots]
            hat, _ = normalise(stream_in[at, :])
            padded[u, pl.ds(8, slots), :] = (hat * gain_1 + bias_1) * valid
            for j in range(width // 128):
                cols = pl.ds(j * 128, 128)
                total = jnp.zeros((slots, 128), F32)
                for k in range(kernel_rows.shape[0]):
                    shift = 8 + k - kernel_rows.shape[0] // 2
                    total = total + kernel_rows[pl.ds(k, 1), cols] * padded[u, pl.ds(shift, slots), cols]
                stream_one[at, cols] = stream_in[at, cols] + total * valid
            low = stream_one[at, :].astype(BF16)
            one_low[at, :] = low
            queries[at, :] = dot_nn(low, w_query[...]).astype(BF16)
            frame_ok = frame_lane < memory_lengths[u]
            for h in range(heads):
                cols = pl.ds(h * HD, HD)
                scores = dot_nt(queries[at, cols], key_of(u, h)) * score_scale
                scores = jnp.where(frame_ok, scores, NEG)
                raised = jnp.exp(scores - jnp.max(scores, axis=-1, keepdims=True))
                prob = raised / jnp.sum(raised, axis=-1, keepdims=True)
                if second:
                    probs[u, h] = prob
                mixed[at, cols] = dot_nn(prob.astype(BF16), value_of(u, h)).astype(BF16)
            sent[u] = dot_nn(mixed[at, :], w_out[...])
            copies.append(swap(sent.at[u], arrived.at[u], sibling))
        if not second:
            beside_one()
            load_in.wait()
            load_back.wait()
        ff_copies = []
        for u in range(utterances):
            at = rows(u)
            copies[u].wait()
            two = stream_one[at, :] + (sent[u] + arrived[u])
            stream_two[at, :] = two
            hat, _ = normalise(two)
            low = (hat * gain_2 + bias_2).astype(BF16)
            norm_low[at, :] = low
            pre = dot_nn(low, w_in[...])
            phi = 0.5 * (1.0 + lax.erf(pre * math.sqrt(0.5)))
            hidden[at, :] = (pre * phi).astype(BF16)
            if second:
                gelu_slope[at, :] = phi + pre * (
                    jnp.exp(-0.5 * pre * pre) * (1.0 / math.sqrt(2.0 * math.pi))
                )
            sent[utterances + u] = dot_nn(hidden[at, :], w_back[...])
            ff_copies.append(swap(sent.at[utterances + u], arrived.at[utterances + u], sibling))
        if not second:
            beside_two()
        for u in range(utterances):
            at = rows(u)
            ff_copies[u].wait()
            three = stream_two[at, :] + (sent[utterances + u] + arrived[utterances + u])
            stream_three[u] = three
            top[0, at, :] = three.astype(BF16)

    stream_in[...] = acoustic[...].astype(F32)

    def beside_one():
        look_up_block(0)
        look_up_block(1)

    def beside_two():
        for k in range(2, per_core):
            look_up_block(k)
        look_up_rest()

    forward(False, beside_one, beside_two)
    table_swap = swap(part3.at[0], arrived3, sibling)
    for copy in load_vocab:
        copy.wait()
    first = vocab_stats(0, local_targets(own_target), 0, w_vocab.shape[0] // 256, 0, 0)
    stats[0, :, pl.ds(0, tokens)] = to_rows(first)
    first_swap = swap(stats.at[0, :, pl.ds(0, tokens)], stats_arrived.at[0, :, pl.ds(0, tokens)], sibling)
    table_swap.wait()
    first_swap.wait()
    log_total, picked = join([stats[0, :, :tokens], stats_arrived[0, :, :tokens]])
    first_loss = (log_total - picked) * meta[0, 1:2, :]
    blend_row = meta[0, 2:3, :] * meta[0, 1:2, :] / (1.0 + jnp.exp(math.log(V) - first_loss))
    blend = to_columns(jnp.concatenate([blend_row] * 8, axis=0))[:, 0:1]
    for u in range(utterances):
        at = rows(u)
        wide_acoustic = acoustic[at, :].astype(F32)
        taken = part3[0, u] + arrived3[u]
        stream_in[at, :] = wide_acoustic + blend[u * slots : (u + 1) * slots] * (taken - wide_acoustic)

    forward(True)
    token_swap = swap(stream_three.at[core], gathered.at[0], pair)
    base = side * half_cols
    wide, narrow = half_cols // 256, half_cols % 256 // 128
    per_group = 2 * wide + narrow
    meta_swap.wait()
    pair_columns = to_columns(meta[1])
    group_target = [local_targets(own_target), local_targets(pair_columns[:, 0:1])]
    group_valid = [own_valid, pair_columns[:, 1:2]]
    own_stats = vocab_stats(0, group_target[0], base, wide, narrow, 0)
    stats[1, :, pl.ds(0, tokens)] = to_rows(own_stats)
    token_swap.wait()
    share_swap = swap(gathered.at[0], gathered.at[1], sibling)
    at_core = pl.ds(pl.multiple_of(core * slots, slots), slots)
    at_other = pl.ds(pl.multiple_of((1 - core) * slots, slots), slots)
    top[1, at_core, :] = gathered[0].astype(BF16)
    share_swap.wait()
    top[1, at_other, :] = gathered[1].astype(BF16)
    pair_stats = vocab_stats(1, group_target[1], base, wide, narrow, per_group)
    stats[1, :, pl.ds(tokens, tokens)] = to_rows(pair_stats)
    stat_swaps = [
        swap(stats.at[1], stats_arrived.at[1], sibling),
        swap(stats.at[1], stats_arrived.at[2], pair),
        swap(stats.at[1], stats_arrived.at[3], cross),
    ]
    for copy in stat_swaps:
        copy.wait()

    def group_blocks(g):
        mine, theirs = pl.ds(g * tokens, tokens), pl.ds((1 - g) * tokens, tokens)
        return [
            stats[1, :, mine],
            stats_arrived[1, :, mine],
            stats_arrived[2, :, theirs],
            stats_arrived[3, :, theirs],
        ]

    log_totals = []
    for g in range(2):
        log_total, picked = join(group_blocks(g))
        log_totals.append(to_columns(jnp.concatenate([log_total] * 8, axis=0))[:, 0:1])
        if g == 0:
            loss = (log_total - picked) * meta[0, 1:2, :]
            for u in range(utterances):
                r.loss_out[pl.ds(u, 1), :] = loss[:, u * slots : (u + 1) * slots]

    plan = Planner()
    steps_all = len(bits)
    trade = not low_bits
    scatter_send, scatter_recv = r.scatter_send, r.scatter_recv

    def make_chunk(index):
        name, start, cols, order = chunk_list(half_cols, width, bits, low_bits, r)[index]
        source, landing = getattr(r, "src_" + name), r.landing[index]
        out = getattr(r, name + "_out")
        rows_here = source.shape[-2]

        def pick(step, which):
            rest = sorted([b for b in bits if b not in order[:step]], reverse=True)
            where = tuple(which if b == order[step] else slice(None) for b in rest)
            if step == 0:
                return source, where + (slice(None), pl.ds(start, cols))
            return landing[step - 1], where + (slice(None), slice(None))

        def send(step):
            b = order[step]
            ref, where = pick(step, 1 - bit_of[b])
            copy = pltpu.make_async_remote_copy(
                src_ref=ref.at[where],
                dst_ref=landing[step],
                send_sem=scatter_send.at[index, step],
                recv_sem=scatter_recv.at[index, step],
                device_id=peer_of[b],
                device_id_type=MESH,
            )
            copy.start()
            return copy

        def take(step, copy):
            copy.wait_recv()
            ref, where = pick(step, bit_of[order[step]])
            got = landing[step]
            at = pl.ds(start, cols)
            last = step == len(order) - 1
            if last and name == "vocab" and trade:
                out[bit_of[0], :, at] = ref[where]
                out[1 - bit_of[0], :, at] = got[...]
            elif last:
                out[:, at] = got[...] + ref[where]
            else:
                got[...] = got[...] + ref[where]

        steps = [
            (link_of(b, bits), rows_here * cols * 4 * 2 ** (steps_all - 1 - s))
            for s, b in enumerate(order)
        ]
        return Chunk(steps, send, take)

    chunks = {}
    for index, (name, start, _, _) in enumerate(chunk_list(half_cols, width, bits, low_bits, r)):
        chunks[name, start] = make_chunk(index)

    def put(name, at, product):
        source = getattr(r, "src_" + name)
        source[..., at] = product.reshape(source.shape[:-1] + (product.shape[1],))

    for g in (1, 0):
        log_column, valid, target = log_totals[g], group_valid[g], group_target[g]

        def slope(j, carry):
            col = pl.multiple_of(j * 128, 128)
            ids = base + col + lax.broadcasted_iota(jnp.int32, (1, 128), 1)
            onehot = jnp.where(ids == target, 1.0, 0.0)
            grad = (jnp.exp(logits[g * per_group + j] - log_column) - onehot) * valid
            grad_logits[pl.ds(g * tokens, tokens), pl.ds(col, 128)] = grad.astype(BF16)
            return carry

        lax.fori_loop(0, per_group, slope, 0)
        part = dot_nn(
            grad_logits[pl.ds(g * tokens, tokens), :],
            w_vocab[pl.ds(pl.multiple_of(base, 128), half_cols), :],
        )
        for u in range(utterances):
            part3[u, g] = part[u * slots : (u + 1) * slots]
    three_swap = swap(part3.at[1 - core], arrived3, sibling)
    top_all = jnp.concatenate([top[0], top[1]], axis=0)
    vocab_starts = sorted(start for name, start in chunks if name == "vocab")
    pair_swap = None
    for i, start in enumerate(vocab_starts):
        stop = (vocab_starts + [half_cols])[i + 1]
        for col in range(start, stop, 256):
            at = pl.ds(col, min(256, stop - col))
            put("vocab", at, dot_tn(top_all, grad_logits[:, at]))
        plan.run_until(1.0 * i)
        plan.post(chunks["vocab", start])
        if pair_swap is None:
            three_swap.wait()
            sent[0] = part3[core, 1] + arrived3[1]
            pair_swap = swap(sent.at[0], arrived.at[0], pair)
            plan.free[link_of(0, bits)] = plan.now + 6.0
    pair_swap.wait()
    grad_three[core] = (part3[core, 0] + arrived3[0]) + arrived[0]
    share_three = swap(grad_three.at[core], arrived.at[1], sibling)
    plan.run_until(9.0)
    share_three.wait()
    grad_three[1 - core] = arrived[1]

    copies = []
    for u in range(utterances):
        at = rows(u)
        low = grad_three[u].astype(BF16)
        branch_low[at, :] = low
        pre = (dot_nt(low, w_back[...]) * gelu_slope[at, :]).astype(BF16)
        grad_pre[at, :] = pre
        sent[utterances + u] = dot_nt(pre, w_in[...])
        copies.append(swap(sent.at[utterances + u], arrived.at[utterances + u], sibling))
    plan.run_until(13.0)
    for name, left, right in (("back", branch_low, hidden), ("in", norm_low, grad_pre)):
        for start in sorted(s for n, s in chunks if n == name):
            at = pl.ds(start, 512)
            put(name, at, dot_tn(left[...], right[:, at]))
            plan.post(chunks[name, start])
    plan.run_until(15.0)

    one_copies = []
    gain_2_total, bias_2_total = 0.0, 0.0
    for u in range(utterances):
        at = rows(u)
        copies[u].wait()
        grad_norm = sent[utterances + u] + arrived[utterances + u]
        hat, scale = normalise(stream_two[at, :])
        gain_2_total = gain_2_total + jnp.sum(grad_norm * hat, axis=0, keepdims=True)
        bias_2_total = bias_2_total + jnp.sum(grad_norm, axis=0, keepdims=True)
        two = grad_three[u] + normalise_back(grad_norm * gain_2, hat, scale)
        grad_two[at, :] = two
        low = two.astype(BF16)
        att_low[at, :] = low
        grad_mixed = dot_nt(low, w_out[...]).astype(BF16)
        for h in range(heads):
            cols = pl.ds(h * HD, HD)
            grad_head = grad_mixed[:, h * HD : (h + 1) * HD]
            prob = probs[u, h]
            grad_prob = dot_nt(grad_head, value_of(u, h))
            spare[pl.ds(u * frames, frames), pl.ds(half + h * HD, HD)] = dot_tn(
                prob.astype(BF16), grad_head
            ).astype(BF16)
            inner = jnp.sum(prob * grad_prob, axis=-1, keepdims=True)
            grad_score = (prob * (grad_prob - inner)).astype(BF16)
            grad_queries[at, cols] = (dot_nn(grad_score, key_of(u, h)) * score_scale).astype(BF16)
            spare[pl.ds(u * frames, frames), cols] = (
                dot_tn(grad_score, queries[at, cols]) * score_scale
            ).astype(BF16)
            plan.run_until(17.0 + 2.0 * (heads * u + h))
        sent[u] = dot_nt(grad_queries[at, :], w_query[...])
        one_copies.append(swap(sent.at[u], arrived.at[u], sibling))
    every = slice(None)
    put("out", every, dot_tn(att_low[...], mixed[...]))
    plan.post(chunks["out", 0])
    put("query", every, dot_tn(one_low[...], grad_queries[...]))
    plan.post(chunks["query", 0])
    plan.run_until(25.0)

    mem_copies = []
    rate_sums = [0.0, 0.0]
    for u in range(utterances):
        total = jnp.zeros((1, width), F32)
        for i in range(row_chunks):
            at = pl.ds(u * frames + i * step_rows, step_rows)
            part = dot_nt(spare[at, :], w_kv[...])
            for j in range(width // 128):
                side_of, tile = j // (width // 256), j % (width // 256)
                index = ((side_of * utterances + u) * row_chunks + i) * (width // 256) + tile
                logits[index] = part[:, j * 128 : (j + 1) * 128]
            total = total + jnp.sum(part, axis=0, keepdims=True)
        tiles = row_chunks * (width // 256)
        mem_copies.append(
            swap(
                logits.at[pl.ds(((1 - core) * utterances + u) * tiles, tiles)],
                mem_arrived.at[pl.ds(u * tiles, tiles)],
                sibling,
            )
        )
        group = jnp.zeros((1, width), jnp.int32) + rate_groups[u]
        for k in range(2):
            rate_sums[k] = rate_sums[k] + jnp.where((group == 1) == (k == 1), total, 0.0)
        plan.run_until(26.5 + 1.5 * u)
    for start in sorted(s for n, s in chunks if n == "kv"):
        at = pl.ds(start, 256)
        put("kv", at, dot_tn(mem_low[...], spare[:, at]))
        plan.post(chunks["kv", start])
        plan.run_until(29.0 + start / 256)

    gain_1_total, bias_1_total = 0.0, 0.0
    for u in range(utterances):
        at = rows(u)
        valid = own_valid[u * slots : (u + 1) * slots]
        one_copies[u].wait()
        one = grad_two[at, :] + (sent[u] + arrived[u])
        grad_two[at, :] = one
        masked = one * valid
        for k in range(kernel_rows.shape[0]):
            shift = 8 + k - kernel_rows.shape[0] // 2
            row = jnp.sum(masked * padded[u, pl.ds(shift, slots), :], axis=0, keepdims=True)
            if u == 0:
                small_sent[0, pl.ds(k, 1), :] = row
            else:
                small_sent[0, pl.ds(k, 1), :] = small_sent[0, pl.ds(k, 1), :] + row
        padded[u, pl.ds(8, slots), :] = masked
        for j in range(width // 128):
            cols = pl.ds(j * 128, 128)
            total = jnp.zeros((slots, 128), F32)
            for k in range(kernel_rows.shape[0]):
                shift = 8 - k + kernel_rows.shape[0] // 2
                total = total + kernel_rows[pl.ds(k, 1), cols] * padded[u, pl.ds(shift, slots), cols]
            stream_one[at, cols] = total * valid
        grad_norm = stream_one[at, :]
        hat, scale = normalise(stream_in[at, :])
        gain_1_total = gain_1_total + jnp.sum(grad_norm * hat, axis=0, keepdims=True)
        bias_1_total = bias_1_total + jnp.sum(grad_norm, axis=0, keepdims=True)
        zero = grad_two[at, :] + normalise_back(grad_norm * gain_1, hat, scale)
        terms[u] = blend[u * slots : (u + 1) * slots] * zero
        r.acoustic_out[at, :] = zero - terms[u]
        plan.run_until(32.0 + 2.0 * u)

    last_taps = kernel_rows.shape[0]
    small_sent[0, pl.ds(last_taps, 12 - last_taps), :] = jnp.zeros((12 - last_taps, width), F32)
    for i, row in enumerate((gain_1_total, bias_1_total, gain_2_total, bias_2_total)):
        small_sent[0, pl.ds(12 + i, 1), :] = row
    for k in range(2):
        small_sent[0, pl.ds(16 + k, 1), :] = rate_sums[k]
    small_sent[0, pl.ds(18, 6), :] = jnp.zeros((6, width), F32)
    small_peers = [peer_of[b] for b in low_bits + bits] + [sibling]

    def small_send(step):
        copy = pltpu.make_async_remote_copy(
            src_ref=small_sent.at[step],
            dst_ref=small_arrived.at[step],
            send_sem=r.small_send.at[step],
            recv_sem=r.small_recv.at[step],
            device_id=small_peers[step],
            device_id_type=MESH,
        )
        copy.start()
        return copy

    def small_take(step, copy):
        copy.wait_recv()
        if step + 1 < len(small_peers):
            small_sent[step + 1] = small_sent[step] + small_arrived[step]
        else:
            r.small_out[pl.ds(0, 16), :] = small_sent[step, pl.ds(0, 16), :]
            r.small_out[pl.ds(16, 8), :] = (
                small_sent[step, pl.ds(16, 8), :] + small_arrived[step, pl.ds(16, 8), :]
            )

    small_links = [link_of(b, bits) for b in low_bits + bits] + ["core"]
    plan.post(Chunk([(l, 24 * width * 4) for l in small_links], small_send, small_take))

    features = width // n_dp
    feature_rows = max(features, 8)
    block_rows = term_blocks.shape[1]
    turned = terms[core].T
    id_row = targets[pl.ds(core, 1), :].astype(F32)
    rest = block_rows - features - 1
    for p in range(n_dp):
        term_blocks[p, pl.ds(0, features), :] = turned[p * features : (p + 1) * features]
        term_blocks[p, pl.ds(features, 1), :] = id_row
        term_blocks[p, pl.ds(features + 1, rest), :] = jnp.zeros((rest, slots), F32)

    def term_copy(k):
        there = lax.rem(me + k, n_dp)
        return pltpu.make_async_remote_copy(
            src_ref=term_blocks.at[there],
            dst_ref=term_arrived.at[me],
            send_sem=r.term_send.at[k],
            recv_sem=r.term_recv.at[k],
            device_id={"dp": there},
            device_id_type=MESH,
        )

    def term_start(k, carry):
        term_copy(k).start()
        return carry

    def term_wait(k, carry):
        term_copy(k).wait()
        return carry

    term_arrived[me] = term_blocks[me]
    lax.fori_loop(1, n_dp, term_start, 0)
    for u in range(utterances):
        mem_copies[u].wait()
        for i in range(row_chunks):
            for j in range(width // 256):
                index = (u * row_chunks + i) * (width // 256) + j
                first_tile = (core * utterances) * row_chunks * (width // 256)
                r.memory_out[pl.ds(u * frames + i * step_rows, step_rows), pl.ds(j * 128, 128)] = (
                    logits[first_tile + index] + mem_arrived[index]
                )
    plan.run_until(45.0)
    lax.fori_loop(1, n_dp, term_wait, 0)
    per_piece = 512 // slots
    blocks_hi = table_out.shape[1] // 256
    batch = 4

    def table_piece(p, fresh):
        found = [term_arrived[p * per_piece + i] for i in range(per_piece)]
        values = jnp.concatenate([f[:feature_rows] for f in found], axis=1)
        ids = jnp.concatenate([f[features : features + 1] for f in found], axis=1).astype(jnp.int32)
        low_ids, high_ids = ids & 255, ids >> 8
        onehot_lo[...] = jnp.where(
            lax.broadcasted_iota(jnp.int32, (256, 512), 0) == low_ids, 1.0, 0.0
        ).astype(BF16)
        coarse = values.astype(BF16).astype(F32)
        both = jnp.concatenate([coarse, values - coarse], axis=0)
        for first_hi in range(0, blocks_hi, batch):
            here = range(first_hi, min(first_hi + batch, blocks_hi))
            masked = jnp.concatenate([jnp.where(high_ids == hi, both, 0.0) for hi in here], axis=0)
            product = dot_nt(masked.astype(BF16), onehot_lo[...])
            for i, hi in enumerate(here):
                top_part = product[2 * i * feature_rows : (2 * i + 1) * feature_rows]
                low_part = product[(2 * i + 1) * feature_rows : (2 * i + 2) * feature_rows]
                at = pl.ds(hi * 256, 256)
                if fresh:
                    table_out[:, at] = top_part + low_part
                else:
                    table_out[:, at] = table_out[:, at] + (top_part + low_part)

    pieces = n_dp // per_piece
    table_piece(0, True)
    if pieces <= 4:
        for p in range(1, pieces):
            plan.run_until(45.0 + 1.5 * p)
            table_piece(p, False)
    else:
        lax.fori_loop(1, pieces, lambda p, c: (table_piece(p, False), c)[1], 0)
    table_swap = swap(table_out, table_theirs, sibling)
    plan.run_until(56.0)
    table_swap.wait()
    table_out[...] = table_out[...] + table_theirs[...]
    plan.finish()


def link_of(bit, bits):
    if bit == bits[-1]:
        return bits[-2]
    return bit


def chunk_list(half_cols, width, bits, low_bits, sizes):
    own = [b for b in bits if b != 0]
    turned = own[1:] + own[:1]
    last = [] if low_bits else [0]
    listing = []
    edges = [half_cols // 128 * k // 4 * 128 for k in range(4)] + [half_cols]
    for k in range(4):
        order = turned if k == 1 else own
        listing.append(("vocab", edges[k], edges[k + 1] - edges[k], order + last))
    units = sizes.units
    for name in ("back", "in"):
        for start in range(0, units, 512):
            listing.append((name, start, 512, bits))
    half = sizes.half
    listing.append(("out", 0, half, bits))
    listing.append(("query", 0, half, bits))
    for start in range(0, 2 * half, 256):
        listing.append(("kv", start, 256, bits))
    return listing


def decoder_call(
    acoustic, memory, embedding, w_query, w_key, w_value, w_out, w_in, w_back, w_vocab, norms,
    fsmn_kernel, rate_table, token_lengths, memory_lengths, rate_groups, glance, targets, n_dp,
):
    utterances = token_lengths.shape[0]
    tokens, width = acoustic.shape
    slots = tokens // utterances
    mem_rows = memory.shape[0]
    half = w_query.shape[1]
    heads = half // HD
    frames = mem_rows // utterances
    units = w_in.shape[1]
    vocab_here = w_vocab.shape[1]
    table_rows = embedding.shape[0]
    half_cols = (vocab_here + 255) // 256 * 128
    w_turned = w_vocab.T
    main = vocab_here // 256 * 256
    mains = table_rows // 2048 * 2048
    tails = jnp.concatenate(
        [
            jnp.pad(w_turned[main:], ((0, 2 * half_cols - vocab_here), (0, 0))),
            jnp.pad(embedding[mains:], ((0, 256 - table_rows + mains), (0, 0))),
        ]
    )
    nbits = n_dp.bit_length() - 1
    steps = nbits
    while width >> steps < 8:
        steps -= 1
    low_bits, bits = list(range(nbits - steps)), list(range(nbits - steps, nbits))
    rows = width >> steps
    features = width // n_dp
    feature_rows = max(features, 8)
    block_rows = feature_rows + 8 if features >= 8 else 8
    blocks_hi = (table_rows + 255) // 256
    sizes = SimpleNamespace(units=units, half=half)
    listing = chunk_list(half_cols, width, bits, low_bits, sizes)
    most = max(len(c[3]) for c in listing)

    f32 = lambda *shape: jax.ShapeDtypeStruct(shape, F32)
    v32 = lambda *shape: pltpu.VMEM(shape, F32)
    v16 = lambda *shape: pltpu.VMEM(shape, BF16)
    dma = lambda *shape: pltpu.SemaphoreType.DMA(shape)
    inputs = dict(
        acoustic=(VMEM, acoustic),
        tails=(VMEM, tails),
        memory=(ANY, memory),
        table=(ANY, embedding),
        w_query_hbm=(ANY, w_query),
        w_key_hbm=(ANY, w_key),
        w_value_hbm=(ANY, w_value),
        w_out_hbm=(ANY, w_out),
        w_in_hbm=(ANY, w_in),
        w_back_hbm=(ANY, w_back),
        w_vocab_hbm=(ANY, w_turned),
        gain_one=(VMEM, norms[0][None]),
        bias_one=(VMEM, norms[1][None]),
        gain_two=(VMEM, norms[2][None]),
        bias_two=(VMEM, norms[3][None]),
        kernel_rows=(VMEM, fsmn_kernel),
        rate_table=(VMEM, rate_table),
        token_lengths=(SMEM, token_lengths),
        memory_lengths=(SMEM, memory_lengths),
        rate_groups=(SMEM, rate_groups),
        glance=(VMEM, glance.reshape(utterances, slots)),
        targets=(VMEM, targets.reshape(utterances, slots)),
    )
    outputs = dict(
        loss_out=f32(utterances, slots),
        acoustic_out=f32(tokens, width),
        memory_out=f32(mem_rows, width // 2),
        table_out=f32(feature_rows, blocks_hi * 256),
        small_out=f32(24, width),
        vocab_out=f32(*(() if low_bits else (2,)), rows, half_cols),
        in_out=f32(rows, units),
        back_out=f32(rows, units),
        query_out=f32(rows, half),
        out_out=f32(rows, half),
        kv_out=f32(rows, 2 * half),
    )
    shape = (2,) * steps + (rows,)
    scratch = dict(
        w_query=v16(width, half),
        w_kv=v16(width, 2 * half),
        w_out=v16(half, width),
        w_in=v16(width, units),
        w_back=v16(units, width),
        w_vocab=v16(2 * half_cols, width),
        mem_low=v16(mem_rows, width),
        kv=v16(mem_rows, 2 * half),
        spare=v16(mem_rows, 2 * half),
        padded=v32(utterances, slots + 16, width),
        stream_in=v32(tokens, width),
        stream_one=v32(tokens, width),
        stream_two=v32(tokens, width),
        stream_three=v32(utterances, slots, width),
        one_low=v16(tokens, width),
        queries=v16(tokens, half),
        probs=v32(utterances, heads, slots, frames),
        mixed=v16(tokens, half),
        norm_low=v16(tokens, width),
        hidden=v16(tokens, units),
        gelu_slope=v32(tokens, units),
        top=v16(2, tokens, width),
        logits=v32(2 * half_cols // 128, tokens, 128),
        grad_logits=v16(2 * tokens, half_cols),
        part3=v32(utterances, 2, slots, width),
        arrived3=v32(2, slots, width),
        grad_three=v32(utterances, slots, width),
        grad_two=v32(tokens, width),
        branch_low=v16(tokens, width),
        grad_pre=v16(tokens, units),
        att_low=v16(tokens, width),
        grad_queries=v16(tokens, half),
        mem_arrived=v32(mem_rows // 256 * (width // 256), 256, 128),
        meta=v32(2, 8, tokens),
        stats=v32(2, 8, 2 * tokens),
        stats_arrived=v32(4, 8, 2 * tokens),
        sent=v32(2 * utterances, slots, width),
        arrived=v32(2 * utterances, slots, width),
        gathered=v32(2, slots, width),
        small_sent=v32(nbits + 1, 24, width),
        small_arrived=v32(nbits + 1, 24, width),
        term_blocks=v32(n_dp, block_rows, slots),
        term_arrived=v32(n_dp, block_rows, slots),
        onehot_lo=v16(256, 512),
        table_theirs=v32(feature_rows, blocks_hi * 256),
        src_vocab=v32(*shape, half_cols),
        src_back=v32(*shape, units),
        src_in=v32(*shape, units),
        src_out=v32(*shape, half),
        src_query=v32(*shape, half),
        src_kv=v32(*shape, 2 * half),
        load_sem=dma(24),
        swap_send=dma(40),
        swap_recv=dma(40),
        scatter_send=dma(len(listing), most),
        scatter_recv=dma(len(listing), most),
        small_send=dma(nbits + 1),
        small_recv=dma(nbits + 1),
        term_send=dma(n_dp),
        term_recv=dma(n_dp),
    )
    landing = [
        [v32(*(2,) * (steps - 1 - s), rows, cols) for s in range(len(order))]
        for _, _, cols, order in listing
    ]
    names = list(inputs) + list(outputs) + list(scratch)
    flat = [ref for chunk in landing for ref in chunk]

    def kernel(*refs):
        named, rest = refs[: len(names)], list(refs[len(names) :])
        lands = [[rest.pop(0) for _ in chunk] for chunk in landing]
        decoder_kernel(
            names + ["landing", "units", "half"], vocab_here, half_cols, table_rows, n_dp, bits,
            low_bits, *named, lands, units, half,
        )

    out = pl.pallas_call(
        kernel,
        out_shape=list(outputs.values()),
        in_specs=[spec for spec, _ in inputs.values()],
        out_specs=[VMEM] * len(outputs),
        scratch_shapes=list(scratch.values()) + flat,
        compiler_params=pltpu.CompilerParams(
            collective_id=1, has_side_effects=True, vmem_limit_bytes=64 << 20
        ),
    )(*[value for _, value in inputs.values()])
    return SimpleNamespace(**dict(zip(outputs, out))), low_bits


def per_device(
    acoustic,
    memory,
    embedding,
    w_query,
    w_key,
    w_value,
    w_out,
    w_in,
    w_back,
    w_vocab,
    gain_one,
    bias_one,
    gain_two,
    bias_two,
    fsmn_kernel,
    rate_table,
    token_lengths,
    memory_lengths,
    rate_groups,
    glance_mask,
    targets,
):
    tok_rows, model_width = acoustic.shape
    half = w_query.shape[1]
    n_dp = lax.axis_size("dp")
    result, low_bits = decoder_call(
        acoustic, memory, embedding, w_query, w_key, w_value, w_out, w_in, w_back, w_vocab,
        (gain_one, bias_one, gain_two, bias_two), fsmn_kernel, rate_table,
        token_lengths, memory_lengths, rate_groups, glance_mask, targets, n_dp,
    )
    vocab = result.vocab_out
    summed = [result.query_out, result.kv_out, result.out_out, result.in_out, result.back_out]
    if low_bits:
        size = 1 << len(low_bits)
        groups = [list(range(g * size, (g + 1) * size)) for g in range(n_dp // size)]
        pairs = [[2 * g, 2 * g + 1] for g in range(n_dp // 2)]
        vocab = lax.all_to_all(
            vocab.reshape(2, vocab.shape[0] // 2, -1), "dp", 0, 0, axis_index_groups=pairs, tiled=True
        )
        summed = [
            lax.psum_scatter(s, "dp", scatter_dimension=0, axis_index_groups=groups, tiled=True)
            for s in summed
        ]
    grad_query, grad_kv, grad_out, grad_in, grad_back = summed
    grad_vocab = jnp.concatenate([vocab[0], vocab[1]], axis=1)[:, : w_vocab.shape[1]]
    own = model_width // n_dp
    small = result.small_out
    grad_rate = small[16:18]
    small = lax.dynamic_slice_in_dim(small, lax.axis_index("dp") * own, own, axis=1)
    return (
        result.loss_out.reshape(tok_rows),
        result.acoustic_out,
        result.memory_out,
        result.table_out[:own, : embedding.shape[0]].T,
        grad_query,
        grad_kv[:, :half],
        grad_kv[:, half:],
        grad_out.T,
        grad_in,
        grad_back.T,
        grad_vocab,
        small[12],
        small[13],
        small[14],
        small[15],
        small[: fsmn_kernel.shape[0]],
        grad_rate,
    )


def solution(mesh):
    return jax.shard_map(
        per_device,
        mesh=mesh,
        in_specs=(
            P("dp", None),
            P("dp", None),
            P(),
            P(None, "mp"),
            P(None, "mp"),
            P(None, "mp"),
            P("mp", None),
            P(None, "mp"),
            P("mp", None),
            P(None, "mp"),
            P(),
            P(),
            P(),
            P(),
            P(),
            P(),
            P("dp"),
            P("dp"),
            P("dp"),
            P("dp"),
            P("dp"),
        ),
        out_specs=(
            P("dp"),
            P("dp", None),
            P("dp", "mp"),
            P(None, "dp"),
            P("dp", "mp"),
            P("dp", "mp"),
            P("dp", "mp"),
            P("mp", "dp"),
            P("dp", "mp"),
            P("mp", "dp"),
            P("dp", "mp"),
            P("dp"),
            P("dp"),
            P("dp"),
            P("dp"),
            P(None, "dp"),
            P(),
        ),
        check_vma=False,
    )
```

```python
from functools import partial
import math
from types import SimpleNamespace

import jax
import jax.numpy as jnp
from jax import lax
from jax.experimental import pallas as pl
from jax.experimental.pallas import tpu as pltpu
from jax.sharding import PartitionSpec as P

HD = 128
V = 8404
EPSILON = 1e-05
MESH = pl.DeviceIdType.MESH
VMEM = pl.BlockSpec(memory_space=pltpu.VMEM)
SMEM = pl.BlockSpec(memory_space=pltpu.SMEM)
ANY = pl.BlockSpec(memory_space=pl.ANY)
F32, BF16 = jnp.float32, jnp.bfloat16
NEG = -1e30


def other_core():
    return {"mp": 1 - lax.axis_index("mp")}


def dot_nn(a, b):
    return lax.dot_general(a, b, (((1,), (0,)), ((), ())), preferred_element_type=F32)


def dot_nt(a, b):
    return lax.dot_general(a, b, (((1,), (1,)), ((), ())), preferred_element_type=F32)


def dot_tn(a, b):
    return lax.dot_general(a, b, (((0,), (0,)), ((), ())), preferred_element_type=F32)


def normalise(rows):
    average = jnp.mean(rows, axis=-1, keepdims=True)
    centred = rows - average
    variance = jnp.mean(centred * centred, axis=-1, keepdims=True)
    scale = lax.rsqrt(variance + EPSILON)
    return centred * scale, scale


def normalise_back(grad_hat, hat, scale):
    first = jnp.mean(grad_hat, axis=-1, keepdims=True)
    second = jnp.mean(grad_hat * hat, axis=-1, keepdims=True)
    return scale * (grad_hat - first - hat * second)


def to_rows(columns):
    lane = lax.broadcasted_iota(jnp.int32, (columns[0].shape[0], 128), 1)
    tile = jnp.zeros(lane.shape, F32)
    for i, column in enumerate(columns):
        tile = jnp.where(lane == i, column, tile)
    return tile.T[:8]


def to_columns(rows):
    return jnp.concatenate([rows] * 16, axis=0).T


class Planner:
    RATE = 0.0425e6
    HOP = 1.5
    BACKLOG = math.inf

    def __init__(self):
        self.now = 0.0
        self.free = {}
        self.flying = []
        self.waiting = []
        self.started = []
        self.count = 0

    def launch(self, item, step):
        link, size = item.steps[step]
        begin = max(self.now, self.free.get(link, 0.0))
        self.free[link] = begin + size / self.RATE
        copy = item.send(step)
        self.started.append(copy)
        self.count += 1
        self.flying.append((self.free[link] + self.HOP, self.count, item, step, copy))

    def release(self):
        kept = []
        for item in self.waiting:
            link = item.steps[0][0]
            if self.free.get(link, 0.0) - self.now < self.BACKLOG:
                self.launch(item, 0)
            else:
                kept.append(item)
        self.waiting = kept

    def post(self, *items):
        self.waiting += items
        self.release()

    def run_until(self, time):
        while self.flying or self.waiting:
            if not self.flying:
                self.now = max(self.now, min(self.free[i.steps[0][0]] for i in self.waiting))
                self.release()
                continue
            first = min(self.flying, key=lambda f: f[:2])
            if first[0] > time:
                break
            self.flying.remove(first)
            self.now = max(self.now, first[0])
            _, _, item, step, copy = first
            item.take(step, copy)
            if step + 1 < len(item.steps):
                self.launch(item, step + 1)
            self.release()
        if time != math.inf:
            self.now = max(self.now, time)
        self.release()

    def finish(self):
        self.run_until(math.inf)
        for copy in self.started:
            copy.wait_send()


class Chunk:
    def __init__(self, steps, send, take):
        self.steps, self.send, self.take = steps, send, take


def decoder_kernel(
    names,
    vocab_here,
    half_cols,
    table_rows,
    n_dp,
    bits,
    low_bits,
    *refs,
):
    r = SimpleNamespace(**dict(zip(names, refs)))
    acoustic, memory, table = r.acoustic, r.memory, r.table
    targets, glance = r.targets, r.glance
    gain_1, bias_1 = r.gain_one[...], r.bias_one[...]
    gain_2, bias_2 = r.gain_two[...], r.bias_two[...]
    kernel_rows, rate_table = r.kernel_rows, r.rate_table
    token_lengths, memory_lengths, rate_groups = r.token_lengths, r.memory_lengths, r.rate_groups
    w_query, w_kv, w_out, w_in, w_back, w_vocab = r.w_query, r.w_kv, r.w_out, r.w_in, r.w_back, r.w_vocab
    mem_low, kv, padded, spare = r.mem_low, r.kv, r.padded, r.spare
    stream_in, stream_one, stream_two, stream_three = r.stream_in, r.stream_one, r.stream_two, r.stream_three
    one_low, queries, probs, mixed = r.one_low, r.queries, r.probs, r.mixed
    norm_low, hidden, gelu_slope, top = r.norm_low, r.hidden, r.gelu_slope, r.top
    logits, grad_logits, part3, arrived3 = r.logits, r.grad_logits, r.part3, r.arrived3
    grad_three, grad_two, branch_low = r.grad_three, r.grad_two, r.branch_low
    grad_pre, att_low, grad_queries = r.grad_pre, r.att_low, r.grad_queries
    mem_arrived, meta, stats, stats_arrived = r.mem_arrived, r.meta, r.stats, r.stats_arrived
    sent, arrived, gathered = r.sent, r.arrived, r.gathered
    small_sent, small_arrived = r.small_sent, r.small_arrived
    terms, term_blocks, term_arrived = grad_three, r.term_blocks, r.term_arrived
    onehot_lo, table_theirs, table_out = r.onehot_lo, r.table_theirs, r.table_out
    swap_send, swap_recv, load_sem = r.swap_send, r.swap_recv, r.load_sem

    utterances, slots = targets.shape
    width = acoustic.shape[1]
    frames = memory.shape[0] // utterances
    half = w_query.shape[1]
    heads = half // HD
    tokens = utterances * slots
    me, core = lax.axis_index("dp"), lax.axis_index("mp")
    side = lax.rem(me, 2)
    sibling = {"mp": 1 - core}
    pair = {"dp": me + 1 - 2 * side}
    cross = {"dp": me + 1 - 2 * side, "mp": 1 - core}
    bit_of = {b: lax.rem(me // (1 << b), 2) for b in low_bits + bits}
    peer_of = {b: {"dp": me + (1 - 2 * bit_of[b]) * (1 << b)} for b in low_bits + bits}
    score_scale = 1.0 / math.sqrt(HD)

    loads = []

    def load(source, target):
        copy = pltpu.make_async_copy(source, target, load_sem.at[len(loads)])
        copy.start()
        loads.append(copy)
        return copy

    load_memory = load(memory, mem_low)
    load_kv = [
        load(r.w_key_hbm, w_kv.at[:, pl.ds(0, half)]),
        load(r.w_value_hbm, w_kv.at[:, pl.ds(half, half)]),
    ]
    load_query = load(r.w_query_hbm, w_query)
    load_out = load(r.w_out_hbm, w_out)

    barrier = pltpu.get_barrier_semaphore()

    def greet(k, carry):
        pl.semaphore_signal(
            barrier, inc=1, device_id={"dp": lax.rem(me + k, n_dp)}, device_id_type=MESH
        )
        return carry

    lax.fori_loop(1, n_dp, greet, 0)
    for device in (sibling, cross):
        pl.semaphore_signal(barrier, inc=1, device_id=device, device_id_type=MESH)

    load_in = load(r.w_in_hbm, w_in)
    load_back = load(r.w_back_hbm, w_back)
    block = 1024
    per_core = table_rows // (2 * block)
    mains = 2 * per_core * block

    def load_table(k):
        at = pl.ds(pl.multiple_of((core * per_core + k) * block, block), block)
        return load(table.at[at, :], spare.at[pl.ds(k % 2 * block, block), :])

    table_loads = [load_table(0), load_table(1)]
    main = vocab_here // 256 * 256
    load_vocab = load(r.w_vocab_hbm.at[pl.ds(0, main), :], w_vocab.at[pl.ds(0, main), :])
    w_vocab[pl.ds(main, w_vocab.shape[0] - main), :] = jnp.zeros((w_vocab.shape[0] - main, width), BF16)
    w_vocab[pl.ds(main, vocab_here - main), :] = r.w_tail[...]
    r.table_rest[...] = jnp.zeros(r.table_rest.shape, BF16)
    r.table_rest[pl.ds(0, table_rows - mains), :] = r.table_tail[...]

    swaps = []

    def swap(source, target, device):
        k = len(swaps)
        copy = pltpu.make_async_remote_copy(
            src_ref=source,
            dst_ref=target,
            send_sem=swap_send.at[k],
            recv_sem=swap_recv.at[k],
            device_id=device,
            device_id_type=MESH,
        )
        copy.start()
        swaps.append(copy)
        return copy

    lane = lax.broadcasted_iota(jnp.int32, (1, slots), 1)
    row_of = lax.broadcasted_iota(jnp.int32, (8, slots), 0)
    for u in range(utterances):
        target_row = targets[pl.ds(u, 1), :].astype(F32)
        glance_row = glance[pl.ds(u, 1), :].astype(F32)
        valid_row = (lane < token_lengths[u]).astype(F32)
        meta[0, :, pl.ds(u * slots, slots)] = jnp.where(
            row_of == 0, target_row, jnp.where(row_of == 1, valid_row, glance_row)
        )
    own_columns = to_columns(meta[0])
    own_target = own_columns[:, 0:1]
    own_valid = own_columns[:, 1:2]

    def rows(u):
        return pl.ds(u * slots, slots)

    load_memory.wait()
    for copy in load_kv:
        copy.wait()
    step_rows = 256
    row_chunks = frames // step_rows

    def kv_step(i, carry):
        at = pl.ds(pl.multiple_of(i * step_rows, step_rows), step_rows)
        group = jnp.zeros((1, width), jnp.int32) + rate_groups[i // row_chunks]
        rate_row = jnp.where(group == 1, rate_table[pl.ds(1, 1), :], rate_table[pl.ds(0, 1), :])
        low = (mem_low[at, :].astype(F32) + rate_row).astype(BF16)
        mem_low[at, :] = low
        kv[at, :] = dot_nn(low, w_kv[...]).astype(BF16)
        return carry

    lax.fori_loop(0, utterances * row_chunks, kv_step, 0)

    edge = jnp.zeros((8, width), F32)
    for u in range(utterances):
        padded[u, pl.ds(0, 8), :] = edge
        padded[u, pl.ds(8 + slots, 8), :] = edge

    pl.semaphore_wait(barrier, n_dp + 1)
    meta_swap = swap(meta.at[0], meta.at[1], pair)
    load_query.wait()
    load_out.wait()

    def key_of(u, h):
        return kv[pl.ds(u * frames, frames), pl.ds(h * HD, HD)]

    def value_of(u, h):
        return kv[pl.ds(u * frames, frames), pl.ds(half + h * HD, HD)]

    frame_lane = lax.broadcasted_iota(jnp.int32, (1, frames), 1)

    def look_up(first_row, count, allowed, source):
        ids = first_row + lax.broadcasted_iota(jnp.int32, (1, count), 1)
        local = jnp.where(allowed, own_target.astype(jnp.int32), -1)
        onehot = jnp.where(ids == local, 1.0, 0.0).astype(BF16)
        return dot_nn(onehot, source)

    def look_up_block(k):
        table_loads[k].wait()
        part = look_up(
            (core * per_core + k) * block, block, True, spare[pl.ds(k % 2 * block, block), :]
        )
        for u in range(utterances):
            piece = part[u * slots : (u + 1) * slots]
            part3[0, u] = piece if k == 0 else part3[0, u] + piece
        if k + 2 < per_core:
            table_loads.append(load_table(k + 2))

    def look_up_rest():
        part = look_up(mains, r.table_rest.shape[0], core == 0, r.table_rest[...])
        for u in range(utterances):
            part3[0, u] = part3[0, u] + part[u * slots : (u + 1) * slots]

    def local_targets(target_column):
        local = target_column.astype(jnp.int32) - core * vocab_here
        return jnp.where((local >= 0) & (local < vocab_here), local, -1)

    def vocab_tile(tile, first, col, target, top_m, picked):
        ids = col + lax.broadcasted_iota(jnp.int32, (1, 128), 1)
        tile = jnp.where(ids < vocab_here, tile, NEG)
        logits[first] = tile
        return jnp.maximum(top_m, tile), picked + jnp.where(ids == target, tile, 0.0)

    def vocab_stats(g, target, base, wide, narrow, first):
        start = (jnp.full((tokens, 128), NEG, F32), jnp.zeros((tokens, 128), F32))

        def step(j, carry):
            col = pl.multiple_of(base + j * 256, 128)
            product = dot_nt(top[g], w_vocab[pl.ds(col, 256), :])
            carry = vocab_tile(product[:, :128], first + 2 * j, col, target, *carry)
            return vocab_tile(product[:, 128:], first + 2 * j + 1, col + 128, target, *carry)

        top_m, picked = lax.fori_loop(0, wide, step, start)
        if narrow:
            col = pl.multiple_of(base + wide * 256, 128)
            product = dot_nt(top[g], w_vocab[pl.ds(col, 128), :])
            top_m, picked = vocab_tile(product, first + 2 * wide, col, target, top_m, picked)
        top_row = jnp.max(top_m, axis=1, keepdims=True)

        def add(j, total):
            return total + jnp.exp(logits[first + j] - top_row)

        total = lax.fori_loop(0, 2 * wide + narrow, add, jnp.zeros((tokens, 128), F32))
        return (
            top_row,
            jnp.sum(total, axis=1, keepdims=True),
            jnp.sum(picked, axis=1, keepdims=True),
        )

    def join(blocks):
        top_value = blocks[0][0:1]
        for b in blocks[1:]:
            top_value = jnp.maximum(top_value, b[0:1])
        total, picked = 0.0, 0.0
        for b in blocks:
            total = total + b[1:2] * jnp.exp(b[0:1] - top_value)
            picked = picked + b[2:3]
        return top_value + jnp.log(total), picked

    def forward(second, beside_one=None, beside_two=None):
        copies = []
        for u in range(utterances):
            at = rows(u)
            valid = own_valid[u * slots : (u + 1) * slots]
            hat, _ = normalise(stream_in[at, :])
            padded[u, pl.ds(8, slots), :] = (hat * gain_1 + bias_1) * valid
            for j in range(width // 128):
                cols = pl.ds(j * 128, 128)
                total = jnp.zeros((slots, 128), F32)
                for k in range(kernel_rows.shape[0]):
                    shift = 8 + k - kernel_rows.shape[0] // 2
                    total = total + kernel_rows[pl.ds(k, 1), cols] * padded[u, pl.ds(shift, slots), cols]
                stream_one[at, cols] = stream_in[at, cols] + total * valid
            low = stream_one[at, :].astype(BF16)
            one_low[at, :] = low
            queries[at, :] = dot_nn(low, w_query[...]).astype(BF16)
            frame_ok = frame_lane < memory_lengths[u]
            for h in range(heads):
                cols = pl.ds(h * HD, HD)
                scores = dot_nt(queries[at, cols], key_of(u, h)) * score_scale
                scores = jnp.where(frame_ok, scores, NEG)
                raised = jnp.exp(scores - jnp.max(scores, axis=-1, keepdims=True))
                prob = raised / jnp.sum(raised, axis=-1, keepdims=True)
                if second:
                    probs[u, h] = prob
                mixed[at, cols] = dot_nn(prob.astype(BF16), value_of(u, h)).astype(BF16)
            sent[u] = dot_nn(mixed[at, :], w_out[...])
            copies.append(swap(sent.at[u], arrived.at[u], sibling))
        if not second:
            beside_one()
            load_in.wait()
            load_back.wait()
        ff_copies = []
        for u in range(utterances):
            at = rows(u)
            copies[u].wait()
            two = stream_one[at, :] + (sent[u] + arrived[u])
            stream_two[at, :] = two
            hat, _ = normalise(two)
            low = (hat * gain_2 + bias_2).astype(BF16)
            norm_low[at, :] = low
            pre = dot_nn(low, w_in[...])
            phi = 0.5 * (1.0 + lax.erf(pre * math.sqrt(0.5)))
            hidden[at, :] = (pre * phi).astype(BF16)
            if second:
                gelu_slope[at, :] = phi + pre * (
                    jnp.exp(-0.5 * pre * pre) * (1.0 / math.sqrt(2.0 * math.pi))
                )
            sent[utterances + u] = dot_nn(hidden[at, :], w_back[...])
            ff_copies.append(swap(sent.at[utterances + u], arrived.at[utterances + u], sibling))
        if not second:
            beside_two()
        for u in range(utterances):
            at = rows(u)
            ff_copies[u].wait()
            three = stream_two[at, :] + (sent[utterances + u] + arrived[utterances + u])
            stream_three[u] = three
            top[0, at, :] = three.astype(BF16)

    stream_in[...] = acoustic[...].astype(F32)

    def beside_one():
        look_up_block(0)
        look_up_block(1)

    def beside_two():
        for k in range(2, per_core):
            look_up_block(k)
        look_up_rest()

    forward(False, beside_one, beside_two)
    table_swap = swap(part3.at[0], arrived3, sibling)
    load_vocab.wait()
    first = vocab_stats(0, local_targets(own_target), 0, w_vocab.shape[0] // 256, 0, 0)
    stats[0, :, pl.ds(0, tokens)] = to_rows(first)
    first_swap = swap(stats.at[0, :, pl.ds(0, tokens)], stats_arrived.at[0, :, pl.ds(0, tokens)], sibling)
    table_swap.wait()
    first_swap.wait()
    log_total, picked = join([stats[0, :, :tokens], stats_arrived[0, :, :tokens]])
    first_loss = (log_total - picked) * meta[0, 1:2, :]
    blend_row = meta[0, 2:3, :] * meta[0, 1:2, :] / (1.0 + jnp.exp(math.log(V) - first_loss))
    blend = to_columns(jnp.concatenate([blend_row] * 8, axis=0))[:, 0:1]
    for u in range(utterances):
        at = rows(u)
        wide_acoustic = acoustic[at, :].astype(F32)
        taken = part3[0, u] + arrived3[u]
        stream_in[at, :] = wide_acoustic + blend[u * slots : (u + 1) * slots] * (taken - wide_acoustic)

    forward(True)
    token_swap = swap(stream_three.at[core], gathered.at[0], pair)
    base = side * half_cols
    wide, narrow = half_cols // 256, half_cols % 256 // 128
    per_group = 2 * wide + narrow
    meta_swap.wait()
    pair_columns = to_columns(meta[1])
    group_target = [local_targets(own_target), local_targets(pair_columns[:, 0:1])]
    group_valid = [own_valid, pair_columns[:, 1:2]]
    own_stats = vocab_stats(0, group_target[0], base, wide, narrow, 0)
    stats[1, :, pl.ds(0, tokens)] = to_rows(own_stats)
    token_swap.wait()
    share_swap = swap(gathered.at[0], gathered.at[1], sibling)
    at_core = pl.ds(pl.multiple_of(core * slots, slots), slots)
    at_other = pl.ds(pl.multiple_of((1 - core) * slots, slots), slots)
    top[1, at_core, :] = gathered[0].astype(BF16)
    share_swap.wait()
    top[1, at_other, :] = gathered[1].astype(BF16)
    pair_stats = vocab_stats(1, group_target[1], base, wide, narrow, per_group)
    stats[1, :, pl.ds(tokens, tokens)] = to_rows(pair_stats)
    stat_swaps = [
        swap(stats.at[1], stats_arrived.at[1], sibling),
        swap(stats.at[1], stats_arrived.at[2], pair),
        swap(stats.at[1], stats_arrived.at[3], cross),
    ]
    for copy in stat_swaps:
        copy.wait()

    def group_blocks(g):
        mine, theirs = pl.ds(g * tokens, tokens), pl.ds((1 - g) * tokens, tokens)
        return [
            stats[1, :, mine],
            stats_arrived[1, :, mine],
            stats_arrived[2, :, theirs],
            stats_arrived[3, :, theirs],
        ]

    log_totals = []
    for g in range(2):
        log_total, picked = join(group_blocks(g))
        log_totals.append(to_columns(jnp.concatenate([log_total] * 8, axis=0))[:, 0:1])
        if g == 0:
            loss = (log_total - picked) * meta[0, 1:2, :]
            for u in range(utterances):
                r.loss_out[pl.ds(u, 1), :] = loss[:, u * slots : (u + 1) * slots]

    plan = Planner()
    steps_all = len(bits)
    trade = not low_bits
    scatter_send, scatter_recv = r.scatter_send, r.scatter_recv

    def make_chunk(index):
        name, start, cols, order = chunk_list(half_cols, width, bits, low_bits, r)[index]
        source, landing = getattr(r, "src_" + name), r.landing[index]
        out = getattr(r, name + "_out")
        rows_here = source.shape[-2]

        def pick(step, which):
            rest = sorted([b for b in bits if b not in order[:step]], reverse=True)
            where = tuple(which if b == order[step] else slice(None) for b in rest)
            if step == 0:
                return source, where + (slice(None), pl.ds(start, cols))
            return landing[step - 1], where + (slice(None), slice(None))

        def send(step):
            b = order[step]
            ref, where = pick(step, 1 - bit_of[b])
            copy = pltpu.make_async_remote_copy(
                src_ref=ref.at[where],
                dst_ref=landing[step],
                send_sem=scatter_send.at[index, step],
                recv_sem=scatter_recv.at[index, step],
                device_id=peer_of[b],
                device_id_type=MESH,
            )
            copy.start()
            return copy

        def take(step, copy):
            copy.wait_recv()
            ref, where = pick(step, bit_of[order[step]])
            got = landing[step]
            at = pl.ds(start, cols)
            last = step == len(order) - 1
            if last and name == "vocab" and trade:
                out[bit_of[0], :, at] = ref[where]
                out[1 - bit_of[0], :, at] = got[...]
            elif last:
                out[:, at] = got[...] + ref[where]
            else:
                got[...] = got[...] + ref[where]

        steps = [
            (link_of(b, bits), rows_here * cols * 4 * 2 ** (steps_all - 1 - s))
            for s, b in enumerate(order)
        ]
        return Chunk(steps, send, take)

    chunks = {}
    for index, (name, start, _, _) in enumerate(chunk_list(half_cols, width, bits, low_bits, r)):
        chunks[name, start] = make_chunk(index)

    def put(name, at, product):
        source = getattr(r, "src_" + name)
        source[..., at] = product.reshape(source.shape[:-1] + (product.shape[1],))

    for g in (1, 0):
        log_column, valid, target = log_totals[g], group_valid[g], group_target[g]

        def slope(j, carry):
            col = pl.multiple_of(j * 128, 128)
            ids = base + col + lax.broadcasted_iota(jnp.int32, (1, 128), 1)
            onehot = jnp.where(ids == target, 1.0, 0.0)
            grad = (jnp.exp(logits[g * per_group + j] - log_column) - onehot) * valid
            grad_logits[pl.ds(g * tokens, tokens), pl.ds(col, 128)] = grad.astype(BF16)
            return carry

        lax.fori_loop(0, per_group, slope, 0)
        part = dot_nn(
            grad_logits[pl.ds(g * tokens, tokens), :],
            w_vocab[pl.ds(pl.multiple_of(base, 128), half_cols), :],
        )
        for u in range(utterances):
            part3[u, g] = part[u * slots : (u + 1) * slots]
    three_swap = swap(part3.at[1 - core], arrived3, sibling)
    top_all = jnp.concatenate([top[0], top[1]], axis=0)
    vocab_starts = sorted(start for name, start in chunks if name == "vocab")
    pair_swap = None
    for i, start in enumerate(vocab_starts):
        stop = (vocab_starts + [half_cols])[i + 1]
        for col in range(start, stop, 256):
            at = pl.ds(col, min(256, stop - col))
            put("vocab", at, dot_tn(top_all, grad_logits[:, at]))
        plan.run_until(1.0 * i)
        plan.post(chunks["vocab", start])
        if pair_swap is None:
            three_swap.wait()
            sent[0] = part3[core, 1] + arrived3[1]
            pair_swap = swap(sent.at[0], arrived.at[0], pair)
            plan.free[link_of(0, bits)] = plan.now + 6.0
    pair_swap.wait()
    grad_three[core] = (part3[core, 0] + arrived3[0]) + arrived[0]
    share_three = swap(grad_three.at[core], arrived.at[1], sibling)
    plan.run_until(9.0)
    share_three.wait()
    grad_three[1 - core] = arrived[1]

    copies = []
    for u in range(utterances):
        at = rows(u)
        low = grad_three[u].astype(BF16)
        branch_low[at, :] = low
        pre = (dot_nt(low, w_back[...]) * gelu_slope[at, :]).astype(BF16)
        grad_pre[at, :] = pre
        sent[utterances + u] = dot_nt(pre, w_in[...])
        copies.append(swap(sent.at[utterances + u], arrived.at[utterances + u], sibling))
    plan.run_until(13.0)
    for name, left, right in (("back", branch_low, hidden), ("in", norm_low, grad_pre)):
        for start in sorted(s for n, s in chunks if n == name):
            at = pl.ds(start, 512)
            put(name, at, dot_tn(left[...], right[:, at]))
            plan.post(chunks[name, start])
    plan.run_until(15.0)

    one_copies = []
    gain_2_total, bias_2_total = 0.0, 0.0
    for u in range(utterances):
        at = rows(u)
        copies[u].wait()
        grad_norm = sent[utterances + u] + arrived[utterances + u]
        hat, scale = normalise(stream_two[at, :])
        gain_2_total = gain_2_total + jnp.sum(grad_norm * hat, axis=0, keepdims=True)
        bias_2_total = bias_2_total + jnp.sum(grad_norm, axis=0, keepdims=True)
        two = grad_three[u] + normalise_back(grad_norm * gain_2, hat, scale)
        grad_two[at, :] = two
        low = two.astype(BF16)
        att_low[at, :] = low
        grad_mixed = dot_nt(low, w_out[...]).astype(BF16)
        for h in range(heads):
            cols = pl.ds(h * HD, HD)
            grad_head = grad_mixed[:, h * HD : (h + 1) * HD]
            prob = probs[u, h]
            grad_prob = dot_nt(grad_head, value_of(u, h))
            spare[pl.ds(u * frames, frames), pl.ds(half + h * HD, HD)] = dot_tn(
                prob.astype(BF16), grad_head
            ).astype(BF16)
            inner = jnp.sum(prob * grad_prob, axis=-1, keepdims=True)
            grad_score = (prob * (grad_prob - inner)).astype(BF16)
            grad_queries[at, cols] = (dot_nn(grad_score, key_of(u, h)) * score_scale).astype(BF16)
            spare[pl.ds(u * frames, frames), cols] = (
                dot_tn(grad_score, queries[at, cols]) * score_scale
            ).astype(BF16)
            plan.run_until(17.0 + 2.0 * (heads * u + h))
        sent[u] = dot_nt(grad_queries[at, :], w_query[...])
        one_copies.append(swap(sent.at[u], arrived.at[u], sibling))
    every = slice(None)
    put("out", every, dot_tn(att_low[...], mixed[...]))
    plan.post(chunks["out", 0])
    put("query", every, dot_tn(one_low[...], grad_queries[...]))
    plan.post(chunks["query", 0])
    plan.run_until(25.0)

    mem_copies = []
    rate_sums = [0.0, 0.0]
    for u in range(utterances):
        total = jnp.zeros((1, width), F32)
        for i in range(row_chunks):
            at = pl.ds(u * frames + i * step_rows, step_rows)
            part = dot_nt(spare[at, :], w_kv[...])
            for j in range(width // 128):
                side_of, tile = j // (width // 256), j % (width // 256)
                index = ((side_of * utterances + u) * row_chunks + i) * (width // 256) + tile
                logits[index] = part[:, j * 128 : (j + 1) * 128]
            total = total + jnp.sum(part, axis=0, keepdims=True)
        tiles = row_chunks * (width // 256)
        mem_copies.append(
            swap(
                logits.at[pl.ds(((1 - core) * utterances + u) * tiles, tiles)],
                mem_arrived.at[pl.ds(u * tiles, tiles)],
                sibling,
            )
        )
        group = jnp.zeros((1, width), jnp.int32) + rate_groups[u]
        for k in range(2):
            rate_sums[k] = rate_sums[k] + jnp.where((group == 1) == (k == 1), total, 0.0)
        plan.run_until(26.5 + 1.5 * u)
    for start in sorted(s for n, s in chunks if n == "kv"):
        at = pl.ds(start, 256)
        put("kv", at, dot_tn(mem_low[...], spare[:, at]))
        plan.post(chunks["kv", start])
        plan.run_until(29.0 + start / 256)

    gain_1_total, bias_1_total = 0.0, 0.0
    for u in range(utterances):
        at = rows(u)
        valid = own_valid[u * slots : (u + 1) * slots]
        one_copies[u].wait()
        one = grad_two[at, :] + (sent[u] + arrived[u])
        grad_two[at, :] = one
        masked = one * valid
        for k in range(kernel_rows.shape[0]):
            shift = 8 + k - kernel_rows.shape[0] // 2
            row = jnp.sum(masked * padded[u, pl.ds(shift, slots), :], axis=0, keepdims=True)
            if u == 0:
                small_sent[0, pl.ds(k, 1), :] = row
            else:
                small_sent[0, pl.ds(k, 1), :] = small_sent[0, pl.ds(k, 1), :] + row
        padded[u, pl.ds(8, slots), :] = masked
        for j in range(width // 128):
            cols = pl.ds(j * 128, 128)
            total = jnp.zeros((slots, 128), F32)
            for k in range(kernel_rows.shape[0]):
                shift = 8 - k + kernel_rows.shape[0] // 2
                total = total + kernel_rows[pl.ds(k, 1), cols] * padded[u, pl.ds(shift, slots), cols]
            stream_one[at, cols] = total * valid
        grad_norm = stream_one[at, :]
        hat, scale = normalise(stream_in[at, :])
        gain_1_total = gain_1_total + jnp.sum(grad_norm * hat, axis=0, keepdims=True)
        bias_1_total = bias_1_total + jnp.sum(grad_norm, axis=0, keepdims=True)
        zero = grad_two[at, :] + normalise_back(grad_norm * gain_1, hat, scale)
        terms[u] = blend[u * slots : (u + 1) * slots] * zero
        r.acoustic_out[at, :] = zero - terms[u]
        plan.run_until(32.0 + 2.0 * u)

    last_taps = kernel_rows.shape[0]
    small_sent[0, pl.ds(last_taps, 12 - last_taps), :] = jnp.zeros((12 - last_taps, width), F32)
    for i, row in enumerate((gain_1_total, bias_1_total, gain_2_total, bias_2_total)):
        small_sent[0, pl.ds(12 + i, 1), :] = row
    for k in range(2):
        small_sent[0, pl.ds(16 + k, 1), :] = rate_sums[k]
    small_sent[0, pl.ds(18, 6), :] = jnp.zeros((6, width), F32)
    small_peers = [peer_of[b] for b in low_bits + bits] + [sibling]

    def small_send(step):
        copy = pltpu.make_async_remote_copy(
            src_ref=small_sent.at[step],
            dst_ref=small_arrived.at[step],
            send_sem=r.small_send.at[step],
            recv_sem=r.small_recv.at[step],
            device_id=small_peers[step],
            device_id_type=MESH,
        )
        copy.start()
        return copy

    def small_take(step, copy):
        copy.wait_recv()
        if step + 1 < len(small_peers):
            small_sent[step + 1] = small_sent[step] + small_arrived[step]
        else:
            r.small_out[pl.ds(0, 16), :] = small_sent[step, pl.ds(0, 16), :]
            r.small_out[pl.ds(16, 8), :] = (
                small_sent[step, pl.ds(16, 8), :] + small_arrived[step, pl.ds(16, 8), :]
            )

    small_links = [link_of(b, bits) for b in low_bits + bits] + ["core"]
    plan.post(Chunk([(l, 24 * width * 4) for l in small_links], small_send, small_take))

    features = width // n_dp
    feature_rows = max(features, 8)
    block_rows = term_blocks.shape[1]
    turned = terms[core].T
    id_row = targets[pl.ds(core, 1), :].astype(F32)
    rest = block_rows - features - 1
    for p in range(n_dp):
        term_blocks[p, pl.ds(0, features), :] = turned[p * features : (p + 1) * features]
        term_blocks[p, pl.ds(features, 1), :] = id_row
        term_blocks[p, pl.ds(features + 1, rest), :] = jnp.zeros((rest, slots), F32)

    def term_copy(k):
        there = lax.rem(me + k, n_dp)
        return pltpu.make_async_remote_copy(
            src_ref=term_blocks.at[there],
            dst_ref=term_arrived.at[me],
            send_sem=r.term_send.at[k],
            recv_sem=r.term_recv.at[k],
            device_id={"dp": there},
            device_id_type=MESH,
        )

    def term_start(k, carry):
        term_copy(k).start()
        return carry

    def term_wait(k, carry):
        term_copy(k).wait()
        return carry

    term_arrived[me] = term_blocks[me]
    lax.fori_loop(1, n_dp, term_start, 0)
    for u in range(utterances):
        mem_copies[u].wait()
        for i in range(row_chunks):
            for j in range(width // 256):
                index = (u * row_chunks + i) * (width // 256) + j
                first_tile = (core * utterances) * row_chunks * (width // 256)
                r.memory_out[pl.ds(u * frames + i * step_rows, step_rows), pl.ds(j * 128, 128)] = (
                    logits[first_tile + index] + mem_arrived[index]
                )
    plan.run_until(45.0)
    lax.fori_loop(1, n_dp, term_wait, 0)
    per_piece = 512 // slots
    blocks_hi = table_out.shape[1] // 256
    batch = 4

    def table_piece(p, fresh):
        found = [term_arrived[p * per_piece + i] for i in range(per_piece)]
        values = jnp.concatenate([f[:feature_rows] for f in found], axis=1)
        ids = jnp.concatenate([f[features : features + 1] for f in found], axis=1).astype(jnp.int32)
        low_ids, high_ids = ids & 255, ids >> 8
        onehot_lo[...] = jnp.where(
            lax.broadcasted_iota(jnp.int32, (256, 512), 0) == low_ids, 1.0, 0.0
        ).astype(BF16)
        coarse = values.astype(BF16).astype(F32)
        both = jnp.concatenate([coarse, values - coarse], axis=0)
        for first_hi in range(0, blocks_hi, batch):
            here = range(first_hi, min(first_hi + batch, blocks_hi))
            masked = jnp.concatenate([jnp.where(high_ids == hi, both, 0.0) for hi in here], axis=0)
            product = dot_nt(masked.astype(BF16), onehot_lo[...])
            for i, hi in enumerate(here):
                top_part = product[2 * i * feature_rows : (2 * i + 1) * feature_rows]
                low_part = product[(2 * i + 1) * feature_rows : (2 * i + 2) * feature_rows]
                at = pl.ds(hi * 256, 256)
                if fresh:
                    table_out[:, at] = top_part + low_part
                else:
                    table_out[:, at] = table_out[:, at] + (top_part + low_part)

    pieces = n_dp // per_piece
    table_piece(0, True)
    if pieces <= 4:
        for p in range(1, pieces):
            plan.run_until(45.0 + 1.5 * p)
            table_piece(p, False)
    else:
        lax.fori_loop(1, pieces, lambda p, c: (table_piece(p, False), c)[1], 0)
    table_swap = swap(table_out, table_theirs, sibling)
    plan.run_until(56.0)
    table_swap.wait()
    table_out[...] = table_out[...] + table_theirs[...]
    plan.finish()


def link_of(bit, bits):
    if bit == bits[-1]:
        return bits[-2]
    return bit


def chunk_list(half_cols, width, bits, low_bits, sizes):
    own = [b for b in bits if b != 0]
    last = [] if low_bits else [0]
    listing = []
    edges = [half_cols // 128 * k // 4 * 128 for k in range(4)] + [half_cols]
    for k in range(4):
        listing.append(("vocab", edges[k], edges[k + 1] - edges[k], own + last))
    units = sizes.units
    for name in ("back", "in"):
        for start in range(0, units, 512):
            listing.append((name, start, 512, bits))
    half = sizes.half
    listing.append(("out", 0, half, bits))
    listing.append(("query", 0, half, bits))
    for start in range(0, 2 * half, 256):
        listing.append(("kv", start, 256, bits))
    return listing


def decoder_call(
    acoustic, memory, embedding, w_query, w_key, w_value, w_out, w_in, w_back, w_vocab, norms,
    fsmn_kernel, rate_table, token_lengths, memory_lengths, rate_groups, glance, targets, n_dp,
):
    utterances = token_lengths.shape[0]
    tokens, width = acoustic.shape
    slots = tokens // utterances
    mem_rows = memory.shape[0]
    half = w_query.shape[1]
    heads = half // HD
    frames = mem_rows // utterances
    units = w_in.shape[1]
    vocab_here = w_vocab.shape[1]
    table_rows = embedding.shape[0]
    half_cols = (vocab_here + 255) // 256 * 128
    w_turned = w_vocab.T
    main = vocab_here // 256 * 256
    mains = table_rows // 2048 * 2048
    nbits = n_dp.bit_length() - 1
    steps = nbits
    while width >> steps < 8:
        steps -= 1
    low_bits, bits = list(range(nbits - steps)), list(range(nbits - steps, nbits))
    rows = width >> steps
    features = width // n_dp
    feature_rows = max(features, 8)
    block_rows = feature_rows + 8 if features >= 8 else 8
    blocks_hi = (table_rows + 255) // 256
    sizes = SimpleNamespace(units=units, half=half)
    listing = chunk_list(half_cols, width, bits, low_bits, sizes)
    most = max(len(c[3]) for c in listing)

    f32 = lambda *shape: jax.ShapeDtypeStruct(shape, F32)
    v32 = lambda *shape: pltpu.VMEM(shape, F32)
    v16 = lambda *shape: pltpu.VMEM(shape, BF16)
    dma = lambda *shape: pltpu.SemaphoreType.DMA(shape)
    inputs = dict(
        acoustic=(VMEM, acoustic),
        w_tail=(VMEM, w_turned[main:]),
        table_tail=(VMEM, embedding[mains:]),
        memory=(ANY, memory),
        table=(ANY, embedding),
        w_query_hbm=(ANY, w_query),
        w_key_hbm=(ANY, w_key),
        w_value_hbm=(ANY, w_value),
        w_out_hbm=(ANY, w_out),
        w_in_hbm=(ANY, w_in),
        w_back_hbm=(ANY, w_back),
        w_vocab_hbm=(ANY, w_turned),
        gain_one=(VMEM, norms[0][None]),
        bias_one=(VMEM, norms[1][None]),
        gain_two=(VMEM, norms[2][None]),
        bias_two=(VMEM, norms[3][None]),
        kernel_rows=(VMEM, fsmn_kernel),
        rate_table=(VMEM, rate_table),
        token_lengths=(SMEM, token_lengths),
        memory_lengths=(SMEM, memory_lengths),
        rate_groups=(SMEM, rate_groups),
        glance=(VMEM, glance.reshape(utterances, slots)),
        targets=(VMEM, targets.reshape(utterances, slots)),
    )
    outputs = dict(
        loss_out=f32(utterances, slots),
        acoustic_out=f32(tokens, width),
        memory_out=f32(mem_rows, width // 2),
        table_out=f32(feature_rows, blocks_hi * 256),
        small_out=f32(24, width),
        vocab_out=f32(*(() if low_bits else (2,)), rows, half_cols),
        in_out=f32(rows, units),
        back_out=f32(rows, units),
        query_out=f32(rows, half),
        out_out=f32(rows, half),
        kv_out=f32(rows, 2 * half),
    )
    shape = (2,) * steps + (rows,)
    scratch = dict(
        w_query=v16(width, half),
        w_kv=v16(width, 2 * half),
        w_out=v16(half, width),
        w_in=v16(width, units),
        w_back=v16(units, width),
        w_vocab=v16(2 * half_cols, width),
        mem_low=v16(mem_rows, width),
        kv=v16(mem_rows, 2 * half),
        spare=v16(mem_rows, 2 * half),
        padded=v32(utterances, slots + 16, width),
        stream_in=v32(tokens, width),
        stream_one=v32(tokens, width),
        stream_two=v32(tokens, width),
        stream_three=v32(utterances, slots, width),
        one_low=v16(tokens, width),
        queries=v16(tokens, half),
        probs=v32(utterances, heads, slots, frames),
        mixed=v16(tokens, half),
        norm_low=v16(tokens, width),
        hidden=v16(tokens, units),
        gelu_slope=v32(tokens, units),
        top=v16(2, tokens, width),
        logits=v32(2 * half_cols // 128, tokens, 128),
        grad_logits=v16(2 * tokens, half_cols),
        part3=v32(utterances, 2, slots, width),
        arrived3=v32(2, slots, width),
        grad_three=v32(utterances, slots, width),
        grad_two=v32(tokens, width),
        branch_low=v16(tokens, width),
        grad_pre=v16(tokens, units),
        att_low=v16(tokens, width),
        grad_queries=v16(tokens, half),
        mem_arrived=v32(mem_rows // 256 * (width // 256), 256, 128),
        meta=v32(2, 8, tokens),
        stats=v32(2, 8, 2 * tokens),
        stats_arrived=v32(4, 8, 2 * tokens),
        sent=v32(2 * utterances, slots, width),
        arrived=v32(2 * utterances, slots, width),
        gathered=v32(2, slots, width),
        small_sent=v32(nbits + 1, 24, width),
        small_arrived=v32(nbits + 1, 24, width),
        term_blocks=v32(n_dp, block_rows, slots),
        term_arrived=v32(n_dp, block_rows, slots),
        onehot_lo=v16(256, 512),
        table_rest=v16((table_rows - mains + 127) // 128 * 128, width),
        table_theirs=v32(feature_rows, blocks_hi * 256),
        src_vocab=v32(*shape, half_cols),
        src_back=v32(*shape, units),
        src_in=v32(*shape, units),
        src_out=v32(*shape, half),
        src_query=v32(*shape, half),
        src_kv=v32(*shape, 2 * half),
        load_sem=dma(24),
        swap_send=dma(40),
        swap_recv=dma(40),
        scatter_send=dma(len(listing), most),
        scatter_recv=dma(len(listing), most),
        small_send=dma(nbits + 1),
        small_recv=dma(nbits + 1),
        term_send=dma(n_dp),
        term_recv=dma(n_dp),
    )
    landing = [
        [v32(*(2,) * (steps - 1 - s), rows, cols) for s in range(len(order))]
        for _, _, cols, order in listing
    ]
    names = list(inputs) + list(outputs) + list(scratch)
    flat = [ref for chunk in landing for ref in chunk]

    def kernel(*refs):
        named, rest = refs[: len(names)], list(refs[len(names) :])
        lands = [[rest.pop(0) for _ in chunk] for chunk in landing]
        decoder_kernel(
            names + ["landing", "units", "half"], vocab_here, half_cols, table_rows, n_dp, bits,
            low_bits, *named, lands, units, half,
        )

    out = pl.pallas_call(
        kernel,
        out_shape=list(outputs.values()),
        in_specs=[spec for spec, _ in inputs.values()],
        out_specs=[VMEM] * len(outputs),
        scratch_shapes=list(scratch.values()) + flat,
        compiler_params=pltpu.CompilerParams(
            collective_id=1, has_side_effects=True, vmem_limit_bytes=64 << 20
        ),
    )(*[value for _, value in inputs.values()])
    return SimpleNamespace(**dict(zip(outputs, out))), low_bits


def deliver_kernel(n_dp, *refs):
    loss, small, table, vocab, kv, query, out, in_, back, acoustic, memory = refs[:11]
    (
        loss_to, gain_one_to, bias_one_to, gain_two_to, bias_two_to, taps_to, rate_to,
        table_to, vocab_to, key_to, value_to, query_to, out_to, in_to, back_to, acoustic_to, memory_to,
    ) = refs[11:28]
    sem = refs[28]
    copies = []
    for source, target in (
        (memory, memory_to), (acoustic, acoustic_to), (in_, in_to), (back, back_to),
        (query, query_to), (out, out_to),
    ):
        copies.append(pltpu.make_async_copy(source, target, sem.at[len(copies)]))
        copies[-1].start()
    slots = loss.shape[1]
    for u in range(loss.shape[0]):
        loss_to[:, pl.ds(u * slots, slots)] = loss[pl.ds(u, 1), :]
    me = lax.axis_index("dp")
    own = small.shape[1] // n_dp
    mine = jnp.zeros((16, own), F32)
    for p in range(n_dp):
        mine = jnp.where(me == p, small[pl.ds(0, 16), p * own : (p + 1) * own], mine)
    taps_to[...] = mine[: taps_to.shape[0]]
    for i, target in enumerate((gain_one_to, bias_one_to, gain_two_to, bias_two_to)):
        target[...] = mine[12 + i : 13 + i]
    rate_to[...] = small[pl.ds(16, 2), :]
    table_to[...] = table[pl.ds(0, table_to.shape[0]), :][:, : table_to.shape[1]]
    half_cols = vocab.shape[2]
    vocab_to[:, pl.ds(0, half_cols)] = vocab[0]
    rest = vocab_to.shape[1] - half_cols
    vocab_to[:, pl.ds(half_cols, rest)] = vocab[1][:, :rest]
    half = key_to.shape[1]
    key_to[...] = kv[:, pl.ds(0, half)]
    value_to[...] = kv[:, pl.ds(half, half)]
    for copy in copies:
        copy.wait()


def per_device(
    acoustic,
    memory,
    embedding,
    w_query,
    w_key,
    w_value,
    w_out,
    w_in,
    w_back,
    w_vocab,
    gain_one,
    bias_one,
    gain_two,
    bias_two,
    fsmn_kernel,
    rate_table,
    token_lengths,
    memory_lengths,
    rate_groups,
    glance_mask,
    targets,
):
    tok_rows, model_width = acoustic.shape
    half = w_query.shape[1]
    n_dp = lax.axis_size("dp")
    result, low_bits = decoder_call(
        acoustic, memory, embedding, w_query, w_key, w_value, w_out, w_in, w_back, w_vocab,
        (gain_one, bias_one, gain_two, bias_two), fsmn_kernel, rate_table,
        token_lengths, memory_lengths, rate_groups, glance_mask, targets, n_dp,
    )
    vocab = result.vocab_out
    summed = [result.query_out, result.kv_out, result.out_out, result.in_out, result.back_out]
    if low_bits:
        size = 1 << len(low_bits)
        groups = [list(range(g * size, (g + 1) * size)) for g in range(n_dp // size)]
        pairs = [[2 * g, 2 * g + 1] for g in range(n_dp // 2)]
        vocab = lax.all_to_all(
            vocab.reshape(2, vocab.shape[0] // 2, -1), "dp", 0, 0, axis_index_groups=pairs, tiled=True
        )
        summed = [
            lax.psum_scatter(s, "dp", scatter_dimension=0, axis_index_groups=groups, tiled=True)
            for s in summed
        ]
    grad_query, grad_kv, grad_out, grad_in, grad_back = summed
    own = model_width // n_dp
    f32 = lambda *shape: jax.ShapeDtypeStruct(shape, F32)
    like = lambda x: jax.ShapeDtypeStruct(x.shape, F32)
    (
        token_loss, gain_1, bias_1, gain_2, bias_2, grad_taps, grad_rate, grad_table, grad_vocab,
        grad_key, grad_value, grad_query, grad_out, grad_in, grad_back, grad_acoustic, grad_memory,
    ) = pl.pallas_call(
        partial(deliver_kernel, n_dp),
        out_shape=[
            f32(1, tok_rows),
            *[f32(1, own)] * 4,
            f32(fsmn_kernel.shape[0], own),
            f32(2, model_width),
            f32(own, embedding.shape[0]),
            f32(own, w_vocab.shape[1]),
            *[f32(own, half)] * 2,
            *[like(x) for x in (grad_query, grad_out, grad_in, grad_back)],
            like(result.acoustic_out),
            like(result.memory_out),
        ],
        in_specs=[VMEM] * 5 + [ANY] * 6,
        out_specs=[VMEM] * 11 + [ANY] * 6,
        scratch_shapes=[pltpu.SemaphoreType.DMA((6,))],
        compiler_params=pltpu.CompilerParams(vmem_limit_bytes=32 << 20),
    )(
        result.loss_out, result.small_out, result.table_out, vocab, grad_kv, grad_query, grad_out,
        grad_in, grad_back, result.acoustic_out, result.memory_out,
    )
    return (
        token_loss.reshape(tok_rows),
        grad_acoustic,
        grad_memory,
        grad_table.T,
        grad_query,
        grad_key,
        grad_value,
        grad_out.T,
        grad_in,
        grad_back.T,
        grad_vocab,
        gain_1.reshape(own),
        bias_1.reshape(own),
        gain_2.reshape(own),
        bias_2.reshape(own),
        grad_taps,
        grad_rate,
    )


def solution(mesh):
    return jax.shard_map(
        per_device,
        mesh=mesh,
        in_specs=(
            P("dp", None),
            P("dp", None),
            P(),
            P(None, "mp"),
            P(None, "mp"),
            P(None, "mp"),
            P("mp", None),
            P(None, "mp"),
            P("mp", None),
            P(None, "mp"),
            P(),
            P(),
            P(),
            P(),
            P(),
            P(),
            P("dp"),
            P("dp"),
            P("dp"),
            P("dp"),
            P("dp"),
        ),
        out_specs=(
            P("dp"),
            P("dp", None),
            P("dp", "mp"),
            P(None, "dp"),
            P("dp", "mp"),
            P("dp", "mp"),
            P("dp", "mp"),
            P("mp", "dp"),
            P("dp", "mp"),
            P("mp", "dp"),
            P("dp", "mp"),
            P("dp"),
            P("dp"),
            P("dp"),
            P("dp"),
            P(None, "dp"),
            P(),
        ),
        check_vma=False,
    )
```

```python
from functools import partial
import math
from types import SimpleNamespace

import jax
import jax.numpy as jnp
from jax import lax
from jax.experimental import pallas as pl
from jax.experimental.pallas import tpu as pltpu
from jax.sharding import PartitionSpec as P

HD = 128
V = 8404
EPSILON = 1e-05
MESH = pl.DeviceIdType.MESH
VMEM = pl.BlockSpec(memory_space=pltpu.VMEM)
SMEM = pl.BlockSpec(memory_space=pltpu.SMEM)
ANY = pl.BlockSpec(memory_space=pl.ANY)
F32, BF16 = jnp.float32, jnp.bfloat16
NEG = -1e30


def other_core():
    return {"mp": 1 - lax.axis_index("mp")}


def dot_nn(a, b):
    return lax.dot_general(a, b, (((1,), (0,)), ((), ())), preferred_element_type=F32)


def dot_nt(a, b):
    return lax.dot_general(a, b, (((1,), (1,)), ((), ())), preferred_element_type=F32)


def dot_tn(a, b):
    return lax.dot_general(a, b, (((0,), (0,)), ((), ())), preferred_element_type=F32)


def normalise(rows):
    average = jnp.mean(rows, axis=-1, keepdims=True)
    centred = rows - average
    variance = jnp.mean(centred * centred, axis=-1, keepdims=True)
    scale = lax.rsqrt(variance + EPSILON)
    return centred * scale, scale


def normalise_back(grad_hat, hat, scale):
    first = jnp.mean(grad_hat, axis=-1, keepdims=True)
    second = jnp.mean(grad_hat * hat, axis=-1, keepdims=True)
    return scale * (grad_hat - first - hat * second)


def to_rows(columns):
    lane = lax.broadcasted_iota(jnp.int32, (columns[0].shape[0], 128), 1)
    tile = jnp.zeros(lane.shape, F32)
    for i, column in enumerate(columns):
        tile = jnp.where(lane == i, column, tile)
    return tile.T[:8]


def to_columns(rows):
    return jnp.concatenate([rows] * 16, axis=0).T


class Planner:
    RATE = 0.045e6
    HOP = 1.5
    BACKLOG = 6.0

    def __init__(self):
        self.now = 0.0
        self.free = {}
        self.flying = []
        self.waiting = []
        self.started = []
        self.count = 0

    def launch(self, item, step):
        link, size = item.steps[step]
        begin = max(self.now, self.free.get(link, 0.0))
        self.free[link] = begin + size / self.RATE
        copy = item.send(step)
        self.started.append(copy)
        self.count += 1
        self.flying.append((self.free[link] + self.HOP, self.count, item, step, copy))

    def release(self):
        kept = []
        for item in self.waiting:
            link = item.steps[0][0]
            if self.free.get(link, 0.0) - self.now < self.BACKLOG:
                self.launch(item, 0)
            else:
                kept.append(item)
        self.waiting = kept

    def post(self, *items):
        self.waiting += items
        self.release()

    def run_until(self, time):
        while self.flying or self.waiting:
            if not self.flying:
                self.now = max(self.now, min(self.free[i.steps[0][0]] for i in self.waiting))
                self.release()
                continue
            first = min(self.flying, key=lambda f: f[:2])
            if first[0] > time:
                break
            self.flying.remove(first)
            self.now = max(self.now, first[0])
            _, _, item, step, copy = first
            item.take(step, copy)
            if step + 1 < len(item.steps):
                self.launch(item, step + 1)
            elif item.follow is not None:
                self.launch(item.follow, 0)
            self.release()
        if time != math.inf:
            self.now = max(self.now, time)
        self.release()

    def finish(self):
        self.run_until(math.inf)
        for copy in self.started:
            copy.wait_send()


class Chunk:
    def __init__(self, steps, send, take):
        self.steps, self.send, self.take, self.follow = steps, send, take, None


class Several:
    def __init__(self, copies):
        self.copies = copies

    def wait_recv(self):
        for copy in self.copies:
            copy.wait_recv()

    def wait_send(self):
        for copy in self.copies:
            copy.wait_send()


def decoder_kernel(
    names,
    vocab_here,
    part_cols,
    table_rows,
    n_dp,
    bits,
    low_bits,
    *refs,
):
    r = SimpleNamespace(**dict(zip(names, refs)))
    acoustic, memory, table = r.acoustic, r.memory, r.table
    targets, glance = r.targets, r.glance
    gain_1, bias_1 = r.gain_one[...], r.bias_one[...]
    gain_2, bias_2 = r.gain_two[...], r.bias_two[...]
    kernel_rows, rate_table = r.kernel_rows, r.rate_table
    token_lengths, memory_lengths, rate_groups = r.token_lengths, r.memory_lengths, r.rate_groups
    w_query, w_kv, w_out, w_in, w_back, w_vocab = r.w_query, r.w_kv, r.w_out, r.w_in, r.w_back, r.w_vocab
    mem_low, kv, padded, spare = r.mem_low, r.kv, r.padded, r.spare
    stream_in, stream_one, stream_two, stream_three = r.stream_in, r.stream_one, r.stream_two, r.stream_three
    one_low, queries, probs, mixed = r.one_low, r.queries, r.probs, r.mixed
    norm_low, hidden, gelu_slope, top = r.norm_low, r.hidden, r.gelu_slope, r.top
    logits, grad_logits, grad_others = r.logits, r.grad_logits, r.grad_others
    taken_mine, taken_theirs = r.taken_mine, r.taken_theirs
    grad_three, grad_two, branch_low = r.grad_three, r.grad_two, r.branch_low
    grad_pre, att_low, grad_queries = r.grad_pre, r.att_low, r.grad_queries
    mem_arrived, meta, stats, stats_arrived = r.mem_arrived, r.meta, r.stats, r.stats_arrived
    sent, arrived, gathered = r.sent, r.arrived, r.gathered
    small_sent, small_arrived = r.small_sent, r.small_arrived
    terms, term_blocks, term_arrived = grad_three, r.term_blocks, r.term_arrived
    onehot_lo, table_theirs, table_out = r.onehot_lo, r.table_theirs, r.table_mine
    swap_send, swap_recv, load_sem = r.swap_send, r.swap_recv, r.load_sem

    utterances, slots = targets.shape
    width = acoustic.shape[1]
    frames = memory.shape[0] // utterances
    half = w_query.shape[1]
    heads = half // HD
    tokens = utterances * slots
    me, core = lax.axis_index("dp"), lax.axis_index("mp")
    sibling = {"mp": 1 - core}
    quarter = lax.rem(me, 4)
    flips = [1 - 2 * lax.rem(me, 2), 2 - 4 * lax.rem(me // 2, 2)]
    mate = [me + flips[0] * (j % 2) + flips[1] * (j // 2) for j in range(4)]
    bit_of = {b: lax.rem(me // (1 << b), 2) for b in low_bits + bits}
    peer_of = {b: {"dp": me + (1 - 2 * bit_of[b]) * (1 << b)} for b in low_bits + bits}
    score_scale = 1.0 / math.sqrt(HD)

    loads = []

    def load(source, target):
        copy = pltpu.make_async_copy(source, target, load_sem.at[len(loads)])
        copy.start()
        loads.append(copy)
        return copy

    load_memory = load(memory, mem_low)
    load_kv = [
        load(r.w_key_hbm, w_kv.at[:, pl.ds(0, half)]),
        load(r.w_value_hbm, w_kv.at[:, pl.ds(half, half)]),
    ]
    load_query = load(r.w_query_hbm, w_query)
    load_out = load(r.w_out_hbm, w_out)

    barrier = pltpu.get_barrier_semaphore()

    def greet(k, carry):
        pl.semaphore_signal(
            barrier, inc=1, device_id={"dp": lax.rem(me + k, n_dp)}, device_id_type=MESH
        )
        return carry

    lax.fori_loop(1, n_dp, greet, 0)
    pl.semaphore_signal(barrier, inc=1, device_id=sibling, device_id_type=MESH)

    load_in = load(r.w_in_hbm, w_in)
    load_back = load(r.w_back_hbm, w_back)
    block = 1024
    per_core = table_rows // (2 * block)
    mains = 2 * per_core * block

    def load_table(k):
        at = pl.ds(pl.multiple_of((core * per_core + k) * block, block), block)
        return load(table.at[at, :], spare.at[pl.ds(k % 2 * block, block), :])

    table_loads = [load_table(0), load_table(1)]
    main = vocab_here // 256 * 256
    load_vocab = load(r.w_vocab_hbm.at[pl.ds(0, main), :], w_vocab.at[pl.ds(0, main), :])
    w_vocab[pl.ds(main, w_vocab.shape[0] - main), :] = jnp.zeros((w_vocab.shape[0] - main, width), BF16)
    w_vocab[pl.ds(main, vocab_here - main), :] = r.w_tail[...]
    r.table_rest[...] = jnp.zeros(r.table_rest.shape, BF16)
    r.table_rest[pl.ds(0, table_rows - mains), :] = r.table_tail[...]

    swaps = []

    def swap(source, target, device):
        k = len(swaps)
        copy = pltpu.make_async_remote_copy(
            src_ref=source,
            dst_ref=target,
            send_sem=swap_send.at[k],
            recv_sem=swap_recv.at[k],
            device_id=device,
            device_id_type=MESH,
        )
        copy.start()
        swaps.append(copy)
        return copy

    lane = lax.broadcasted_iota(jnp.int32, (1, slots), 1)
    row_of = lax.broadcasted_iota(jnp.int32, (8, slots), 0)
    for u in range(utterances):
        target_row = targets[pl.ds(u, 1), :].astype(F32)
        glance_row = glance[pl.ds(u, 1), :].astype(F32)
        valid_row = (lane < token_lengths[u]).astype(F32)
        meta[0, :, pl.ds(u * slots, slots)] = jnp.where(
            row_of == 0, target_row, jnp.where(row_of == 1, valid_row, glance_row)
        )
    own_columns = to_columns(meta[0])
    own_target = own_columns[:, 0:1]
    own_valid = own_columns[:, 1:2]

    def rows(u):
        return pl.ds(u * slots, slots)

    load_memory.wait()
    for copy in load_kv:
        copy.wait()
    step_rows = 256
    row_chunks = frames // step_rows

    def kv_step(i, carry):
        at = pl.ds(pl.multiple_of(i * step_rows, step_rows), step_rows)
        group = jnp.zeros((1, width), jnp.int32) + rate_groups[i // row_chunks]
        rate_row = jnp.where(group == 1, rate_table[pl.ds(1, 1), :], rate_table[pl.ds(0, 1), :])
        low = (mem_low[at, :].astype(F32) + rate_row).astype(BF16)
        mem_low[at, :] = low
        kv[at, :] = dot_nn(low, w_kv[...]).astype(BF16)
        return carry

    lax.fori_loop(0, utterances * row_chunks, kv_step, 0)

    edge = jnp.zeros((8, width), F32)
    for u in range(utterances):
        padded[u, pl.ds(0, 8), :] = edge
        padded[u, pl.ds(8 + slots, 8), :] = edge

    pl.semaphore_wait(barrier, n_dp)
    load_query.wait()
    load_out.wait()

    def key_of(u, h):
        return kv[pl.ds(u * frames, frames), pl.ds(h * HD, HD)]

    def value_of(u, h):
        return kv[pl.ds(u * frames, frames), pl.ds(half + h * HD, HD)]

    frame_lane = lax.broadcasted_iota(jnp.int32, (1, frames), 1)

    def look_up(first_row, count, allowed, source):
        ids = first_row + lax.broadcasted_iota(jnp.int32, (1, count), 1)
        local = jnp.where(allowed, own_target.astype(jnp.int32), -1)
        onehot = jnp.where(ids == local, 1.0, 0.0).astype(BF16)
        return dot_nn(onehot, source)

    def look_up_block(k):
        table_loads[k].wait()
        part = look_up(
            (core * per_core + k) * block, block, True, spare[pl.ds(k % 2 * block, block), :]
        )
        for u in range(utterances):
            piece = part[u * slots : (u + 1) * slots]
            taken_mine[u] = piece if k == 0 else taken_mine[u] + piece
        if k + 2 < per_core:
            table_loads.append(load_table(k + 2))

    def look_up_rest():
        part = look_up(mains, r.table_rest.shape[0], core == 0, r.table_rest[...])
        for u in range(utterances):
            taken_mine[u] = taken_mine[u] + part[u * slots : (u + 1) * slots]

    def local_targets(target_column):
        local = target_column.astype(jnp.int32) - core * vocab_here
        return jnp.where((local >= 0) & (local < vocab_here), local, -1)

    def vocab_tile(tile, first, col, target, top_m, picked):
        ids = col + lax.broadcasted_iota(jnp.int32, (1, 128), 1)
        tile = jnp.where(ids < vocab_here, tile, NEG)
        logits[first] = tile
        return jnp.maximum(top_m, tile), picked + jnp.where(ids == target, tile, 0.0)

    def vocab_stats(target):
        start = (jnp.full((tokens, 128), NEG, F32), jnp.zeros((tokens, 128), F32))

        def step(j, carry):
            col = pl.multiple_of(j * 256, 256)
            product = dot_nt(top[0], w_vocab[pl.ds(col, 256), :])
            carry = vocab_tile(product[:, :128], 2 * j, col, target, *carry)
            return vocab_tile(product[:, 128:], 2 * j + 1, col + 128, target, *carry)

        top_m, picked = lax.fori_loop(0, w_vocab.shape[0] // 256, step, start)
        top_row = jnp.max(top_m, axis=1, keepdims=True)

        def add(j, total):
            return total + jnp.exp(logits[j] - top_row)

        total = lax.fori_loop(0, w_vocab.shape[0] // 128, add, jnp.zeros((tokens, 128), F32))
        return (
            top_row,
            jnp.sum(total, axis=1, keepdims=True),
            jnp.sum(picked, axis=1, keepdims=True),
        )

    def join(blocks):
        top_value = blocks[0][0:1]
        for b in blocks[1:]:
            top_value = jnp.maximum(top_value, b[0:1])
        total, picked = 0.0, 0.0
        for b in blocks:
            total = total + b[1:2] * jnp.exp(b[0:1] - top_value)
            picked = picked + b[2:3]
        return top_value + jnp.log(total), picked

    def forward(second, beside_one=None, beside_two=None):
        copies = []
        for u in range(utterances):
            at = rows(u)
            valid = own_valid[u * slots : (u + 1) * slots]
            hat, _ = normalise(stream_in[at, :])
            padded[u, pl.ds(8, slots), :] = (hat * gain_1 + bias_1) * valid
            for j in range(width // 128):
                cols = pl.ds(j * 128, 128)
                total = jnp.zeros((slots, 128), F32)
                for k in range(kernel_rows.shape[0]):
                    shift = 8 + k - kernel_rows.shape[0] // 2
                    total = total + kernel_rows[pl.ds(k, 1), cols] * padded[u, pl.ds(shift, slots), cols]
                stream_one[at, cols] = stream_in[at, cols] + total * valid
            low = stream_one[at, :].astype(BF16)
            one_low[at, :] = low
            queries[at, :] = dot_nn(low, w_query[...]).astype(BF16)
            frame_ok = frame_lane < memory_lengths[u]
            for h in range(heads):
                cols = pl.ds(h * HD, HD)
                scores = dot_nt(queries[at, cols], key_of(u, h)) * score_scale
                scores = jnp.where(frame_ok, scores, NEG)
                raised = jnp.exp(scores - jnp.max(scores, axis=-1, keepdims=True))
                prob = raised * (1.0 / jnp.sum(raised, axis=-1, keepdims=True))
                if second:
                    probs[u, h] = prob
                mixed[at, cols] = dot_nn(prob.astype(BF16), value_of(u, h)).astype(BF16)
            sent[u] = dot_nn(mixed[at, :], w_out[...])
            copies.append(swap(sent.at[u], arrived.at[u], sibling))
        if not second:
            beside_one()
            load_in.wait()
            load_back.wait()
        ff_copies = []
        for u in range(utterances):
            at = rows(u)
            copies[u].wait()
            two = stream_one[at, :] + (sent[u] + arrived[u])
            stream_two[at, :] = two
            hat, _ = normalise(two)
            low = (hat * gain_2 + bias_2).astype(BF16)
            norm_low[at, :] = low
            pre = dot_nn(low, w_in[...])
            phi = 0.5 * (1.0 + lax.erf(pre * math.sqrt(0.5)))
            hidden[at, :] = (pre * phi).astype(BF16)
            if second:
                gelu_slope[at, :] = phi + pre * (
                    jnp.exp(-0.5 * pre * pre) * (1.0 / math.sqrt(2.0 * math.pi))
                )
            sent[utterances + u] = dot_nn(hidden[at, :], w_back[...])
            ff_copies.append(swap(sent.at[utterances + u], arrived.at[utterances + u], sibling))
        if not second:
            beside_two()
        for u in range(utterances):
            at = rows(u)
            ff_copies[u].wait()
            three = stream_two[at, :] + (sent[utterances + u] + arrived[utterances + u])
            stream_three[u] = three
            top[0, at, :] = three.astype(BF16)

    stream_in[...] = acoustic[...].astype(F32)

    def beside_one():
        look_up_block(0)
        look_up_block(1)

    def beside_two():
        for k in range(2, per_core):
            look_up_block(k)
        look_up_rest()

    forward(False, beside_one, beside_two)
    table_swap = swap(taken_mine, taken_theirs, sibling)
    load_vocab.wait()
    own_local = local_targets(own_target)
    stats[0] = to_rows(vocab_stats(own_local))
    first_swap = swap(stats.at[0], stats_arrived.at[0], sibling)
    table_swap.wait()
    first_swap.wait()
    log_total, picked = join([stats[0], stats_arrived[0]])
    first_loss = (log_total - picked) * meta[0, 1:2, :]
    blend_row = meta[0, 2:3, :] * meta[0, 1:2, :] / (1.0 + jnp.exp(math.log(V) - first_loss))
    blend = to_columns(jnp.concatenate([blend_row] * 8, axis=0))[:, 0:1]
    for u in range(utterances):
        at = rows(u)
        wide_acoustic = acoustic[at, :].astype(F32)
        taken = taken_mine[u] + taken_theirs[u]
        stream_in[at, :] = wide_acoustic + blend[u * slots : (u + 1) * slots] * (taken - wide_acoustic)

    forward(True)
    token_swaps = [
        swap(stream_three.at[core], gathered.at[j - 1, 0], {"dp": mate[j]}) for j in range(1, 4)
    ]
    stats[1] = to_rows(vocab_stats(own_local))
    stat_swap = swap(stats.at[1], stats_arrived.at[1], sibling)
    stat_swap.wait()
    log_total, picked = join([stats[1], stats_arrived[1]])
    loss = (log_total - picked) * meta[0, 1:2, :]
    for u in range(utterances):
        r.loss_out[pl.ds(u, 1), :] = loss[:, u * slots : (u + 1) * slots]
    meta[0] = jnp.where(
        lax.broadcasted_iota(jnp.int32, (8, tokens), 0) == 3, log_total, meta[0]
    )
    meta_swaps = [swap(meta.at[0], meta.at[j], {"dp": mate[j]}) for j in range(1, 4)]

    log_column = to_columns(meta[0])[:, 3:4]

    def slope(j, carry):
        col = pl.multiple_of(j * 128, 128)
        ids = col + lax.broadcasted_iota(jnp.int32, (1, 128), 1)
        onehot = jnp.where(ids == own_local, 1.0, 0.0)
        grad = (jnp.exp(logits[j] - log_column) - onehot) * own_valid
        grad_logits[:, pl.ds(col, 128)] = grad.astype(BF16)
        return carry

    lax.fori_loop(0, w_vocab.shape[0] // 128, slope, 0)
    three_copies = []
    for u in range(utterances):
        sent[u] = dot_nn(grad_logits[rows(u), :], w_vocab[...])
        three_copies.append(swap(sent.at[u], arrived.at[u], sibling))

    plan = Planner()
    steps_all = len(bits)
    scatter_send, scatter_recv = r.scatter_send, r.scatter_recv

    def make_chunk(index):
        name, start, cols, order = chunk_list(part_cols, width, bits, low_bits, r)[index]
        source, landing = getattr(r, "src_" + name), r.landing[index]
        out = r.vocab_sum if name == "vocab" and not low_bits else getattr(r, name + "_out")
        rows_here = source.shape[-2]

        def pick(step, which):
            rest = sorted([b for b in bits if b not in order[:step]], reverse=True)
            where = tuple(which if b == order[step] else slice(None) for b in rest)
            if step == 0:
                return source, where + (slice(None), pl.ds(start, cols))
            return landing[step - 1], where + (slice(None), slice(None))

        def send(step):
            b = order[step]
            ref, where = pick(step, 1 - bit_of[b])
            copy = pltpu.make_async_remote_copy(
                src_ref=ref.at[where],
                dst_ref=landing[step],
                send_sem=scatter_send.at[index, step],
                recv_sem=scatter_recv.at[index, step],
                device_id=peer_of[b],
                device_id_type=MESH,
            )
            copy.start()
            return copy

        def take(step, copy):
            copy.wait_recv()
            ref, where = pick(step, bit_of[order[step]])
            got = landing[step]
            at = pl.ds(start, cols)
            if step < len(order) - 1:
                got[...] = got[...] + ref[where]
            elif name == "vocab":
                out[..., at] = got[...] + ref[where]
            else:
                out[:, at] = got[...] + ref[where]

        steps = [
            (link_of(b, bits), rows_here * cols * 4 * 2 ** (steps_all - 1 - s))
            for s, b in enumerate(order)
        ]
        return Chunk(steps, send, take)

    def make_trade(start, cols):
        summed, traded = r.vocab_sum, r.vocab_traded
        at = pl.ds(start, cols)

        def send(step):
            copies = []
            for j in range(1, 4):
                to = lax.rem(mate[j], 4)
                copies.append(
                    pltpu.make_async_remote_copy(
                        src_ref=summed.at[to // 2, lax.rem(to, 2), :, at],
                        dst_ref=traded.at[j - 1, :, at],
                        send_sem=r.trade_send.at[start // 128, j - 1],
                        recv_sem=r.trade_recv.at[start // 128, j - 1],
                        device_id={"dp": mate[j]},
                        device_id_type=MESH,
                    )
                )
                copies[-1].start()
            return Several(copies)

        def take(step, copies):
            copies.wait_recv()
            for j in range(1, 4):
                r.vocab_out[lax.rem(mate[j], 4), :, at] = traded[j - 1, :, at]
            r.vocab_out[quarter, :, at] = summed[quarter // 2, lax.rem(quarter, 2), :, at]

        return Chunk([(0, 2 * r.src_vocab.shape[-2] * cols * 4)], send, take)

    chunks = {}
    for index, (name, start, cols, _) in enumerate(chunk_list(part_cols, width, bits, low_bits, r)):
        chunks[name, start] = make_chunk(index)
        if name == "vocab" and not low_bits:
            chunks[name, start].follow = make_trade(start, cols)

    def put(name, at, product):
        source = getattr(r, "src_" + name)
        source[..., at] = product.reshape(source.shape[:-1] + (product.shape[1],))

    copies = []
    for u in range(utterances):
        at = rows(u)
        three_copies[u].wait()
        three = sent[u] + arrived[u]
        grad_three[u] = three
        low = three.astype(BF16)
        branch_low[at, :] = low
        pre = (dot_nt(low, w_back[...]) * gelu_slope[at, :]).astype(BF16)
        grad_pre[at, :] = pre
        sent[utterances + u] = dot_nt(pre, w_in[...])
        copies.append(swap(sent.at[utterances + u], arrived.at[utterances + u], sibling))
    plan.run_until(4.0)
    for name, left, right in (("back", branch_low, hidden), ("in", norm_low, grad_pre)):
        left_turned = left[...].T
        for start in sorted(s for n, s in chunks if n == name):
            at = pl.ds(start, 512)
            put(name, at, dot_nn(left_turned, right[:, at]))
            plan.run_until(plan.now + 0.5)
            plan.post(chunks[name, start])

    at_core = pl.ds(pl.multiple_of(core * slots, slots), slots)
    at_other = pl.ds(pl.multiple_of((1 - core) * slots, slots), slots)
    share_swaps = []
    for j in range(1, 4):
        token_swaps[j - 1].wait()
        share_swaps.append(swap(gathered.at[j - 1, 0], gathered.at[j - 1, 1], sibling))
        top[j, at_core, :] = gathered[j - 1, 0].astype(BF16)
    base = pl.multiple_of(
        quarter * part_cols - quarter // 3 * (4 * part_cols - w_vocab.shape[0]), 128
    )
    pieces = [(c, 256) for c in range(0, part_cols // 256 * 256, 256)]
    if part_cols % 256:
        pieces.append((part_cols // 256 * 256, part_cols % 256))
    for j in range(1, 4):
        meta_swaps[j - 1].wait()
        columns = to_columns(meta[j])
        target, valid, log_total = local_targets(columns[:, 0:1]), columns[:, 1:2], columns[:, 3:4]
        share_swaps[j - 1].wait()
        top[j, at_other, :] = gathered[j - 1, 1].astype(BF16)
        for col, cols in pieces:
            ids = base + col + lax.broadcasted_iota(jnp.int32, (1, cols), 1)
            tile = dot_nt(top[j], w_vocab[pl.ds(base + col, cols), :])
            tile = jnp.where(ids < vocab_here, tile, NEG)
            grad = (jnp.exp(tile - log_total) - jnp.where(ids == target, 1.0, 0.0)) * valid
            grad_others[pl.ds((j - 1) * tokens, tokens), pl.ds(col, cols)] = grad.astype(BF16)
        plan.run_until(plan.now + 0.8)
    top_turned = r.top_turned
    for j in range(4):
        top_turned[:, pl.ds(j * tokens, tokens)] = top[j].T
    starts = sorted(start for name, start in chunks if name == "vocab")
    for start, stop in zip(starts, starts[1:] + [part_cols]):
        for col in range(start, stop, 256):
            cols = min(256, stop - col)
            product = dot_nn(top_turned[:, pl.ds(0, tokens)], grad_logits[:, pl.ds(base + col, cols)])
            product = product + dot_nn(
                top_turned[:, pl.ds(tokens, 3 * tokens)], grad_others[:, pl.ds(col, cols)]
            )
            put("vocab", pl.ds(col, cols), product)
        plan.run_until(plan.now + 0.7)
        plan.post(chunks["vocab", start])

    one_copies = []
    gain_2_total, bias_2_total = 0.0, 0.0
    for u in range(utterances):
        at = rows(u)
        copies[u].wait()
        grad_norm = sent[utterances + u] + arrived[utterances + u]
        hat, scale = normalise(stream_two[at, :])
        gain_2_total = gain_2_total + jnp.sum(grad_norm * hat, axis=0, keepdims=True)
        bias_2_total = bias_2_total + jnp.sum(grad_norm, axis=0, keepdims=True)
        two = grad_three[u] + normalise_back(grad_norm * gain_2, hat, scale)
        grad_two[at, :] = two
        low = two.astype(BF16)
        att_low[at, :] = low
        grad_mixed = dot_nt(low, w_out[...]).astype(BF16)
        for h in range(heads):
            cols = pl.ds(h * HD, HD)
            grad_head = grad_mixed[:, h * HD : (h + 1) * HD]
            prob = probs[u, h]
            grad_prob = dot_nt(grad_head, value_of(u, h))
            spare[pl.ds(u * frames, frames), pl.ds(half + h * HD, HD)] = dot_tn(
                prob.astype(BF16), grad_head
            ).astype(BF16)
            inner = jnp.sum(prob * grad_prob, axis=-1, keepdims=True)
            grad_score = (prob * (grad_prob - inner)).astype(BF16)
            grad_queries[at, cols] = (dot_nn(grad_score, key_of(u, h)) * score_scale).astype(BF16)
            spare[pl.ds(u * frames, frames), cols] = (
                dot_tn(grad_score, queries[at, cols]) * score_scale
            ).astype(BF16)
            plan.run_until(plan.now + 1.5)
        sent[u] = dot_nt(grad_queries[at, :], w_query[...])
        one_copies.append(swap(sent.at[u], arrived.at[u], sibling))
    every = slice(None)
    put("out", every, dot_tn(att_low[...], mixed[...]))
    plan.post(chunks["out", 0])
    put("query", every, dot_tn(one_low[...], grad_queries[...]))
    plan.post(chunks["query", 0])
    plan.run_until(plan.now + 1.0)

    mem_copies = []
    rate_sums = [0.0, 0.0]
    for u in range(utterances):
        total = jnp.zeros((1, width), F32)
        for i in range(row_chunks):
            at = pl.ds(u * frames + i * step_rows, step_rows)
            part = dot_nt(spare[at, :], w_kv[...])
            for j in range(width // 128):
                side_of, tile = j // (width // 256), j % (width // 256)
                index = ((side_of * utterances + u) * row_chunks + i) * (width // 256) + tile
                logits[index] = part[:, j * 128 : (j + 1) * 128]
            total = total + jnp.sum(part, axis=0, keepdims=True)
        tiles = row_chunks * (width // 256)
        mem_copies.append(
            swap(
                logits.at[pl.ds(((1 - core) * utterances + u) * tiles, tiles)],
                mem_arrived.at[pl.ds(u * tiles, tiles)],
                sibling,
            )
        )
        group = jnp.zeros((1, width), jnp.int32) + rate_groups[u]
        for k in range(2):
            rate_sums[k] = rate_sums[k] + jnp.where((group == 1) == (k == 1), total, 0.0)
        plan.run_until(plan.now + 1.2)
    span = frames // 2
    for k in range(2 * utterances):
        at = pl.ds(k * span, span)
        product = dot_tn(mem_low[at, :], spare[at, :])
        product = product.reshape(r.src_kv.shape)
        r.src_kv[...] = product if k == 0 else r.src_kv[...] + product
    plan.run_until(plan.now + 2.0)
    plan.post(*[chunks["kv", start] for start in sorted(s for n, s in chunks if n == "kv")])

    gain_1_total, bias_1_total = 0.0, 0.0
    for u in range(utterances):
        at = rows(u)
        valid = own_valid[u * slots : (u + 1) * slots]
        one_copies[u].wait()
        one = grad_two[at, :] + (sent[u] + arrived[u])
        grad_two[at, :] = one
        masked = one * valid
        for k in range(kernel_rows.shape[0]):
            shift = 8 + k - kernel_rows.shape[0] // 2
            row = jnp.sum(masked * padded[u, pl.ds(shift, slots), :], axis=0, keepdims=True)
            if u == 0:
                small_sent[0, pl.ds(k, 1), :] = row
            else:
                small_sent[0, pl.ds(k, 1), :] = small_sent[0, pl.ds(k, 1), :] + row
        padded[u, pl.ds(8, slots), :] = masked
        for j in range(width // 128):
            cols = pl.ds(j * 128, 128)
            total = jnp.zeros((slots, 128), F32)
            for k in range(kernel_rows.shape[0]):
                shift = 8 - k + kernel_rows.shape[0] // 2
                total = total + kernel_rows[pl.ds(k, 1), cols] * padded[u, pl.ds(shift, slots), cols]
            stream_one[at, cols] = total * valid
        grad_norm = stream_one[at, :]
        hat, scale = normalise(stream_in[at, :])
        gain_1_total = gain_1_total + jnp.sum(grad_norm * hat, axis=0, keepdims=True)
        bias_1_total = bias_1_total + jnp.sum(grad_norm, axis=0, keepdims=True)
        zero = grad_two[at, :] + normalise_back(grad_norm * gain_1, hat, scale)
        terms[u] = blend[u * slots : (u + 1) * slots] * zero
        stream_one[at, :] = zero - terms[u]
        plan.run_until(plan.now + 1.5)

    last_taps = kernel_rows.shape[0]
    small_sent[0, pl.ds(last_taps, 12 - last_taps), :] = jnp.zeros((12 - last_taps, width), F32)
    for i, row in enumerate((gain_1_total, bias_1_total, gain_2_total, bias_2_total)):
        small_sent[0, pl.ds(12 + i, 1), :] = row
    for k in range(2):
        small_sent[0, pl.ds(16 + k, 1), :] = rate_sums[k]
    small_sent[0, pl.ds(18, 6), :] = jnp.zeros((6, width), F32)
    small_peers = [peer_of[b] for b in low_bits + bits] + [sibling]

    def small_send(step):
        copy = pltpu.make_async_remote_copy(
            src_ref=small_sent.at[step],
            dst_ref=small_arrived.at[step],
            send_sem=r.small_send.at[step],
            recv_sem=r.small_recv.at[step],
            device_id=small_peers[step],
            device_id_type=MESH,
        )
        copy.start()
        return copy

    def small_take(step, copy):
        copy.wait_recv()
        if step + 1 < len(small_peers):
            small_sent[step + 1] = small_sent[step] + small_arrived[step]
        else:
            r.small_out[pl.ds(0, 16), :] = small_sent[step, pl.ds(0, 16), :]
            r.small_out[pl.ds(16, 8), :] = (
                small_sent[step, pl.ds(16, 8), :] + small_arrived[step, pl.ds(16, 8), :]
            )

    small_links = [link_of(b, bits) for b in low_bits + bits] + ["core"]
    plan.post(Chunk([(l, 24 * width * 4) for l in small_links], small_send, small_take))

    features = width // n_dp
    feature_rows = max(features, 8)
    block_rows = term_blocks.shape[1]
    turned = terms[core].T
    id_row = targets[pl.ds(core, 1), :].astype(F32)
    rest = block_rows - features - 1
    for p in range(n_dp):
        term_blocks[p, pl.ds(0, features), :] = turned[p * features : (p + 1) * features]
        term_blocks[p, pl.ds(features, 1), :] = id_row
        term_blocks[p, pl.ds(features + 1, rest), :] = jnp.zeros((rest, slots), F32)

    def term_copy(k):
        there = lax.rem(me + k, n_dp)
        return pltpu.make_async_remote_copy(
            src_ref=term_blocks.at[there],
            dst_ref=term_arrived.at[me],
            send_sem=r.term_send.at[k],
            recv_sem=r.term_recv.at[k],
            device_id={"dp": there},
            device_id_type=MESH,
        )

    def term_start(k, carry):
        term_copy(k).start()
        return carry

    def term_wait(k, carry):
        term_copy(k).wait()
        return carry

    term_arrived[me] = term_blocks[me]
    lax.fori_loop(1, n_dp, term_start, 0)
    stores = []

    def store(source, target):
        copy = pltpu.make_async_copy(source, target, r.store_sem.at[len(stores)])
        copy.start()
        stores.append(copy)

    store(stream_one, r.acoustic_out)
    for u in range(utterances):
        mem_copies[u].wait()
        for i in range(row_chunks):
            for j in range(width // 256):
                index = (u * row_chunks + i) * (width // 256) + j
                first_tile = (core * utterances) * row_chunks * (width // 256)
                mem_arrived[index] = logits[first_tile + index] + mem_arrived[index]
                at = pl.ds(u * frames + i * step_rows, step_rows)
                store(mem_arrived.at[index], r.memory_out.at[at, pl.ds(j * 128, 128)])
    plan.run_until(plan.now + 8.0)
    lax.fori_loop(1, n_dp, term_wait, 0)
    per_piece = 512 // slots
    blocks_hi = table_out.shape[1] // 256
    batch = 4

    def table_piece(p, fresh):
        found = [term_arrived[p * per_piece + i] for i in range(per_piece)]
        values = jnp.concatenate([f[:feature_rows] for f in found], axis=1)
        ids = jnp.concatenate([f[features : features + 1] for f in found], axis=1).astype(jnp.int32)
        low_ids, high_ids = ids & 255, ids >> 8
        onehot_lo[...] = jnp.where(
            lax.broadcasted_iota(jnp.int32, (256, 512), 0) == low_ids, 1.0, 0.0
        ).astype(BF16)
        coarse = values.astype(BF16).astype(F32)
        both = jnp.concatenate([coarse, values - coarse], axis=0)
        for first_hi in range(0, blocks_hi, batch):
            here = range(first_hi, min(first_hi + batch, blocks_hi))
            masked = jnp.concatenate([jnp.where(high_ids == hi, both, 0.0) for hi in here], axis=0)
            product = dot_nt(masked.astype(BF16), onehot_lo[...])
            for i, hi in enumerate(here):
                top_part = product[2 * i * feature_rows : (2 * i + 1) * feature_rows]
                low_part = product[(2 * i + 1) * feature_rows : (2 * i + 2) * feature_rows]
                at = pl.ds(hi * 256, 256)
                if fresh:
                    table_out[:, at] = top_part + low_part
                else:
                    table_out[:, at] = table_out[:, at] + (top_part + low_part)

    pieces = n_dp // per_piece
    table_piece(0, True)
    if pieces <= 4:
        for p in range(1, pieces):
            plan.run_until(plan.now + 1.5)
            table_piece(p, False)
    else:
        lax.fori_loop(1, pieces, lambda p, c: (table_piece(p, False), c)[1], 0)
    table_swap = swap(table_out, table_theirs, sibling)
    plan.run_until(plan.now + 3.0)
    table_swap.wait()
    table_out[...] = table_out[...] + table_theirs[...]
    store(table_out, r.table_out)
    plan.finish()
    for copy in stores:
        copy.wait()


def link_of(bit, bits):
    if bit == bits[-1]:
        return bits[-2]
    return bit


def chunk_list(part_cols, width, bits, low_bits, sizes):
    turned = [bits[1], bits[0]] + bits[2:]
    listing = []
    tiles = part_cols // 128
    edges = [tiles * k // 3 * 128 for k in range(4)]
    for k in range(3):
        order = [b for b in bits if b > 1]
        listing.append(("vocab", edges[k], edges[k + 1] - edges[k], order))
    for name, order in (("back", turned), ("in", bits)):
        for start in range(0, sizes.units, 512):
            listing.append((name, start, 512, order))
    listing.append(("out", 0, sizes.half, turned))
    listing.append(("query", 0, sizes.half, bits))
    for k, start in enumerate(range(0, 2 * sizes.half, 256)):
        listing.append(("kv", start, 256, [bits, turned][k % 2]))
    return listing


def decoder_call(
    acoustic, memory, embedding, w_query, w_key, w_value, w_out, w_in, w_back, w_vocab, norms,
    fsmn_kernel, rate_table, token_lengths, memory_lengths, rate_groups, glance, targets, n_dp,
):
    utterances = token_lengths.shape[0]
    tokens, width = acoustic.shape
    slots = tokens // utterances
    mem_rows = memory.shape[0]
    half = w_query.shape[1]
    heads = half // HD
    frames = mem_rows // utterances
    units = w_in.shape[1]
    vocab_here = w_vocab.shape[1]
    table_rows = embedding.shape[0]
    part_cols = ((vocab_here + 127) // 128 + 3) // 4 * 128
    all_cols = (vocab_here + 255) // 256 * 256
    w_turned = w_vocab.T
    main = vocab_here // 256 * 256
    mains = table_rows // 2048 * 2048
    nbits = n_dp.bit_length() - 1
    steps = nbits
    while width >> steps < 8:
        steps -= 1
    low_bits, bits = list(range(nbits - steps)), list(range(nbits - steps, nbits))
    rows = width >> steps
    features = width // n_dp
    feature_rows = max(features, 8)
    block_rows = feature_rows + 8 if features >= 8 else 8
    blocks_hi = (table_rows + 255) // 256
    sizes = SimpleNamespace(units=units, half=half)
    plane = [b for b in bits if b < 2]
    listing = chunk_list(part_cols, width, bits, low_bits, sizes)
    most = max(len(c[3]) for c in listing)

    f32 = lambda *shape: jax.ShapeDtypeStruct(shape, F32)
    v32 = lambda *shape: pltpu.VMEM(shape, F32)
    v16 = lambda *shape: pltpu.VMEM(shape, BF16)
    dma = lambda *shape: pltpu.SemaphoreType.DMA(shape)
    inputs = dict(
        acoustic=(VMEM, acoustic),
        w_tail=(VMEM, w_turned[main:]),
        table_tail=(VMEM, embedding[mains:]),
        memory=(ANY, memory),
        table=(ANY, embedding),
        w_query_hbm=(ANY, w_query),
        w_key_hbm=(ANY, w_key),
        w_value_hbm=(ANY, w_value),
        w_out_hbm=(ANY, w_out),
        w_in_hbm=(ANY, w_in),
        w_back_hbm=(ANY, w_back),
        w_vocab_hbm=(ANY, w_turned),
        gain_one=(VMEM, norms[0][None]),
        bias_one=(VMEM, norms[1][None]),
        gain_two=(VMEM, norms[2][None]),
        bias_two=(VMEM, norms[3][None]),
        kernel_rows=(VMEM, fsmn_kernel),
        rate_table=(VMEM, rate_table),
        token_lengths=(SMEM, token_lengths),
        memory_lengths=(SMEM, memory_lengths),
        rate_groups=(SMEM, rate_groups),
        glance=(VMEM, glance.reshape(utterances, slots)),
        targets=(VMEM, targets.reshape(utterances, slots)),
    )
    outputs = dict(
        loss_out=f32(utterances, slots),
        small_out=f32(24, width),
        vocab_out=f32(*((2,) * len(plane) if low_bits else (4,)), rows, part_cols),
        in_out=f32(rows, units),
        back_out=f32(rows, units),
        query_out=f32(rows, half),
        out_out=f32(rows, half),
        kv_out=f32(rows, 2 * half),
        acoustic_out=f32(tokens, width),
        memory_out=f32(mem_rows, width // 2),
        table_out=f32(feature_rows, blocks_hi * 256),
    )
    shape = (2,) * steps + (rows,)
    scratch = dict(
        w_query=v16(width, half),
        w_kv=v16(width, 2 * half),
        w_out=v16(half, width),
        w_in=v16(width, units),
        w_back=v16(units, width),
        w_vocab=v16(all_cols, width),
        mem_low=v16(mem_rows, width),
        kv=v16(mem_rows, 2 * half),
        spare=v16(mem_rows, 2 * half),
        padded=v32(utterances, slots + 16, width),
        stream_in=v32(tokens, width),
        stream_one=v32(tokens, width),
        stream_two=v32(tokens, width),
        stream_three=v32(utterances, slots, width),
        one_low=v16(tokens, width),
        queries=v16(tokens, half),
        probs=v32(utterances, heads, slots, frames),
        mixed=v16(tokens, half),
        norm_low=v16(tokens, width),
        hidden=v16(tokens, units),
        gelu_slope=v32(tokens, units),
        top=v16(4, tokens, width),
        logits=v32(all_cols // 128, tokens, 128),
        grad_logits=v16(tokens, all_cols),
        grad_others=v16(3 * tokens, part_cols),
        top_turned=v16(width, 4 * tokens),
        taken_mine=v32(utterances, slots, width),
        taken_theirs=v32(utterances, slots, width),
        grad_three=v32(utterances, slots, width),
        grad_two=v32(tokens, width),
        branch_low=v16(tokens, width),
        grad_pre=v16(tokens, units),
        att_low=v16(tokens, width),
        grad_queries=v16(tokens, half),
        mem_arrived=v32(mem_rows // 256 * (width // 256), 256, 128),
        meta=v32(4, 8, tokens),
        stats=v32(2, 8, tokens),
        stats_arrived=v32(2, 8, tokens),
        sent=v32(2 * utterances, slots, width),
        arrived=v32(2 * utterances, slots, width),
        gathered=v32(3, 2, slots, width),
        small_sent=v32(nbits + 1, 24, width),
        small_arrived=v32(nbits + 1, 24, width),
        term_blocks=v32(n_dp, block_rows, slots),
        term_arrived=v32(n_dp, block_rows, slots),
        onehot_lo=v16(256, 512),
        table_rest=v16((table_rows - mains + 127) // 128 * 128, width),
        table_theirs=v32(feature_rows, blocks_hi * 256),
        table_mine=v32(feature_rows, blocks_hi * 256),
        src_vocab=v32(*shape, part_cols),
        src_back=v32(*shape, units),
        vocab_sum=v32(*(2,) * len(plane), rows, part_cols),
        vocab_traded=v32(3, rows, part_cols),
        src_in=v32(*shape, units),
        src_out=v32(*shape, half),
        src_query=v32(*shape, half),
        src_kv=v32(*shape, 2 * half),
        load_sem=dma(24),
        store_sem=dma(24),
        trade_send=dma(part_cols // 128, 3),
        trade_recv=dma(part_cols // 128, 3),
        swap_send=dma(40),
        swap_recv=dma(40),
        scatter_send=dma(len(listing), most),
        scatter_recv=dma(len(listing), most),
        small_send=dma(nbits + 1),
        small_recv=dma(nbits + 1),
        term_send=dma(n_dp),
        term_recv=dma(n_dp),
    )
    landing = [
        [v32(*(2,) * (steps - 1 - s), rows, cols) for s in range(len(order))]
        for _, _, cols, order in listing
    ]
    names = list(inputs) + list(outputs) + list(scratch)
    flat = [ref for chunk in landing for ref in chunk]

    def kernel(*refs):
        named, rest = refs[: len(names)], list(refs[len(names) :])
        lands = [[rest.pop(0) for _ in chunk] for chunk in landing]
        decoder_kernel(
            names + ["landing", "units", "half"], vocab_here, part_cols, table_rows, n_dp, bits,
            low_bits, *named, lands, units, half,
        )

    out = pl.pallas_call(
        kernel,
        out_shape=list(outputs.values()),
        in_specs=[spec for spec, _ in inputs.values()],
        out_specs=[VMEM] * (len(outputs) - 3) + [ANY] * 3,
        scratch_shapes=list(scratch.values()) + flat,
        compiler_params=pltpu.CompilerParams(
            collective_id=1, has_side_effects=True, vmem_limit_bytes=64 << 20
        ),
    )(*[value for _, value in inputs.values()])
    return SimpleNamespace(**dict(zip(outputs, out))), low_bits


def deliver_kernel(n_dp, *refs):
    loss_from, small_from, table_from, vocab_from, kv_from = refs[:5]
    query, out, in_, back, acoustic, memory = refs[5:11]
    (
        loss_to, gain_one_to, bias_one_to, gain_two_to, bias_two_to, taps_to, rate_to,
        table_to, vocab_to, key_to, value_to, query_to, out_to, in_to, back_to, acoustic_to, memory_to,
    ) = refs[11:28]
    loss, small, table, vocab, kv, sem = refs[28:]
    copies = []
    for source, target in (
        (loss_from, loss), (small_from, small), (table_from, table), (vocab_from, vocab), (kv_from, kv),
        (memory, memory_to), (acoustic, acoustic_to), (in_, in_to), (back, back_to),
        (query, query_to), (out, out_to),
    ):
        copies.append(pltpu.make_async_copy(source, target, sem.at[len(copies)]))
        copies[-1].start()
    for copy in copies[:5]:
        copy.wait()
    slots = loss.shape[1]
    for u in range(loss.shape[0]):
        loss_to[:, pl.ds(u * slots, slots)] = loss[pl.ds(u, 1), :]
    me = lax.axis_index("dp")
    own = small.shape[1] // n_dp
    mine = jnp.zeros((16, own), F32)
    for p in range(n_dp):
        mine = jnp.where(me == p, small[pl.ds(0, 16), p * own : (p + 1) * own], mine)
    taps_to[...] = mine[: taps_to.shape[0]]
    for i, target in enumerate((gain_one_to, bias_one_to, gain_two_to, bias_two_to)):
        target[...] = mine[12 + i : 13 + i]
    rate_to[...] = small[pl.ds(16, 2), :]
    table_to[...] = table[pl.ds(0, table_to.shape[0]), :][:, : table_to.shape[1]]
    part_cols = vocab.shape[2]
    vocab_here = vocab_to.shape[1]
    last = (vocab_here + 255) // 256 * 256 - part_cols
    for k in range(3):
        vocab_to[:, pl.ds(k * part_cols, part_cols)] = vocab[k]
    rest = vocab_here - 3 * part_cols
    skip = 3 * part_cols - last
    vocab_to[:, pl.ds(3 * part_cols, rest)] = vocab[3][:, skip : skip + rest]
    half = key_to.shape[1]
    key_to[...] = kv[:, pl.ds(0, half)]
    value_to[...] = kv[:, pl.ds(half, half)]
    for copy in copies[5:]:
        copy.wait()


def per_device(
    acoustic,
    memory,
    embedding,
    w_query,
    w_key,
    w_value,
    w_out,
    w_in,
    w_back,
    w_vocab,
    gain_one,
    bias_one,
    gain_two,
    bias_two,
    fsmn_kernel,
    rate_table,
    token_lengths,
    memory_lengths,
    rate_groups,
    glance_mask,
    targets,
):
    tok_rows, model_width = acoustic.shape
    half = w_query.shape[1]
    n_dp = lax.axis_size("dp")
    result, low_bits = decoder_call(
        acoustic, memory, embedding, w_query, w_key, w_value, w_out, w_in, w_back, w_vocab,
        (gain_one, bias_one, gain_two, bias_two), fsmn_kernel, rate_table,
        token_lengths, memory_lengths, rate_groups, glance_mask, targets, n_dp,
    )
    vocab = result.vocab_out
    summed = [result.query_out, result.kv_out, result.out_out, result.in_out, result.back_out]
    if low_bits:
        size = 1 << len(low_bits)
        groups = [list(range(g * size, (g + 1) * size)) for g in range(n_dp // size)]
        planes = [list(range(4 * g, 4 * g + 4)) for g in range(n_dp // 4)]
        own_rows = model_width // n_dp
        vocab = lax.all_to_all(
            vocab.reshape(4, own_rows, -1), "dp", 0, 0, axis_index_groups=planes, tiled=True
        )
        summed = [
            lax.psum_scatter(s, "dp", scatter_dimension=0, axis_index_groups=groups, tiled=True)
            for s in summed
        ]
    grad_query, grad_kv, grad_out, grad_in, grad_back = summed
    own = model_width // n_dp
    f32 = lambda *shape: jax.ShapeDtypeStruct(shape, F32)
    like = lambda x: jax.ShapeDtypeStruct(x.shape, F32)
    (
        token_loss, gain_1, bias_1, gain_2, bias_2, grad_taps, grad_rate, grad_table, grad_vocab,
        grad_key, grad_value, grad_query, grad_out, grad_in, grad_back, grad_acoustic, grad_memory,
    ) = pl.pallas_call(
        partial(deliver_kernel, n_dp),
        out_shape=[
            f32(1, tok_rows),
            *[f32(1, own)] * 4,
            f32(fsmn_kernel.shape[0], own),
            f32(2, model_width),
            f32(own, embedding.shape[0]),
            f32(own, w_vocab.shape[1]),
            *[f32(own, half)] * 2,
            *[like(x) for x in (grad_query, grad_out, grad_in, grad_back)],
            like(result.acoustic_out),
            like(result.memory_out),
        ],
        in_specs=[ANY] * 11,
        out_specs=[VMEM] * 11 + [ANY] * 6,
        scratch_shapes=[
            pltpu.VMEM(x.shape, F32)
            for x in (result.loss_out, result.small_out, result.table_out, vocab, grad_kv)
        ]
        + [pltpu.SemaphoreType.DMA((11,))],
        compiler_params=pltpu.CompilerParams(vmem_limit_bytes=60 << 20),
    )(
        result.loss_out, result.small_out, result.table_out, vocab, grad_kv, grad_query, grad_out,
        grad_in, grad_back, result.acoustic_out, result.memory_out,
    )
    return (
        token_loss.reshape(tok_rows),
        grad_acoustic,
        grad_memory,
        grad_table.T,
        grad_query,
        grad_key,
        grad_value,
        grad_out.T,
        grad_in,
        grad_back.T,
        grad_vocab,
        gain_1.reshape(own),
        bias_1.reshape(own),
        gain_2.reshape(own),
        bias_2.reshape(own),
        grad_taps,
        grad_rate,
    )


def solution(mesh):
    return jax.shard_map(
        per_device,
        mesh=mesh,
        in_specs=(
            P("dp", None),
            P("dp", None),
            P(),
            P(None, "mp"),
            P(None, "mp"),
            P(None, "mp"),
            P("mp", None),
            P(None, "mp"),
            P("mp", None),
            P(None, "mp"),
            P(),
            P(),
            P(),
            P(),
            P(),
            P(),
            P("dp"),
            P("dp"),
            P("dp"),
            P("dp"),
            P("dp"),
        ),
        out_specs=(
            P("dp"),
            P("dp", None),
            P("dp", "mp"),
            P(None, "dp"),
            P("dp", "mp"),
            P("dp", "mp"),
            P("dp", "mp"),
            P("mp", "dp"),
            P("dp", "mp"),
            P("mp", "dp"),
            P("dp", "mp"),
            P("dp"),
            P("dp"),
            P("dp"),
            P("dp"),
            P(None, "dp"),
            P(),
        ),
        check_vma=False,
    )
```

```python
from functools import partial
import math
from types import SimpleNamespace

import jax
import jax.numpy as jnp
from jax import lax
from jax.experimental import pallas as pl
from jax.experimental.pallas import tpu as pltpu
from jax.sharding import PartitionSpec as P

HD = 128
V = 8404
EPSILON = 1e-05
MESH = pl.DeviceIdType.MESH
VMEM = pl.BlockSpec(memory_space=pltpu.VMEM)
SMEM = pl.BlockSpec(memory_space=pltpu.SMEM)
ANY = pl.BlockSpec(memory_space=pl.ANY)
F32, BF16 = jnp.float32, jnp.bfloat16
NEG = -1e30


def other_core():
    return {"mp": 1 - lax.axis_index("mp")}


def dot_nn(a, b):
    return lax.dot_general(a, b, (((1,), (0,)), ((), ())), preferred_element_type=F32)


def dot_nt(a, b):
    return lax.dot_general(a, b, (((1,), (1,)), ((), ())), preferred_element_type=F32)


def dot_tn(a, b):
    return lax.dot_general(a, b, (((0,), (0,)), ((), ())), preferred_element_type=F32)


def normalise(rows):
    average = jnp.mean(rows, axis=-1, keepdims=True)
    centred = rows - average
    variance = jnp.mean(centred * centred, axis=-1, keepdims=True)
    scale = lax.rsqrt(variance + EPSILON)
    return centred * scale, scale


def normalise_back(grad_hat, hat, scale):
    first = jnp.mean(grad_hat, axis=-1, keepdims=True)
    second = jnp.mean(grad_hat * hat, axis=-1, keepdims=True)
    return scale * (grad_hat - first - hat * second)


def to_rows(columns):
    lane = lax.broadcasted_iota(jnp.int32, (columns[0].shape[0], 128), 1)
    tile = jnp.zeros(lane.shape, F32)
    for i, column in enumerate(columns):
        tile = jnp.where(lane == i, column, tile)
    return tile.T[:8]


def to_columns(rows):
    return jnp.concatenate([rows] * 16, axis=0).T


class Planner:
    RATE = 0.045e6
    HOP = 1.5
    BACKLOG = 6.0

    def __init__(self):
        self.now = 0.0
        self.free = {}
        self.flying = []
        self.waiting = []
        self.started = []
        self.count = 0

    def launch(self, item, step):
        link, size = item.steps[step]
        begin = max(self.now, self.free.get(link, 0.0))
        self.free[link] = begin + size / self.RATE
        copy = item.send(step)
        self.started.append(copy)
        self.count += 1
        self.flying.append((self.free[link] + self.HOP, self.count, item, step, copy))

    def release(self):
        kept = []
        for item in self.waiting:
            link = item.steps[0][0]
            if self.free.get(link, 0.0) - self.now < self.BACKLOG:
                self.launch(item, 0)
            else:
                kept.append(item)
        self.waiting = kept

    def post(self, *items):
        self.waiting += items
        self.release()

    def run_until(self, time):
        while self.flying or self.waiting:
            if not self.flying:
                self.now = max(self.now, min(self.free[i.steps[0][0]] for i in self.waiting))
                self.release()
                continue
            first = min(self.flying, key=lambda f: f[:2])
            if first[0] > time:
                break
            self.flying.remove(first)
            self.now = max(self.now, first[0])
            _, _, item, step, copy = first
            item.take(step, copy)
            if step + 1 < len(item.steps):
                self.launch(item, step + 1)
            elif item.follow is not None:
                self.launch(item.follow, 0)
            self.release()
        if time != math.inf:
            self.now = max(self.now, time)
        self.release()

    def finish(self):
        self.run_until(math.inf)
        for copy in self.started:
            copy.wait_send()


class Chunk:
    def __init__(self, steps, send, take):
        self.steps, self.send, self.take, self.follow = steps, send, take, None


class Several:
    def __init__(self, copies):
        self.copies = copies

    def wait_recv(self):
        for copy in self.copies:
            copy.wait_recv()

    def wait_send(self):
        for copy in self.copies:
            copy.wait_send()


def decoder_kernel(
    names,
    vocab_here,
    part_cols,
    table_rows,
    n_dp,
    bits,
    low_bits,
    *refs,
):
    r = SimpleNamespace(**dict(zip(names, refs)))
    acoustic, memory, table = r.acoustic, r.memory, r.table
    targets, glance = r.targets, r.glance
    gain_1, bias_1 = r.gain_one[...], r.bias_one[...]
    gain_2, bias_2 = r.gain_two[...], r.bias_two[...]
    kernel_rows, rate_table = r.kernel_rows, r.rate_table
    token_lengths, memory_lengths, rate_groups = r.token_lengths, r.memory_lengths, r.rate_groups
    w_query, w_kv, w_out, w_in, w_back, w_vocab = r.w_query, r.w_kv, r.w_out, r.w_in, r.w_back, r.w_vocab
    mem_low, kv, padded, spare = r.mem_low, r.kv, r.padded, r.spare
    stream_in, stream_one, stream_two, stream_three = r.stream_in, r.stream_one, r.stream_two, r.stream_three
    one_low, queries, probs, mixed = r.one_low, r.queries, r.probs, r.mixed
    norm_low, hidden, gelu_slope, top = r.norm_low, r.hidden, r.gelu_slope, r.top
    logits, grad_logits, grad_others = r.logits, r.grad_logits, r.grad_others
    taken_mine, taken_theirs = r.taken_mine, r.taken_theirs
    grad_three, grad_two, branch_low = r.grad_three, r.grad_two, r.branch_low
    grad_pre, att_low, grad_queries = r.grad_pre, r.att_low, r.grad_queries
    mem_arrived, meta, stats, stats_arrived = r.mem_arrived, r.meta, r.stats, r.stats_arrived
    sent, arrived, gathered = r.sent, r.arrived, r.gathered
    small_sent, small_arrived = r.small_sent, r.small_arrived
    terms, term_blocks, term_arrived = grad_three, r.term_blocks, r.term_arrived
    onehot_lo, table_theirs, table_out = r.onehot_lo, r.table_theirs, r.table_mine
    swap_send, swap_recv, load_sem = r.swap_send, r.swap_recv, r.load_sem

    utterances, slots = targets.shape
    width = acoustic.shape[1]
    frames = memory.shape[0] // utterances
    half = w_query.shape[1]
    heads = half // HD
    tokens = utterances * slots
    me, core = lax.axis_index("dp"), lax.axis_index("mp")
    sibling = {"mp": 1 - core}
    quarter = lax.rem(me, 4)
    flips = [1 - 2 * lax.rem(me, 2), 2 - 4 * lax.rem(me // 2, 2)]
    mate = [me + flips[0] * (j % 2) + flips[1] * (j // 2) for j in range(4)]
    bit_of = {b: lax.rem(me // (1 << b), 2) for b in low_bits + bits}
    peer_of = {b: {"dp": me + (1 - 2 * bit_of[b]) * (1 << b)} for b in low_bits + bits}
    score_scale = 1.0 / math.sqrt(HD)

    loads = []

    def load(source, target):
        copy = pltpu.make_async_copy(source, target, load_sem.at[len(loads)])
        copy.start()
        loads.append(copy)
        return copy

    load_memory = load(memory, mem_low)
    load_kv = [
        load(r.w_key_hbm, w_kv.at[:, pl.ds(0, half)]),
        load(r.w_value_hbm, w_kv.at[:, pl.ds(half, half)]),
    ]
    load_query = load(r.w_query_hbm, w_query)
    load_out = load(r.w_out_hbm, w_out)

    barrier = pltpu.get_barrier_semaphore()

    def greet(k, carry):
        pl.semaphore_signal(
            barrier, inc=1, device_id={"dp": lax.rem(me + k, n_dp)}, device_id_type=MESH
        )
        return carry

    lax.fori_loop(1, n_dp, greet, 0)
    pl.semaphore_signal(barrier, inc=1, device_id=sibling, device_id_type=MESH)

    load_in = load(r.w_in_hbm, w_in)
    load_back = load(r.w_back_hbm, w_back)
    block = 1024
    per_core = table_rows // (2 * block)
    mains = 2 * per_core * block

    def load_table(k):
        at = pl.ds(pl.multiple_of((core * per_core + k) * block, block), block)
        return load(table.at[at, :], spare.at[pl.ds(k % 2 * block, block), :])

    table_loads = [load_table(0), load_table(1)]
    main = vocab_here // 256 * 256
    load_vocab = load(r.w_vocab_hbm.at[pl.ds(0, main), :], w_vocab.at[pl.ds(0, main), :])
    w_vocab[pl.ds(main, w_vocab.shape[0] - main), :] = jnp.zeros((w_vocab.shape[0] - main, width), BF16)
    w_vocab[pl.ds(main, vocab_here - main), :] = r.w_tail[...]
    r.table_rest[...] = jnp.zeros(r.table_rest.shape, BF16)
    r.table_rest[pl.ds(0, table_rows - mains), :] = r.table_tail[...]

    swaps = []

    def swap(source, target, device):
        k = len(swaps)
        copy = pltpu.make_async_remote_copy(
            src_ref=source,
            dst_ref=target,
            send_sem=swap_send.at[k],
            recv_sem=swap_recv.at[k],
            device_id=device,
            device_id_type=MESH,
        )
        copy.start()
        swaps.append(copy)
        return copy

    lane = lax.broadcasted_iota(jnp.int32, (1, slots), 1)
    row_of = lax.broadcasted_iota(jnp.int32, (8, slots), 0)
    for u in range(utterances):
        target_row = targets[pl.ds(u, 1), :].astype(F32)
        glance_row = glance[pl.ds(u, 1), :].astype(F32)
        valid_row = (lane < token_lengths[u]).astype(F32)
        meta[0, :, pl.ds(u * slots, slots)] = jnp.where(
            row_of == 0, target_row, jnp.where(row_of == 1, valid_row, glance_row)
        )
    own_columns = to_columns(meta[0])
    own_target = own_columns[:, 0:1]
    own_valid = own_columns[:, 1:2]

    def rows(u):
        return pl.ds(u * slots, slots)

    load_memory.wait()
    for copy in load_kv:
        copy.wait()
    step_rows = 256
    row_chunks = frames // step_rows

    def kv_step(i, carry):
        at = pl.ds(pl.multiple_of(i * step_rows, step_rows), step_rows)
        group = jnp.zeros((1, width), jnp.int32) + rate_groups[i // row_chunks]
        rate_row = jnp.where(group == 1, rate_table[pl.ds(1, 1), :], rate_table[pl.ds(0, 1), :])
        low = (mem_low[at, :].astype(F32) + rate_row).astype(BF16)
        mem_low[at, :] = low
        kv[at, :] = dot_nn(low, w_kv[...]).astype(BF16)
        return carry

    lax.fori_loop(0, utterances * row_chunks, kv_step, 0)

    edge = jnp.zeros((8, width), F32)
    for u in range(utterances):
        padded[u, pl.ds(0, 8), :] = edge
        padded[u, pl.ds(8 + slots, 8), :] = edge

    pl.semaphore_wait(barrier, n_dp)
    load_query.wait()
    load_out.wait()

    def key_of(u, h):
        return kv[pl.ds(u * frames, frames), pl.ds(h * HD, HD)]

    def value_of(u, h):
        return kv[pl.ds(u * frames, frames), pl.ds(half + h * HD, HD)]

    frame_lane = lax.broadcasted_iota(jnp.int32, (1, frames), 1)

    def look_up(first_row, count, allowed, source):
        ids = first_row + lax.broadcasted_iota(jnp.int32, (1, count), 1)
        local = jnp.where(allowed, own_target.astype(jnp.int32), -1)
        onehot = jnp.where(ids == local, 1.0, 0.0).astype(BF16)
        return dot_nn(onehot, source)

    def look_up_block(k):
        table_loads[k].wait()
        part = look_up(
            (core * per_core + k) * block, block, True, spare[pl.ds(k % 2 * block, block), :]
        )
        for u in range(utterances):
            piece = part[u * slots : (u + 1) * slots]
            taken_mine[u] = piece if k == 0 else taken_mine[u] + piece
        if k + 2 < per_core:
            table_loads.append(load_table(k + 2))

    def look_up_rest():
        part = look_up(mains, r.table_rest.shape[0], core == 0, r.table_rest[...])
        for u in range(utterances):
            taken_mine[u] = taken_mine[u] + part[u * slots : (u + 1) * slots]

    def local_targets(target_column):
        local = target_column.astype(jnp.int32) - core * vocab_here
        return jnp.where((local >= 0) & (local < vocab_here), local, -1)

    def vocab_tile(tile, first, col, target, top_m, picked):
        ids = col + lax.broadcasted_iota(jnp.int32, (1, 128), 1)
        tile = jnp.where(ids < vocab_here, tile, NEG)
        logits[first] = tile
        return jnp.maximum(top_m, tile), picked + jnp.where(ids == target, tile, 0.0)

    def vocab_stats(target):
        start = (jnp.full((tokens, 128), NEG, F32), jnp.zeros((tokens, 128), F32))

        def step(j, carry):
            col = pl.multiple_of(j * 256, 256)
            product = dot_nt(top[0], w_vocab[pl.ds(col, 256), :])
            carry = vocab_tile(product[:, :128], 2 * j, col, target, *carry)
            return vocab_tile(product[:, 128:], 2 * j + 1, col + 128, target, *carry)

        top_m, picked = lax.fori_loop(0, w_vocab.shape[0] // 256, step, start)
        top_row = jnp.max(top_m, axis=1, keepdims=True)

        def add(j, total):
            return total + jnp.exp(logits[j] - top_row)

        total = lax.fori_loop(0, w_vocab.shape[0] // 128, add, jnp.zeros((tokens, 128), F32))
        return (
            top_row,
            jnp.sum(total, axis=1, keepdims=True),
            jnp.sum(picked, axis=1, keepdims=True),
        )

    def join(blocks):
        top_value = blocks[0][0:1]
        for b in blocks[1:]:
            top_value = jnp.maximum(top_value, b[0:1])
        total, picked = 0.0, 0.0
        for b in blocks:
            total = total + b[1:2] * jnp.exp(b[0:1] - top_value)
            picked = picked + b[2:3]
        return top_value + jnp.log(total), picked

    def forward(second, beside_one=None, beside_two=None):
        copies = []
        for u in range(utterances):
            at = rows(u)
            valid = own_valid[u * slots : (u + 1) * slots]
            hat, _ = normalise(stream_in[at, :])
            padded[u, pl.ds(8, slots), :] = (hat * gain_1 + bias_1) * valid
            for j in range(width // 128):
                cols = pl.ds(j * 128, 128)
                total = jnp.zeros((slots, 128), F32)
                for k in range(kernel_rows.shape[0]):
                    shift = 8 + k - kernel_rows.shape[0] // 2
                    total = total + kernel_rows[pl.ds(k, 1), cols] * padded[u, pl.ds(shift, slots), cols]
                stream_one[at, cols] = stream_in[at, cols] + total * valid
            low = stream_one[at, :].astype(BF16)
            one_low[at, :] = low
            queries[at, :] = dot_nn(low, w_query[...]).astype(BF16)
            frame_ok = frame_lane < memory_lengths[u]
            for h in range(heads):
                cols = pl.ds(h * HD, HD)
                scores = dot_nt(queries[at, cols], key_of(u, h)) * score_scale
                scores = jnp.where(frame_ok, scores, NEG)
                raised = jnp.exp(scores - jnp.max(scores, axis=-1, keepdims=True))
                prob = raised * (1.0 / jnp.sum(raised, axis=-1, keepdims=True))
                if second:
                    probs[u, h] = prob
                mixed[at, cols] = dot_nn(prob.astype(BF16), value_of(u, h)).astype(BF16)
            sent[u] = dot_nn(mixed[at, :], w_out[...])
            copies.append(swap(sent.at[u], arrived.at[u], sibling))
        if not second:
            beside_one()
            load_in.wait()
            load_back.wait()
        ff_copies = []
        for u in range(utterances):
            at = rows(u)
            copies[u].wait()
            two = stream_one[at, :] + (sent[u] + arrived[u])
            stream_two[at, :] = two
            hat, _ = normalise(two)
            low = (hat * gain_2 + bias_2).astype(BF16)
            norm_low[at, :] = low
            pre = dot_nn(low, w_in[...])
            phi = 0.5 * (1.0 + lax.erf(pre * math.sqrt(0.5)))
            hidden[at, :] = (pre * phi).astype(BF16)
            if second:
                gelu_slope[at, :] = phi + pre * (
                    jnp.exp(-0.5 * pre * pre) * (1.0 / math.sqrt(2.0 * math.pi))
                )
            sent[utterances + u] = dot_nn(hidden[at, :], w_back[...])
            ff_copies.append(swap(sent.at[utterances + u], arrived.at[utterances + u], sibling))
        if not second:
            beside_two()
        for u in range(utterances):
            at = rows(u)
            ff_copies[u].wait()
            three = stream_two[at, :] + (sent[utterances + u] + arrived[utterances + u])
            stream_three[u] = three
            top[0, at, :] = three.astype(BF16)

    stream_in[...] = acoustic[...].astype(F32)

    def beside_one():
        look_up_block(0)
        look_up_block(1)

    def beside_two():
        for k in range(2, per_core):
            look_up_block(k)
        look_up_rest()

    forward(False, beside_one, beside_two)
    table_swap = swap(taken_mine, taken_theirs, sibling)
    load_vocab.wait()
    own_local = local_targets(own_target)
    stats[0] = to_rows(vocab_stats(own_local))
    first_swap = swap(stats.at[0], stats_arrived.at[0], sibling)
    table_swap.wait()
    first_swap.wait()
    log_total, picked = join([stats[0], stats_arrived[0]])
    first_loss = (log_total - picked) * meta[0, 1:2, :]
    blend_row = meta[0, 2:3, :] * meta[0, 1:2, :] / (1.0 + jnp.exp(math.log(V) - first_loss))
    blend = to_columns(jnp.concatenate([blend_row] * 8, axis=0))[:, 0:1]
    for u in range(utterances):
        at = rows(u)
        wide_acoustic = acoustic[at, :].astype(F32)
        taken = taken_mine[u] + taken_theirs[u]
        stream_in[at, :] = wide_acoustic + blend[u * slots : (u + 1) * slots] * (taken - wide_acoustic)

    forward(True)
    token_swaps = [
        swap(stream_three.at[core], gathered.at[j - 1, 0], {"dp": mate[j]}) for j in range(1, 4)
    ]
    stats[1] = to_rows(vocab_stats(own_local))
    stat_swap = swap(stats.at[1], stats_arrived.at[1], sibling)
    stat_swap.wait()
    log_total, picked = join([stats[1], stats_arrived[1]])
    loss = (log_total - picked) * meta[0, 1:2, :]
    for u in range(utterances):
        r.loss_out[pl.ds(u, 1), :] = loss[:, u * slots : (u + 1) * slots]
    meta[0] = jnp.where(
        lax.broadcasted_iota(jnp.int32, (8, tokens), 0) == 3, log_total, meta[0]
    )
    meta_swaps = [swap(meta.at[0], meta.at[j], {"dp": mate[j]}) for j in range(1, 4)]

    log_column = to_columns(meta[0])[:, 3:4]

    def slope(j, carry):
        col = pl.multiple_of(j * 128, 128)
        ids = col + lax.broadcasted_iota(jnp.int32, (1, 128), 1)
        onehot = jnp.where(ids == own_local, 1.0, 0.0)
        grad = (jnp.exp(logits[j] - log_column) - onehot) * own_valid
        grad_logits[:, pl.ds(col, 128)] = grad.astype(BF16)
        return carry

    lax.fori_loop(0, w_vocab.shape[0] // 128, slope, 0)
    three_copies = []
    for u in range(utterances):
        sent[u] = dot_nn(grad_logits[rows(u), :], w_vocab[...])
        three_copies.append(swap(sent.at[u], arrived.at[u], sibling))

    plan = Planner()
    steps_all = len(bits)
    scatter_send, scatter_recv = r.scatter_send, r.scatter_recv

    def make_chunk(index):
        name, start, cols, order = chunk_list(part_cols, width, bits, low_bits, r)[index]
        source, landing = getattr(r, "src_" + name), r.landing[index]
        out = r.vocab_sum if name == "vocab" and not low_bits else getattr(r, name + "_out")
        rows_here = source.shape[-2]

        def pick(step, which):
            rest = sorted([b for b in bits if b not in order[:step]], reverse=True)
            where = tuple(which if b == order[step] else slice(None) for b in rest)
            if step == 0:
                return source, where + (slice(None), pl.ds(start, cols))
            return landing[step - 1], where + (slice(None), slice(None))

        def send(step):
            b = order[step]
            ref, where = pick(step, 1 - bit_of[b])
            copy = pltpu.make_async_remote_copy(
                src_ref=ref.at[where],
                dst_ref=landing[step],
                send_sem=scatter_send.at[index, step],
                recv_sem=scatter_recv.at[index, step],
                device_id=peer_of[b],
                device_id_type=MESH,
            )
            copy.start()
            return copy

        def take(step, copy):
            copy.wait_recv()
            ref, where = pick(step, bit_of[order[step]])
            got = landing[step]
            at = pl.ds(start, cols)
            if step < len(order) - 1:
                got[...] = got[...] + ref[where]
            elif name == "vocab":
                out[..., at] = got[...] + ref[where]
            else:
                out[:, at] = got[...] + ref[where]

        steps = [
            (link_of(b, bits), rows_here * cols * 4 * 2 ** (steps_all - 1 - s))
            for s, b in enumerate(order)
        ]
        return Chunk(steps, send, take)

    def make_trade(start, cols):
        summed, traded = r.vocab_sum, r.vocab_traded
        at = pl.ds(start, cols)

        def send(step):
            copies = []
            for j in range(1, 4):
                to = lax.rem(mate[j], 4)
                copies.append(
                    pltpu.make_async_remote_copy(
                        src_ref=summed.at[to // 2, lax.rem(to, 2), :, at],
                        dst_ref=traded.at[j - 1, :, at],
                        send_sem=r.trade_send.at[start // 128, j - 1],
                        recv_sem=r.trade_recv.at[start // 128, j - 1],
                        device_id={"dp": mate[j]},
                        device_id_type=MESH,
                    )
                )
                copies[-1].start()
            return Several(copies)

        def take(step, copies):
            copies.wait_recv()
            for j in range(1, 4):
                r.vocab_out[lax.rem(mate[j], 4), :, at] = traded[j - 1, :, at]
            r.vocab_out[quarter, :, at] = summed[quarter // 2, lax.rem(quarter, 2), :, at]

        return Chunk([(0, 2 * r.src_vocab.shape[-2] * cols * 4)], send, take)

    chunks = {}
    for index, (name, start, cols, _) in enumerate(chunk_list(part_cols, width, bits, low_bits, r)):
        chunks[name, start] = make_chunk(index)
        if name == "vocab" and not low_bits:
            chunks[name, start].follow = make_trade(start, cols)

    def put(name, at, product):
        source = getattr(r, "src_" + name)
        source[..., at] = product.reshape(source.shape[:-1] + (product.shape[1],))

    copies = []
    for u in range(utterances):
        at = rows(u)
        three_copies[u].wait()
        three = sent[u] + arrived[u]
        grad_three[u] = three
        low = three.astype(BF16)
        branch_low[at, :] = low
        pre = (dot_nt(low, w_back[...]) * gelu_slope[at, :]).astype(BF16)
        grad_pre[at, :] = pre
        sent[utterances + u] = dot_nt(pre, w_in[...])
        copies.append(swap(sent.at[utterances + u], arrived.at[utterances + u], sibling))
    plan.run_until(4.0)
    for name, left, right in (("back", branch_low, hidden), ("in", norm_low, grad_pre)):
        left_turned = left[...].T
        for start in sorted(s for n, s in chunks if n == name):
            at = pl.ds(start, 512)
            put(name, at, dot_nn(left_turned, right[:, at]))
            plan.run_until(plan.now + 0.5)
            plan.post(chunks[name, start])

    at_core = pl.ds(pl.multiple_of(core * slots, slots), slots)
    at_other = pl.ds(pl.multiple_of((1 - core) * slots, slots), slots)
    share_swaps = []
    for j in range(1, 4):
        token_swaps[j - 1].wait()
        share_swaps.append(swap(gathered.at[j - 1, 0], gathered.at[j - 1, 1], sibling))
        top[j, at_core, :] = gathered[j - 1, 0].astype(BF16)
    base = pl.multiple_of(
        quarter * part_cols - quarter // 3 * (4 * part_cols - w_vocab.shape[0]), 128
    )
    pieces = [(c, 256) for c in range(0, part_cols // 256 * 256, 256)]
    if part_cols % 256:
        pieces.append((part_cols // 256 * 256, part_cols % 256))
    for j in range(1, 4):
        meta_swaps[j - 1].wait()
        columns = to_columns(meta[j])
        target, valid, log_total = local_targets(columns[:, 0:1]), columns[:, 1:2], columns[:, 3:4]
        share_swaps[j - 1].wait()
        top[j, at_other, :] = gathered[j - 1, 1].astype(BF16)
        for col, cols in pieces:
            ids = base + col + lax.broadcasted_iota(jnp.int32, (1, cols), 1)
            tile = dot_nt(top[j], w_vocab[pl.ds(base + col, cols), :])
            tile = jnp.where(ids < vocab_here, tile, NEG)
            grad = (jnp.exp(tile - log_total) - jnp.where(ids == target, 1.0, 0.0)) * valid
            grad_others[pl.ds((j - 1) * tokens, tokens), pl.ds(col, cols)] = grad.astype(BF16)
        plan.run_until(plan.now + 0.8)
    top_turned = r.top_turned
    for j in range(4):
        top_turned[:, pl.ds(j * tokens, tokens)] = top[j].T
    starts = sorted(start for name, start in chunks if name == "vocab")
    for start, stop in zip(starts, starts[1:] + [part_cols]):
        for col in range(start, stop, 256):
            cols = min(256, stop - col)
            product = dot_nn(top_turned[:, pl.ds(0, tokens)], grad_logits[:, pl.ds(base + col, cols)])
            product = product + dot_nn(
                top_turned[:, pl.ds(tokens, 3 * tokens)], grad_others[:, pl.ds(col, cols)]
            )
            put("vocab", pl.ds(col, cols), product)
        plan.run_until(plan.now + 0.7)
        plan.post(chunks["vocab", start])

    one_copies = []
    gain_2_total, bias_2_total = 0.0, 0.0
    for u in range(utterances):
        at = rows(u)
        copies[u].wait()
        grad_norm = sent[utterances + u] + arrived[utterances + u]
        hat, scale = normalise(stream_two[at, :])
        gain_2_total = gain_2_total + jnp.sum(grad_norm * hat, axis=0, keepdims=True)
        bias_2_total = bias_2_total + jnp.sum(grad_norm, axis=0, keepdims=True)
        two = grad_three[u] + normalise_back(grad_norm * gain_2, hat, scale)
        grad_two[at, :] = two
        low = two.astype(BF16)
        att_low[at, :] = low
        grad_mixed = dot_nt(low, w_out[...]).astype(BF16)
        for h in range(heads):
            cols = pl.ds(h * HD, HD)
            grad_head = grad_mixed[:, h * HD : (h + 1) * HD]
            prob = probs[u, h]
            grad_prob = dot_nt(grad_head, value_of(u, h))
            spare[pl.ds(u * frames, frames), pl.ds(half + h * HD, HD)] = dot_tn(
                prob.astype(BF16), grad_head
            ).astype(BF16)
            inner = jnp.sum(prob * grad_prob, axis=-1, keepdims=True)
            grad_score = (prob * (grad_prob - inner)).astype(BF16)
            grad_queries[at, cols] = (dot_nn(grad_score, key_of(u, h)) * score_scale).astype(BF16)
            spare[pl.ds(u * frames, frames), cols] = (
                dot_tn(grad_score, queries[at, cols]) * score_scale
            ).astype(BF16)
            plan.run_until(plan.now + 1.5)
        sent[u] = dot_nt(grad_queries[at, :], w_query[...])
        one_copies.append(swap(sent.at[u], arrived.at[u], sibling))
    every = slice(None)
    put("out", every, dot_tn(att_low[...], mixed[...]))
    plan.post(chunks["out", 0])
    put("query", every, dot_tn(one_low[...], grad_queries[...]))
    plan.post(chunks["query", 0])
    plan.run_until(plan.now + 1.0)

    mem_copies = []
    rate_sums = [0.0, 0.0]
    for u in range(utterances):
        total = jnp.zeros((1, width), F32)
        for i in range(row_chunks):
            at = pl.ds(u * frames + i * step_rows, step_rows)
            part = dot_nt(spare[at, :], w_kv[...])
            for j in range(width // 128):
                side_of, tile = j // (width // 256), j % (width // 256)
                index = ((side_of * utterances + u) * row_chunks + i) * (width // 256) + tile
                logits[index] = part[:, j * 128 : (j + 1) * 128]
            total = total + jnp.sum(part, axis=0, keepdims=True)
        tiles = row_chunks * (width // 256)
        mem_copies.append(
            swap(
                logits.at[pl.ds(((1 - core) * utterances + u) * tiles, tiles)],
                mem_arrived.at[pl.ds(u * tiles, tiles)],
                sibling,
            )
        )
        group = jnp.zeros((1, width), jnp.int32) + rate_groups[u]
        for k in range(2):
            rate_sums[k] = rate_sums[k] + jnp.where((group == 1) == (k == 1), total, 0.0)
        plan.run_until(plan.now + 1.2)
    span = frames // 2
    for k in range(2 * utterances):
        at = pl.ds(k * span, span)
        product = dot_tn(mem_low[at, :], spare[at, :])
        product = product.reshape(r.src_kv.shape)
        r.src_kv[...] = product if k == 0 else r.src_kv[...] + product
    plan.run_until(plan.now + 2.0)
    plan.post(*[chunks["kv", start] for start in sorted(s for n, s in chunks if n == "kv")])

    gain_1_total, bias_1_total = 0.0, 0.0
    for u in range(utterances):
        at = rows(u)
        valid = own_valid[u * slots : (u + 1) * slots]
        one_copies[u].wait()
        one = grad_two[at, :] + (sent[u] + arrived[u])
        grad_two[at, :] = one
        masked = one * valid
        for k in range(kernel_rows.shape[0]):
            shift = 8 + k - kernel_rows.shape[0] // 2
            row = jnp.sum(masked * padded[u, pl.ds(shift, slots), :], axis=0, keepdims=True)
            if u == 0:
                small_sent[0, pl.ds(k, 1), :] = row
            else:
                small_sent[0, pl.ds(k, 1), :] = small_sent[0, pl.ds(k, 1), :] + row
        padded[u, pl.ds(8, slots), :] = masked
        for j in range(width // 128):
            cols = pl.ds(j * 128, 128)
            total = jnp.zeros((slots, 128), F32)
            for k in range(kernel_rows.shape[0]):
                shift = 8 - k + kernel_rows.shape[0] // 2
                total = total + kernel_rows[pl.ds(k, 1), cols] * padded[u, pl.ds(shift, slots), cols]
            stream_one[at, cols] = total * valid
        grad_norm = stream_one[at, :]
        hat, scale = normalise(stream_in[at, :])
        gain_1_total = gain_1_total + jnp.sum(grad_norm * hat, axis=0, keepdims=True)
        bias_1_total = bias_1_total + jnp.sum(grad_norm, axis=0, keepdims=True)
        zero = grad_two[at, :] + normalise_back(grad_norm * gain_1, hat, scale)
        terms[u] = blend[u * slots : (u + 1) * slots] * zero
        stream_one[at, :] = zero - terms[u]
        plan.run_until(plan.now + 1.5)

    last_taps = kernel_rows.shape[0]
    small_sent[0, pl.ds(last_taps, 12 - last_taps), :] = jnp.zeros((12 - last_taps, width), F32)
    for i, row in enumerate((gain_1_total, bias_1_total, gain_2_total, bias_2_total)):
        small_sent[0, pl.ds(12 + i, 1), :] = row
    for k in range(2):
        small_sent[0, pl.ds(16 + k, 1), :] = rate_sums[k]
    small_sent[0, pl.ds(18, 6), :] = jnp.zeros((6, width), F32)
    small_peers = [peer_of[b] for b in low_bits + bits] + [sibling]

    def small_send(step):
        copy = pltpu.make_async_remote_copy(
            src_ref=small_sent.at[step],
            dst_ref=small_arrived.at[step],
            send_sem=r.small_send.at[step],
            recv_sem=r.small_recv.at[step],
            device_id=small_peers[step],
            device_id_type=MESH,
        )
        copy.start()
        return copy

    def small_take(step, copy):
        copy.wait_recv()
        if step + 1 < len(small_peers):
            small_sent[step + 1] = small_sent[step] + small_arrived[step]
        else:
            r.small_out[pl.ds(0, 16), :] = small_sent[step, pl.ds(0, 16), :]
            r.small_out[pl.ds(16, 8), :] = (
                small_sent[step, pl.ds(16, 8), :] + small_arrived[step, pl.ds(16, 8), :]
            )

    small_links = [link_of(b, bits) for b in low_bits + bits] + ["core"]
    plan.post(Chunk([(l, 24 * width * 4) for l in small_links], small_send, small_take))

    features = width // n_dp
    feature_rows = max(features, 8)
    block_rows = term_blocks.shape[1]
    turned = terms[core].T
    id_row = targets[pl.ds(core, 1), :].astype(F32)
    rest = block_rows - features - 1
    for p in range(n_dp):
        term_blocks[p, pl.ds(0, features), :] = turned[p * features : (p + 1) * features]
        term_blocks[p, pl.ds(features, 1), :] = id_row
        term_blocks[p, pl.ds(features + 1, rest), :] = jnp.zeros((rest, slots), F32)

    def term_copy(k):
        there = lax.rem(me + k, n_dp)
        return pltpu.make_async_remote_copy(
            src_ref=term_blocks.at[there],
            dst_ref=term_arrived.at[me],
            send_sem=r.term_send.at[k],
            recv_sem=r.term_recv.at[k],
            device_id={"dp": there},
            device_id_type=MESH,
        )

    def term_start(k, carry):
        term_copy(k).start()
        return carry

    def term_wait(k, carry):
        term_copy(k).wait()
        return carry

    term_arrived[me] = term_blocks[me]
    lax.fori_loop(1, n_dp, term_start, 0)
    stores = []

    def store(source, target):
        copy = pltpu.make_async_copy(source, target, r.store_sem.at[len(stores)])
        copy.start()
        stores.append(copy)

    store(stream_one, r.acoustic_out)
    for u in range(utterances):
        mem_copies[u].wait()
        for i in range(row_chunks):
            for j in range(width // 256):
                index = (u * row_chunks + i) * (width // 256) + j
                first_tile = (core * utterances) * row_chunks * (width // 256)
                mem_arrived[index] = logits[first_tile + index] + mem_arrived[index]
                at = pl.ds(u * frames + i * step_rows, step_rows)
                store(mem_arrived.at[index], r.memory_out.at[at, pl.ds(j * 128, 128)])
    plan.run_until(plan.now + 8.0)
    lax.fori_loop(1, n_dp, term_wait, 0)
    per_piece = 512 // slots
    blocks_hi = table_out.shape[1] // 256
    batch = 4

    def table_piece(p, fresh):
        found = [term_arrived[p * per_piece + i] for i in range(per_piece)]
        values = jnp.concatenate([f[:feature_rows] for f in found], axis=1)
        ids = jnp.concatenate([f[features : features + 1] for f in found], axis=1).astype(jnp.int32)
        low_ids, high_ids = ids & 255, ids >> 8
        onehot_lo[...] = jnp.where(
            lax.broadcasted_iota(jnp.int32, (256, 512), 0) == low_ids, 1.0, 0.0
        ).astype(BF16)
        coarse = values.astype(BF16).astype(F32)
        both = jnp.concatenate([coarse, values - coarse], axis=0)
        for first_hi in range(0, blocks_hi, batch):
            here = range(first_hi, min(first_hi + batch, blocks_hi))
            masked = jnp.concatenate([jnp.where(high_ids == hi, both, 0.0) for hi in here], axis=0)
            product = dot_nt(masked.astype(BF16), onehot_lo[...])
            for i, hi in enumerate(here):
                top_part = product[2 * i * feature_rows : (2 * i + 1) * feature_rows]
                low_part = product[(2 * i + 1) * feature_rows : (2 * i + 2) * feature_rows]
                at = pl.ds(hi * 256, 256)
                if fresh:
                    table_out[:, at] = top_part + low_part
                else:
                    table_out[:, at] = table_out[:, at] + (top_part + low_part)

    pieces = n_dp // per_piece
    table_piece(0, True)
    if pieces <= 4:
        for p in range(1, pieces):
            plan.run_until(plan.now + 1.5)
            table_piece(p, False)
    else:
        lax.fori_loop(1, pieces, lambda p, c: (table_piece(p, False), c)[1], 0)
    table_swap = swap(table_out, table_theirs, sibling)
    plan.run_until(plan.now + 3.0)
    table_swap.wait()
    table_out[...] = table_out[...] + table_theirs[...]
    store(table_out, r.table_out)
    plan.finish()
    for copy in stores:
        copy.wait()


def link_of(bit, bits):
    if bit == bits[-1]:
        return bits[-2]
    return bit


def chunk_list(part_cols, width, bits, low_bits, sizes):
    turned = [bits[1], bits[0]] + bits[2:]
    listing = []
    tiles = part_cols // 128
    edges = [tiles * k // 3 * 128 for k in range(4)]
    for k in range(3):
        order = [b for b in bits if b > 1]
        listing.append(("vocab", edges[k], edges[k + 1] - edges[k], order))
    for name, order in (("back", turned), ("in", bits)):
        for start in range(0, sizes.units, 512):
            listing.append((name, start, 512, order))
    listing.append(("out", 0, sizes.half, turned))
    listing.append(("query", 0, sizes.half, bits))
    for k, start in enumerate(range(0, 2 * sizes.half, 256)):
        listing.append(("kv", start, 256, [bits, turned][k % 2]))
    return listing


def decoder_call(
    acoustic, memory, embedding, w_query, w_key, w_value, w_out, w_in, w_back, w_vocab, norms,
    fsmn_kernel, rate_table, token_lengths, memory_lengths, rate_groups, glance, targets, n_dp,
):
    utterances = token_lengths.shape[0]
    tokens, width = acoustic.shape
    slots = tokens // utterances
    mem_rows = memory.shape[0]
    half = w_query.shape[1]
    heads = half // HD
    frames = mem_rows // utterances
    units = w_in.shape[1]
    vocab_here = w_vocab.shape[1]
    table_rows = embedding.shape[0]
    part_cols = ((vocab_here + 127) // 128 + 3) // 4 * 128
    all_cols = (vocab_here + 255) // 256 * 256
    w_turned = w_vocab.T
    main = vocab_here // 256 * 256
    mains = table_rows // 2048 * 2048
    nbits = n_dp.bit_length() - 1
    steps = nbits
    while width >> steps < 8:
        steps -= 1
    low_bits, bits = list(range(nbits - steps)), list(range(nbits - steps, nbits))
    rows = width >> steps
    features = width // n_dp
    feature_rows = max(features, 8)
    block_rows = feature_rows + 8 if features >= 8 else 8
    blocks_hi = (table_rows + 255) // 256
    sizes = SimpleNamespace(units=units, half=half)
    plane = [b for b in bits if b < 2]
    listing = chunk_list(part_cols, width, bits, low_bits, sizes)
    most = max(len(c[3]) for c in listing)

    f32 = lambda *shape: jax.ShapeDtypeStruct(shape, F32)
    v32 = lambda *shape: pltpu.VMEM(shape, F32)
    v16 = lambda *shape: pltpu.VMEM(shape, BF16)
    dma = lambda *shape: pltpu.SemaphoreType.DMA(shape)
    inputs = dict(
        acoustic=(VMEM, acoustic),
        w_tail=(VMEM, w_turned[main:]),
        table_tail=(VMEM, embedding[mains:]),
        memory=(ANY, memory),
        table=(ANY, embedding),
        w_query_hbm=(ANY, w_query),
        w_key_hbm=(ANY, w_key),
        w_value_hbm=(ANY, w_value),
        w_out_hbm=(ANY, w_out),
        w_in_hbm=(ANY, w_in),
        w_back_hbm=(ANY, w_back),
        w_vocab_hbm=(ANY, w_turned),
        gain_one=(VMEM, norms[0][None]),
        bias_one=(VMEM, norms[1][None]),
        gain_two=(VMEM, norms[2][None]),
        bias_two=(VMEM, norms[3][None]),
        kernel_rows=(VMEM, fsmn_kernel),
        rate_table=(VMEM, rate_table),
        token_lengths=(SMEM, token_lengths),
        memory_lengths=(SMEM, memory_lengths),
        rate_groups=(SMEM, rate_groups),
        glance=(VMEM, glance.reshape(utterances, slots)),
        targets=(VMEM, targets.reshape(utterances, slots)),
    )
    outputs = dict(
        loss_out=f32(utterances, slots),
        small_out=f32(24, width),
        vocab_out=f32(*((2,) * len(plane) if low_bits else (4,)), rows, part_cols),
        in_out=f32(rows, units),
        back_out=f32(rows, units),
        query_out=f32(rows, half),
        out_out=f32(rows, half),
        kv_out=f32(rows, 2 * half),
        acoustic_out=f32(tokens, width),
        memory_out=f32(mem_rows, width // 2),
        table_out=f32(feature_rows, blocks_hi * 256),
    )
    shape = (2,) * steps + (rows,)
    scratch = dict(
        w_query=v16(width, half),
        w_kv=v16(width, 2 * half),
        w_out=v16(half, width),
        w_in=v16(width, units),
        w_back=v16(units, width),
        w_vocab=v16(all_cols, width),
        mem_low=v16(mem_rows, width),
        kv=v16(mem_rows, 2 * half),
        spare=v16(mem_rows, 2 * half),
        padded=v32(utterances, slots + 16, width),
        stream_in=v32(tokens, width),
        stream_one=v32(tokens, width),
        stream_two=v32(tokens, width),
        stream_three=v32(utterances, slots, width),
        one_low=v16(tokens, width),
        queries=v16(tokens, half),
        probs=v32(utterances, heads, slots, frames),
        mixed=v16(tokens, half),
        norm_low=v16(tokens, width),
        hidden=v16(tokens, units),
        gelu_slope=v32(tokens, units),
        top=v16(4, tokens, width),
        logits=v32(all_cols // 128, tokens, 128),
        grad_logits=v16(tokens, all_cols),
        grad_others=v16(3 * tokens, part_cols),
        top_turned=v16(width, 4 * tokens),
        taken_mine=v32(utterances, slots, width),
        taken_theirs=v32(utterances, slots, width),
        grad_three=v32(utterances, slots, width),
        grad_two=v32(tokens, width),
        branch_low=v16(tokens, width),
        grad_pre=v16(tokens, units),
        att_low=v16(tokens, width),
        grad_queries=v16(tokens, half),
        mem_arrived=v32(mem_rows // 256 * (width // 256), 256, 128),
        meta=v32(4, 8, tokens),
        stats=v32(2, 8, tokens),
        stats_arrived=v32(2, 8, tokens),
        sent=v32(2 * utterances, slots, width),
        arrived=v32(2 * utterances, slots, width),
        gathered=v32(3, 2, slots, width),
        small_sent=v32(nbits + 1, 24, width),
        small_arrived=v32(nbits + 1, 24, width),
        term_blocks=v32(n_dp, block_rows, slots),
        term_arrived=v32(n_dp, block_rows, slots),
        onehot_lo=v16(256, 512),
        table_rest=v16((table_rows - mains + 127) // 128 * 128, width),
        table_theirs=v32(feature_rows, blocks_hi * 256),
        table_mine=v32(feature_rows, blocks_hi * 256),
        src_vocab=v32(*shape, part_cols),
        src_back=v32(*shape, units),
        vocab_sum=v32(*(2,) * len(plane), rows, part_cols),
        vocab_traded=v32(3, rows, part_cols),
        src_in=v32(*shape, units),
        src_out=v32(*shape, half),
        src_query=v32(*shape, half),
        src_kv=v32(*shape, 2 * half),
        load_sem=dma(24),
        store_sem=dma(24),
        trade_send=dma(part_cols // 128, 3),
        trade_recv=dma(part_cols // 128, 3),
        swap_send=dma(40),
        swap_recv=dma(40),
        scatter_send=dma(len(listing), most),
        scatter_recv=dma(len(listing), most),
        small_send=dma(nbits + 1),
        small_recv=dma(nbits + 1),
        term_send=dma(n_dp),
        term_recv=dma(n_dp),
    )
    landing = [
        [v32(*(2,) * (steps - 1 - s), rows, cols) for s in range(len(order))]
        for _, _, cols, order in listing
    ]
    names = list(inputs) + list(outputs) + list(scratch)
    flat = [ref for chunk in landing for ref in chunk]

    def kernel(*refs):
        named, rest = refs[: len(names)], list(refs[len(names) :])
        lands = [[rest.pop(0) for _ in chunk] for chunk in landing]
        decoder_kernel(
            names + ["landing", "units", "half"], vocab_here, part_cols, table_rows, n_dp, bits,
            low_bits, *named, lands, units, half,
        )

    out = pl.pallas_call(
        kernel,
        out_shape=list(outputs.values()),
        in_specs=[spec for spec, _ in inputs.values()],
        out_specs=[VMEM] * (len(outputs) - 3) + [ANY] * 3,
        scratch_shapes=list(scratch.values()) + flat,
        compiler_params=pltpu.CompilerParams(
            collective_id=1, has_side_effects=True, vmem_limit_bytes=64 << 20
        ),
    )(*[value for _, value in inputs.values()])
    return SimpleNamespace(**dict(zip(outputs, out))), low_bits


def deliver_kernel(n_dp, *refs):
    sources, targets, held, sem_in, sem_out = refs[:11], refs[11:28], refs[28:39], refs[39], refs[40]
    loss, small, table, vocab, kv = held[:5]
    (
        loss_to, gain_one_to, bias_one_to, gain_two_to, bias_two_to, taps_to, rate_to,
        table_to, vocab_to, key_to, value_to,
    ) = targets[:11]
    reads, writes = [], []
    for i, (source, buffer) in enumerate(zip(sources, held)):
        reads.append(pltpu.make_async_copy(source, buffer, sem_in.at[i]))
        reads[-1].start()
    for i in range(5, 11):
        reads[i].wait()
        writes.append(pltpu.make_async_copy(held[i], targets[6 + i], sem_out.at[i]))
        writes[-1].start()
    for i in range(5):
        reads[i].wait()
    slots = loss.shape[1]
    for u in range(loss.shape[0]):
        loss_to[:, pl.ds(u * slots, slots)] = loss[pl.ds(u, 1), :]
    me = lax.axis_index("dp")
    own = small.shape[1] // n_dp
    mine = jnp.zeros((16, own), F32)
    for p in range(n_dp):
        mine = jnp.where(me == p, small[pl.ds(0, 16), p * own : (p + 1) * own], mine)
    taps_to[...] = mine[: taps_to.shape[0]]
    for i, target in enumerate((gain_one_to, bias_one_to, gain_two_to, bias_two_to)):
        target[...] = mine[12 + i : 13 + i]
    rate_to[...] = small[pl.ds(16, 2), :]
    table_to[...] = table[pl.ds(0, table_to.shape[0]), :][:, : table_to.shape[1]]
    part_cols = vocab.shape[2]
    vocab_here = vocab_to.shape[1]
    last = (vocab_here + 255) // 256 * 256 - part_cols
    for k in range(3):
        vocab_to[:, pl.ds(k * part_cols, part_cols)] = vocab[k]
    rest = vocab_here - 3 * part_cols
    skip = 3 * part_cols - last
    vocab_to[:, pl.ds(3 * part_cols, rest)] = vocab[3][:, skip : skip + rest]
    half = key_to.shape[1]
    key_to[...] = kv[:, pl.ds(0, half)]
    value_to[...] = kv[:, pl.ds(half, half)]
    for copy in writes:
        copy.wait()


def per_device(
    acoustic,
    memory,
    embedding,
    w_query,
    w_key,
    w_value,
    w_out,
    w_in,
    w_back,
    w_vocab,
    gain_one,
    bias_one,
    gain_two,
    bias_two,
    fsmn_kernel,
    rate_table,
    token_lengths,
    memory_lengths,
    rate_groups,
    glance_mask,
    targets,
):
    tok_rows, model_width = acoustic.shape
    half = w_query.shape[1]
    n_dp = lax.axis_size("dp")
    result, low_bits = decoder_call(
        acoustic, memory, embedding, w_query, w_key, w_value, w_out, w_in, w_back, w_vocab,
        (gain_one, bias_one, gain_two, bias_two), fsmn_kernel, rate_table,
        token_lengths, memory_lengths, rate_groups, glance_mask, targets, n_dp,
    )
    vocab = result.vocab_out
    summed = [result.query_out, result.kv_out, result.out_out, result.in_out, result.back_out]
    if low_bits:
        size = 1 << len(low_bits)
        groups = [list(range(g * size, (g + 1) * size)) for g in range(n_dp // size)]
        planes = [list(range(4 * g, 4 * g + 4)) for g in range(n_dp // 4)]
        own_rows = model_width // n_dp
        vocab = lax.all_to_all(
            vocab.reshape(4, own_rows, -1), "dp", 0, 0, axis_index_groups=planes, tiled=True
        )
        summed = [
            lax.psum_scatter(s, "dp", scatter_dimension=0, axis_index_groups=groups, tiled=True)
            for s in summed
        ]
    grad_query, grad_kv, grad_out, grad_in, grad_back = summed
    own = model_width // n_dp
    f32 = lambda *shape: jax.ShapeDtypeStruct(shape, F32)
    like = lambda x: jax.ShapeDtypeStruct(x.shape, F32)
    handed = (
        result.loss_out, result.small_out, result.table_out, vocab, grad_kv, grad_query, grad_out,
        grad_in, grad_back, result.acoustic_out, result.memory_out,
    )
    (
        token_loss, gain_1, bias_1, gain_2, bias_2, grad_taps, grad_rate, grad_table, grad_vocab,
        grad_key, grad_value, grad_query, grad_out, grad_in, grad_back, grad_acoustic, grad_memory,
    ) = pl.pallas_call(
        partial(deliver_kernel, n_dp),
        out_shape=[
            f32(1, tok_rows),
            *[f32(1, own)] * 4,
            f32(fsmn_kernel.shape[0], own),
            f32(2, model_width),
            f32(own, embedding.shape[0]),
            f32(own, w_vocab.shape[1]),
            *[f32(own, half)] * 2,
            *[like(x) for x in (grad_query, grad_out, grad_in, grad_back)],
            like(result.acoustic_out),
            like(result.memory_out),
        ],
        in_specs=[ANY] * 11,
        out_specs=[VMEM] * 11 + [ANY] * 6,
        scratch_shapes=[pltpu.VMEM(x.shape, F32) for x in handed]
        + [pltpu.SemaphoreType.DMA((11,)), pltpu.SemaphoreType.DMA((11,))],
        compiler_params=pltpu.CompilerParams(vmem_limit_bytes=60 << 20),
    )(*handed)
    return (
        token_loss.reshape(tok_rows),
        grad_acoustic,
        grad_memory,
        grad_table.T,
        grad_query,
        grad_key,
        grad_value,
        grad_out.T,
        grad_in,
        grad_back.T,
        grad_vocab,
        gain_1.reshape(own),
        bias_1.reshape(own),
        gain_2.reshape(own),
        bias_2.reshape(own),
        grad_taps,
        grad_rate,
    )


def solution(mesh):
    return jax.shard_map(
        per_device,
        mesh=mesh,
        in_specs=(
            P("dp", None),
            P("dp", None),
            P(),
            P(None, "mp"),
            P(None, "mp"),
            P(None, "mp"),
            P("mp", None),
            P(None, "mp"),
            P("mp", None),
            P(None, "mp"),
            P(),
            P(),
            P(),
            P(),
            P(),
            P(),
            P("dp"),
            P("dp"),
            P("dp"),
            P("dp"),
            P("dp"),
        ),
        out_specs=(
            P("dp"),
            P("dp", None),
            P("dp", "mp"),
            P(None, "dp"),
            P("dp", "mp"),
            P("dp", "mp"),
            P("dp", "mp"),
            P("mp", "dp"),
            P("dp", "mp"),
            P("mp", "dp"),
            P("dp", "mp"),
            P("dp"),
            P("dp"),
            P("dp"),
            P("dp"),
            P(None, "dp"),
            P(),
        ),
        check_vma=False,
    )
```

```python
from functools import partial
import math
from types import SimpleNamespace

import jax
import jax.numpy as jnp
from jax import lax
from jax.experimental import pallas as pl
from jax.experimental.pallas import tpu as pltpu
from jax.sharding import PartitionSpec as P

HD = 128
V = 8404
EPSILON = 1e-05
MESH = pl.DeviceIdType.MESH
VMEM = pl.BlockSpec(memory_space=pltpu.VMEM)
SMEM = pl.BlockSpec(memory_space=pltpu.SMEM)
ANY = pl.BlockSpec(memory_space=pl.ANY)
F32, BF16 = jnp.float32, jnp.bfloat16
NEG = -1e30


def other_core():
    return {"mp": 1 - lax.axis_index("mp")}


def dot_nn(a, b):
    return lax.dot_general(a, b, (((1,), (0,)), ((), ())), preferred_element_type=F32)


def dot_nt(a, b):
    return lax.dot_general(a, b, (((1,), (1,)), ((), ())), preferred_element_type=F32)


def dot_tn(a, b):
    return lax.dot_general(a, b, (((0,), (0,)), ((), ())), preferred_element_type=F32)


def normalise(rows):
    average = jnp.mean(rows, axis=-1, keepdims=True)
    centred = rows - average
    variance = jnp.mean(centred * centred, axis=-1, keepdims=True)
    scale = lax.rsqrt(variance + EPSILON)
    return centred * scale, scale


def normalise_back(grad_hat, hat, scale):
    first = jnp.mean(grad_hat, axis=-1, keepdims=True)
    second = jnp.mean(grad_hat * hat, axis=-1, keepdims=True)
    return scale * (grad_hat - first - hat * second)


def to_rows(columns):
    lane = lax.broadcasted_iota(jnp.int32, (columns[0].shape[0], 128), 1)
    tile = jnp.zeros(lane.shape, F32)
    for i, column in enumerate(columns):
        tile = jnp.where(lane == i, column, tile)
    return tile.T[:8]


def to_columns(rows):
    return jnp.concatenate([rows] * 16, axis=0).T


class Planner:
    RATE = 0.045e6
    HOP = 1.5
    BACKLOG = 3.0

    def __init__(self):
        self.now = 0.0
        self.free = {}
        self.flying = []
        self.waiting = []
        self.started = []
        self.count = 0

    def launch(self, item, step):
        link, size = item.steps[step]
        begin = max(self.now, self.free.get(link, 0.0))
        self.free[link] = begin + size / self.RATE
        copy = item.send(step)
        self.started.append(copy)
        self.count += 1
        self.flying.append((self.free[link] + self.HOP, self.count, item, step, copy))

    def release(self):
        kept = []
        for item in self.waiting:
            link = item.steps[0][0]
            if self.free.get(link, 0.0) - self.now < self.BACKLOG:
                self.launch(item, 0)
            else:
                kept.append(item)
        self.waiting = kept

    def post(self, *items):
        self.waiting += items
        self.release()

    def run_until(self, time):
        while self.flying or self.waiting:
            if not self.flying:
                self.now = max(self.now, min(self.free[i.steps[0][0]] for i in self.waiting))
                self.release()
                continue
            first = min(self.flying, key=lambda f: f[:2])
            if first[0] > time:
                break
            self.flying.remove(first)
            self.now = max(self.now, first[0])
            _, _, item, step, copy = first
            item.take(step, copy)
            if step + 1 < len(item.steps):
                self.launch(item, step + 1)
            elif item.follow is not None:
                self.launch(item.follow, 0)
            self.release()
        if time != math.inf:
            self.now = max(self.now, time)
        self.release()

    def finish(self):
        self.run_until(math.inf)
        for copy in self.started:
            copy.wait_send()


class Chunk:
    def __init__(self, steps, send, take):
        self.steps, self.send, self.take, self.follow = steps, send, take, None


class Several:
    def __init__(self, copies):
        self.copies = copies

    def wait_recv(self):
        for copy in self.copies:
            copy.wait_recv()

    def wait_send(self):
        for copy in self.copies:
            copy.wait_send()


def decoder_kernel(
    names,
    vocab_here,
    part_cols,
    table_rows,
    n_dp,
    bits,
    low_bits,
    *refs,
):
    r = SimpleNamespace(**dict(zip(names, refs)))
    acoustic, memory, table = r.acoustic, r.memory, r.table
    targets, glance = r.targets, r.glance
    gain_1, bias_1 = r.gain_one[...], r.bias_one[...]
    gain_2, bias_2 = r.gain_two[...], r.bias_two[...]
    kernel_rows, rate_table = r.kernel_rows, r.rate_table
    token_lengths, memory_lengths, rate_groups = r.token_lengths, r.memory_lengths, r.rate_groups
    w_query, w_kv, w_out, w_in, w_back, w_vocab = r.w_query, r.w_kv, r.w_out, r.w_in, r.w_back, r.w_vocab
    mem_low, kv, padded, spare = r.mem_low, r.kv, r.padded, r.spare
    stream_in, stream_one, stream_two, stream_three = r.stream_in, r.stream_one, r.stream_two, r.stream_three
    one_low, queries, probs, mixed = r.one_low, r.queries, r.probs, r.mixed
    norm_low, hidden, gelu_slope, top = r.norm_low, r.hidden, r.gelu_slope, r.top
    logits, grad_logits, grad_others = r.logits, r.grad_logits, r.grad_others
    taken_mine, taken_theirs = r.taken_mine, r.taken_theirs
    grad_three, grad_two, branch_low = r.grad_three, r.grad_two, r.branch_low
    grad_pre, att_low, grad_queries = r.grad_pre, r.att_low, r.grad_queries
    mem_arrived, meta, stats, stats_arrived = r.mem_arrived, r.meta, r.stats, r.stats_arrived
    sent, arrived, gathered = r.sent, r.arrived, r.gathered
    small_sent, small_arrived = r.small_sent, r.small_arrived
    terms, term_blocks, term_arrived = grad_three, r.term_blocks, r.term_arrived
    onehot_lo, table_theirs, table_out = r.onehot_lo, r.table_theirs, r.table_mine
    swap_send, swap_recv, load_sem = r.swap_send, r.swap_recv, r.load_sem

    utterances, slots = targets.shape
    width = acoustic.shape[1]
    frames = memory.shape[0] // utterances
    half = w_query.shape[1]
    heads = half // HD
    tokens = utterances * slots
    me, core = lax.axis_index("dp"), lax.axis_index("mp")
    sibling = {"mp": 1 - core}
    quarter = lax.rem(me, 4)
    flips = [1 - 2 * lax.rem(me, 2), 2 - 4 * lax.rem(me // 2, 2)]
    mate = [me + flips[0] * (j % 2) + flips[1] * (j // 2) for j in range(4)]
    bit_of = {b: lax.rem(me // (1 << b), 2) for b in low_bits + bits}
    peer_of = {b: {"dp": me + (1 - 2 * bit_of[b]) * (1 << b)} for b in low_bits + bits}
    score_scale = 1.0 / math.sqrt(HD)

    loads = []

    def load(source, target):
        copy = pltpu.make_async_copy(source, target, load_sem.at[len(loads)])
        copy.start()
        loads.append(copy)
        return copy

    load_memory = load(memory, mem_low)
    load_kv = [
        load(r.w_key_hbm, w_kv.at[:, pl.ds(0, half)]),
        load(r.w_value_hbm, w_kv.at[:, pl.ds(half, half)]),
    ]
    load_query = load(r.w_query_hbm, w_query)
    load_out = load(r.w_out_hbm, w_out)

    barrier = pltpu.get_barrier_semaphore()

    def greet(k, carry):
        pl.semaphore_signal(
            barrier, inc=1, device_id={"dp": lax.rem(me + k, n_dp)}, device_id_type=MESH
        )
        return carry

    lax.fori_loop(1, n_dp, greet, 0)
    pl.semaphore_signal(barrier, inc=1, device_id=sibling, device_id_type=MESH)

    load_in = load(r.w_in_hbm, w_in)
    load_back = load(r.w_back_hbm, w_back)
    block = 1024
    per_core = table_rows // (2 * block)
    mains = 2 * per_core * block

    def load_table(k):
        at = pl.ds(pl.multiple_of((core * per_core + k) * block, block), block)
        return load(table.at[at, :], spare.at[pl.ds(k % 2 * block, block), :])

    table_loads = [load_table(0), load_table(1)]
    main = 4 * part_cols
    load_vocab = load(r.w_vocab_hbm, w_vocab)
    w_rest = r.w_rest
    w_rest[...] = jnp.zeros(w_rest.shape, BF16)
    r.table_rest[...] = jnp.zeros(r.table_rest.shape, BF16)
    r.table_rest[pl.ds(0, table_rows - mains), :] = r.table_tail[...]

    swaps = []

    def swap(source, target, device):
        k = len(swaps)
        copy = pltpu.make_async_remote_copy(
            src_ref=source,
            dst_ref=target,
            send_sem=swap_send.at[k],
            recv_sem=swap_recv.at[k],
            device_id=device,
            device_id_type=MESH,
        )
        copy.start()
        swaps.append(copy)
        return copy

    lane = lax.broadcasted_iota(jnp.int32, (1, slots), 1)
    row_of = lax.broadcasted_iota(jnp.int32, (8, slots), 0)
    for u in range(utterances):
        target_row = targets[pl.ds(u, 1), :].astype(F32)
        glance_row = glance[pl.ds(u, 1), :].astype(F32)
        valid_row = (lane < token_lengths[u]).astype(F32)
        meta[0, :, pl.ds(u * slots, slots)] = jnp.where(
            row_of == 0, target_row, jnp.where(row_of == 1, valid_row, glance_row)
        )
    own_columns = to_columns(meta[0])
    own_target = own_columns[:, 0:1]
    own_valid = own_columns[:, 1:2]

    def rows(u):
        return pl.ds(u * slots, slots)

    edge = jnp.zeros((8, width), F32)
    for u in range(utterances):
        padded[u, pl.ds(0, 8), :] = edge
        padded[u, pl.ds(8 + slots, 8), :] = edge

    step_rows = 256
    row_chunks = frames // step_rows

    def key_of(u, h):
        return kv[pl.ds(u * frames, frames), pl.ds(h * HD, HD)]

    def value_of(u, h):
        return kv[pl.ds(u * frames, frames), pl.ds(half + h * HD, HD)]

    frame_lane = lax.broadcasted_iota(jnp.int32, (1, frames), 1)

    def look_up(first_row, count, allowed, source):
        ids = first_row + lax.broadcasted_iota(jnp.int32, (1, count), 1)
        local = jnp.where(allowed, own_target.astype(jnp.int32), -1)
        onehot = jnp.where(ids == local, 1.0, 0.0).astype(BF16)
        return dot_nn(onehot, source)

    def look_up_block(k):
        table_loads[k].wait()
        part = look_up(
            (core * per_core + k) * block, block, True, spare[pl.ds(k % 2 * block, block), :]
        )
        for u in range(utterances):
            piece = part[u * slots : (u + 1) * slots]
            taken_mine[u] = piece if k == 0 else taken_mine[u] + piece
        if k + 2 < per_core:
            table_loads.append(load_table(k + 2))

    def look_up_rest():
        part = look_up(mains, r.table_rest.shape[0], core == 0, r.table_rest[...])
        for u in range(utterances):
            taken_mine[u] = taken_mine[u] + part[u * slots : (u + 1) * slots]

    def local_targets(target_column):
        local = target_column.astype(jnp.int32) - core * vocab_here
        return jnp.where((local >= 0) & (local < vocab_here), local, -1)

    def vocab_stats(target):
        tiles = main // 128
        step_tiles = 4

        def step(j, carry):
            top_m, picked = carry
            col = pl.multiple_of(j * (step_tiles * 128), step_tiles * 128)
            product = dot_nt(top[0], w_vocab[pl.ds(col, step_tiles * 128), :])
            for i in range(step_tiles):
                tile = product[:, i * 128 : (i + 1) * 128]
                ids = col + i * 128 + lax.broadcasted_iota(jnp.int32, (1, 128), 1)
                logits[j * step_tiles + i] = tile
                top_m = jnp.maximum(top_m, tile)
                picked = picked + jnp.where(ids == target, tile, 0.0)
            return top_m, picked

        ids = main + lax.broadcasted_iota(jnp.int32, (1, 128), 1)
        last = jnp.where(ids < vocab_here, dot_nt(top[0], w_rest[...]), NEG)
        logits[tiles] = last
        picked = jnp.where(ids == target, last, 0.0)
        top_m, picked = lax.fori_loop(0, tiles // step_tiles, step, (last, picked))
        top_row = jnp.max(top_m, axis=1, keepdims=True)

        def add(j, total):
            for i in range(3):
                total = total + jnp.exp(logits[3 * j + i] - top_row)
            return total

        total = lax.fori_loop(0, (tiles + 1) // 3, add, jnp.zeros((tokens, 128), F32))
        return (
            top_row,
            jnp.sum(total, axis=1, keepdims=True),
            jnp.sum(picked, axis=1, keepdims=True),
        )

    def join(blocks):
        top_value = blocks[0][0:1]
        for b in blocks[1:]:
            top_value = jnp.maximum(top_value, b[0:1])
        total, picked = 0.0, 0.0
        for b in blocks:
            total = total + b[1:2] * jnp.exp(b[0:1] - top_value)
            picked = picked + b[2:3]
        return top_value + jnp.log(total), picked

    def memory_block(u):
        at = rows(u)
        valid = own_valid[u * slots : (u + 1) * slots]
        hat, _ = normalise(stream_in[at, :])
        padded[u, pl.ds(8, slots), :] = (hat * gain_1 + bias_1) * valid
        for j in range(width // 128):
            cols = pl.ds(j * 128, 128)
            total = jnp.zeros((slots, 128), F32)
            for k in range(kernel_rows.shape[0]):
                shift = 8 + k - kernel_rows.shape[0] // 2
                total = total + kernel_rows[pl.ds(k, 1), cols] * padded[u, pl.ds(shift, slots), cols]
            stream_one[at, cols] = stream_in[at, cols] + total * valid
        low = stream_one[at, :].astype(BF16)
        one_low[at, :] = low
        queries[at, :] = dot_nn(low, w_query[...]).astype(BF16)

    def forward(second, beside_one=None, beside_two=None):
        copies = []
        for u in range(utterances):
            at = rows(u)
            if second:
                memory_block(u)
            frame_ok = frame_lane < memory_lengths[u]
            for h in range(heads):
                cols = pl.ds(h * HD, HD)
                scores = dot_nt(queries[at, cols], key_of(u, h)) * score_scale
                scores = jnp.where(frame_ok, scores, NEG)
                raised = jnp.exp(scores - jnp.max(scores, axis=-1, keepdims=True))
                prob = raised * (1.0 / jnp.sum(raised, axis=-1, keepdims=True))
                if second:
                    probs[u, h] = prob
                mixed[at, cols] = dot_nn(prob.astype(BF16), value_of(u, h)).astype(BF16)
            sent[u] = dot_nn(mixed[at, :], w_out[...])
            copies.append(swap(sent.at[u], arrived.at[u], sibling))
        if not second:
            beside_one()
            load_in.wait()
            load_back.wait()
        ff_copies = []
        for u in range(utterances):
            at = rows(u)
            copies[u].wait()
            two = stream_one[at, :] + (sent[u] + arrived[u])
            stream_two[at, :] = two
            hat, _ = normalise(two)
            low = (hat * gain_2 + bias_2).astype(BF16)
            norm_low[at, :] = low
            pre = dot_nn(low, w_in[...])
            phi = 0.5 * (1.0 + lax.erf(pre * math.sqrt(0.5)))
            hidden[at, :] = (pre * phi).astype(BF16)
            if second:
                gelu_slope[at, :] = phi + pre * (
                    jnp.exp(-0.5 * pre * pre) * (1.0 / math.sqrt(2.0 * math.pi))
                )
            sent[utterances + u] = dot_nn(hidden[at, :], w_back[...])
            ff_copies.append(swap(sent.at[utterances + u], arrived.at[utterances + u], sibling))
        if not second:
            beside_two()
        for u in range(utterances):
            at = rows(u)
            ff_copies[u].wait()
            three = stream_two[at, :] + (sent[utterances + u] + arrived[utterances + u])
            stream_three[u] = three
            top[0, at, :] = three.astype(BF16)

    stream_in[...] = acoustic[...].astype(F32)

    def beside_one():
        look_up_block(0)
        look_up_block(1)

    def beside_two():
        for k in range(2, per_core):
            look_up_block(k)
        look_up_rest()

    load_query.wait()
    for u in range(utterances):
        memory_block(u)
    load_memory.wait()
    for copy in load_kv:
        copy.wait()
    kv_rows = 512
    kv_chunks = frames // kv_rows

    def kv_step(i, carry):
        at = pl.ds(pl.multiple_of(i * kv_rows, kv_rows), kv_rows)
        group = jnp.zeros((1, width), jnp.int32) + rate_groups[i // kv_chunks]
        rate_row = jnp.where(group == 1, rate_table[pl.ds(1, 1), :], rate_table[pl.ds(0, 1), :])
        low = (mem_low[at, :].astype(F32) + rate_row).astype(BF16)
        mem_low[at, :] = low
        kv[at, :] = dot_nn(low, w_kv[...]).astype(BF16)
        return carry

    lax.fori_loop(0, utterances * kv_chunks, kv_step, 0)

    pl.semaphore_wait(barrier, n_dp)
    load_out.wait()
    forward(False, beside_one, beside_two)
    table_swap = swap(taken_mine, taken_theirs, sibling)
    load_vocab.wait()
    w_rest[pl.ds(0, vocab_here - main), :] = w_vocab[pl.ds(main, vocab_here - main), :]
    own_local = local_targets(own_target)
    stats[0] = to_rows(vocab_stats(own_local))
    first_swap = swap(stats.at[0], stats_arrived.at[0], sibling)
    table_swap.wait()
    first_swap.wait()
    log_total, picked = join([stats[0], stats_arrived[0]])
    first_loss = (log_total - picked) * meta[0, 1:2, :]
    blend_row = meta[0, 2:3, :] * meta[0, 1:2, :] / (1.0 + jnp.exp(math.log(V) - first_loss))
    blend = to_columns(jnp.concatenate([blend_row] * 8, axis=0))[:, 0:1]
    for u in range(utterances):
        at = rows(u)
        wide_acoustic = acoustic[at, :].astype(F32)
        taken = taken_mine[u] + taken_theirs[u]
        stream_in[at, :] = wide_acoustic + blend[u * slots : (u + 1) * slots] * (taken - wide_acoustic)

    forward(True)
    token_swaps = [
        swap(stream_three.at[core], gathered.at[j - 1, 0], {"dp": mate[j]}) for j in range(1, 4)
    ]
    stats[1] = to_rows(vocab_stats(own_local))
    stat_swap = swap(stats.at[1], stats_arrived.at[1], sibling)
    stat_swap.wait()
    log_total, picked = join([stats[1], stats_arrived[1]])
    loss = (log_total - picked) * meta[0, 1:2, :]
    for u in range(utterances):
        r.loss_out[pl.ds(u, 1), :] = loss[:, u * slots : (u + 1) * slots]
    meta[0] = jnp.where(
        lax.broadcasted_iota(jnp.int32, (8, tokens), 0) == 3, log_total, meta[0]
    )
    meta_swaps = [swap(meta.at[0], meta.at[j], {"dp": mate[j]}) for j in range(1, 4)]

    log_column = to_columns(meta[0])[:, 3:4]

    def slope(j, carry):
        col = pl.multiple_of(j * 128, 128)
        ids = col + lax.broadcasted_iota(jnp.int32, (1, 128), 1)
        onehot = jnp.where(ids == own_local, 1.0, 0.0)
        grad = (jnp.exp(logits[j] - log_column) - onehot) * own_valid
        grad_logits[:, pl.ds(col, 128)] = grad.astype(BF16)
        return carry

    lax.fori_loop(0, main // 128 + 1, slope, 0)
    three_copies = []
    for u in range(utterances):
        sent[u] = dot_nn(grad_logits[rows(u), pl.ds(0, main)], w_vocab[pl.ds(0, main), :]) + dot_nn(
            grad_logits[rows(u), pl.ds(main, 128)], w_rest[...]
        )
        three_copies.append(swap(sent.at[u], arrived.at[u], sibling))

    plan = Planner()
    steps_all = len(bits)
    scatter_send, scatter_recv = r.scatter_send, r.scatter_recv

    def make_chunk(index):
        name, start, cols, order = chunk_list(part_cols, width, bits, low_bits, r)[index]
        source, landing = getattr(r, "src_" + name), r.landing[index]
        if name == "kv":
            out, out_start = (r.key_out, r.value_out)[start // cols], 0
        else:
            out = r.vocab_sum if name == "vocab" and not low_bits else getattr(r, name + "_out")
            out_start = start
        rows_here = source.shape[-2]

        def pick(step, which):
            rest = sorted([b for b in bits if b not in order[:step]], reverse=True)
            where = tuple(which if b == order[step] else slice(None) for b in rest)
            if step == 0:
                return source, where + (slice(None), pl.ds(start, cols))
            return landing[step - 1], where + (slice(None), slice(None))

        def send(step):
            b = order[step]
            ref, where = pick(step, 1 - bit_of[b])
            copy = pltpu.make_async_remote_copy(
                src_ref=ref.at[where],
                dst_ref=landing[step],
                send_sem=scatter_send.at[index, step],
                recv_sem=scatter_recv.at[index, step],
                device_id=peer_of[b],
                device_id_type=MESH,
            )
            copy.start()
            return copy

        def take(step, copy):
            copy.wait_recv()
            ref, where = pick(step, bit_of[order[step]])
            got = landing[step]
            at = pl.ds(out_start, cols)
            if step < len(order) - 1:
                got[...] = got[...] + ref[where]
            elif name == "vocab":
                out[..., at] = got[...] + ref[where]
            else:
                out[:, at] = got[...] + ref[where]

        steps = [
            (link_of(b, bits), rows_here * cols * 4 * 2 ** (steps_all - 1 - s))
            for s, b in enumerate(order)
        ]
        return Chunk(steps, send, take)

    def make_trade(start, cols):
        summed, traded = r.vocab_sum, r.vocab_traded
        at = pl.ds(start, cols)

        def send(step):
            copies = []
            for j in range(1, 4):
                to = lax.rem(mate[j], 4)
                copies.append(
                    pltpu.make_async_remote_copy(
                        src_ref=summed.at[to // 2, lax.rem(to, 2), :, at],
                        dst_ref=traded.at[j - 1, :, at],
                        send_sem=r.trade_send.at[start // 128, j - 1],
                        recv_sem=r.trade_recv.at[start // 128, j - 1],
                        device_id={"dp": mate[j]},
                        device_id_type=MESH,
                    )
                )
                copies[-1].start()
            return Several(copies)

        def take(step, copies):
            copies.wait_recv()
            for j in range(1, 4):
                there = pl.multiple_of(lax.rem(mate[j], 4) * part_cols + start, 128)
                r.vocab_out[:, pl.ds(there, cols)] = traded[j - 1, :, at]
            here = pl.multiple_of(base + start, 128)
            r.vocab_out[:, pl.ds(here, cols)] = summed[quarter // 2, lax.rem(quarter, 2), :, at]

        return Chunk([(0, 2 * r.src_vocab.shape[-2] * cols * 4)], send, take)

    chunks = {}
    for index, (name, start, cols, _) in enumerate(chunk_list(part_cols, width, bits, low_bits, r)):
        chunks[name, start] = make_chunk(index)
        if name == "vocab" and not low_bits:
            chunks[name, start].follow = make_trade(start, cols)

    def put(name, at, product):
        source = getattr(r, "src_" + name)
        source[..., at] = product.reshape(source.shape[:-1] + (product.shape[1],))

    copies = []
    for u in range(utterances):
        at = rows(u)
        three_copies[u].wait()
        three = sent[u] + arrived[u]
        grad_three[u] = three
        low = three.astype(BF16)
        branch_low[at, :] = low
        pre = (dot_nt(low, w_back[...]) * gelu_slope[at, :]).astype(BF16)
        grad_pre[at, :] = pre
        sent[utterances + u] = dot_nt(pre, w_in[...])
        copies.append(swap(sent.at[utterances + u], arrived.at[utterances + u], sibling))
    plan.run_until(4.0)
    for name, left, right in (("back", branch_low, hidden), ("in", norm_low, grad_pre)):
        left_turned = left[...].T
        for start in sorted(s for n, s in chunks if n == name):
            at = pl.ds(start, 512)
            put(name, at, dot_nn(left_turned, right[:, at]))
            plan.run_until(plan.now + 0.5)
            plan.post(chunks[name, start])

    at_core = pl.ds(pl.multiple_of(core * slots, slots), slots)
    at_other = pl.ds(pl.multiple_of((1 - core) * slots, slots), slots)
    share_swaps = []
    for j in range(1, 4):
        token_swaps[j - 1].wait()
        share_swaps.append(swap(gathered.at[j - 1, 0], gathered.at[j - 1, 1], sibling))
        top[j, at_core, :] = gathered[j - 1, 0].astype(BF16)
    base = pl.multiple_of(quarter * part_cols, part_cols)
    pieces = [(c, 256) for c in range(0, part_cols, 256)]
    for j in range(1, 4):
        meta_swaps[j - 1].wait()
        columns = to_columns(meta[j])
        target, valid, log_total = local_targets(columns[:, 0:1]), columns[:, 1:2], columns[:, 3:4]
        share_swaps[j - 1].wait()
        top[j, at_other, :] = gathered[j - 1, 1].astype(BF16)
        for col, cols in pieces:
            ids = base + col + lax.broadcasted_iota(jnp.int32, (1, cols), 1)
            tile = dot_nt(top[j], w_vocab[pl.ds(base + col, cols), :])
            grad = (jnp.exp(tile - log_total) - jnp.where(ids == target, 1.0, 0.0)) * valid
            grad_others[pl.ds((j - 1) * tokens, tokens), pl.ds(col, cols)] = grad.astype(BF16)
        plan.run_until(plan.now + 0.8)
    top_turned = r.top_turned
    for j in range(4):
        top_turned[:, pl.ds(j * tokens, tokens)] = top[j].T
    put("rest", slice(None), dot_nn(top_turned[:, pl.ds(0, tokens)], grad_logits[:, pl.ds(main, 128)]))
    starts = sorted(start for name, start in chunks if name == "vocab")
    for start, stop in zip(starts, starts[1:] + [part_cols]):
        for col in range(start, stop, 256):
            cols = min(256, stop - col)
            product = dot_nn(top_turned[:, pl.ds(0, tokens)], grad_logits[:, pl.ds(base + col, cols)])
            product = product + dot_nn(
                top_turned[:, pl.ds(tokens, 3 * tokens)], grad_others[:, pl.ds(col, cols)]
            )
            put("vocab", pl.ds(col, cols), product)
        plan.run_until(plan.now + 0.7)
        plan.post(chunks["vocab", start])
    plan.post(chunks["rest", 0])

    one_copies = []
    gain_2_total, bias_2_total = 0.0, 0.0
    for u in range(utterances):
        at = rows(u)
        copies[u].wait()
        grad_norm = sent[utterances + u] + arrived[utterances + u]
        hat, scale = normalise(stream_two[at, :])
        gain_2_total = gain_2_total + jnp.sum(grad_norm * hat, axis=0, keepdims=True)
        bias_2_total = bias_2_total + jnp.sum(grad_norm, axis=0, keepdims=True)
        two = grad_three[u] + normalise_back(grad_norm * gain_2, hat, scale)
        grad_two[at, :] = two
        low = two.astype(BF16)
        att_low[at, :] = low
        grad_mixed = dot_nt(low, w_out[...]).astype(BF16)
        for h in range(heads):
            cols = pl.ds(h * HD, HD)
            grad_head = grad_mixed[:, h * HD : (h + 1) * HD]
            prob = probs[u, h]
            grad_prob = dot_nt(grad_head, value_of(u, h))
            spare[pl.ds(u * frames, frames), pl.ds(half + h * HD, HD)] = dot_tn(
                prob.astype(BF16), grad_head
            ).astype(BF16)
            inner = jnp.sum(prob * grad_prob, axis=-1, keepdims=True)
            grad_score = (prob * (grad_prob - inner)).astype(BF16)
            grad_queries[at, cols] = (dot_nn(grad_score, key_of(u, h)) * score_scale).astype(BF16)
            spare[pl.ds(u * frames, frames), cols] = (
                dot_tn(grad_score, queries[at, cols]) * score_scale
            ).astype(BF16)
            plan.run_until(plan.now + 1.5)
        sent[u] = dot_nt(grad_queries[at, :], w_query[...])
        one_copies.append(swap(sent.at[u], arrived.at[u], sibling))
    every = slice(None)
    put("out", every, dot_tn(att_low[...], mixed[...]))
    plan.post(chunks["out", 0])
    put("query", every, dot_tn(one_low[...], grad_queries[...]))
    plan.post(chunks["query", 0])
    plan.run_until(plan.now + 1.0)

    mem_copies = []
    rate_sums = [0.0, 0.0]
    for u in range(utterances):
        total = jnp.zeros((1, width), F32)
        for i in range(row_chunks):
            at = pl.ds(u * frames + i * step_rows, step_rows)
            part = dot_nt(spare[at, :], w_kv[...])
            for j in range(width // 128):
                side_of, tile = j // (width // 256), j % (width // 256)
                index = ((side_of * utterances + u) * row_chunks + i) * (width // 256) + tile
                logits[index] = part[:, j * 128 : (j + 1) * 128]
            total = total + jnp.sum(part, axis=0, keepdims=True)
        tiles = row_chunks * (width // 256)
        mem_copies.append(
            swap(
                logits.at[pl.ds(((1 - core) * utterances + u) * tiles, tiles)],
                mem_arrived.at[pl.ds(u * tiles, tiles)],
                sibling,
            )
        )
        group = jnp.zeros((1, width), jnp.int32) + rate_groups[u]
        for k in range(2):
            rate_sums[k] = rate_sums[k] + jnp.where((group == 1) == (k == 1), total, 0.0)
        plan.run_until(plan.now + 1.2)
    span = frames // 2
    for k in range(2 * utterances):
        at = pl.ds(k * span, span)
        product = dot_tn(mem_low[at, :], spare[at, :])
        product = product.reshape(r.src_kv.shape)
        r.src_kv[...] = product if k == 0 else r.src_kv[...] + product
    plan.run_until(plan.now + 2.0)
    plan.post(*[chunks["kv", start] for start in sorted(s for n, s in chunks if n == "kv")])

    gain_1_total, bias_1_total = 0.0, 0.0
    for u in range(utterances):
        at = rows(u)
        valid = own_valid[u * slots : (u + 1) * slots]
        one_copies[u].wait()
        one = grad_two[at, :] + (sent[u] + arrived[u])
        grad_two[at, :] = one
        masked = one * valid
        for k in range(kernel_rows.shape[0]):
            shift = 8 + k - kernel_rows.shape[0] // 2
            row = jnp.sum(masked * padded[u, pl.ds(shift, slots), :], axis=0, keepdims=True)
            if u == 0:
                small_sent[0, pl.ds(k, 1), :] = row
            else:
                small_sent[0, pl.ds(k, 1), :] = small_sent[0, pl.ds(k, 1), :] + row
        padded[u, pl.ds(8, slots), :] = masked
        for j in range(width // 128):
            cols = pl.ds(j * 128, 128)
            total = jnp.zeros((slots, 128), F32)
            for k in range(kernel_rows.shape[0]):
                shift = 8 - k + kernel_rows.shape[0] // 2
                total = total + kernel_rows[pl.ds(k, 1), cols] * padded[u, pl.ds(shift, slots), cols]
            stream_one[at, cols] = total * valid
        grad_norm = stream_one[at, :]
        hat, scale = normalise(stream_in[at, :])
        gain_1_total = gain_1_total + jnp.sum(grad_norm * hat, axis=0, keepdims=True)
        bias_1_total = bias_1_total + jnp.sum(grad_norm, axis=0, keepdims=True)
        zero = grad_two[at, :] + normalise_back(grad_norm * gain_1, hat, scale)
        terms[u] = blend[u * slots : (u + 1) * slots] * zero
        stream_one[at, :] = zero - terms[u]
        plan.run_until(plan.now + 1.5)

    last_taps = kernel_rows.shape[0]
    small_sent[0, pl.ds(last_taps, 12 - last_taps), :] = jnp.zeros((12 - last_taps, width), F32)
    for i, row in enumerate((gain_1_total, bias_1_total, gain_2_total, bias_2_total)):
        small_sent[0, pl.ds(12 + i, 1), :] = row
    for k in range(2):
        small_sent[0, pl.ds(16 + k, 1), :] = rate_sums[k]
    small_sent[0, pl.ds(18, 6), :] = jnp.zeros((6, width), F32)
    small_peers = [peer_of[b] for b in low_bits + bits] + [sibling]

    def small_send(step):
        copy = pltpu.make_async_remote_copy(
            src_ref=small_sent.at[step],
            dst_ref=small_arrived.at[step],
            send_sem=r.small_send.at[step],
            recv_sem=r.small_recv.at[step],
            device_id=small_peers[step],
            device_id_type=MESH,
        )
        copy.start()
        return copy

    def small_take(step, copy):
        copy.wait_recv()
        if step + 1 < len(small_peers):
            small_sent[step + 1] = small_sent[step] + small_arrived[step]
        else:
            r.small_out[pl.ds(0, 16), :] = small_sent[step, pl.ds(0, 16), :]
            r.small_out[pl.ds(16, 8), :] = (
                small_sent[step, pl.ds(16, 8), :] + small_arrived[step, pl.ds(16, 8), :]
            )

    small_links = [link_of(b, bits) for b in low_bits + bits] + ["core"]
    plan.post(Chunk([(l, 24 * width * 4) for l in small_links], small_send, small_take))

    features = width // n_dp
    feature_rows = max(features, 8)
    block_rows = term_blocks.shape[1]
    turned = terms[core].T
    id_row = targets[pl.ds(core, 1), :].astype(F32)
    rest = block_rows - features - 1
    for p in range(n_dp):
        term_blocks[p, pl.ds(0, features), :] = turned[p * features : (p + 1) * features]
        term_blocks[p, pl.ds(features, 1), :] = id_row
        term_blocks[p, pl.ds(features + 1, rest), :] = jnp.zeros((rest, slots), F32)

    def term_copy(k):
        there = lax.rem(me + k, n_dp)
        return pltpu.make_async_remote_copy(
            src_ref=term_blocks.at[there],
            dst_ref=term_arrived.at[me],
            send_sem=r.term_send.at[k],
            recv_sem=r.term_recv.at[k],
            device_id={"dp": there},
            device_id_type=MESH,
        )

    def term_start(k, carry):
        term_copy(k).start()
        return carry

    def term_wait(k, carry):
        term_copy(k).wait()
        return carry

    term_arrived[me] = term_blocks[me]
    lax.fori_loop(1, n_dp, term_start, 0)
    stores = []

    def store(source, target):
        copy = pltpu.make_async_copy(source, target, r.store_sem.at[len(stores)])
        copy.start()
        stores.append(copy)

    store(stream_one, r.acoustic_out)
    for u in range(utterances):
        mem_copies[u].wait()
        for i in range(row_chunks):
            for j in range(width // 256):
                index = (u * row_chunks + i) * (width // 256) + j
                first_tile = (core * utterances) * row_chunks * (width // 256)
                mem_arrived[index] = logits[first_tile + index] + mem_arrived[index]
                at = pl.ds(u * frames + i * step_rows, step_rows)
                store(mem_arrived.at[index], r.memory_out.at[at, pl.ds(j * 128, 128)])
    plan.run_until(plan.now + 8.0)
    lax.fori_loop(1, n_dp, term_wait, 0)
    per_piece = 512 // slots
    blocks_hi = table_out.shape[1] // 256
    batch = 4

    def table_piece(p, fresh):
        found = [term_arrived[p * per_piece + i] for i in range(per_piece)]
        values = jnp.concatenate([f[:feature_rows] for f in found], axis=1)
        ids = jnp.concatenate([f[features : features + 1] for f in found], axis=1).astype(jnp.int32)
        low_ids, high_ids = ids & 255, ids >> 8
        onehot_lo[...] = jnp.where(
            lax.broadcasted_iota(jnp.int32, (256, 512), 0) == low_ids, 1.0, 0.0
        ).astype(BF16)
        coarse = values.astype(BF16).astype(F32)
        both = jnp.concatenate([coarse, values - coarse], axis=0)
        for first_hi in range(0, blocks_hi, batch):
            here = range(first_hi, min(first_hi + batch, blocks_hi))
            masked = jnp.concatenate([jnp.where(high_ids == hi, both, 0.0) for hi in here], axis=0)
            product = dot_nt(masked.astype(BF16), onehot_lo[...])
            for i, hi in enumerate(here):
                top_part = product[2 * i * feature_rows : (2 * i + 1) * feature_rows]
                low_part = product[(2 * i + 1) * feature_rows : (2 * i + 2) * feature_rows]
                at = pl.ds(hi * 256, 256)
                if fresh:
                    table_out[:, at] = top_part + low_part
                else:
                    table_out[:, at] = table_out[:, at] + (top_part + low_part)

    pieces = n_dp // per_piece
    table_piece(0, True)
    if pieces <= 4:
        for p in range(1, pieces):
            plan.run_until(plan.now + 1.5)
            table_piece(p, False)
    else:
        lax.fori_loop(1, pieces, lambda p, c: (table_piece(p, False), c)[1], 0)
    table_swap = swap(table_out, table_theirs, sibling)
    plan.run_until(plan.now + 3.0)
    table_swap.wait()
    whole_table = r.whole_table
    whole_table[...] = (
        table_out[pl.ds(0, whole_table.shape[0]), :] + table_theirs[pl.ds(0, whole_table.shape[0]), :]
    )[:, :table_rows]
    store(whole_table, r.table_out)
    plan.finish()
    if not low_bits:
        rest = vocab_here - main
        r.vocab_out[:, pl.ds(main, rest)] = r.rest_out[...][:, :rest]
    for copy in stores:
        copy.wait()


def link_of(bit, bits):
    if bit == bits[-1]:
        return bits[-2]
    return bit


def chunk_list(part_cols, width, bits, low_bits, sizes):
    turned = [bits[1], bits[0]] + bits[2:]
    listing = []
    for start in range(0, part_cols, 512):
        listing.append(("vocab", start, 512, [b for b in bits if b > 1]))
    listing.append(("rest", 0, 128, bits))
    for name, order in (("back", turned), ("in", bits)):
        for start in range(0, sizes.units, 512):
            if name == "in" and start:
                order = [bits[2], bits[0], bits[1]] + bits[3:]
            listing.append((name, start, 512, order))
    listing.append(("out", 0, sizes.half, turned))
    listing.append(("query", 0, sizes.half, bits))
    for k, start in enumerate(range(0, 2 * sizes.half, 256)):
        listing.append(("kv", start, 256, [bits, turned][k % 2]))
    return listing


def decoder_call(
    acoustic, memory, embedding, w_query, w_key, w_value, w_out, w_in, w_back, w_vocab, norms,
    fsmn_kernel, rate_table, token_lengths, memory_lengths, rate_groups, glance, targets, n_dp,
):
    utterances = token_lengths.shape[0]
    tokens, width = acoustic.shape
    slots = tokens // utterances
    mem_rows = memory.shape[0]
    half = w_query.shape[1]
    heads = half // HD
    frames = mem_rows // utterances
    units = w_in.shape[1]
    vocab_here = w_vocab.shape[1]
    table_rows = embedding.shape[0]
    part_cols = vocab_here // 512 * 128
    all_cols = 4 * part_cols + 128
    w_turned = w_vocab.T
    mains = table_rows // 2048 * 2048
    nbits = n_dp.bit_length() - 1
    steps = nbits
    while width >> steps < 8:
        steps -= 1
    low_bits, bits = list(range(nbits - steps)), list(range(nbits - steps, nbits))
    rows = width >> steps
    features = width // n_dp
    feature_rows = max(features, 8)
    block_rows = feature_rows + 8 if features >= 8 else 8
    blocks_hi = (table_rows + 255) // 256
    sizes = SimpleNamespace(units=units, half=half)
    plane = [b for b in bits if b < 2]
    listing = chunk_list(part_cols, width, bits, low_bits, sizes)
    most = max(len(c[3]) for c in listing)

    f32 = lambda *shape: jax.ShapeDtypeStruct(shape, F32)
    v32 = lambda *shape: pltpu.VMEM(shape, F32)
    v16 = lambda *shape: pltpu.VMEM(shape, BF16)
    dma = lambda *shape: pltpu.SemaphoreType.DMA(shape)
    inputs = dict(
        acoustic=(VMEM, acoustic),
        table_tail=(VMEM, embedding[mains:]),
        memory=(ANY, memory),
        table=(ANY, embedding),
        w_query_hbm=(ANY, w_query),
        w_key_hbm=(ANY, w_key),
        w_value_hbm=(ANY, w_value),
        w_out_hbm=(ANY, w_out),
        w_in_hbm=(ANY, w_in),
        w_back_hbm=(ANY, w_back),
        w_vocab_hbm=(ANY, w_turned),
        gain_one=(VMEM, norms[0][None]),
        bias_one=(VMEM, norms[1][None]),
        gain_two=(VMEM, norms[2][None]),
        bias_two=(VMEM, norms[3][None]),
        kernel_rows=(VMEM, fsmn_kernel),
        rate_table=(VMEM, rate_table),
        token_lengths=(SMEM, token_lengths),
        memory_lengths=(SMEM, memory_lengths),
        rate_groups=(SMEM, rate_groups),
        glance=(VMEM, glance.reshape(utterances, slots)),
        targets=(VMEM, targets.reshape(utterances, slots)),
    )
    outputs = dict(
        loss_out=f32(utterances, slots),
        small_out=f32(24, width),
        vocab_out=f32(2, rows, part_cols) if low_bits else f32(rows, vocab_here),
        rest_out=f32(rows, 128),
        in_out=f32(rows, units),
        back_out=f32(rows, units),
        query_out=f32(rows, half),
        out_out=f32(rows, half),
        key_out=f32(rows, half),
        value_out=f32(rows, half),
        acoustic_out=f32(tokens, width),
        memory_out=f32(mem_rows, width // 2),
        table_out=f32(features, table_rows),
    )
    shape = (2,) * steps + (rows,)
    scratch = dict(
        w_query=v16(width, half),
        w_kv=v16(width, 2 * half),
        w_out=v16(half, width),
        w_in=v16(width, units),
        w_back=v16(units, width),
        w_vocab=v16(vocab_here, width),
        w_rest=v16(128, width),
        mem_low=v16(mem_rows, width),
        kv=v16(mem_rows, 2 * half),
        spare=v16(mem_rows, 2 * half),
        padded=v32(utterances, slots + 16, width),
        stream_in=v32(tokens, width),
        stream_one=v32(tokens, width),
        stream_two=v32(tokens, width),
        stream_three=v32(utterances, slots, width),
        one_low=v16(tokens, width),
        queries=v16(tokens, half),
        probs=v32(utterances, heads, slots, frames),
        mixed=v16(tokens, half),
        norm_low=v16(tokens, width),
        hidden=v16(tokens, units),
        gelu_slope=v32(tokens, units),
        top=v16(4, tokens, width),
        logits=v32(all_cols // 128, tokens, 128),
        grad_logits=v16(tokens, all_cols),
        grad_others=v16(3 * tokens, part_cols),
        top_turned=v16(width, 4 * tokens),
        taken_mine=v32(utterances, slots, width),
        taken_theirs=v32(utterances, slots, width),
        grad_three=v32(utterances, slots, width),
        grad_two=v32(tokens, width),
        branch_low=v16(tokens, width),
        grad_pre=v16(tokens, units),
        att_low=v16(tokens, width),
        grad_queries=v16(tokens, half),
        mem_arrived=v32(mem_rows // 256 * (width // 256), 256, 128),
        meta=v32(4, 8, tokens),
        stats=v32(2, 8, tokens),
        stats_arrived=v32(2, 8, tokens),
        sent=v32(2 * utterances, slots, width),
        arrived=v32(2 * utterances, slots, width),
        gathered=v32(3, 2, slots, width),
        small_sent=v32(nbits + 1, 24, width),
        small_arrived=v32(nbits + 1, 24, width),
        term_blocks=v32(n_dp, block_rows, slots),
        term_arrived=v32(n_dp, block_rows, slots),
        onehot_lo=v16(256, 512),
        table_rest=v16((table_rows - mains + 127) // 128 * 128, width),
        table_theirs=v32(feature_rows, blocks_hi * 256),
        table_mine=v32(feature_rows, blocks_hi * 256),
        src_vocab=v32(*shape, part_cols),
        src_rest=v32(*shape, 128),
        whole_table=v32(features, table_rows),
        src_back=v32(*shape, units),
        vocab_sum=v32(*(2,) * len(plane), rows, part_cols),
        vocab_traded=v32(3, rows, part_cols),
        src_in=v32(*shape, units),
        src_out=v32(*shape, half),
        src_query=v32(*shape, half),
        src_kv=v32(*shape, 2 * half),
        load_sem=dma(24),
        store_sem=dma(24),
        trade_send=dma(part_cols // 128, 3),
        trade_recv=dma(part_cols // 128, 3),
        swap_send=dma(40),
        swap_recv=dma(40),
        scatter_send=dma(len(listing), most),
        scatter_recv=dma(len(listing), most),
        small_send=dma(nbits + 1),
        small_recv=dma(nbits + 1),
        term_send=dma(n_dp),
        term_recv=dma(n_dp),
    )
    landing = [
        [v32(*(2,) * (steps - 1 - s), rows, cols) for s in range(len(order))]
        for _, _, cols, order in listing
    ]
    names = list(inputs) + list(outputs) + list(scratch)
    flat = [ref for chunk in landing for ref in chunk]

    def kernel(*refs):
        named, rest = refs[: len(names)], list(refs[len(names) :])
        lands = [[rest.pop(0) for _ in chunk] for chunk in landing]
        decoder_kernel(
            names + ["landing", "units", "half"], vocab_here, part_cols, table_rows, n_dp, bits,
            low_bits, *named, lands, units, half,
        )

    out = pl.pallas_call(
        kernel,
        out_shape=list(outputs.values()),
        in_specs=[spec for spec, _ in inputs.values()],
        out_specs=[VMEM] * (len(outputs) - 3) + [ANY] * 3,
        scratch_shapes=list(scratch.values()) + flat,
        compiler_params=pltpu.CompilerParams(
            collective_id=1, has_side_effects=True, vmem_limit_bytes=64 << 20
        ),
    )(*[value for _, value in inputs.values()])
    return SimpleNamespace(**dict(zip(outputs, out))), low_bits


def deliver_kernel(n_dp, n_passed, *refs):
    n = n_passed + 2
    sources, targets, held = refs[:n], refs[n : 2 * n + 5], refs[2 * n + 5 : 3 * n + 5]
    sem_in, sem_out = refs[3 * n + 5 :]
    reads, writes = [], []
    for i, (source, buffer) in enumerate(zip(sources, held)):
        reads.append(pltpu.make_async_copy(source, buffer, sem_in.at[i]))
        reads[-1].start()
    for i in range(n_passed):
        reads[i].wait()
        writes.append(pltpu.make_async_copy(held[i], targets[i], sem_out.at[i]))
        writes[-1].start()
    reads[n_passed].wait()
    reads[n_passed + 1].wait()
    loss, small = held[n_passed:]
    loss_to, gain_one_to, bias_one_to, gain_two_to, bias_two_to, taps_to, rate_to = targets[n_passed:]
    slots = loss.shape[1]
    for u in range(loss.shape[0]):
        loss_to[:, pl.ds(u * slots, slots)] = loss[pl.ds(u, 1), :]
    me = lax.axis_index("dp")
    own = small.shape[1] // n_dp
    mine = jnp.zeros((16, own), F32)
    for p in range(n_dp):
        mine = jnp.where(me == p, small[pl.ds(0, 16), p * own : (p + 1) * own], mine)
    taps_to[...] = mine[: taps_to.shape[0]]
    for i, target in enumerate((gain_one_to, bias_one_to, gain_two_to, bias_two_to)):
        target[...] = mine[12 + i : 13 + i]
    rate_to[...] = small[pl.ds(16, 2), :]
    for copy in writes:
        copy.wait()


def per_device(
    acoustic,
    memory,
    embedding,
    w_query,
    w_key,
    w_value,
    w_out,
    w_in,
    w_back,
    w_vocab,
    gain_one,
    bias_one,
    gain_two,
    bias_two,
    fsmn_kernel,
    rate_table,
    token_lengths,
    memory_lengths,
    rate_groups,
    glance_mask,
    targets,
):
    tok_rows, model_width = acoustic.shape
    half = w_query.shape[1]
    n_dp = lax.axis_size("dp")
    result, low_bits = decoder_call(
        acoustic, memory, embedding, w_query, w_key, w_value, w_out, w_in, w_back, w_vocab,
        (gain_one, bias_one, gain_two, bias_two), fsmn_kernel, rate_table,
        token_lengths, memory_lengths, rate_groups, glance_mask, targets, n_dp,
    )
    vocab = result.vocab_out
    summed = [
        result.query_out, result.key_out, result.value_out, result.out_out, result.in_out,
        result.back_out,
    ]
    if low_bits:
        size = 1 << len(low_bits)
        groups = [list(range(g * size, (g + 1) * size)) for g in range(n_dp // size)]
        planes = [list(range(4 * g, 4 * g + 4)) for g in range(n_dp // 4)]
        vocab = lax.all_to_all(
            vocab.reshape(4, model_width // n_dp, -1), "dp", 0, 0, axis_index_groups=planes, tiled=True
        )
        *summed, rest = [
            lax.psum_scatter(s, "dp", scatter_dimension=0, axis_index_groups=groups, tiled=True)
            for s in (*summed, result.rest_out)
        ]
        vocab = jnp.concatenate([*vocab, rest], axis=1)[:, : w_vocab.shape[1]]
    own = model_width // n_dp
    f32 = lambda *shape: jax.ShapeDtypeStruct(shape, F32)
    like = lambda x: jax.ShapeDtypeStruct(x.shape, F32)
    passed = (result.memory_out, result.table_out, result.acoustic_out, vocab, *summed)
    handed = (*passed, result.loss_out, result.small_out)
    (
        grad_memory, grad_table, grad_acoustic, grad_vocab, grad_query, grad_key, grad_value,
        grad_out, grad_in, grad_back, token_loss, gain_1, bias_1, gain_2, bias_2, grad_taps, grad_rate,
    ) = pl.pallas_call(
        partial(deliver_kernel, n_dp, len(passed)),
        out_shape=[
            *[like(x) for x in passed],
            f32(1, tok_rows),
            *[f32(1, own)] * 4,
            f32(fsmn_kernel.shape[0], own),
            f32(2, model_width),
        ],
        in_specs=[ANY] * len(handed),
        out_specs=[ANY] * len(passed) + [VMEM] * 7,
        scratch_shapes=[pltpu.VMEM(x.shape, F32) for x in handed]
        + [pltpu.SemaphoreType.DMA((len(handed),)), pltpu.SemaphoreType.DMA((len(handed),))],
        compiler_params=pltpu.CompilerParams(vmem_limit_bytes=60 << 20),
    )(*handed)
    return (
        token_loss.reshape(tok_rows),
        grad_acoustic,
        grad_memory,
        grad_table.T,
        grad_query,
        grad_key,
        grad_value,
        grad_out.T,
        grad_in,
        grad_back.T,
        grad_vocab,
        gain_1.reshape(own),
        bias_1.reshape(own),
        gain_2.reshape(own),
        bias_2.reshape(own),
        grad_taps,
        grad_rate,
    )


def solution(mesh):
    return jax.shard_map(
        per_device,
        mesh=mesh,
        in_specs=(
            P("dp", None),
            P("dp", None),
            P(),
            P(None, "mp"),
            P(None, "mp"),
            P(None, "mp"),
            P("mp", None),
            P(None, "mp"),
            P("mp", None),
            P(None, "mp"),
            P(),
            P(),
            P(),
            P(),
            P(),
            P(),
            P("dp"),
            P("dp"),
            P("dp"),
            P("dp"),
            P("dp"),
        ),
        out_specs=(
            P("dp"),
            P("dp", None),
            P("dp", "mp"),
            P(None, "dp"),
            P("dp", "mp"),
            P("dp", "mp"),
            P("dp", "mp"),
            P("mp", "dp"),
            P("dp", "mp"),
            P("mp", "dp"),
            P("dp", "mp"),
            P("dp"),
            P("dp"),
            P("dp"),
            P("dp"),
            P(None, "dp"),
            P(),
        ),
        check_vma=False,
    )
```

```python
from functools import partial
import math
from types import SimpleNamespace

import jax
import jax.numpy as jnp
from jax import lax
from jax.experimental import pallas as pl
from jax.experimental.pallas import tpu as pltpu
from jax.sharding import PartitionSpec as P

HD = 128
V = 8404
EPSILON = 1e-05
MESH = pl.DeviceIdType.MESH
VMEM = pl.BlockSpec(memory_space=pltpu.VMEM)
SMEM = pl.BlockSpec(memory_space=pltpu.SMEM)
ANY = pl.BlockSpec(memory_space=pl.ANY)
F32, BF16 = jnp.float32, jnp.bfloat16
NEG = -1e30


def other_core():
    return {"mp": 1 - lax.axis_index("mp")}


def dot_nn(a, b):
    return lax.dot_general(a, b, (((1,), (0,)), ((), ())), preferred_element_type=F32)


def dot_nt(a, b):
    return lax.dot_general(a, b, (((1,), (1,)), ((), ())), preferred_element_type=F32)


def dot_tn(a, b):
    return lax.dot_general(a, b, (((0,), (0,)), ((), ())), preferred_element_type=F32)


def normalise(rows):
    average = jnp.mean(rows, axis=-1, keepdims=True)
    centred = rows - average
    variance = jnp.mean(centred * centred, axis=-1, keepdims=True)
    scale = lax.rsqrt(variance + EPSILON)
    return centred * scale, scale


def normalise_back(grad_hat, hat, scale):
    first = jnp.mean(grad_hat, axis=-1, keepdims=True)
    second = jnp.mean(grad_hat * hat, axis=-1, keepdims=True)
    return scale * (grad_hat - first - hat * second)


def side_by_side(columns):
    lane = lax.broadcasted_iota(jnp.int32, (columns[0].shape[0], 128), 1)
    tile = jnp.zeros(lane.shape, F32)
    for i, column in enumerate(columns):
        tile = jnp.where(lane == i, column, tile)
    return tile


def to_rows(columns):
    return side_by_side(columns).T[:8]


def to_columns(rows):
    return jnp.concatenate([rows] * 16, axis=0).T


class Planner:
    RATE = 0.045e6
    HOP = 1.5
    BACKLOG = 3.0

    def __init__(self):
        self.now = 0.0
        self.free = {}
        self.flying = []
        self.waiting = []
        self.started = []
        self.count = 0

    def launch(self, item, step):
        link, size = item.steps[step]
        begin = max(self.now, self.free.get(link, 0.0))
        self.free[link] = begin + size / self.RATE
        copy = item.send(step)
        self.started.append(copy)
        self.count += 1
        self.flying.append((self.free[link] + self.HOP, self.count, item, step, copy))

    def release(self):
        kept = []
        for item in self.waiting:
            link = item.steps[0][0]
            if self.free.get(link, 0.0) - self.now < self.BACKLOG:
                self.launch(item, 0)
            else:
                kept.append(item)
        self.waiting = kept

    def post(self, *items):
        self.waiting += items
        self.release()

    def run_until(self, time):
        while self.flying or self.waiting:
            if not self.flying:
                self.now = max(self.now, min(self.free[i.steps[0][0]] for i in self.waiting))
                self.release()
                continue
            first = min(self.flying, key=lambda f: f[:2])
            if first[0] > time:
                break
            self.flying.remove(first)
            self.now = max(self.now, first[0])
            _, _, item, step, copy = first
            item.take(step, copy)
            if step + 1 < len(item.steps):
                self.launch(item, step + 1)
            elif item.follow is not None:
                self.launch(item.follow, 0)
            self.release()
        if time != math.inf:
            self.now = max(self.now, time)
        self.release()

    def finish(self):
        self.run_until(math.inf)
        for copy in self.started:
            copy.wait_send()


class Chunk:
    def __init__(self, steps, send, take):
        self.steps, self.send, self.take, self.follow = steps, send, take, None


class Several:
    def __init__(self, copies):
        self.copies = copies

    def wait_recv(self):
        for copy in self.copies:
            copy.wait_recv()

    def wait_send(self):
        for copy in self.copies:
            copy.wait_send()


def decoder_kernel(
    names,
    vocab_here,
    part_cols,
    table_rows,
    n_dp,
    bits,
    low_bits,
    *refs,
):
    r = SimpleNamespace(**dict(zip(names, refs)))
    acoustic, memory, table = r.acoustic, r.memory, r.table
    targets, glance = r.targets, r.glance
    gain_1, bias_1 = r.gain_one[...], r.bias_one[...]
    gain_2, bias_2 = r.gain_two[...], r.bias_two[...]
    kernel_rows, rate_table = r.kernel_rows, r.rate_table
    token_lengths, memory_lengths, rate_groups = r.token_lengths, r.memory_lengths, r.rate_groups
    w_query, w_kv, w_out, w_in, w_back, w_vocab = r.w_query, r.w_kv, r.w_out, r.w_in, r.w_back, r.w_vocab
    mem_low, kv, padded, spare = r.mem_low, r.kv, r.padded, r.spare
    stream_in, stream_one, stream_two, stream_three = r.stream_in, r.stream_one, r.stream_two, r.stream_three
    one_low, queries, probs, mixed = r.one_low, r.queries, r.probs, r.mixed
    norm_low, hidden, gelu_slope, top = r.norm_low, r.hidden, r.gelu_slope, r.top
    logits, grad_logits, grad_others = r.logits, r.grad_logits, r.grad_others
    taken_mine, taken_theirs = r.taken_mine, r.taken_theirs
    grad_three, grad_two, branch_low = r.grad_three, r.grad_two, r.branch_low
    grad_pre, att_low, grad_queries = r.grad_pre, r.att_low, r.grad_queries
    mem_arrived, meta, stats, stats_arrived = r.mem_arrived, r.meta, r.stats, r.stats_arrived
    sent, arrived, gathered = r.sent, r.arrived, r.gathered
    small_sent, small_arrived = r.small_sent, r.small_arrived
    terms, term_blocks, term_arrived = grad_three, r.term_blocks, r.term_arrived
    onehot_lo, table_theirs, table_out = r.onehot_lo, r.table_theirs, r.table_mine
    swap_send, swap_recv, load_sem = r.swap_send, r.swap_recv, r.load_sem

    utterances, slots = targets.shape
    width = acoustic.shape[1]
    frames = memory.shape[0] // utterances
    half = w_query.shape[1]
    heads = half // HD
    tokens = utterances * slots
    me, core = lax.axis_index("dp"), lax.axis_index("mp")
    sibling = {"mp": 1 - core}
    quarter = lax.rem(me, 4)
    flips = [1 - 2 * lax.rem(me, 2), 2 - 4 * lax.rem(me // 2, 2)]
    mate = [me + flips[0] * (j % 2) + flips[1] * (j // 2) for j in range(4)]
    bit_of = {b: lax.rem(me // (1 << b), 2) for b in low_bits + bits}
    peer_of = {b: {"dp": me + (1 - 2 * bit_of[b]) * (1 << b)} for b in low_bits + bits}
    score_scale = 1.0 / math.sqrt(HD)

    loads = []

    def load(source, target):
        copy = pltpu.make_async_copy(source, target, load_sem.at[len(loads)])
        copy.start()
        loads.append(copy)
        return copy

    load_memory = load(memory, mem_low)
    load_kv = [
        load(r.w_key_hbm, w_kv.at[:, pl.ds(0, half)]),
        load(r.w_value_hbm, w_kv.at[:, pl.ds(half, half)]),
    ]
    load_query = load(r.w_query_hbm, w_query)
    load_out = load(r.w_out_hbm, w_out)

    barrier = pltpu.get_barrier_semaphore()

    def greet(k, carry):
        pl.semaphore_signal(
            barrier, inc=1, device_id={"dp": lax.rem(me + k, n_dp)}, device_id_type=MESH
        )
        return carry

    lax.fori_loop(1, n_dp, greet, 0)
    pl.semaphore_signal(barrier, inc=1, device_id=sibling, device_id_type=MESH)

    load_in = load(r.w_in_hbm, w_in)
    load_back = load(r.w_back_hbm, w_back)
    block = 1024
    per_core = table_rows // (2 * block)
    mains = 2 * per_core * block

    def load_table(k):
        at = pl.ds(pl.multiple_of((core * per_core + k) * block, block), block)
        return load(table.at[at, :], spare.at[pl.ds(k % 2 * block, block), :])

    table_loads = [load_table(0), load_table(1)]
    main = 4 * part_cols
    load_vocab = load(r.w_vocab_hbm, w_vocab)
    w_rest = r.w_rest
    w_rest[...] = jnp.zeros(w_rest.shape, BF16)
    r.table_rest[...] = jnp.zeros(r.table_rest.shape, BF16)
    r.table_rest[pl.ds(0, table_rows - mains), :] = r.table_tail[...]

    swaps = []

    def swap(source, target, device):
        k = len(swaps)
        copy = pltpu.make_async_remote_copy(
            src_ref=source,
            dst_ref=target,
            send_sem=swap_send.at[k],
            recv_sem=swap_recv.at[k],
            device_id=device,
            device_id_type=MESH,
        )
        copy.start()
        swaps.append(copy)
        return copy

    lane = lax.broadcasted_iota(jnp.int32, (1, slots), 1)
    row_of = lax.broadcasted_iota(jnp.int32, (8, slots), 0)
    for u in range(utterances):
        target_row = targets[pl.ds(u, 1), :].astype(F32)
        glance_row = glance[pl.ds(u, 1), :].astype(F32)
        valid_row = (lane < token_lengths[u]).astype(F32)
        meta[0, :, pl.ds(u * slots, slots)] = jnp.where(
            row_of == 0, target_row, jnp.where(row_of == 1, valid_row, glance_row)
        )
    own_columns = to_columns(meta[0])
    own_target = own_columns[:, 0:1]
    own_valid = own_columns[:, 1:2]

    def rows(u):
        return pl.ds(u * slots, slots)

    edge = jnp.zeros((8, width), F32)
    for u in range(utterances):
        padded[u, pl.ds(0, 8), :] = edge
        padded[u, pl.ds(8 + slots, 8), :] = edge

    step_rows = 256
    row_chunks = frames // step_rows

    def key_of(u, h):
        return kv[pl.ds(u * frames, frames), pl.ds(h * HD, HD)]

    def value_of(u, h):
        return kv[pl.ds(u * frames, frames), pl.ds(half + h * HD, HD)]

    frame_lane = lax.broadcasted_iota(jnp.int32, (1, frames), 1)

    def look_up(first_row, count, allowed, source):
        ids = first_row + lax.broadcasted_iota(jnp.int32, (1, count), 1)
        local = jnp.where(allowed, own_target.astype(jnp.int32), -1)
        onehot = jnp.where(ids == local, 1.0, 0.0).astype(BF16)
        return dot_nn(onehot, source)

    def look_up_block(k):
        table_loads[k].wait()
        part = look_up(
            (core * per_core + k) * block, block, True, spare[pl.ds(k % 2 * block, block), :]
        )
        for u in range(utterances):
            piece = part[u * slots : (u + 1) * slots]
            taken_mine[u] = piece if k == 0 else taken_mine[u] + piece
        if k + 2 < per_core:
            table_loads.append(load_table(k + 2))

    def look_up_rest():
        part = look_up(mains, r.table_rest.shape[0], core == 0, r.table_rest[...])
        for u in range(utterances):
            taken_mine[u] = taken_mine[u] + part[u * slots : (u + 1) * slots]

    def local_targets(target_column):
        local = target_column.astype(jnp.int32) - core * vocab_here
        return jnp.where((local >= 0) & (local < vocab_here), local, -1)

    def vocab_stats(target):
        tiles = main // 128
        step_tiles = 4

        ids = main + lax.broadcasted_iota(jnp.int32, (1, 128), 1)
        last = jnp.where(ids < vocab_here, dot_nt(top[0], w_rest[...]), NEG)
        logits[tiles] = last
        top_m, picked = last, jnp.where(ids == target, last, 0.0)
        for j in range(tiles // step_tiles):
            col = j * step_tiles * 128
            product = dot_nt(top[0], w_vocab[pl.ds(col, step_tiles * 128), :])
            for i in range(step_tiles):
                tile = product[:, i * 128 : (i + 1) * 128]
                ids = col + i * 128 + lax.broadcasted_iota(jnp.int32, (1, 128), 1)
                logits[j * step_tiles + i] = tile
                top_m = jnp.maximum(top_m, tile)
                picked = picked + jnp.where(ids == target, tile, 0.0)
        top_row = jnp.max(top_m, axis=1, keepdims=True)

        def add(j, total):
            for i in range(3):
                total = total + jnp.exp(logits[3 * j + i] - top_row)
            return total

        total = lax.fori_loop(0, (tiles + 1) // 3, add, jnp.zeros((tokens, 128), F32))
        return (
            top_row,
            jnp.sum(total, axis=1, keepdims=True),
            jnp.sum(picked, axis=1, keepdims=True),
        )

    def join(mine, theirs):
        top_value = jnp.maximum(mine[0], theirs[0])
        total = mine[1] * jnp.exp(mine[0] - top_value) + theirs[1] * jnp.exp(theirs[0] - top_value)
        return top_value + jnp.log(total), mine[2] + theirs[2]

    def memory_block(u):
        at = rows(u)
        valid = own_valid[u * slots : (u + 1) * slots]
        hat, _ = normalise(stream_in[at, :])
        padded[u, pl.ds(8, slots), :] = (hat * gain_1 + bias_1) * valid
        for j in range(width // 128):
            cols = pl.ds(j * 128, 128)
            total = jnp.zeros((slots, 128), F32)
            for k in range(kernel_rows.shape[0]):
                shift = 8 + k - kernel_rows.shape[0] // 2
                total = total + kernel_rows[pl.ds(k, 1), cols] * padded[u, pl.ds(shift, slots), cols]
            stream_one[at, cols] = stream_in[at, cols] + total * valid
        low = stream_one[at, :].astype(BF16)
        one_low[at, :] = low
        queries[at, :] = dot_nn(low, w_query[...]).astype(BF16)

    def forward(second, beside_one=None, beside_two=None):
        copies = []
        for u in range(utterances):
            at = rows(u)
            if second:
                memory_block(u)
            frame_ok = frame_lane < memory_lengths[u]
            for h in range(heads):
                cols = pl.ds(h * HD, HD)
                scores = dot_nt(queries[at, cols], key_of(u, h)) * score_scale
                scores = jnp.where(frame_ok, scores, NEG)
                raised = jnp.exp(scores - jnp.max(scores, axis=-1, keepdims=True))
                prob = raised * (1.0 / jnp.sum(raised, axis=-1, keepdims=True))
                if second:
                    probs[u, h] = prob
                mixed[at, cols] = dot_nn(prob.astype(BF16), value_of(u, h)).astype(BF16)
            sent[u] = dot_nn(mixed[at, :], w_out[...])
            copies.append(swap(sent.at[u], arrived.at[u], sibling))
        if not second:
            beside_one()
            load_in.wait()
            load_back.wait()
        ff_copies = []
        for u in range(utterances):
            at = rows(u)
            copies[u].wait()
            two = stream_one[at, :] + (sent[u] + arrived[u])
            stream_two[at, :] = two
            hat, _ = normalise(two)
            low = (hat * gain_2 + bias_2).astype(BF16)
            norm_low[at, :] = low
            pre = dot_nn(low, w_in[...])
            phi = 0.5 * (1.0 + lax.erf(pre * math.sqrt(0.5)))
            hidden[at, :] = (pre * phi).astype(BF16)
            if second:
                gelu_slope[at, :] = phi + pre * (
                    jnp.exp(-0.5 * pre * pre) * (1.0 / math.sqrt(2.0 * math.pi))
                )
            sent[utterances + u] = dot_nn(hidden[at, :], w_back[...])
            ff_copies.append(swap(sent.at[utterances + u], arrived.at[utterances + u], sibling))
        if not second:
            beside_two()
        for u in range(utterances):
            at = rows(u)
            ff_copies[u].wait()
            three = stream_two[at, :] + (sent[utterances + u] + arrived[utterances + u])
            stream_three[u] = three
            top[0, at, :] = three.astype(BF16)

    stream_in[...] = acoustic[...].astype(F32)

    def beside_one():
        look_up_block(0)
        look_up_block(1)

    def beside_two():
        for k in range(2, per_core):
            look_up_block(k)
        look_up_rest()

    load_query.wait()
    for u in range(utterances):
        memory_block(u)
    load_memory.wait()
    for copy in load_kv:
        copy.wait()
    kv_rows = 512
    kv_chunks = frames // kv_rows

    def kv_step(i, carry):
        at = pl.ds(pl.multiple_of(i * kv_rows, kv_rows), kv_rows)
        group = jnp.zeros((1, width), jnp.int32) + rate_groups[i // kv_chunks]
        rate_row = jnp.where(group == 1, rate_table[pl.ds(1, 1), :], rate_table[pl.ds(0, 1), :])
        low = (mem_low[at, :].astype(F32) + rate_row).astype(BF16)
        mem_low[at, :] = low
        kv[at, :] = dot_nn(low, w_kv[...]).astype(BF16)
        return carry

    lax.fori_loop(0, utterances * kv_chunks, kv_step, 0)

    pl.semaphore_wait(barrier, n_dp)
    load_out.wait()
    forward(False, beside_one, beside_two)
    table_swap = swap(taken_mine, taken_theirs, sibling)
    load_vocab.wait()
    w_rest[pl.ds(0, vocab_here - main), :] = w_vocab[pl.ds(main, vocab_here - main), :]
    own_local = local_targets(own_target)
    mine = vocab_stats(own_local)
    stats[0] = side_by_side(mine)
    first_swap = swap(stats.at[0], stats_arrived.at[0], sibling)
    table_swap.wait()
    first_swap.wait()
    log_total, picked = join(mine, [stats_arrived[0, :, i : i + 1] for i in range(3)])
    first_loss = (log_total - picked) * own_valid
    blend = own_columns[:, 2:3] * own_valid / (1.0 + jnp.exp(math.log(V) - first_loss))
    for u in range(utterances):
        at = rows(u)
        wide_acoustic = acoustic[at, :].astype(F32)
        taken = taken_mine[u] + taken_theirs[u]
        stream_in[at, :] = wide_acoustic + blend[u * slots : (u + 1) * slots] * (taken - wide_acoustic)

    forward(True)
    token_swaps = [
        swap(stream_three.at[core], gathered.at[j - 1, 0], {"dp": mate[j]}) for j in (1, 2)
    ]
    mine = vocab_stats(own_local)
    stats[1] = side_by_side(mine)
    stat_swap = swap(stats.at[1], stats_arrived.at[1], sibling)
    for copy in token_swaps:
        copy.wait()
    part = slots // 2
    relays = [
        swap(gathered.at[0, 0, pl.ds(0, part)], gathered.at[2, 0, pl.ds(0, part)], {"dp": mate[2]}),
        swap(gathered.at[1, 0, pl.ds(part, part)], gathered.at[2, 0, pl.ds(part, part)], {"dp": mate[1]}),
    ]
    share_swaps = [swap(gathered.at[j, 0], gathered.at[j, 1], sibling) for j in range(2)]
    stat_swap.wait()
    log_column, picked = join(mine, [stats_arrived[1, :, i : i + 1] for i in range(3)])

    def slope(j, carry):
        col = pl.multiple_of(j * 128, 128)
        ids = col + lax.broadcasted_iota(jnp.int32, (1, 128), 1)
        onehot = jnp.where(ids == own_local, 1.0, 0.0)
        grad = (jnp.exp(logits[j] - log_column) - onehot) * own_valid
        grad_logits[:, pl.ds(col, 128)] = grad.astype(BF16)
        return carry

    lax.fori_loop(0, main // 128 + 1, slope, 0, unroll=3)
    three_copies = []
    for u in range(utterances):
        sent[u] = dot_nn(grad_logits[rows(u), pl.ds(0, main)], w_vocab[pl.ds(0, main), :]) + dot_nn(
            grad_logits[rows(u), pl.ds(main, 128)], w_rest[...]
        )
        three_copies.append(swap(sent.at[u], arrived.at[u], sibling))
    meta[0] = to_rows([own_target, own_valid, log_column, (log_column - picked) * own_valid])
    meta_swaps = [swap(meta.at[0], meta.at[j], {"dp": mate[j]}) for j in range(1, 4)]
    for u in range(utterances):
        r.loss_out[pl.ds(u, 1), :] = meta[0, 3:4, u * slots : (u + 1) * slots]

    plan = Planner()
    steps_all = len(bits)
    scatter_send, scatter_recv = r.scatter_send, r.scatter_recv

    def make_chunk(index):
        name, start, cols, order = chunk_list(part_cols, width, bits, low_bits, r)[index]
        source, landing = getattr(r, "src_" + name), r.landing[index]
        if name == "kv":
            out, out_start = (r.key_out, r.value_out)[start // cols], 0
        else:
            out = r.vocab_sum if name == "vocab" and not low_bits else getattr(r, name + "_out")
            out_start = start
        rows_here = source.shape[-2]

        def pick(step, which):
            rest = sorted([b for b in bits if b not in order[:step]], reverse=True)
            where = tuple(which if b == order[step] else slice(None) for b in rest)
            if step == 0:
                return source, where + (slice(None), pl.ds(start, cols))
            return landing[step - 1], where + (slice(None), slice(None))

        def send(step):
            b = order[step]
            ref, where = pick(step, 1 - bit_of[b])
            copy = pltpu.make_async_remote_copy(
                src_ref=ref.at[where],
                dst_ref=landing[step],
                send_sem=scatter_send.at[index, step],
                recv_sem=scatter_recv.at[index, step],
                device_id=peer_of[b],
                device_id_type=MESH,
            )
            copy.start()
            return copy

        def take(step, copy):
            copy.wait_recv()
            ref, where = pick(step, bit_of[order[step]])
            got = landing[step]
            at = pl.ds(out_start, cols)
            if step < len(order) - 1:
                got[...] = got[...] + ref[where]
            elif name == "vocab":
                out[..., at] = got[...] + ref[where]
            else:
                out[:, at] = got[...] + ref[where]

        steps = [
            (link_of(b, bits), rows_here * cols * 4 * 2 ** (steps_all - 1 - s))
            for s, b in enumerate(order)
        ]
        return Chunk(steps, send, take)

    def make_trade(start, cols):
        summed, traded = r.vocab_sum, r.vocab_traded
        at = pl.ds(start, cols)

        def send(step):
            copies = []
            for j in range(1, 4):
                to = lax.rem(mate[j], 4)
                copies.append(
                    pltpu.make_async_remote_copy(
                        src_ref=summed.at[to // 2, lax.rem(to, 2), :, at],
                        dst_ref=traded.at[j - 1, :, at],
                        send_sem=r.trade_send.at[start // 128, j - 1],
                        recv_sem=r.trade_recv.at[start // 128, j - 1],
                        device_id={"dp": mate[j]},
                        device_id_type=MESH,
                    )
                )
                copies[-1].start()
            return Several(copies)

        def take(step, copies):
            copies.wait_recv()
            for j in range(1, 4):
                there = pl.multiple_of(lax.rem(mate[j], 4) * part_cols + start, 128)
                r.vocab_out[:, pl.ds(there, cols)] = traded[j - 1, :, at]
            here = pl.multiple_of(base + start, 128)
            r.vocab_out[:, pl.ds(here, cols)] = summed[quarter // 2, lax.rem(quarter, 2), :, at]

        return Chunk([(0, 2 * r.src_vocab.shape[-2] * cols * 4)], send, take)

    chunks = {}
    for index, (name, start, cols, _) in enumerate(chunk_list(part_cols, width, bits, low_bits, r)):
        chunks[name, start] = make_chunk(index)
        if name == "vocab" and not low_bits:
            chunks[name, start].follow = make_trade(start, cols)

    def put(name, at, product):
        source = getattr(r, "src_" + name)
        source[..., at] = product.reshape(source.shape[:-1] + (product.shape[1],))

    at_core = pl.ds(pl.multiple_of(core * slots, slots), slots)
    at_other = pl.ds(pl.multiple_of((1 - core) * slots, slots), slots)
    base = pl.multiple_of(quarter * part_cols, part_cols)
    pieces = [(c, 256) for c in range(0, part_cols, 256)]
    for j in range(1, 4):
        if j == 2:
            for copy in relays:
                copy.wait()
            share_swaps.append(swap(gathered.at[2, 0], gathered.at[2, 1], sibling))
        meta_swaps[j - 1].wait()
        columns = to_columns(meta[j])
        target, valid, log_total = local_targets(columns[:, 0:1]), columns[:, 1:2], columns[:, 2:3]
        top[j, at_core, :] = gathered[j - 1, 0].astype(BF16)
        share_swaps[j - 1].wait()
        top[j, at_other, :] = gathered[j - 1, 1].astype(BF16)
        for col, cols in pieces:
            ids = base + col + lax.broadcasted_iota(jnp.int32, (1, cols), 1)
            tile = dot_nt(top[j], w_vocab[pl.ds(base + col, cols), :])
            grad = (jnp.exp(tile - log_total) - jnp.where(ids == target, 1.0, 0.0)) * valid
            grad_others[pl.ds((j - 1) * tokens, tokens), pl.ds(col, cols)] = grad.astype(BF16)
    top_turned = r.top_turned
    for j in range(4):
        top_turned[:, pl.ds(j * tokens, tokens)] = top[j].T
    plan.run_until(9.0)
    put("rest", slice(None), dot_nn(top_turned[:, pl.ds(0, tokens)], grad_logits[:, pl.ds(main, 128)]))
    starts = sorted(start for name, start in chunks if name == "vocab")
    for start, stop in zip(starts, starts[1:] + [part_cols]):
        for col in range(start, stop, 256):
            cols = min(256, stop - col)
            product = dot_nn(top_turned[:, pl.ds(0, tokens)], grad_logits[:, pl.ds(base + col, cols)])
            product = product + dot_nn(
                top_turned[:, pl.ds(tokens, 3 * tokens)], grad_others[:, pl.ds(col, cols)]
            )
            put("vocab", pl.ds(col, cols), product)
        plan.run_until(plan.now + 0.7)
        plan.post(chunks["vocab", start])
    plan.post(chunks["rest", 0])

    copies = []
    for u in range(utterances):
        at = rows(u)
        three_copies[u].wait()
        three = sent[u] + arrived[u]
        grad_three[u] = three
        low = three.astype(BF16)
        branch_low[at, :] = low
        pre = (dot_nt(low, w_back[...]) * gelu_slope[at, :]).astype(BF16)
        grad_pre[at, :] = pre
        sent[utterances + u] = dot_nt(pre, w_in[...])
        copies.append(swap(sent.at[utterances + u], arrived.at[utterances + u], sibling))
    plan.run_until(plan.now + 3.0)
    for name, left, right in (("back", branch_low, hidden), ("in", norm_low, grad_pre)):
        left_turned = left[...].T
        for start in sorted(s for n, s in chunks if n == name):
            at = pl.ds(start, 512)
            put(name, at, dot_nn(left_turned, right[:, at]))
            plan.run_until(plan.now + 0.5)
            plan.post(chunks[name, start])

    one_copies = []
    gain_2_total, bias_2_total = 0.0, 0.0
    for u in range(utterances):
        at = rows(u)
        copies[u].wait()
        grad_norm = sent[utterances + u] + arrived[utterances + u]
        hat, scale = normalise(stream_two[at, :])
        gain_2_total = gain_2_total + jnp.sum(grad_norm * hat, axis=0, keepdims=True)
        bias_2_total = bias_2_total + jnp.sum(grad_norm, axis=0, keepdims=True)
        two = grad_three[u] + normalise_back(grad_norm * gain_2, hat, scale)
        grad_two[at, :] = two
        low = two.astype(BF16)
        att_low[at, :] = low
        grad_mixed = dot_nt(low, w_out[...]).astype(BF16)
        for h in range(heads):
            cols = pl.ds(h * HD, HD)
            grad_head = grad_mixed[:, h * HD : (h + 1) * HD]
            prob = probs[u, h]
            grad_prob = dot_nt(grad_head, value_of(u, h))
            spare[pl.ds(u * frames, frames), pl.ds(half + h * HD, HD)] = dot_tn(
                prob.astype(BF16), grad_head
            ).astype(BF16)
            inner = jnp.sum(prob * grad_prob, axis=-1, keepdims=True)
            grad_score = (prob * (grad_prob - inner)).astype(BF16)
            grad_queries[at, cols] = (dot_nn(grad_score, key_of(u, h)) * score_scale).astype(BF16)
            spare[pl.ds(u * frames, frames), cols] = (
                dot_tn(grad_score, queries[at, cols]) * score_scale
            ).astype(BF16)
            plan.run_until(plan.now + 1.5)
        sent[u] = dot_nt(grad_queries[at, :], w_query[...])
        one_copies.append(swap(sent.at[u], arrived.at[u], sibling))
    every = slice(None)
    put("out", every, dot_tn(att_low[...], mixed[...]))
    plan.post(chunks["out", 0])
    put("query", every, dot_tn(one_low[...], grad_queries[...]))
    plan.post(chunks["query", 0])
    plan.run_until(plan.now + 1.0)

    mem_copies = []
    rate_sums = [0.0, 0.0]
    for u in range(utterances):
        total = jnp.zeros((1, width), F32)
        for i in range(row_chunks):
            at = pl.ds(u * frames + i * step_rows, step_rows)
            part = dot_nt(spare[at, :], w_kv[...])
            for j in range(width // 128):
                side_of, tile = j // (width // 256), j % (width // 256)
                index = ((side_of * utterances + u) * row_chunks + i) * (width // 256) + tile
                logits[index] = part[:, j * 128 : (j + 1) * 128]
            total = total + jnp.sum(part, axis=0, keepdims=True)
        tiles = row_chunks * (width // 256)
        mem_copies.append(
            swap(
                logits.at[pl.ds(((1 - core) * utterances + u) * tiles, tiles)],
                mem_arrived.at[pl.ds(u * tiles, tiles)],
                sibling,
            )
        )
        group = jnp.zeros((1, width), jnp.int32) + rate_groups[u]
        for k in range(2):
            rate_sums[k] = rate_sums[k] + jnp.where((group == 1) == (k == 1), total, 0.0)
        plan.run_until(plan.now + 1.2)
    span = frames // 2
    for k in range(2 * utterances):
        at = pl.ds(k * span, span)
        product = dot_tn(mem_low[at, :], spare[at, :])
        product = product.reshape(r.src_kv.shape)
        r.src_kv[...] = product if k == 0 else r.src_kv[...] + product
    plan.run_until(plan.now + 2.0)
    plan.post(*[chunks["kv", start] for start in sorted(s for n, s in chunks if n == "kv")])

    gain_1_total, bias_1_total = 0.0, 0.0
    for u in range(utterances):
        at = rows(u)
        valid = own_valid[u * slots : (u + 1) * slots]
        one_copies[u].wait()
        one = grad_two[at, :] + (sent[u] + arrived[u])
        grad_two[at, :] = one
        masked = one * valid
        for k in range(kernel_rows.shape[0]):
            shift = 8 + k - kernel_rows.shape[0] // 2
            row = jnp.sum(masked * padded[u, pl.ds(shift, slots), :], axis=0, keepdims=True)
            if u == 0:
                small_sent[0, pl.ds(k, 1), :] = row
            else:
                small_sent[0, pl.ds(k, 1), :] = small_sent[0, pl.ds(k, 1), :] + row
        padded[u, pl.ds(8, slots), :] = masked
        for j in range(width // 128):
            cols = pl.ds(j * 128, 128)
            total = jnp.zeros((slots, 128), F32)
            for k in range(kernel_rows.shape[0]):
                shift = 8 - k + kernel_rows.shape[0] // 2
                total = total + kernel_rows[pl.ds(k, 1), cols] * padded[u, pl.ds(shift, slots), cols]
            stream_one[at, cols] = total * valid
        grad_norm = stream_one[at, :]
        hat, scale = normalise(stream_in[at, :])
        gain_1_total = gain_1_total + jnp.sum(grad_norm * hat, axis=0, keepdims=True)
        bias_1_total = bias_1_total + jnp.sum(grad_norm, axis=0, keepdims=True)
        zero = grad_two[at, :] + normalise_back(grad_norm * gain_1, hat, scale)
        terms[u] = blend[u * slots : (u + 1) * slots] * zero
        stream_one[at, :] = zero - terms[u]
        plan.run_until(plan.now + 1.5)

    last_taps = kernel_rows.shape[0]
    small_sent[0, pl.ds(last_taps, 12 - last_taps), :] = jnp.zeros((12 - last_taps, width), F32)
    for i, row in enumerate((gain_1_total, bias_1_total, gain_2_total, bias_2_total)):
        small_sent[0, pl.ds(12 + i, 1), :] = row
    for k in range(2):
        small_sent[0, pl.ds(16 + k, 1), :] = rate_sums[k]
    small_sent[0, pl.ds(18, 6), :] = jnp.zeros((6, width), F32)
    small_peers = [peer_of[b] for b in low_bits + bits] + [sibling]

    def small_send(step):
        copy = pltpu.make_async_remote_copy(
            src_ref=small_sent.at[step],
            dst_ref=small_arrived.at[step],
            send_sem=r.small_send.at[step],
            recv_sem=r.small_recv.at[step],
            device_id=small_peers[step],
            device_id_type=MESH,
        )
        copy.start()
        return copy

    def small_take(step, copy):
        copy.wait_recv()
        if step + 1 < len(small_peers):
            small_sent[step + 1] = small_sent[step] + small_arrived[step]
        else:
            r.small_out[pl.ds(0, 16), :] = small_sent[step, pl.ds(0, 16), :]
            r.small_out[pl.ds(16, 8), :] = (
                small_sent[step, pl.ds(16, 8), :] + small_arrived[step, pl.ds(16, 8), :]
            )

    small_links = [link_of(b, bits) for b in low_bits + bits] + ["core"]
    plan.post(Chunk([(l, 24 * width * 4) for l in small_links], small_send, small_take))

    features = width // n_dp
    feature_rows = max(features, 8)
    block_rows = term_blocks.shape[1]
    turned = terms[core].T
    id_row = targets[pl.ds(core, 1), :].astype(F32)
    rest = block_rows - features - 1
    for p in range(n_dp):
        term_blocks[p, pl.ds(0, features), :] = turned[p * features : (p + 1) * features]
        term_blocks[p, pl.ds(features, 1), :] = id_row
        term_blocks[p, pl.ds(features + 1, rest), :] = jnp.zeros((rest, slots), F32)

    def term_copy(k):
        there = lax.rem(me + k, n_dp)
        return pltpu.make_async_remote_copy(
            src_ref=term_blocks.at[there],
            dst_ref=term_arrived.at[me],
            send_sem=r.term_send.at[k],
            recv_sem=r.term_recv.at[k],
            device_id={"dp": there},
            device_id_type=MESH,
        )

    def term_start(k, carry):
        term_copy(k).start()
        return carry

    def term_wait(k, carry):
        term_copy(k).wait()
        return carry

    term_arrived[me] = term_blocks[me]
    lax.fori_loop(1, n_dp, term_start, 0)
    stores = []

    def store(source, target):
        copy = pltpu.make_async_copy(source, target, r.store_sem.at[len(stores)])
        copy.start()
        stores.append(copy)

    store(stream_one, r.acoustic_out)
    for u in range(utterances):
        mem_copies[u].wait()
        for i in range(row_chunks):
            for j in range(width // 256):
                index = (u * row_chunks + i) * (width // 256) + j
                first_tile = (core * utterances) * row_chunks * (width // 256)
                mem_arrived[index] = logits[first_tile + index] + mem_arrived[index]
                at = pl.ds(u * frames + i * step_rows, step_rows)
                store(mem_arrived.at[index], r.memory_out.at[at, pl.ds(j * 128, 128)])
    plan.run_until(plan.now + 8.0)
    lax.fori_loop(1, n_dp, term_wait, 0)
    per_piece = 512 // slots
    blocks_hi = table_out.shape[1] // 256
    batch = 4

    def table_piece(p, fresh):
        found = [term_arrived[p * per_piece + i] for i in range(per_piece)]
        values = jnp.concatenate([f[:feature_rows] for f in found], axis=1)
        ids = jnp.concatenate([f[features : features + 1] for f in found], axis=1).astype(jnp.int32)
        low_ids, high_ids = ids & 255, ids >> 8
        onehot_lo[...] = jnp.where(
            lax.broadcasted_iota(jnp.int32, (256, 512), 0) == low_ids, 1.0, 0.0
        ).astype(BF16)
        coarse = values.astype(BF16).astype(F32)
        both = jnp.concatenate([coarse, values - coarse], axis=0)
        for first_hi in range(0, blocks_hi, batch):
            here = range(first_hi, min(first_hi + batch, blocks_hi))
            masked = jnp.concatenate([jnp.where(high_ids == hi, both, 0.0) for hi in here], axis=0)
            product = dot_nt(masked.astype(BF16), onehot_lo[...])
            for i, hi in enumerate(here):
                top_part = product[2 * i * feature_rows : (2 * i + 1) * feature_rows]
                low_part = product[(2 * i + 1) * feature_rows : (2 * i + 2) * feature_rows]
                at = pl.ds(hi * 256, 256)
                if fresh:
                    table_out[:, at] = top_part + low_part
                else:
                    table_out[:, at] = table_out[:, at] + (top_part + low_part)

    pieces = n_dp // per_piece
    table_piece(0, True)
    if pieces <= 4:
        for p in range(1, pieces):
            plan.run_until(plan.now + 1.5)
            table_piece(p, False)
    else:
        lax.fori_loop(1, pieces, lambda p, c: (table_piece(p, False), c)[1], 0)
    table_swap = swap(table_out, table_theirs, sibling)
    plan.run_until(plan.now + 3.0)
    table_swap.wait()
    whole_table = r.whole_table
    whole_table[...] = (
        table_out[pl.ds(0, whole_table.shape[0]), :] + table_theirs[pl.ds(0, whole_table.shape[0]), :]
    )[:, :table_rows]
    store(whole_table, r.table_out)
    plan.finish()
    if not low_bits:
        rest = vocab_here - main
        r.vocab_out[:, pl.ds(main, rest)] = r.rest_out[...][:, :rest]
    for copy in stores:
        copy.wait()


def link_of(bit, bits):
    if bit == bits[-1]:
        return bits[-2]
    return bit


def chunk_list(part_cols, width, bits, low_bits, sizes):
    turned = [bits[1], bits[0]] + bits[2:]
    listing = []
    for start in range(0, part_cols, 512):
        listing.append(("vocab", start, 512, [b for b in bits if b > 1]))
    listing.append(("rest", 0, 128, bits))
    for name, order in (("back", turned), ("in", bits)):
        for start in range(0, sizes.units, 512):
            if name == "in" and start:
                order = [bits[2], bits[0], bits[1]] + bits[3:]
            listing.append((name, start, 512, order))
    listing.append(("out", 0, sizes.half, turned))
    listing.append(("query", 0, sizes.half, bits))
    for k, start in enumerate(range(0, 2 * sizes.half, 256)):
        listing.append(("kv", start, 256, [bits, turned][k % 2]))
    return listing


def decoder_call(
    acoustic, memory, embedding, w_query, w_key, w_value, w_out, w_in, w_back, w_vocab, norms,
    fsmn_kernel, rate_table, token_lengths, memory_lengths, rate_groups, glance, targets, n_dp,
):
    utterances = token_lengths.shape[0]
    tokens, width = acoustic.shape
    slots = tokens // utterances
    mem_rows = memory.shape[0]
    half = w_query.shape[1]
    heads = half // HD
    frames = mem_rows // utterances
    units = w_in.shape[1]
    vocab_here = w_vocab.shape[1]
    table_rows = embedding.shape[0]
    part_cols = vocab_here // 512 * 128
    all_cols = 4 * part_cols + 128
    w_turned = w_vocab.T
    mains = table_rows // 2048 * 2048
    nbits = n_dp.bit_length() - 1
    steps = nbits
    while width >> steps < 8:
        steps -= 1
    low_bits, bits = list(range(nbits - steps)), list(range(nbits - steps, nbits))
    rows = width >> steps
    features = width // n_dp
    feature_rows = max(features, 8)
    block_rows = feature_rows + 8 if features >= 8 else 8
    blocks_hi = (table_rows + 255) // 256
    sizes = SimpleNamespace(units=units, half=half)
    plane = [b for b in bits if b < 2]
    listing = chunk_list(part_cols, width, bits, low_bits, sizes)
    most = max(len(c[3]) for c in listing)

    f32 = lambda *shape: jax.ShapeDtypeStruct(shape, F32)
    v32 = lambda *shape: pltpu.VMEM(shape, F32)
    v16 = lambda *shape: pltpu.VMEM(shape, BF16)
    dma = lambda *shape: pltpu.SemaphoreType.DMA(shape)
    inputs = dict(
        acoustic=(VMEM, acoustic),
        table_tail=(VMEM, embedding[mains:]),
        memory=(ANY, memory),
        table=(ANY, embedding),
        w_query_hbm=(ANY, w_query),
        w_key_hbm=(ANY, w_key),
        w_value_hbm=(ANY, w_value),
        w_out_hbm=(ANY, w_out),
        w_in_hbm=(ANY, w_in),
        w_back_hbm=(ANY, w_back),
        w_vocab_hbm=(ANY, w_turned),
        gain_one=(VMEM, norms[0][None]),
        bias_one=(VMEM, norms[1][None]),
        gain_two=(VMEM, norms[2][None]),
        bias_two=(VMEM, norms[3][None]),
        kernel_rows=(VMEM, fsmn_kernel),
        rate_table=(VMEM, rate_table),
        token_lengths=(SMEM, token_lengths),
        memory_lengths=(SMEM, memory_lengths),
        rate_groups=(SMEM, rate_groups),
        glance=(VMEM, glance.reshape(utterances, slots)),
        targets=(VMEM, targets.reshape(utterances, slots)),
    )
    outputs = dict(
        loss_out=f32(utterances, slots),
        small_out=f32(24, width),
        vocab_out=f32(2, rows, part_cols) if low_bits else f32(rows, vocab_here),
        rest_out=f32(rows, 128),
        in_out=f32(rows, units),
        back_out=f32(rows, units),
        query_out=f32(rows, half),
        out_out=f32(rows, half),
        key_out=f32(rows, half),
        value_out=f32(rows, half),
        acoustic_out=f32(tokens, width),
        memory_out=f32(mem_rows, width // 2),
        table_out=f32(features, table_rows),
    )
    shape = (2,) * steps + (rows,)
    scratch = dict(
        w_query=v16(width, half),
        w_kv=v16(width, 2 * half),
        w_out=v16(half, width),
        w_in=v16(width, units),
        w_back=v16(units, width),
        w_vocab=v16(vocab_here, width),
        w_rest=v16(128, width),
        mem_low=v16(mem_rows, width),
        kv=v16(mem_rows, 2 * half),
        spare=v16(mem_rows, 2 * half),
        padded=v32(utterances, slots + 16, width),
        stream_in=v32(tokens, width),
        stream_one=v32(tokens, width),
        stream_two=v32(tokens, width),
        stream_three=v32(utterances, slots, width),
        one_low=v16(tokens, width),
        queries=v16(tokens, half),
        probs=v32(utterances, heads, slots, frames),
        mixed=v16(tokens, half),
        norm_low=v16(tokens, width),
        hidden=v16(tokens, units),
        gelu_slope=v32(tokens, units),
        top=v16(4, tokens, width),
        logits=v32(all_cols // 128, tokens, 128),
        grad_logits=v16(tokens, all_cols),
        grad_others=v16(3 * tokens, part_cols),
        top_turned=v16(width, 4 * tokens),
        taken_mine=v32(utterances, slots, width),
        taken_theirs=v32(utterances, slots, width),
        grad_three=v32(utterances, slots, width),
        grad_two=v32(tokens, width),
        branch_low=v16(tokens, width),
        grad_pre=v16(tokens, units),
        att_low=v16(tokens, width),
        grad_queries=v16(tokens, half),
        mem_arrived=v32(mem_rows // 256 * (width // 256), 256, 128),
        meta=v32(4, 8, tokens),
        stats=v32(2, tokens, 128),
        stats_arrived=v32(2, tokens, 128),
        sent=v32(2 * utterances, slots, width),
        arrived=v32(2 * utterances, slots, width),
        gathered=v32(3, 2, slots, width),
        small_sent=v32(nbits + 1, 24, width),
        small_arrived=v32(nbits + 1, 24, width),
        term_blocks=v32(n_dp, block_rows, slots),
        term_arrived=v32(n_dp, block_rows, slots),
        onehot_lo=v16(256, 512),
        table_rest=v16((table_rows - mains + 127) // 128 * 128, width),
        table_theirs=v32(feature_rows, blocks_hi * 256),
        table_mine=v32(feature_rows, blocks_hi * 256),
        src_vocab=v32(*shape, part_cols),
        src_rest=v32(*shape, 128),
        whole_table=v32(features, table_rows),
        src_back=v32(*shape, units),
        vocab_sum=v32(*(2,) * len(plane), rows, part_cols),
        vocab_traded=v32(3, rows, part_cols),
        src_in=v32(*shape, units),
        src_out=v32(*shape, half),
        src_query=v32(*shape, half),
        src_kv=v32(*shape, 2 * half),
        load_sem=dma(24),
        store_sem=dma(24),
        trade_send=dma(part_cols // 128, 3),
        trade_recv=dma(part_cols // 128, 3),
        swap_send=dma(40),
        swap_recv=dma(40),
        scatter_send=dma(len(listing), most),
        scatter_recv=dma(len(listing), most),
        small_send=dma(nbits + 1),
        small_recv=dma(nbits + 1),
        term_send=dma(n_dp),
        term_recv=dma(n_dp),
    )
    landing = [
        [v32(*(2,) * (steps - 1 - s), rows, cols) for s in range(len(order))]
        for _, _, cols, order in listing
    ]
    names = list(inputs) + list(outputs) + list(scratch)
    flat = [ref for chunk in landing for ref in chunk]

    def kernel(*refs):
        named, rest = refs[: len(names)], list(refs[len(names) :])
        lands = [[rest.pop(0) for _ in chunk] for chunk in landing]
        decoder_kernel(
            names + ["landing", "units", "half"], vocab_here, part_cols, table_rows, n_dp, bits,
            low_bits, *named, lands, units, half,
        )

    out = pl.pallas_call(
        kernel,
        out_shape=list(outputs.values()),
        in_specs=[spec for spec, _ in inputs.values()],
        out_specs=[VMEM] * (len(outputs) - 3) + [ANY] * 3,
        scratch_shapes=list(scratch.values()) + flat,
        compiler_params=pltpu.CompilerParams(
            collective_id=1, has_side_effects=True, vmem_limit_bytes=64 << 20
        ),
    )(*[value for _, value in inputs.values()])
    return SimpleNamespace(**dict(zip(outputs, out))), low_bits


def deliver_kernel(n_dp, n_passed, *refs):
    n = n_passed + 2
    sources, targets, held = refs[:n], refs[n : 2 * n + 5], refs[2 * n + 5 : 3 * n + 5]
    sem_in, sem_out = refs[3 * n + 5 :]
    reads, writes = [], []
    pieces = []
    for i in range(n):
        rows = sources[i].shape[0]
        count = 4 if rows >= 1024 else 1
        for k in range(count):
            at = pl.ds(k * (rows // count), rows // count)
            pieces.append((i, at) if count > 1 else (i, None))
    for k, (i, at) in enumerate(pieces):
        source, buffer = (sources[i], held[i]) if at is None else (sources[i].at[at], held[i].at[at])
        reads.append(pltpu.make_async_copy(source, buffer, sem_in.at[k]))
        reads[-1].start()
    for k, (i, at) in enumerate(pieces):
        reads[k].wait()
        if i < n_passed:
            buffer, target = (held[i], targets[i]) if at is None else (held[i].at[at], targets[i].at[at])
            writes.append(pltpu.make_async_copy(buffer, target, sem_out.at[k]))
            writes[-1].start()
    loss, small = held[n_passed:]
    loss_to, gain_one_to, bias_one_to, gain_two_to, bias_two_to, taps_to, rate_to = targets[n_passed:]
    slots = loss.shape[1]
    for u in range(loss.shape[0]):
        loss_to[:, pl.ds(u * slots, slots)] = loss[pl.ds(u, 1), :]
    me = lax.axis_index("dp")
    own = small.shape[1] // n_dp
    mine = jnp.zeros((16, own), F32)
    for p in range(n_dp):
        mine = jnp.where(me == p, small[pl.ds(0, 16), p * own : (p + 1) * own], mine)
    taps_to[...] = mine[: taps_to.shape[0]]
    for i, target in enumerate((gain_one_to, bias_one_to, gain_two_to, bias_two_to)):
        target[...] = mine[12 + i : 13 + i]
    rate_to[...] = small[pl.ds(16, 2), :]
    for copy in writes:
        copy.wait()


def per_device(
    acoustic,
    memory,
    embedding,
    w_query,
    w_key,
    w_value,
    w_out,
    w_in,
    w_back,
    w_vocab,
    gain_one,
    bias_one,
    gain_two,
    bias_two,
    fsmn_kernel,
    rate_table,
    token_lengths,
    memory_lengths,
    rate_groups,
    glance_mask,
    targets,
):
    tok_rows, model_width = acoustic.shape
    half = w_query.shape[1]
    n_dp = lax.axis_size("dp")
    result, low_bits = decoder_call(
        acoustic, memory, embedding, w_query, w_key, w_value, w_out, w_in, w_back, w_vocab,
        (gain_one, bias_one, gain_two, bias_two), fsmn_kernel, rate_table,
        token_lengths, memory_lengths, rate_groups, glance_mask, targets, n_dp,
    )
    vocab = result.vocab_out
    summed = [
        result.query_out, result.key_out, result.value_out, result.out_out, result.in_out,
        result.back_out,
    ]
    if low_bits:
        size = 1 << len(low_bits)
        groups = [list(range(g * size, (g + 1) * size)) for g in range(n_dp // size)]
        planes = [list(range(4 * g, 4 * g + 4)) for g in range(n_dp // 4)]
        vocab = lax.all_to_all(
            vocab.reshape(4, model_width // n_dp, -1), "dp", 0, 0, axis_index_groups=planes, tiled=True
        )
        *summed, rest = [
            lax.psum_scatter(s, "dp", scatter_dimension=0, axis_index_groups=groups, tiled=True)
            for s in (*summed, result.rest_out)
        ]
        vocab = jnp.concatenate([*vocab, rest], axis=1)[:, : w_vocab.shape[1]]
    own = model_width // n_dp
    f32 = lambda *shape: jax.ShapeDtypeStruct(shape, F32)
    like = lambda x: jax.ShapeDtypeStruct(x.shape, F32)
    passed = (result.memory_out, result.table_out, result.acoustic_out, vocab, *summed)
    handed = (*passed, result.loss_out, result.small_out)
    (
        grad_memory, grad_table, grad_acoustic, grad_vocab, grad_query, grad_key, grad_value,
        grad_out, grad_in, grad_back, token_loss, gain_1, bias_1, gain_2, bias_2, grad_taps, grad_rate,
    ) = pl.pallas_call(
        partial(deliver_kernel, n_dp, len(passed)),
        out_shape=[
            *[like(x) for x in passed],
            f32(1, tok_rows),
            *[f32(1, own)] * 4,
            f32(fsmn_kernel.shape[0], own),
            f32(2, model_width),
        ],
        in_specs=[ANY] * len(handed),
        out_specs=[ANY] * len(passed) + [VMEM] * 7,
        scratch_shapes=[pltpu.VMEM(x.shape, F32) for x in handed]
        + [pltpu.SemaphoreType.DMA((len(handed) + 3,)), pltpu.SemaphoreType.DMA((len(handed) + 3,))],
        compiler_params=pltpu.CompilerParams(vmem_limit_bytes=60 << 20),
    )(*handed)
    return (
        token_loss.reshape(tok_rows),
        grad_acoustic,
        grad_memory,
        grad_table.T,
        grad_query,
        grad_key,
        grad_value,
        grad_out.T,
        grad_in,
        grad_back.T,
        grad_vocab,
        gain_1.reshape(own),
        bias_1.reshape(own),
        gain_2.reshape(own),
        bias_2.reshape(own),
        grad_taps,
        grad_rate,
    )


def solution(mesh):
    return jax.shard_map(
        per_device,
        mesh=mesh,
        in_specs=(
            P("dp", None),
            P("dp", None),
            P(),
            P(None, "mp"),
            P(None, "mp"),
            P(None, "mp"),
            P("mp", None),
            P(None, "mp"),
            P("mp", None),
            P(None, "mp"),
            P(),
            P(),
            P(),
            P(),
            P(),
            P(),
            P("dp"),
            P("dp"),
            P("dp"),
            P("dp"),
            P("dp"),
        ),
        out_specs=(
            P("dp"),
            P("dp", None),
            P("dp", "mp"),
            P(None, "dp"),
            P("dp", "mp"),
            P("dp", "mp"),
            P("dp", "mp"),
            P("mp", "dp"),
            P("dp", "mp"),
            P("mp", "dp"),
            P("dp", "mp"),
            P("dp"),
            P("dp"),
            P("dp"),
            P("dp"),
            P(None, "dp"),
            P(),
        ),
        check_vma=False,
    )
```

```python
from functools import partial
import math
from types import SimpleNamespace

import jax
import jax.numpy as jnp
from jax import lax
from jax.experimental import pallas as pl
from jax.experimental.pallas import tpu as pltpu
from jax.sharding import PartitionSpec as P

HD = 128
V = 8404
EPSILON = 1e-05
MESH = pl.DeviceIdType.MESH
VMEM = pl.BlockSpec(memory_space=pltpu.VMEM)
SMEM = pl.BlockSpec(memory_space=pltpu.SMEM)
ANY = pl.BlockSpec(memory_space=pl.ANY)
F32, BF16 = jnp.float32, jnp.bfloat16
NEG = -1e30


def other_core():
    return {"mp": 1 - lax.axis_index("mp")}


def dot_nn(a, b):
    return lax.dot_general(a, b, (((1,), (0,)), ((), ())), preferred_element_type=F32)


def dot_nt(a, b):
    return lax.dot_general(a, b, (((1,), (1,)), ((), ())), preferred_element_type=F32)


def dot_tn(a, b):
    return lax.dot_general(a, b, (((0,), (0,)), ((), ())), preferred_element_type=F32)


def normalise(rows):
    average = jnp.mean(rows, axis=-1, keepdims=True)
    centred = rows - average
    variance = jnp.mean(centred * centred, axis=-1, keepdims=True)
    scale = lax.rsqrt(variance + EPSILON)
    return centred * scale, scale


def normalise_back(grad_hat, hat, scale):
    first = jnp.mean(grad_hat, axis=-1, keepdims=True)
    second = jnp.mean(grad_hat * hat, axis=-1, keepdims=True)
    return scale * (grad_hat - first - hat * second)


def side_by_side(columns):
    lane = lax.broadcasted_iota(jnp.int32, (columns[0].shape[0], 128), 1)
    tile = jnp.zeros(lane.shape, F32)
    for i, column in enumerate(columns):
        tile = jnp.where(lane == i, column, tile)
    return tile


def to_rows(columns):
    return side_by_side(columns).T[:8]


def to_columns(rows):
    return jnp.concatenate([rows] * 16, axis=0).T


class Planner:
    RATE = 0.045e6
    HOP = 1.5
    BACKLOG = 3.0

    def __init__(self):
        self.now = 0.0
        self.free = {}
        self.flying = []
        self.waiting = []
        self.started = []
        self.count = 0

    def launch(self, item, step):
        link, size = item.steps[step]
        begin = max(self.now, self.free.get(link, 0.0))
        self.free[link] = begin + size / self.RATE
        copy = item.send(step)
        self.started.append(copy)
        self.count += 1
        self.flying.append((self.free[link] + self.HOP, self.count, item, step, copy))

    def release(self):
        kept = []
        for item in self.waiting:
            link = item.steps[0][0]
            if self.free.get(link, 0.0) - self.now < self.BACKLOG:
                self.launch(item, 0)
            else:
                kept.append(item)
        self.waiting = kept

    def post(self, *items):
        self.waiting += items
        self.release()

    def run_until(self, time):
        while self.flying or self.waiting:
            if not self.flying:
                self.now = max(self.now, min(self.free[i.steps[0][0]] for i in self.waiting))
                self.release()
                continue
            first = min(self.flying, key=lambda f: f[:2])
            if first[0] > time:
                break
            self.flying.remove(first)
            self.now = max(self.now, first[0])
            _, _, item, step, copy = first
            item.take(step, copy)
            if step + 1 < len(item.steps):
                self.launch(item, step + 1)
            elif item.follow is not None:
                self.launch(item.follow, 0)
            self.release()
        if time != math.inf:
            self.now = max(self.now, time)
        self.release()

    def finish(self):
        self.run_until(math.inf)
        for copy in self.started:
            copy.wait_send()


class Chunk:
    def __init__(self, steps, send, take):
        self.steps, self.send, self.take, self.follow = steps, send, take, None


class Several:
    def __init__(self, copies):
        self.copies = copies

    def wait_recv(self):
        for copy in self.copies:
            copy.wait_recv()

    def wait_send(self):
        for copy in self.copies:
            copy.wait_send()


def decoder_kernel(
    names,
    vocab_here,
    part_cols,
    table_rows,
    n_dp,
    bits,
    low_bits,
    *refs,
):
    r = SimpleNamespace(**dict(zip(names, refs)))
    acoustic, memory, table = r.acoustic, r.memory, r.table
    targets, glance = r.targets, r.glance
    gain_1, bias_1 = r.gain_one[...], r.bias_one[...]
    gain_2, bias_2 = r.gain_two[...], r.bias_two[...]
    kernel_rows, rate_table = r.kernel_rows, r.rate_table
    token_lengths, memory_lengths, rate_groups = r.token_lengths, r.memory_lengths, r.rate_groups
    w_query, w_kv, w_out, w_in, w_back, w_vocab = r.w_query, r.w_kv, r.w_out, r.w_in, r.w_back, r.w_vocab
    mem_low, kv, padded, spare = r.mem_low, r.kv, r.padded, r.spare
    stream_in, stream_one, stream_two, stream_three = r.stream_in, r.stream_one, r.stream_two, r.stream_three
    one_low, queries, probs, mixed = r.one_low, r.queries, r.probs, r.mixed
    norm_low, hidden, gelu_slope, top = r.norm_low, r.hidden, r.gelu_slope, r.top
    logits, grad_logits, grad_others = r.logits, r.grad_logits, r.grad_others
    taken_mine, taken_theirs = r.taken_mine, r.taken_theirs
    grad_three, grad_two, branch_low = r.grad_three, r.grad_two, r.branch_low
    grad_pre, att_low, grad_queries = r.grad_pre, r.att_low, r.grad_queries
    mem_arrived, meta, stats, stats_arrived = r.mem_arrived, r.meta, r.stats, r.stats_arrived
    sent, arrived, gathered = r.sent, r.arrived, r.gathered
    small_sent, small_arrived = r.small_sent, r.small_arrived
    terms, term_blocks, term_arrived = grad_three, r.term_blocks, r.term_arrived
    onehot_lo, table_theirs, table_out = r.onehot_lo, r.table_theirs, r.table_mine
    swap_send, swap_recv, load_sem = r.swap_send, r.swap_recv, r.load_sem

    utterances, slots = targets.shape
    width = acoustic.shape[1]
    frames = memory.shape[0] // utterances
    half = w_query.shape[1]
    heads = half // HD
    tokens = utterances * slots
    me, core = lax.axis_index("dp"), lax.axis_index("mp")
    sibling = {"mp": 1 - core}
    quarter = lax.rem(me, 4)
    flips = [1 - 2 * lax.rem(me, 2), 2 - 4 * lax.rem(me // 2, 2)]
    mate = [me + flips[0] * (j % 2) + flips[1] * (j // 2) for j in range(4)]
    bit_of = {b: lax.rem(me // (1 << b), 2) for b in low_bits + bits}
    peer_of = {b: {"dp": me + (1 - 2 * bit_of[b]) * (1 << b)} for b in low_bits + bits}
    score_scale = 1.0 / math.sqrt(HD)

    loads = []

    def load(source, target):
        copy = pltpu.make_async_copy(source, target, load_sem.at[len(loads)])
        copy.start()
        loads.append(copy)
        return copy

    load_memory = load(memory, mem_low)
    load_kv = [
        load(r.w_key_hbm, w_kv.at[:, pl.ds(0, half)]),
        load(r.w_value_hbm, w_kv.at[:, pl.ds(half, half)]),
    ]
    load_query = load(r.w_query_hbm, w_query)
    load_out = load(r.w_out_hbm, w_out)

    barrier = pltpu.get_barrier_semaphore()

    def greet(k, carry):
        pl.semaphore_signal(
            barrier, inc=1, device_id={"dp": lax.rem(me + k, n_dp)}, device_id_type=MESH
        )
        return carry

    lax.fori_loop(1, n_dp, greet, 0)
    pl.semaphore_signal(barrier, inc=1, device_id=sibling, device_id_type=MESH)

    load_in = load(r.w_in_hbm, w_in)
    load_back = load(r.w_back_hbm, w_back)
    block = 1024
    per_core = table_rows // (2 * block)
    mains = 2 * per_core * block

    def load_table(k):
        at = pl.ds(pl.multiple_of((core * per_core + k) * block, block), block)
        return load(table.at[at, :], spare.at[pl.ds(k % 2 * block, block), :])

    table_loads = [load_table(0), load_table(1)]
    main = 4 * part_cols
    load_vocab = load(r.w_vocab_hbm, w_vocab)
    w_rest = r.w_rest
    w_rest[...] = jnp.zeros(w_rest.shape, BF16)
    r.table_rest[...] = jnp.zeros(r.table_rest.shape, BF16)
    r.table_rest[pl.ds(0, table_rows - mains), :] = r.table_tail[...]

    swaps = []

    def swap(source, target, device):
        k = len(swaps)
        copy = pltpu.make_async_remote_copy(
            src_ref=source,
            dst_ref=target,
            send_sem=swap_send.at[k],
            recv_sem=swap_recv.at[k],
            device_id=device,
            device_id_type=MESH,
        )
        copy.start()
        swaps.append(copy)
        return copy

    lane = lax.broadcasted_iota(jnp.int32, (1, slots), 1)
    row_of = lax.broadcasted_iota(jnp.int32, (8, slots), 0)
    for u in range(utterances):
        target_row = targets[pl.ds(u, 1), :].astype(F32)
        glance_row = glance[pl.ds(u, 1), :].astype(F32)
        valid_row = (lane < token_lengths[u]).astype(F32)
        meta[0, :, pl.ds(u * slots, slots)] = jnp.where(
            row_of == 0, target_row, jnp.where(row_of == 1, valid_row, glance_row)
        )
    own_columns = to_columns(meta[0])
    own_target = own_columns[:, 0:1]
    own_valid = own_columns[:, 1:2]

    def rows(u):
        return pl.ds(u * slots, slots)

    edge = jnp.zeros((8, width), F32)
    for u in range(utterances):
        padded[u, pl.ds(0, 8), :] = edge
        padded[u, pl.ds(8 + slots, 8), :] = edge

    step_rows = 256
    row_chunks = frames // step_rows

    def key_of(u, h):
        return kv[pl.ds(u * frames, frames), pl.ds(h * HD, HD)]

    def value_of(u, h):
        return kv[pl.ds(u * frames, frames), pl.ds(half + h * HD, HD)]

    frame_lane = lax.broadcasted_iota(jnp.int32, (1, frames), 1)

    def look_up(first_row, count, allowed, source):
        ids = first_row + lax.broadcasted_iota(jnp.int32, (1, count), 1)
        local = jnp.where(allowed, own_target.astype(jnp.int32), -1)
        onehot = jnp.where(ids == local, 1.0, 0.0).astype(BF16)
        return dot_nn(onehot, source)

    def look_up_block(k):
        table_loads[k].wait()
        part = look_up(
            (core * per_core + k) * block, block, True, spare[pl.ds(k % 2 * block, block), :]
        )
        for u in range(utterances):
            piece = part[u * slots : (u + 1) * slots]
            taken_mine[u] = piece if k == 0 else taken_mine[u] + piece
        if k + 2 < per_core:
            table_loads.append(load_table(k + 2))

    def look_up_rest():
        part = look_up(mains, r.table_rest.shape[0], core == 0, r.table_rest[...])
        for u in range(utterances):
            taken_mine[u] = taken_mine[u] + part[u * slots : (u + 1) * slots]

    def local_targets(target_column):
        local = target_column.astype(jnp.int32) - core * vocab_here
        return jnp.where((local >= 0) & (local < vocab_here), local, -1)

    def vocab_stats(target):
        tiles = main // 128
        step_tiles = 4

        ids = main + lax.broadcasted_iota(jnp.int32, (1, 128), 1)
        last = jnp.where(ids < vocab_here, dot_nt(top[0], w_rest[...]), NEG)
        logits[tiles] = last
        top_m, picked = last, jnp.where(ids == target, last, 0.0)
        for j in range(tiles // step_tiles):
            col = j * step_tiles * 128
            product = dot_nt(top[0], w_vocab[pl.ds(col, step_tiles * 128), :])
            for i in range(step_tiles):
                tile = product[:, i * 128 : (i + 1) * 128]
                ids = col + i * 128 + lax.broadcasted_iota(jnp.int32, (1, 128), 1)
                logits[j * step_tiles + i] = tile
                top_m = jnp.maximum(top_m, tile)
                picked = picked + jnp.where(ids == target, tile, 0.0)
        top_row = jnp.max(top_m, axis=1, keepdims=True)

        def add(j, total):
            for i in range(3):
                total = total + jnp.exp(logits[3 * j + i] - top_row)
            return total

        total = lax.fori_loop(0, (tiles + 1) // 3, add, jnp.zeros((tokens, 128), F32))
        return (
            top_row,
            jnp.sum(total, axis=1, keepdims=True),
            jnp.sum(picked, axis=1, keepdims=True),
        )

    def join(mine, theirs):
        top_value = jnp.maximum(mine[0], theirs[0])
        total = mine[1] * jnp.exp(mine[0] - top_value) + theirs[1] * jnp.exp(theirs[0] - top_value)
        return top_value + jnp.log(total), mine[2] + theirs[2]

    def memory_block(u):
        at = rows(u)
        valid = own_valid[u * slots : (u + 1) * slots]
        hat, _ = normalise(stream_in[at, :])
        padded[u, pl.ds(8, slots), :] = (hat * gain_1 + bias_1) * valid
        for j in range(width // 128):
            cols = pl.ds(j * 128, 128)
            total = jnp.zeros((slots, 128), F32)
            for k in range(kernel_rows.shape[0]):
                shift = 8 + k - kernel_rows.shape[0] // 2
                total = total + kernel_rows[pl.ds(k, 1), cols] * padded[u, pl.ds(shift, slots), cols]
            stream_one[at, cols] = stream_in[at, cols] + total * valid
        low = stream_one[at, :].astype(BF16)
        one_low[at, :] = low
        queries[at, :] = dot_nn(low, w_query[...]).astype(BF16)

    def forward(second, beside_one=None, beside_two=None):
        copies = []
        for u in range(utterances):
            at = rows(u)
            if second:
                memory_block(u)
            frame_ok = frame_lane < memory_lengths[u]
            for h in range(heads):
                cols = pl.ds(h * HD, HD)
                scores = dot_nt(queries[at, cols], key_of(u, h)) * score_scale
                scores = jnp.where(frame_ok, scores, NEG)
                raised = jnp.exp(scores - jnp.max(scores, axis=-1, keepdims=True))
                prob = raised * (1.0 / jnp.sum(raised, axis=-1, keepdims=True))
                if second:
                    probs[u, h] = prob
                mixed[at, cols] = dot_nn(prob.astype(BF16), value_of(u, h)).astype(BF16)
            sent[u] = dot_nn(mixed[at, :], w_out[...])
            copies.append(swap(sent.at[u], arrived.at[u], sibling))
        if not second:
            beside_one()
            load_in.wait()
            load_back.wait()
        ff_copies = []
        for u in range(utterances):
            at = rows(u)
            copies[u].wait()
            two = stream_one[at, :] + (sent[u] + arrived[u])
            stream_two[at, :] = two
            hat, _ = normalise(two)
            low = (hat * gain_2 + bias_2).astype(BF16)
            norm_low[at, :] = low
            pre = dot_nn(low, w_in[...])
            phi = 0.5 * (1.0 + lax.erf(pre * math.sqrt(0.5)))
            hidden[at, :] = (pre * phi).astype(BF16)
            if second:
                gelu_slope[at, :] = phi + pre * (
                    jnp.exp(-0.5 * pre * pre) * (1.0 / math.sqrt(2.0 * math.pi))
                )
            sent[utterances + u] = dot_nn(hidden[at, :], w_back[...])
            ff_copies.append(swap(sent.at[utterances + u], arrived.at[utterances + u], sibling))
        if not second:
            beside_two()
        for u in range(utterances):
            at = rows(u)
            ff_copies[u].wait()
            three = stream_two[at, :] + (sent[utterances + u] + arrived[utterances + u])
            stream_three[u] = three
            top[0, at, :] = three.astype(BF16)

    stream_in[...] = acoustic[...].astype(F32)

    def beside_one():
        look_up_block(0)
        look_up_block(1)

    def beside_two():
        for k in range(2, per_core):
            look_up_block(k)
        look_up_rest()

    load_query.wait()
    for u in range(utterances):
        memory_block(u)
    load_memory.wait()
    for copy in load_kv:
        copy.wait()
    kv_rows = 512
    kv_chunks = frames // kv_rows

    def kv_step(i, carry):
        at = pl.ds(pl.multiple_of(i * kv_rows, kv_rows), kv_rows)
        group = jnp.zeros((1, width), jnp.int32) + rate_groups[i // kv_chunks]
        rate_row = jnp.where(group == 1, rate_table[pl.ds(1, 1), :], rate_table[pl.ds(0, 1), :])
        low = (mem_low[at, :].astype(F32) + rate_row).astype(BF16)
        mem_low[at, :] = low
        kv[at, :] = dot_nn(low, w_kv[...]).astype(BF16)
        return carry

    lax.fori_loop(0, utterances * kv_chunks, kv_step, 0)

    pl.semaphore_wait(barrier, n_dp)
    load_out.wait()
    forward(False, beside_one, beside_two)
    table_swap = swap(taken_mine, taken_theirs, sibling)
    load_vocab.wait()
    w_rest[pl.ds(0, vocab_here - main), :] = w_vocab[pl.ds(main, vocab_here - main), :]
    own_local = local_targets(own_target)
    mine = vocab_stats(own_local)
    stats[0] = side_by_side(mine)
    first_swap = swap(stats.at[0], stats_arrived.at[0], sibling)
    table_swap.wait()
    first_swap.wait()
    log_total, picked = join(mine, [stats_arrived[0, :, i : i + 1] for i in range(3)])
    first_loss = (log_total - picked) * own_valid
    blend = own_columns[:, 2:3] * own_valid / (1.0 + jnp.exp(math.log(V) - first_loss))
    for u in range(utterances):
        at = rows(u)
        wide_acoustic = acoustic[at, :].astype(F32)
        taken = taken_mine[u] + taken_theirs[u]
        stream_in[at, :] = wide_acoustic + blend[u * slots : (u + 1) * slots] * (taken - wide_acoustic)

    forward(True)
    token_swaps = [
        swap(stream_three.at[core], gathered.at[j - 1, 0], {"dp": mate[j]}) for j in (1, 2)
    ]
    mine = vocab_stats(own_local)
    stats[1] = side_by_side(mine)
    stat_swap = swap(stats.at[1], stats_arrived.at[1], sibling)
    stat_swap.wait()
    log_column, picked = join(mine, [stats_arrived[1, :, i : i + 1] for i in range(3)])

    def slope(j, carry):
        col = pl.multiple_of(j * 128, 128)
        ids = col + lax.broadcasted_iota(jnp.int32, (1, 128), 1)
        onehot = jnp.where(ids == own_local, 1.0, 0.0)
        grad = (jnp.exp(logits[j] - log_column) - onehot) * own_valid
        grad_logits[:, pl.ds(col, 128)] = grad.astype(BF16)
        return carry

    lax.fori_loop(0, main // 128 + 1, slope, 0, unroll=3)
    three_copies = []
    for u in range(utterances):
        sent[u] = dot_nn(grad_logits[rows(u), pl.ds(0, main)], w_vocab[pl.ds(0, main), :]) + dot_nn(
            grad_logits[rows(u), pl.ds(main, 128)], w_rest[...]
        )
        three_copies.append(swap(sent.at[u], arrived.at[u], sibling))
    for copy in token_swaps:
        copy.wait()
    part = slots // 2
    relays = [
        swap(gathered.at[0, 0, pl.ds(0, part)], gathered.at[2, 0, pl.ds(0, part)], {"dp": mate[2]}),
        swap(gathered.at[1, 0, pl.ds(part, part)], gathered.at[2, 0, pl.ds(part, part)], {"dp": mate[1]}),
    ]
    share_swaps = [swap(gathered.at[j, 0], gathered.at[j, 1], sibling) for j in range(2)]
    meta[0] = to_rows([own_target, own_valid, log_column, (log_column - picked) * own_valid])
    meta_swaps = [swap(meta.at[0], meta.at[j], {"dp": mate[j]}) for j in range(1, 4)]
    for u in range(utterances):
        r.loss_out[pl.ds(u, 1), :] = meta[0, 3:4, u * slots : (u + 1) * slots]

    plan = Planner()
    steps_all = len(bits)
    scatter_send, scatter_recv = r.scatter_send, r.scatter_recv

    def make_chunk(index):
        name, start, cols, order = chunk_list(part_cols, width, bits, low_bits, r)[index]
        source, landing = getattr(r, "src_" + name), r.landing[index]
        if name == "kv":
            out, out_start = (r.key_out, r.value_out)[start // cols], 0
        else:
            out = r.vocab_sum if name == "vocab" and not low_bits else getattr(r, name + "_out")
            out_start = start
        rows_here = source.shape[-2]

        def pick(step, which):
            rest = sorted([b for b in bits if b not in order[:step]], reverse=True)
            where = tuple(which if b == order[step] else slice(None) for b in rest)
            if step == 0:
                return source, where + (slice(None), pl.ds(start, cols))
            return landing[step - 1], where + (slice(None), slice(None))

        def send(step):
            b = order[step]
            ref, where = pick(step, 1 - bit_of[b])
            copy = pltpu.make_async_remote_copy(
                src_ref=ref.at[where],
                dst_ref=landing[step],
                send_sem=scatter_send.at[index, step],
                recv_sem=scatter_recv.at[index, step],
                device_id=peer_of[b],
                device_id_type=MESH,
            )
            copy.start()
            return copy

        def take(step, copy):
            copy.wait_recv()
            ref, where = pick(step, bit_of[order[step]])
            got = landing[step]
            at = pl.ds(out_start, cols)
            if step < len(order) - 1:
                got[...] = got[...] + ref[where]
            elif name == "vocab":
                out[..., at] = got[...] + ref[where]
            else:
                out[:, at] = got[...] + ref[where]

        steps = [
            (link_of(b, bits), rows_here * cols * 4 * 2 ** (steps_all - 1 - s))
            for s, b in enumerate(order)
        ]
        return Chunk(steps, send, take)

    def make_trade(start, cols):
        summed, traded = r.vocab_sum, r.vocab_traded
        at = pl.ds(start, cols)

        def send(step):
            copies = []
            for j in range(1, 4):
                to = lax.rem(mate[j], 4)
                copies.append(
                    pltpu.make_async_remote_copy(
                        src_ref=summed.at[to // 2, lax.rem(to, 2), :, at],
                        dst_ref=traded.at[j - 1, :, at],
                        send_sem=r.trade_send.at[start // 128, j - 1],
                        recv_sem=r.trade_recv.at[start // 128, j - 1],
                        device_id={"dp": mate[j]},
                        device_id_type=MESH,
                    )
                )
                copies[-1].start()
            return Several(copies)

        def take(step, copies):
            copies.wait_recv()
            for j in range(1, 4):
                there = pl.multiple_of(lax.rem(mate[j], 4) * part_cols + start, 128)
                r.vocab_out[:, pl.ds(there, cols)] = traded[j - 1, :, at]
            here = pl.multiple_of(base + start, 128)
            r.vocab_out[:, pl.ds(here, cols)] = summed[quarter // 2, lax.rem(quarter, 2), :, at]

        return Chunk([(0, 2 * r.src_vocab.shape[-2] * cols * 4)], send, take)

    chunks = {}
    for index, (name, start, cols, _) in enumerate(chunk_list(part_cols, width, bits, low_bits, r)):
        chunks[name, start] = make_chunk(index)
        if name == "vocab" and not low_bits:
            chunks[name, start].follow = make_trade(start, cols)

    def put(name, at, product):
        source = getattr(r, "src_" + name)
        source[..., at] = product.reshape(source.shape[:-1] + (product.shape[1],))

    copies = []
    for u in range(utterances):
        at = rows(u)
        three_copies[u].wait()
        three = sent[u] + arrived[u]
        grad_three[u] = three
        low = three.astype(BF16)
        branch_low[at, :] = low
        pre = (dot_nt(low, w_back[...]) * gelu_slope[at, :]).astype(BF16)
        grad_pre[at, :] = pre
        sent[utterances + u] = dot_nt(pre, w_in[...])
        copies.append(swap(sent.at[utterances + u], arrived.at[utterances + u], sibling))
    plan.run_until(plan.now + 8.0)
    for name, left, right in (("back", branch_low, hidden), ("in", norm_low, grad_pre)):
        left_turned = left[...].T
        for start in sorted(s for n, s in chunks if n == name):
            at = pl.ds(start, 512)
            put(name, at, dot_nn(left_turned, right[:, at]))
            plan.run_until(plan.now + 0.5)
            plan.post(chunks[name, start])

    at_core = pl.ds(pl.multiple_of(core * slots, slots), slots)
    at_other = pl.ds(pl.multiple_of((1 - core) * slots, slots), slots)
    base = pl.multiple_of(quarter * part_cols, part_cols)
    pieces = [(c, 256) for c in range(0, part_cols, 256)]
    for j in range(1, 4):
        if j == 2:
            for copy in relays:
                copy.wait()
            share_swaps.append(swap(gathered.at[2, 0], gathered.at[2, 1], sibling))
        meta_swaps[j - 1].wait()
        columns = to_columns(meta[j])
        target, valid, log_total = local_targets(columns[:, 0:1]), columns[:, 1:2], columns[:, 2:3]
        top[j, at_core, :] = gathered[j - 1, 0].astype(BF16)
        share_swaps[j - 1].wait()
        top[j, at_other, :] = gathered[j - 1, 1].astype(BF16)
        for col, cols in pieces:
            ids = base + col + lax.broadcasted_iota(jnp.int32, (1, cols), 1)
            tile = dot_nt(top[j], w_vocab[pl.ds(base + col, cols), :])
            grad = (jnp.exp(tile - log_total) - jnp.where(ids == target, 1.0, 0.0)) * valid
            grad_others[pl.ds((j - 1) * tokens, tokens), pl.ds(col, cols)] = grad.astype(BF16)
    top_turned = r.top_turned
    for j in range(4):
        top_turned[:, pl.ds(j * tokens, tokens)] = top[j].T
    plan.run_until(plan.now + 4.0)
    put("rest", slice(None), dot_nn(top_turned[:, pl.ds(0, tokens)], grad_logits[:, pl.ds(main, 128)]))
    starts = sorted(start for name, start in chunks if name == "vocab")
    for start, stop in zip(starts, starts[1:] + [part_cols]):
        for col in range(start, stop, 256):
            cols = min(256, stop - col)
            product = dot_nn(top_turned[:, pl.ds(0, tokens)], grad_logits[:, pl.ds(base + col, cols)])
            product = product + dot_nn(
                top_turned[:, pl.ds(tokens, 3 * tokens)], grad_others[:, pl.ds(col, cols)]
            )
            put("vocab", pl.ds(col, cols), product)
        plan.run_until(plan.now + 0.7)
        plan.post(chunks["vocab", start])
    plan.post(chunks["rest", 0])

    one_copies = []
    gain_2_total, bias_2_total = 0.0, 0.0
    for u in range(utterances):
        at = rows(u)
        copies[u].wait()
        grad_norm = sent[utterances + u] + arrived[utterances + u]
        hat, scale = normalise(stream_two[at, :])
        gain_2_total = gain_2_total + jnp.sum(grad_norm * hat, axis=0, keepdims=True)
        bias_2_total = bias_2_total + jnp.sum(grad_norm, axis=0, keepdims=True)
        two = grad_three[u] + normalise_back(grad_norm * gain_2, hat, scale)
        grad_two[at, :] = two
        low = two.astype(BF16)
        att_low[at, :] = low
        grad_mixed = dot_nt(low, w_out[...]).astype(BF16)
        for h in range(heads):
            cols = pl.ds(h * HD, HD)
            grad_head = grad_mixed[:, h * HD : (h + 1) * HD]
            prob = probs[u, h]
            grad_prob = dot_nt(grad_head, value_of(u, h))
            spare[pl.ds(u * frames, frames), pl.ds(half + h * HD, HD)] = dot_tn(
                prob.astype(BF16), grad_head
            ).astype(BF16)
            inner = jnp.sum(prob * grad_prob, axis=-1, keepdims=True)
            grad_score = (prob * (grad_prob - inner)).astype(BF16)
            grad_queries[at, cols] = (dot_nn(grad_score, key_of(u, h)) * score_scale).astype(BF16)
            spare[pl.ds(u * frames, frames), cols] = (
                dot_tn(grad_score, queries[at, cols]) * score_scale
            ).astype(BF16)
            plan.run_until(plan.now + 1.5)
        sent[u] = dot_nt(grad_queries[at, :], w_query[...])
        one_copies.append(swap(sent.at[u], arrived.at[u], sibling))
    every = slice(None)
    put("out", every, dot_tn(att_low[...], mixed[...]))
    plan.post(chunks["out", 0])
    put("query", every, dot_tn(one_low[...], grad_queries[...]))
    plan.post(chunks["query", 0])
    plan.run_until(plan.now + 1.0)

    mem_copies = []
    rate_sums = [0.0, 0.0]
    for u in range(utterances):
        total = jnp.zeros((1, width), F32)
        for i in range(row_chunks):
            at = pl.ds(u * frames + i * step_rows, step_rows)
            part = dot_nt(spare[at, :], w_kv[...])
            for j in range(width // 128):
                side_of, tile = j // (width // 256), j % (width // 256)
                index = ((side_of * utterances + u) * row_chunks + i) * (width // 256) + tile
                logits[index] = part[:, j * 128 : (j + 1) * 128]
            total = total + jnp.sum(part, axis=0, keepdims=True)
        tiles = row_chunks * (width // 256)
        mem_copies.append(
            swap(
                logits.at[pl.ds(((1 - core) * utterances + u) * tiles, tiles)],
                mem_arrived.at[pl.ds(u * tiles, tiles)],
                sibling,
            )
        )
        group = jnp.zeros((1, width), jnp.int32) + rate_groups[u]
        for k in range(2):
            rate_sums[k] = rate_sums[k] + jnp.where((group == 1) == (k == 1), total, 0.0)
        plan.run_until(plan.now + 1.2)
    span = frames // 2
    for k in range(2 * utterances):
        at = pl.ds(k * span, span)
        product = dot_tn(mem_low[at, :], spare[at, :])
        product = product.reshape(r.src_kv.shape)
        r.src_kv[...] = product if k == 0 else r.src_kv[...] + product
    plan.run_until(plan.now + 2.0)
    plan.post(*[chunks["kv", start] for start in sorted(s for n, s in chunks if n == "kv")])

    gain_1_total, bias_1_total = 0.0, 0.0
    for u in range(utterances):
        at = rows(u)
        valid = own_valid[u * slots : (u + 1) * slots]
        one_copies[u].wait()
        one = grad_two[at, :] + (sent[u] + arrived[u])
        grad_two[at, :] = one
        masked = one * valid
        for k in range(kernel_rows.shape[0]):
            shift = 8 + k - kernel_rows.shape[0] // 2
            row = jnp.sum(masked * padded[u, pl.ds(shift, slots), :], axis=0, keepdims=True)
            if u == 0:
                small_sent[0, pl.ds(k, 1), :] = row
            else:
                small_sent[0, pl.ds(k, 1), :] = small_sent[0, pl.ds(k, 1), :] + row
        padded[u, pl.ds(8, slots), :] = masked
        for j in range(width // 128):
            cols = pl.ds(j * 128, 128)
            total = jnp.zeros((slots, 128), F32)
            for k in range(kernel_rows.shape[0]):
                shift = 8 - k + kernel_rows.shape[0] // 2
                total = total + kernel_rows[pl.ds(k, 1), cols] * padded[u, pl.ds(shift, slots), cols]
            stream_one[at, cols] = total * valid
        grad_norm = stream_one[at, :]
        hat, scale = normalise(stream_in[at, :])
        gain_1_total = gain_1_total + jnp.sum(grad_norm * hat, axis=0, keepdims=True)
        bias_1_total = bias_1_total + jnp.sum(grad_norm, axis=0, keepdims=True)
        zero = grad_two[at, :] + normalise_back(grad_norm * gain_1, hat, scale)
        terms[u] = blend[u * slots : (u + 1) * slots] * zero
        stream_one[at, :] = zero - terms[u]
        plan.run_until(plan.now + 1.5)

    last_taps = kernel_rows.shape[0]
    small_sent[0, pl.ds(last_taps, 12 - last_taps), :] = jnp.zeros((12 - last_taps, width), F32)
    for i, row in enumerate((gain_1_total, bias_1_total, gain_2_total, bias_2_total)):
        small_sent[0, pl.ds(12 + i, 1), :] = row
    for k in range(2):
        small_sent[0, pl.ds(16 + k, 1), :] = rate_sums[k]
    small_sent[0, pl.ds(18, 6), :] = jnp.zeros((6, width), F32)
    small_peers = [peer_of[b] for b in low_bits + bits] + [sibling]

    def small_send(step):
        copy = pltpu.make_async_remote_copy(
            src_ref=small_sent.at[step],
            dst_ref=small_arrived.at[step],
            send_sem=r.small_send.at[step],
            recv_sem=r.small_recv.at[step],
            device_id=small_peers[step],
            device_id_type=MESH,
        )
        copy.start()
        return copy

    def small_take(step, copy):
        copy.wait_recv()
        if step + 1 < len(small_peers):
            small_sent[step + 1] = small_sent[step] + small_arrived[step]
        else:
            r.small_out[pl.ds(0, 16), :] = small_sent[step, pl.ds(0, 16), :]
            r.small_out[pl.ds(16, 8), :] = (
                small_sent[step, pl.ds(16, 8), :] + small_arrived[step, pl.ds(16, 8), :]
            )

    small_links = [link_of(b, bits) for b in low_bits + bits] + ["core"]
    plan.post(Chunk([(l, 24 * width * 4) for l in small_links], small_send, small_take))

    features = width // n_dp
    feature_rows = max(features, 8)
    block_rows = term_blocks.shape[1]
    turned = terms[core].T
    id_row = targets[pl.ds(core, 1), :].astype(F32)
    rest = block_rows - features - 1
    for p in range(n_dp):
        term_blocks[p, pl.ds(0, features), :] = turned[p * features : (p + 1) * features]
        term_blocks[p, pl.ds(features, 1), :] = id_row
        term_blocks[p, pl.ds(features + 1, rest), :] = jnp.zeros((rest, slots), F32)

    def term_copy(k):
        there = lax.rem(me + k, n_dp)
        return pltpu.make_async_remote_copy(
            src_ref=term_blocks.at[there],
            dst_ref=term_arrived.at[me],
            send_sem=r.term_send.at[k],
            recv_sem=r.term_recv.at[k],
            device_id={"dp": there},
            device_id_type=MESH,
        )

    def term_start(k, carry):
        term_copy(k).start()
        return carry

    def term_wait(k, carry):
        term_copy(k).wait()
        return carry

    term_arrived[me] = term_blocks[me]
    lax.fori_loop(1, n_dp, term_start, 0)
    stores = []

    def store(source, target):
        copy = pltpu.make_async_copy(source, target, r.store_sem.at[len(stores)])
        copy.start()
        stores.append(copy)

    store(stream_one, r.acoustic_out)
    for u in range(utterances):
        mem_copies[u].wait()
        for i in range(row_chunks):
            for j in range(width // 256):
                index = (u * row_chunks + i) * (width // 256) + j
                first_tile = (core * utterances) * row_chunks * (width // 256)
                mem_arrived[index] = logits[first_tile + index] + mem_arrived[index]
                at = pl.ds(u * frames + i * step_rows, step_rows)
                store(mem_arrived.at[index], r.memory_out.at[at, pl.ds(j * 128, 128)])
    plan.run_until(plan.now + 8.0)
    lax.fori_loop(1, n_dp, term_wait, 0)
    per_piece = 512 // slots
    blocks_hi = table_out.shape[1] // 256
    batch = 4

    def table_piece(p, fresh):
        found = [term_arrived[p * per_piece + i] for i in range(per_piece)]
        values = jnp.concatenate([f[:feature_rows] for f in found], axis=1)
        ids = jnp.concatenate([f[features : features + 1] for f in found], axis=1).astype(jnp.int32)
        low_ids, high_ids = ids & 255, ids >> 8
        onehot_lo[...] = jnp.where(
            lax.broadcasted_iota(jnp.int32, (256, 512), 0) == low_ids, 1.0, 0.0
        ).astype(BF16)
        coarse = values.astype(BF16).astype(F32)
        both = jnp.concatenate([coarse, values - coarse], axis=0)
        for first_hi in range(0, blocks_hi, batch):
            here = range(first_hi, min(first_hi + batch, blocks_hi))
            masked = jnp.concatenate([jnp.where(high_ids == hi, both, 0.0) for hi in here], axis=0)
            product = dot_nt(masked.astype(BF16), onehot_lo[...])
            for i, hi in enumerate(here):
                top_part = product[2 * i * feature_rows : (2 * i + 1) * feature_rows]
                low_part = product[(2 * i + 1) * feature_rows : (2 * i + 2) * feature_rows]
                at = pl.ds(hi * 256, 256)
                if fresh:
                    table_out[:, at] = top_part + low_part
                else:
                    table_out[:, at] = table_out[:, at] + (top_part + low_part)

    pieces = n_dp // per_piece
    table_piece(0, True)
    if pieces <= 4:
        for p in range(1, pieces):
            plan.run_until(plan.now + 1.5)
            table_piece(p, False)
    else:
        lax.fori_loop(1, pieces, lambda p, c: (table_piece(p, False), c)[1], 0)
    table_swap = swap(table_out, table_theirs, sibling)
    plan.run_until(plan.now + 8.0)
    table_swap.wait()
    whole_table = r.whole_table
    whole_table[...] = (
        table_out[pl.ds(0, whole_table.shape[0]), :] + table_theirs[pl.ds(0, whole_table.shape[0]), :]
    )[:, :table_rows]
    store(whole_table, r.table_out)
    plan.finish()
    if not low_bits:
        rest = vocab_here - main
        r.vocab_out[:, pl.ds(main, rest)] = r.rest_out[...][:, :rest]
    for copy in stores:
        copy.wait()


def link_of(bit, bits):
    if bit == bits[-1]:
        return bits[-2]
    return bit


def chunk_list(part_cols, width, bits, low_bits, sizes):
    turned = [bits[1], bits[0]] + bits[2:]
    listing = []
    for start in range(0, part_cols, 512):
        listing.append(("vocab", start, 512, [b for b in bits if b > 1]))
    listing.append(("rest", 0, 128, bits))
    for name, order in (("back", turned), ("in", bits)):
        for start in range(0, sizes.units, 512):
            if name == "in" and start:
                order = [bits[2], bits[0], bits[1]] + bits[3:]
            listing.append((name, start, 512, order))
    listing.append(("out", 0, sizes.half, turned))
    listing.append(("query", 0, sizes.half, bits))
    for k, start in enumerate(range(0, 2 * sizes.half, 256)):
        listing.append(("kv", start, 256, [bits, turned][k % 2]))
    return listing


def decoder_call(
    acoustic, memory, embedding, w_query, w_key, w_value, w_out, w_in, w_back, w_vocab, norms,
    fsmn_kernel, rate_table, token_lengths, memory_lengths, rate_groups, glance, targets, n_dp,
):
    utterances = token_lengths.shape[0]
    tokens, width = acoustic.shape
    slots = tokens // utterances
    mem_rows = memory.shape[0]
    half = w_query.shape[1]
    heads = half // HD
    frames = mem_rows // utterances
    units = w_in.shape[1]
    vocab_here = w_vocab.shape[1]
    table_rows = embedding.shape[0]
    part_cols = vocab_here // 512 * 128
    all_cols = 4 * part_cols + 128
    w_turned = w_vocab.T
    mains = table_rows // 2048 * 2048
    nbits = n_dp.bit_length() - 1
    steps = nbits
    while width >> steps < 8:
        steps -= 1
    low_bits, bits = list(range(nbits - steps)), list(range(nbits - steps, nbits))
    rows = width >> steps
    features = width // n_dp
    feature_rows = max(features, 8)
    block_rows = feature_rows + 8 if features >= 8 else 8
    blocks_hi = (table_rows + 255) // 256
    sizes = SimpleNamespace(units=units, half=half)
    plane = [b for b in bits if b < 2]
    listing = chunk_list(part_cols, width, bits, low_bits, sizes)
    most = max(len(c[3]) for c in listing)

    f32 = lambda *shape: jax.ShapeDtypeStruct(shape, F32)
    v32 = lambda *shape: pltpu.VMEM(shape, F32)
    v16 = lambda *shape: pltpu.VMEM(shape, BF16)
    dma = lambda *shape: pltpu.SemaphoreType.DMA(shape)
    inputs = dict(
        acoustic=(VMEM, acoustic),
        table_tail=(VMEM, embedding[mains:]),
        memory=(ANY, memory),
        table=(ANY, embedding),
        w_query_hbm=(ANY, w_query),
        w_key_hbm=(ANY, w_key),
        w_value_hbm=(ANY, w_value),
        w_out_hbm=(ANY, w_out),
        w_in_hbm=(ANY, w_in),
        w_back_hbm=(ANY, w_back),
        w_vocab_hbm=(ANY, w_turned),
        gain_one=(VMEM, norms[0][None]),
        bias_one=(VMEM, norms[1][None]),
        gain_two=(VMEM, norms[2][None]),
        bias_two=(VMEM, norms[3][None]),
        kernel_rows=(VMEM, fsmn_kernel),
        rate_table=(VMEM, rate_table),
        token_lengths=(SMEM, token_lengths),
        memory_lengths=(SMEM, memory_lengths),
        rate_groups=(SMEM, rate_groups),
        glance=(VMEM, glance.reshape(utterances, slots)),
        targets=(VMEM, targets.reshape(utterances, slots)),
    )
    outputs = dict(
        loss_out=f32(utterances, slots),
        small_out=f32(24, width),
        vocab_out=f32(2, rows, part_cols) if low_bits else f32(rows, vocab_here),
        rest_out=f32(rows, 128),
        in_out=f32(rows, units),
        back_out=f32(rows, units),
        query_out=f32(rows, half),
        out_out=f32(rows, half),
        key_out=f32(rows, half),
        value_out=f32(rows, half),
        acoustic_out=f32(tokens, width),
        memory_out=f32(mem_rows, width // 2),
        table_out=f32(features, table_rows),
    )
    shape = (2,) * steps + (rows,)
    scratch = dict(
        w_query=v16(width, half),
        w_kv=v16(width, 2 * half),
        w_out=v16(half, width),
        w_in=v16(width, units),
        w_back=v16(units, width),
        w_vocab=v16(vocab_here, width),
        w_rest=v16(128, width),
        mem_low=v16(mem_rows, width),
        kv=v16(mem_rows, 2 * half),
        spare=v16(mem_rows, 2 * half),
        padded=v32(utterances, slots + 16, width),
        stream_in=v32(tokens, width),
        stream_one=v32(tokens, width),
        stream_two=v32(tokens, width),
        stream_three=v32(utterances, slots, width),
        one_low=v16(tokens, width),
        queries=v16(tokens, half),
        probs=v32(utterances, heads, slots, frames),
        mixed=v16(tokens, half),
        norm_low=v16(tokens, width),
        hidden=v16(tokens, units),
        gelu_slope=v32(tokens, units),
        top=v16(4, tokens, width),
        logits=v32(all_cols // 128, tokens, 128),
        grad_logits=v16(tokens, all_cols),
        grad_others=v16(3 * tokens, part_cols),
        top_turned=v16(width, 4 * tokens),
        taken_mine=v32(utterances, slots, width),
        taken_theirs=v32(utterances, slots, width),
        grad_three=v32(utterances, slots, width),
        grad_two=v32(tokens, width),
        branch_low=v16(tokens, width),
        grad_pre=v16(tokens, units),
        att_low=v16(tokens, width),
        grad_queries=v16(tokens, half),
        mem_arrived=v32(mem_rows // 256 * (width // 256), 256, 128),
        meta=v32(4, 8, tokens),
        stats=v32(2, tokens, 128),
        stats_arrived=v32(2, tokens, 128),
        sent=v32(2 * utterances, slots, width),
        arrived=v32(2 * utterances, slots, width),
        gathered=v32(3, 2, slots, width),
        small_sent=v32(nbits + 1, 24, width),
        small_arrived=v32(nbits + 1, 24, width),
        term_blocks=v32(n_dp, block_rows, slots),
        term_arrived=v32(n_dp, block_rows, slots),
        onehot_lo=v16(256, 512),
        table_rest=v16((table_rows - mains + 127) // 128 * 128, width),
        table_theirs=v32(feature_rows, blocks_hi * 256),
        table_mine=v32(feature_rows, blocks_hi * 256),
        src_vocab=v32(*shape, part_cols),
        src_rest=v32(*shape, 128),
        whole_table=v32(features, table_rows),
        src_back=v32(*shape, units),
        vocab_sum=v32(*(2,) * len(plane), rows, part_cols),
        vocab_traded=v32(3, rows, part_cols),
        src_in=v32(*shape, units),
        src_out=v32(*shape, half),
        src_query=v32(*shape, half),
        src_kv=v32(*shape, 2 * half),
        load_sem=dma(24),
        store_sem=dma(24),
        trade_send=dma(part_cols // 128, 3),
        trade_recv=dma(part_cols // 128, 3),
        swap_send=dma(40),
        swap_recv=dma(40),
        scatter_send=dma(len(listing), most),
        scatter_recv=dma(len(listing), most),
        small_send=dma(nbits + 1),
        small_recv=dma(nbits + 1),
        term_send=dma(n_dp),
        term_recv=dma(n_dp),
    )
    landing = [
        [v32(*(2,) * (steps - 1 - s), rows, cols) for s in range(len(order))]
        for _, _, cols, order in listing
    ]
    names = list(inputs) + list(outputs) + list(scratch)
    flat = [ref for chunk in landing for ref in chunk]

    def kernel(*refs):
        named, rest = refs[: len(names)], list(refs[len(names) :])
        lands = [[rest.pop(0) for _ in chunk] for chunk in landing]
        decoder_kernel(
            names + ["landing", "units", "half"], vocab_here, part_cols, table_rows, n_dp, bits,
            low_bits, *named, lands, units, half,
        )

    out = pl.pallas_call(
        kernel,
        out_shape=list(outputs.values()),
        in_specs=[spec for spec, _ in inputs.values()],
        out_specs=[VMEM] * (len(outputs) - 3) + [ANY] * 3,
        scratch_shapes=list(scratch.values()) + flat,
        compiler_params=pltpu.CompilerParams(
            collective_id=1, has_side_effects=True, vmem_limit_bytes=64 << 20
        ),
    )(*[value for _, value in inputs.values()])
    return SimpleNamespace(**dict(zip(outputs, out))), low_bits


def deliver_kernel(n_dp, n_passed, *refs):
    n = n_passed + 2
    sources, targets, held = refs[:n], refs[n : 2 * n + 5], refs[2 * n + 5 : 3 * n + 5]
    sem_in, sem_out = refs[3 * n + 5 :]
    reads, writes = [], []
    for i, (source, buffer) in enumerate(zip(sources, held)):
        reads.append(pltpu.make_async_copy(source, buffer, sem_in.at[i]))
        reads[-1].start()
    for i in range(n_passed):
        reads[i].wait()
        writes.append(pltpu.make_async_copy(held[i], targets[i], sem_out.at[i]))
        writes[-1].start()
    reads[n_passed].wait()
    reads[n_passed + 1].wait()
    loss, small = held[n_passed:]
    loss_to, gain_one_to, bias_one_to, gain_two_to, bias_two_to, taps_to, rate_to = targets[n_passed:]
    slots = loss.shape[1]
    for u in range(loss.shape[0]):
        loss_to[:, pl.ds(u * slots, slots)] = loss[pl.ds(u, 1), :]
    me = lax.axis_index("dp")
    own = small.shape[1] // n_dp
    mine = jnp.zeros((16, own), F32)
    for p in range(n_dp):
        mine = jnp.where(me == p, small[pl.ds(0, 16), p * own : (p + 1) * own], mine)
    taps_to[...] = mine[: taps_to.shape[0]]
    for i, target in enumerate((gain_one_to, bias_one_to, gain_two_to, bias_two_to)):
        target[...] = mine[12 + i : 13 + i]
    rate_to[...] = small[pl.ds(16, 2), :]
    for copy in writes:
        copy.wait()


def per_device(
    acoustic,
    memory,
    embedding,
    w_query,
    w_key,
    w_value,
    w_out,
    w_in,
    w_back,
    w_vocab,
    gain_one,
    bias_one,
    gain_two,
    bias_two,
    fsmn_kernel,
    rate_table,
    token_lengths,
    memory_lengths,
    rate_groups,
    glance_mask,
    targets,
):
    tok_rows, model_width = acoustic.shape
    half = w_query.shape[1]
    n_dp = lax.axis_size("dp")
    result, low_bits = decoder_call(
        acoustic, memory, embedding, w_query, w_key, w_value, w_out, w_in, w_back, w_vocab,
        (gain_one, bias_one, gain_two, bias_two), fsmn_kernel, rate_table,
        token_lengths, memory_lengths, rate_groups, glance_mask, targets, n_dp,
    )
    vocab = result.vocab_out
    summed = [
        result.query_out, result.key_out, result.value_out, result.out_out, result.in_out,
        result.back_out,
    ]
    if low_bits:
        size = 1 << len(low_bits)
        groups = [list(range(g * size, (g + 1) * size)) for g in range(n_dp // size)]
        planes = [list(range(4 * g, 4 * g + 4)) for g in range(n_dp // 4)]
        vocab = lax.all_to_all(
            vocab.reshape(4, model_width // n_dp, -1), "dp", 0, 0, axis_index_groups=planes, tiled=True
        )
        *summed, rest = [
            lax.psum_scatter(s, "dp", scatter_dimension=0, axis_index_groups=groups, tiled=True)
            for s in (*summed, result.rest_out)
        ]
        vocab = jnp.concatenate([*vocab, rest], axis=1)[:, : w_vocab.shape[1]]
    own = model_width // n_dp
    f32 = lambda *shape: jax.ShapeDtypeStruct(shape, F32)
    like = lambda x: jax.ShapeDtypeStruct(x.shape, F32)
    passed = (result.memory_out, result.table_out, result.acoustic_out, vocab, *summed)
    handed = (*passed, result.loss_out, result.small_out)
    (
        grad_memory, grad_table, grad_acoustic, grad_vocab, grad_query, grad_key, grad_value,
        grad_out, grad_in, grad_back, token_loss, gain_1, bias_1, gain_2, bias_2, grad_taps, grad_rate,
    ) = pl.pallas_call(
        partial(deliver_kernel, n_dp, len(passed)),
        out_shape=[
            *[like(x) for x in passed],
            f32(1, tok_rows),
            *[f32(1, own)] * 4,
            f32(fsmn_kernel.shape[0], own),
            f32(2, model_width),
        ],
        in_specs=[ANY] * len(handed),
        out_specs=[ANY] * len(passed) + [VMEM] * 7,
        scratch_shapes=[pltpu.VMEM(x.shape, F32) for x in handed]
        + [pltpu.SemaphoreType.DMA((len(handed),)), pltpu.SemaphoreType.DMA((len(handed),))],
        compiler_params=pltpu.CompilerParams(vmem_limit_bytes=60 << 20),
    )(*handed)
    return (
        token_loss.reshape(tok_rows),
        grad_acoustic,
        grad_memory,
        grad_table.T,
        grad_query,
        grad_key,
        grad_value,
        grad_out.T,
        grad_in,
        grad_back.T,
        grad_vocab,
        gain_1.reshape(own),
        bias_1.reshape(own),
        gain_2.reshape(own),
        bias_2.reshape(own),
        grad_taps,
        grad_rate,
    )


def solution(mesh):
    return jax.shard_map(
        per_device,
        mesh=mesh,
        in_specs=(
            P("dp", None),
            P("dp", None),
            P(),
            P(None, "mp"),
            P(None, "mp"),
            P(None, "mp"),
            P("mp", None),
            P(None, "mp"),
            P("mp", None),
            P(None, "mp"),
            P(),
            P(),
            P(),
            P(),
            P(),
            P(),
            P("dp"),
            P("dp"),
            P("dp"),
            P("dp"),
            P("dp"),
        ),
        out_specs=(
            P("dp"),
            P("dp", None),
            P("dp", "mp"),
            P(None, "dp"),
            P("dp", "mp"),
            P("dp", "mp"),
            P("dp", "mp"),
            P("mp", "dp"),
            P("dp", "mp"),
            P("mp", "dp"),
            P("dp", "mp"),
            P("dp"),
            P("dp"),
            P("dp"),
            P("dp"),
            P(None, "dp"),
            P(),
        ),
        check_vma=False,
    )
```

```python
from functools import partial
import math
from types import SimpleNamespace

import jax
import jax.numpy as jnp
from jax import lax
from jax.experimental import pallas as pl
from jax.experimental.pallas import tpu as pltpu
from jax.sharding import PartitionSpec as P

HD = 128
V = 8404
EPSILON = 1e-05
MESH = pl.DeviceIdType.MESH
VMEM = pl.BlockSpec(memory_space=pltpu.VMEM)
SMEM = pl.BlockSpec(memory_space=pltpu.SMEM)
ANY = pl.BlockSpec(memory_space=pl.ANY)
F32, BF16 = jnp.float32, jnp.bfloat16
NEG = -1e30


def other_core():
    return {"mp": 1 - lax.axis_index("mp")}


def dot_nn(a, b):
    return lax.dot_general(a, b, (((1,), (0,)), ((), ())), preferred_element_type=F32)


def dot_nt(a, b):
    return lax.dot_general(a, b, (((1,), (1,)), ((), ())), preferred_element_type=F32)


def dot_tn(a, b):
    return lax.dot_general(a, b, (((0,), (0,)), ((), ())), preferred_element_type=F32)


def normalise(rows):
    average = jnp.mean(rows, axis=-1, keepdims=True)
    centred = rows - average
    variance = jnp.mean(centred * centred, axis=-1, keepdims=True)
    scale = lax.rsqrt(variance + EPSILON)
    return centred * scale, scale


def normalise_back(grad_hat, hat, scale):
    first = jnp.mean(grad_hat, axis=-1, keepdims=True)
    second = jnp.mean(grad_hat * hat, axis=-1, keepdims=True)
    return scale * (grad_hat - first - hat * second)


def side_by_side(columns):
    lane = lax.broadcasted_iota(jnp.int32, (columns[0].shape[0], 128), 1)
    tile = jnp.zeros(lane.shape, F32)
    for i, column in enumerate(columns):
        tile = jnp.where(lane == i, column, tile)
    return tile


def to_rows(columns):
    return side_by_side(columns).T[:8]


def to_columns(rows):
    return jnp.concatenate([rows] * 16, axis=0).T


class Planner:
    RATE = 0.045e6
    HOP = 1.5
    AHEAD = 4.0
    LINK_MOST = 2
    MOST = 6

    def __init__(self):
        self.now = 0.0
        self.free = {}
        self.flying = []
        self.ready = []
        self.started = []
        self.count = 0

    def way_left(self, item, step):
        return sum(size for _, size in item.steps[step:]) / self.RATE + self.HOP * len(item.steps[step:])

    def launch(self, item, step):
        link, size = item.steps[step]
        begin = max(self.now, self.free.get(link, 0.0))
        self.free[link] = begin + size / self.RATE
        copy = item.send(step)
        self.started.append(copy)
        self.count += 1
        self.flying.append((self.free[link] + self.HOP, self.count, item, step, copy, link))

    def pump(self):
        while True:
            live = [f[5] for f in self.flying if f[0] - self.HOP > self.now]
            if len(live) >= self.MOST:
                return
            best = None
            for item, step in self.ready:
                link = item.steps[step][0]
                if live.count(link) >= self.LINK_MOST or self.free.get(link, 0.0) - self.now > self.AHEAD:
                    continue
                key = (live.count(link), -self.way_left(item, step))
                if best is None or key < best[0]:
                    best = (key, item, step)
            if best is None:
                return
            self.ready.remove(best[1:])
            self.launch(*best[1:])

    def post(self, *items):
        self.ready += [(item, 0) for item in items]
        self.pump()

    def run_until(self, time):
        while self.flying or self.ready:
            if not self.flying:
                self.now = max(self.now, min(self.free[i.steps[k][0]] for i, k in self.ready))
                self.pump()
                continue
            first = min(self.flying, key=lambda f: f[:2])
            if first[0] > time:
                break
            self.flying.remove(first)
            self.now = max(self.now, first[0])
            _, _, item, step, copy, _ = first
            item.take(step, copy)
            if step + 1 < len(item.steps):
                self.ready.append((item, step + 1))
            elif item.follow is not None:
                self.ready.append((item.follow, 0))
            self.pump()
        if time != math.inf:
            self.now = max(self.now, time)
        self.pump()

    def finish(self):
        self.run_until(math.inf)
        for copy in self.started:
            copy.wait_send()


class Chunk:
    def __init__(self, steps, send, take):
        self.steps, self.send, self.take, self.follow = steps, send, take, None


class Several:
    def __init__(self, copies):
        self.copies = copies

    def wait_recv(self):
        for copy in self.copies:
            copy.wait_recv()

    def wait_send(self):
        for copy in self.copies:
            copy.wait_send()


def decoder_kernel(
    names,
    vocab_here,
    part_cols,
    table_rows,
    n_dp,
    bits,
    low_bits,
    *refs,
):
    r = SimpleNamespace(**dict(zip(names, refs)))
    acoustic, memory, table = r.acoustic, r.memory, r.table
    targets, glance = r.targets, r.glance
    gain_1, bias_1 = r.gain_one[...], r.bias_one[...]
    gain_2, bias_2 = r.gain_two[...], r.bias_two[...]
    kernel_rows, rate_table = r.kernel_rows, r.rate_table
    token_lengths, memory_lengths, rate_groups = r.token_lengths, r.memory_lengths, r.rate_groups
    w_query, w_kv, w_out, w_in, w_back, w_vocab = r.w_query, r.w_kv, r.w_out, r.w_in, r.w_back, r.w_vocab
    mem_low, kv, padded, spare = r.mem_low, r.kv, r.padded, r.spare
    stream_in, stream_one, stream_two, stream_three = r.stream_in, r.stream_one, r.stream_two, r.stream_three
    one_low, queries, probs, mixed = r.one_low, r.queries, r.probs, r.mixed
    norm_low, hidden, gelu_slope, top = r.norm_low, r.hidden, r.gelu_slope, r.top
    logits, grad_logits, grad_others = r.logits, r.grad_logits, r.grad_others
    taken_mine, taken_theirs = r.taken_mine, r.taken_theirs
    grad_three, grad_two, branch_low = r.grad_three, r.grad_two, r.branch_low
    grad_pre, att_low, grad_queries = r.grad_pre, r.att_low, r.grad_queries
    mem_arrived, meta, stats, stats_arrived = r.mem_arrived, r.meta, r.stats, r.stats_arrived
    sent, arrived, gathered = r.sent, r.arrived, r.gathered
    small_sent, small_arrived = r.small_sent, r.small_arrived
    terms, term_blocks, term_arrived = grad_three, r.term_blocks, r.term_arrived
    onehot_lo, table_theirs, table_out = r.onehot_lo, r.table_theirs, r.table_mine
    swap_send, swap_recv, load_sem = r.swap_send, r.swap_recv, r.load_sem

    utterances, slots = targets.shape
    width = acoustic.shape[1]
    frames = memory.shape[0] // utterances
    half = w_query.shape[1]
    heads = half // HD
    tokens = utterances * slots
    me, core = lax.axis_index("dp"), lax.axis_index("mp")
    sibling = {"mp": 1 - core}
    quarter = lax.rem(me, 4)
    flips = [1 - 2 * lax.rem(me, 2), 2 - 4 * lax.rem(me // 2, 2)]
    mate = [me + flips[0] * (j % 2) + flips[1] * (j // 2) for j in range(4)]
    bit_of = {b: lax.rem(me // (1 << b), 2) for b in low_bits + bits}
    peer_of = {b: {"dp": me + (1 - 2 * bit_of[b]) * (1 << b)} for b in low_bits + bits}
    score_scale = 1.0 / math.sqrt(HD)

    loads = []

    def load(source, target):
        copy = pltpu.make_async_copy(source, target, load_sem.at[len(loads)])
        copy.start()
        loads.append(copy)
        return copy

    load_memory = load(memory, mem_low)
    load_kv = [
        load(r.w_key_hbm, w_kv.at[:, pl.ds(0, half)]),
        load(r.w_value_hbm, w_kv.at[:, pl.ds(half, half)]),
    ]
    load_query = load(r.w_query_hbm, w_query)
    load_out = load(r.w_out_hbm, w_out)

    barrier = pltpu.get_barrier_semaphore()

    def greet(k, carry):
        pl.semaphore_signal(
            barrier, inc=1, device_id={"dp": lax.rem(me + k, n_dp)}, device_id_type=MESH
        )
        return carry

    lax.fori_loop(1, n_dp, greet, 0)
    pl.semaphore_signal(barrier, inc=1, device_id=sibling, device_id_type=MESH)

    load_in = load(r.w_in_hbm, w_in)
    load_back = load(r.w_back_hbm, w_back)
    block = 1024
    per_core = table_rows // (2 * block)
    mains = 2 * per_core * block

    def load_table(k):
        at = pl.ds(pl.multiple_of((core * per_core + k) * block, block), block)
        return load(table.at[at, :], spare.at[pl.ds(k % 2 * block, block), :])

    table_loads = [load_table(0), load_table(1)]
    main = 4 * part_cols
    load_vocab = load(r.w_vocab_hbm, w_vocab)
    w_rest = r.w_rest
    w_rest[...] = jnp.zeros(w_rest.shape, BF16)
    r.table_rest[...] = jnp.zeros(r.table_rest.shape, BF16)
    r.table_rest[pl.ds(0, table_rows - mains), :] = r.table_tail[...]

    swaps = []

    def swap(source, target, device):
        k = len(swaps)
        copy = pltpu.make_async_remote_copy(
            src_ref=source,
            dst_ref=target,
            send_sem=swap_send.at[k],
            recv_sem=swap_recv.at[k],
            device_id=device,
            device_id_type=MESH,
        )
        copy.start()
        swaps.append(copy)
        return copy

    lane = lax.broadcasted_iota(jnp.int32, (1, slots), 1)
    row_of = lax.broadcasted_iota(jnp.int32, (8, slots), 0)
    for u in range(utterances):
        target_row = targets[pl.ds(u, 1), :].astype(F32)
        glance_row = glance[pl.ds(u, 1), :].astype(F32)
        valid_row = (lane < token_lengths[u]).astype(F32)
        meta[0, :, pl.ds(u * slots, slots)] = jnp.where(
            row_of == 0, target_row, jnp.where(row_of == 1, valid_row, glance_row)
        )
    own_columns = to_columns(meta[0])
    own_target = own_columns[:, 0:1]
    own_valid = own_columns[:, 1:2]

    def rows(u):
        return pl.ds(u * slots, slots)

    edge = jnp.zeros((8, width), F32)
    for u in range(utterances):
        padded[u, pl.ds(0, 8), :] = edge
        padded[u, pl.ds(8 + slots, 8), :] = edge

    step_rows = 256
    row_chunks = frames // step_rows

    def key_of(u, h):
        return kv[pl.ds(u * frames, frames), pl.ds(h * HD, HD)]

    def value_of(u, h):
        return kv[pl.ds(u * frames, frames), pl.ds(half + h * HD, HD)]

    frame_lane = lax.broadcasted_iota(jnp.int32, (1, frames), 1)

    def look_up(first_row, count, allowed, source):
        ids = first_row + lax.broadcasted_iota(jnp.int32, (1, count), 1)
        local = jnp.where(allowed, own_target.astype(jnp.int32), -1)
        onehot = jnp.where(ids == local, 1.0, 0.0).astype(BF16)
        return dot_nn(onehot, source)

    def look_up_block(k):
        table_loads[k].wait()
        part = look_up(
            (core * per_core + k) * block, block, True, spare[pl.ds(k % 2 * block, block), :]
        )
        for u in range(utterances):
            piece = part[u * slots : (u + 1) * slots]
            taken_mine[u] = piece if k == 0 else taken_mine[u] + piece
        if k + 2 < per_core:
            table_loads.append(load_table(k + 2))

    def look_up_rest():
        part = look_up(mains, r.table_rest.shape[0], core == 0, r.table_rest[...])
        for u in range(utterances):
            taken_mine[u] = taken_mine[u] + part[u * slots : (u + 1) * slots]

    def local_targets(target_column):
        local = target_column.astype(jnp.int32) - core * vocab_here
        return jnp.where((local >= 0) & (local < vocab_here), local, -1)

    def vocab_stats(target):
        tiles = main // 128
        step_tiles = 4

        ids = main + lax.broadcasted_iota(jnp.int32, (1, 128), 1)
        last = jnp.where(ids < vocab_here, dot_nt(top[0], w_rest[...]), NEG)
        logits[tiles] = last
        top_m, picked = last, jnp.where(ids == target, last, 0.0)
        for j in range(tiles // step_tiles):
            col = j * step_tiles * 128
            product = dot_nt(top[0], w_vocab[pl.ds(col, step_tiles * 128), :])
            for i in range(step_tiles):
                tile = product[:, i * 128 : (i + 1) * 128]
                ids = col + i * 128 + lax.broadcasted_iota(jnp.int32, (1, 128), 1)
                logits[j * step_tiles + i] = tile
                top_m = jnp.maximum(top_m, tile)
                picked = picked + jnp.where(ids == target, tile, 0.0)
        top_row = jnp.max(top_m, axis=1, keepdims=True)

        def add(j, total):
            for i in range(3):
                total = total + jnp.exp(logits[3 * j + i] - top_row)
            return total

        total = lax.fori_loop(0, (tiles + 1) // 3, add, jnp.zeros((tokens, 128), F32))
        return (
            top_row,
            jnp.sum(total, axis=1, keepdims=True),
            jnp.sum(picked, axis=1, keepdims=True),
        )

    def join(mine, theirs):
        top_value = jnp.maximum(mine[0], theirs[0])
        total = mine[1] * jnp.exp(mine[0] - top_value) + theirs[1] * jnp.exp(theirs[0] - top_value)
        return top_value + jnp.log(total), mine[2] + theirs[2]

    def memory_block(u):
        at = rows(u)
        valid = own_valid[u * slots : (u + 1) * slots]
        hat, _ = normalise(stream_in[at, :])
        padded[u, pl.ds(8, slots), :] = (hat * gain_1 + bias_1) * valid
        for j in range(width // 128):
            cols = pl.ds(j * 128, 128)
            total = jnp.zeros((slots, 128), F32)
            for k in range(kernel_rows.shape[0]):
                shift = 8 + k - kernel_rows.shape[0] // 2
                total = total + kernel_rows[pl.ds(k, 1), cols] * padded[u, pl.ds(shift, slots), cols]
            stream_one[at, cols] = stream_in[at, cols] + total * valid
        low = stream_one[at, :].astype(BF16)
        one_low[at, :] = low
        queries[at, :] = dot_nn(low, w_query[...]).astype(BF16)

    def forward(second, beside_one=None, beside_two=None):
        copies = []
        for u in range(utterances):
            at = rows(u)
            if second:
                memory_block(u)
            frame_ok = frame_lane < memory_lengths[u]
            for h in range(heads):
                cols = pl.ds(h * HD, HD)
                scores = dot_nt(queries[at, cols], key_of(u, h)) * score_scale
                scores = jnp.where(frame_ok, scores, NEG)
                raised = jnp.exp(scores - jnp.max(scores, axis=-1, keepdims=True))
                prob = raised * (1.0 / jnp.sum(raised, axis=-1, keepdims=True))
                if second:
                    probs[u, h] = prob
                mixed[at, cols] = dot_nn(prob.astype(BF16), value_of(u, h)).astype(BF16)
            sent[u] = dot_nn(mixed[at, :], w_out[...])
            copies.append(swap(sent.at[u], arrived.at[u], sibling))
        if not second:
            beside_one()
            load_in.wait()
            load_back.wait()
        ff_copies = []
        for u in range(utterances):
            at = rows(u)
            copies[u].wait()
            two = stream_one[at, :] + (sent[u] + arrived[u])
            stream_two[at, :] = two
            hat, _ = normalise(two)
            low = (hat * gain_2 + bias_2).astype(BF16)
            norm_low[at, :] = low
            pre = dot_nn(low, w_in[...])
            phi = 0.5 * (1.0 + lax.erf(pre * math.sqrt(0.5)))
            hidden[at, :] = (pre * phi).astype(BF16)
            if second:
                gelu_slope[at, :] = phi + pre * (
                    jnp.exp(-0.5 * pre * pre) * (1.0 / math.sqrt(2.0 * math.pi))
                )
            sent[utterances + u] = dot_nn(hidden[at, :], w_back[...])
            ff_copies.append(swap(sent.at[utterances + u], arrived.at[utterances + u], sibling))
        if not second:
            beside_two()
        for u in range(utterances):
            at = rows(u)
            ff_copies[u].wait()
            three = stream_two[at, :] + (sent[utterances + u] + arrived[utterances + u])
            stream_three[u] = three
            top[0, at, :] = three.astype(BF16)

    stream_in[...] = acoustic[...].astype(F32)

    def beside_one():
        look_up_block(0)
        look_up_block(1)

    def beside_two():
        for k in range(2, per_core):
            look_up_block(k)
        look_up_rest()

    load_query.wait()
    for u in range(utterances):
        memory_block(u)
    load_memory.wait()
    for copy in load_kv:
        copy.wait()
    kv_rows = 512
    kv_chunks = frames // kv_rows

    def kv_step(i, carry):
        at = pl.ds(pl.multiple_of(i * kv_rows, kv_rows), kv_rows)
        group = jnp.zeros((1, width), jnp.int32) + rate_groups[i // kv_chunks]
        rate_row = jnp.where(group == 1, rate_table[pl.ds(1, 1), :], rate_table[pl.ds(0, 1), :])
        low = (mem_low[at, :].astype(F32) + rate_row).astype(BF16)
        mem_low[at, :] = low
        kv[at, :] = dot_nn(low, w_kv[...]).astype(BF16)
        return carry

    lax.fori_loop(0, utterances * kv_chunks, kv_step, 0)

    pl.semaphore_wait(barrier, n_dp)
    load_out.wait()
    forward(False, beside_one, beside_two)
    table_swap = swap(taken_mine, taken_theirs, sibling)
    load_vocab.wait()
    w_rest[pl.ds(0, vocab_here - main), :] = w_vocab[pl.ds(main, vocab_here - main), :]
    own_local = local_targets(own_target)
    mine = vocab_stats(own_local)
    stats[0] = side_by_side(mine)
    first_swap = swap(stats.at[0], stats_arrived.at[0], sibling)
    table_swap.wait()
    first_swap.wait()
    log_total, picked = join(mine, [stats_arrived[0, :, i : i + 1] for i in range(3)])
    first_loss = (log_total - picked) * own_valid
    blend = own_columns[:, 2:3] * own_valid / (1.0 + jnp.exp(math.log(V) - first_loss))
    for u in range(utterances):
        at = rows(u)
        wide_acoustic = acoustic[at, :].astype(F32)
        taken = taken_mine[u] + taken_theirs[u]
        stream_in[at, :] = wide_acoustic + blend[u * slots : (u + 1) * slots] * (taken - wide_acoustic)

    forward(True)
    token_swaps = [
        swap(stream_three.at[core], gathered.at[j - 1, 0], {"dp": mate[j]}) for j in (1, 2)
    ]
    mine = vocab_stats(own_local)
    stats[1] = side_by_side(mine)
    stat_swap = swap(stats.at[1], stats_arrived.at[1], sibling)
    stat_swap.wait()
    log_column, picked = join(mine, [stats_arrived[1, :, i : i + 1] for i in range(3)])

    def slope(j, carry):
        col = pl.multiple_of(j * 128, 128)
        ids = col + lax.broadcasted_iota(jnp.int32, (1, 128), 1)
        onehot = jnp.where(ids == own_local, 1.0, 0.0)
        grad = (jnp.exp(logits[j] - log_column) - onehot) * own_valid
        grad_logits[:, pl.ds(col, 128)] = grad.astype(BF16)
        return carry

    lax.fori_loop(0, main // 128 + 1, slope, 0, unroll=3)
    three_copies = []
    for u in range(utterances):
        sent[u] = dot_nn(grad_logits[rows(u), pl.ds(0, main)], w_vocab[pl.ds(0, main), :]) + dot_nn(
            grad_logits[rows(u), pl.ds(main, 128)], w_rest[...]
        )
        three_copies.append(swap(sent.at[u], arrived.at[u], sibling))
    for copy in token_swaps:
        copy.wait()
    part = slots // 2
    relays = [
        swap(gathered.at[0, 0, pl.ds(0, part)], gathered.at[2, 0, pl.ds(0, part)], {"dp": mate[2]}),
        swap(gathered.at[1, 0, pl.ds(part, part)], gathered.at[2, 0, pl.ds(part, part)], {"dp": mate[1]}),
    ]
    share_swaps = [swap(gathered.at[j, 0], gathered.at[j, 1], sibling) for j in range(2)]
    meta[0] = to_rows([own_target, own_valid, log_column, (log_column - picked) * own_valid])
    meta_swaps = [swap(meta.at[0], meta.at[j], {"dp": mate[j]}) for j in range(1, 4)]
    for u in range(utterances):
        r.loss_out[pl.ds(u, 1), :] = meta[0, 3:4, u * slots : (u + 1) * slots]

    plan = Planner()
    steps_all = len(bits)
    scatter_send, scatter_recv = r.scatter_send, r.scatter_recv

    def make_chunk(index):
        name, start, cols, order = chunk_list(part_cols, width, bits, low_bits, r)[index]
        source, landing = getattr(r, "src_" + name), r.landing[index]
        if name == "kv":
            out, out_start = (r.key_out, r.value_out)[start // cols], 0
        else:
            out = r.vocab_sum if name == "vocab" and not low_bits else getattr(r, name + "_out")
            out_start = start
        rows_here = source.shape[-2]

        def pick(step, which):
            rest = sorted([b for b in bits if b not in order[:step]], reverse=True)
            where = tuple(which if b == order[step] else slice(None) for b in rest)
            if step == 0:
                return source, where + (slice(None), pl.ds(start, cols))
            return landing[step - 1], where + (slice(None), slice(None))

        def send(step):
            b = order[step]
            ref, where = pick(step, 1 - bit_of[b])
            copy = pltpu.make_async_remote_copy(
                src_ref=ref.at[where],
                dst_ref=landing[step],
                send_sem=scatter_send.at[index, step],
                recv_sem=scatter_recv.at[index, step],
                device_id=peer_of[b],
                device_id_type=MESH,
            )
            copy.start()
            return copy

        def take(step, copy):
            copy.wait_recv()
            ref, where = pick(step, bit_of[order[step]])
            got = landing[step]
            at = pl.ds(out_start, cols)
            if step < len(order) - 1:
                got[...] = got[...] + ref[where]
            elif name == "vocab":
                out[..., at] = got[...] + ref[where]
            else:
                out[:, at] = got[...] + ref[where]

        steps = [
            (link_of(b, bits), rows_here * cols * 4 * 2 ** (steps_all - 1 - s))
            for s, b in enumerate(order)
        ]
        return Chunk(steps, send, take)

    def make_trade(start, cols):
        summed, traded = r.vocab_sum, r.vocab_traded
        at = pl.ds(start, cols)

        def send(step):
            copies = []
            for j in range(1, 4):
                to = lax.rem(mate[j], 4)
                copies.append(
                    pltpu.make_async_remote_copy(
                        src_ref=summed.at[to // 2, lax.rem(to, 2), :, at],
                        dst_ref=traded.at[j - 1, :, at],
                        send_sem=r.trade_send.at[start // 128, j - 1],
                        recv_sem=r.trade_recv.at[start // 128, j - 1],
                        device_id={"dp": mate[j]},
                        device_id_type=MESH,
                    )
                )
                copies[-1].start()
            return Several(copies)

        def take(step, copies):
            copies.wait_recv()
            for j in range(1, 4):
                there = pl.multiple_of(lax.rem(mate[j], 4) * part_cols + start, 128)
                r.vocab_out[:, pl.ds(there, cols)] = traded[j - 1, :, at]
            here = pl.multiple_of(base + start, 128)
            r.vocab_out[:, pl.ds(here, cols)] = summed[quarter // 2, lax.rem(quarter, 2), :, at]

        return Chunk([(0, 2 * r.src_vocab.shape[-2] * cols * 4)], send, take)

    chunks = {}
    for index, (name, start, cols, _) in enumerate(chunk_list(part_cols, width, bits, low_bits, r)):
        chunks[name, start] = make_chunk(index)
        if name == "vocab" and not low_bits:
            chunks[name, start].follow = make_trade(start, cols)

    def put(name, at, product):
        source = getattr(r, "src_" + name)
        source[..., at] = product.reshape(source.shape[:-1] + (product.shape[1],))

    copies = []
    for u in range(utterances):
        at = rows(u)
        three_copies[u].wait()
        three = sent[u] + arrived[u]
        grad_three[u] = three
        low = three.astype(BF16)
        branch_low[at, :] = low
        pre = (dot_nt(low, w_back[...]) * gelu_slope[at, :]).astype(BF16)
        grad_pre[at, :] = pre
        sent[utterances + u] = dot_nt(pre, w_in[...])
        copies.append(swap(sent.at[utterances + u], arrived.at[utterances + u], sibling))
    plan.run_until(plan.now + 8.0)
    for name, left, right in (("back", branch_low, hidden), ("in", norm_low, grad_pre)):
        left_turned = left[...].T
        for start in sorted(s for n, s in chunks if n == name):
            at = pl.ds(start, 512)
            put(name, at, dot_nn(left_turned, right[:, at]))
            plan.run_until(plan.now + 0.5)
            plan.post(chunks[name, start])

    at_core = pl.ds(pl.multiple_of(core * slots, slots), slots)
    at_other = pl.ds(pl.multiple_of((1 - core) * slots, slots), slots)
    base = pl.multiple_of(quarter * part_cols, part_cols)
    pieces = [(c, 256) for c in range(0, part_cols, 256)]
    for j in range(1, 4):
        if j == 2:
            for copy in relays:
                copy.wait()
            share_swaps.append(swap(gathered.at[2, 0], gathered.at[2, 1], sibling))
        meta_swaps[j - 1].wait()
        columns = to_columns(meta[j])
        target, valid, log_total = local_targets(columns[:, 0:1]), columns[:, 1:2], columns[:, 2:3]
        top[j, at_core, :] = gathered[j - 1, 0].astype(BF16)
        share_swaps[j - 1].wait()
        top[j, at_other, :] = gathered[j - 1, 1].astype(BF16)
        for col, cols in pieces:
            ids = base + col + lax.broadcasted_iota(jnp.int32, (1, cols), 1)
            tile = dot_nt(top[j], w_vocab[pl.ds(base + col, cols), :])
            grad = (jnp.exp(tile - log_total) - jnp.where(ids == target, 1.0, 0.0)) * valid
            grad_others[pl.ds((j - 1) * tokens, tokens), pl.ds(col, cols)] = grad.astype(BF16)
    top_turned = r.top_turned
    for j in range(4):
        top_turned[:, pl.ds(j * tokens, tokens)] = top[j].T
    plan.run_until(plan.now + 4.0)
    put("rest", slice(None), dot_nn(top_turned[:, pl.ds(0, tokens)], grad_logits[:, pl.ds(main, 128)]))
    starts = sorted(start for name, start in chunks if name == "vocab")
    for start, stop in zip(starts, starts[1:] + [part_cols]):
        for col in range(start, stop, 256):
            cols = min(256, stop - col)
            product = dot_nn(top_turned[:, pl.ds(0, tokens)], grad_logits[:, pl.ds(base + col, cols)])
            product = product + dot_nn(
                top_turned[:, pl.ds(tokens, 3 * tokens)], grad_others[:, pl.ds(col, cols)]
            )
            put("vocab", pl.ds(col, cols), product)
        plan.run_until(plan.now + 0.4)
        plan.post(chunks["vocab", start])
    plan.post(chunks["rest", 0])

    one_copies = []
    gain_2_total, bias_2_total = 0.0, 0.0
    for u in range(utterances):
        at = rows(u)
        copies[u].wait()
        grad_norm = sent[utterances + u] + arrived[utterances + u]
        hat, scale = normalise(stream_two[at, :])
        gain_2_total = gain_2_total + jnp.sum(grad_norm * hat, axis=0, keepdims=True)
        bias_2_total = bias_2_total + jnp.sum(grad_norm, axis=0, keepdims=True)
        two = grad_three[u] + normalise_back(grad_norm * gain_2, hat, scale)
        grad_two[at, :] = two
        low = two.astype(BF16)
        att_low[at, :] = low
        grad_mixed = dot_nt(low, w_out[...]).astype(BF16)
        for h in range(heads):
            cols = pl.ds(h * HD, HD)
            grad_head = grad_mixed[:, h * HD : (h + 1) * HD]
            prob = probs[u, h]
            grad_prob = dot_nt(grad_head, value_of(u, h))
            spare[pl.ds(u * frames, frames), pl.ds(half + h * HD, HD)] = dot_tn(
                prob.astype(BF16), grad_head
            ).astype(BF16)
            inner = jnp.sum(prob * grad_prob, axis=-1, keepdims=True)
            grad_score = (prob * (grad_prob - inner)).astype(BF16)
            grad_queries[at, cols] = (dot_nn(grad_score, key_of(u, h)) * score_scale).astype(BF16)
            spare[pl.ds(u * frames, frames), cols] = (
                dot_tn(grad_score, queries[at, cols]) * score_scale
            ).astype(BF16)
            plan.run_until(plan.now + 1.5)
        sent[u] = dot_nt(grad_queries[at, :], w_query[...])
        one_copies.append(swap(sent.at[u], arrived.at[u], sibling))
    every = slice(None)
    put("out", every, dot_tn(att_low[...], mixed[...]))
    plan.post(chunks["out", 0])
    put("query", every, dot_tn(one_low[...], grad_queries[...]))
    plan.post(chunks["query", 0])
    plan.run_until(plan.now + 1.0)

    mem_copies = []
    rate_sums = [0.0, 0.0]
    for u in range(utterances):
        total = jnp.zeros((1, width), F32)
        for i in range(row_chunks):
            at = pl.ds(u * frames + i * step_rows, step_rows)
            part = dot_nt(spare[at, :], w_kv[...])
            for j in range(width // 128):
                side_of, tile = j // (width // 256), j % (width // 256)
                index = ((side_of * utterances + u) * row_chunks + i) * (width // 256) + tile
                logits[index] = part[:, j * 128 : (j + 1) * 128]
            total = total + jnp.sum(part, axis=0, keepdims=True)
        tiles = row_chunks * (width // 256)
        mem_copies.append(
            swap(
                logits.at[pl.ds(((1 - core) * utterances + u) * tiles, tiles)],
                mem_arrived.at[pl.ds(u * tiles, tiles)],
                sibling,
            )
        )
        group = jnp.zeros((1, width), jnp.int32) + rate_groups[u]
        for k in range(2):
            rate_sums[k] = rate_sums[k] + jnp.where((group == 1) == (k == 1), total, 0.0)
        plan.run_until(plan.now + 1.2)
    span = frames // 2
    for k in range(2 * utterances):
        at = pl.ds(k * span, span)
        product = dot_tn(mem_low[at, :], spare[at, :])
        product = product.reshape(r.src_kv.shape)
        r.src_kv[...] = product if k == 0 else r.src_kv[...] + product
    plan.run_until(plan.now + 2.0)
    plan.post(*[chunks["kv", start] for start in sorted(s for n, s in chunks if n == "kv")])

    gain_1_total, bias_1_total = 0.0, 0.0
    for u in range(utterances):
        at = rows(u)
        valid = own_valid[u * slots : (u + 1) * slots]
        one_copies[u].wait()
        one = grad_two[at, :] + (sent[u] + arrived[u])
        grad_two[at, :] = one
        masked = one * valid
        for k in range(kernel_rows.shape[0]):
            shift = 8 + k - kernel_rows.shape[0] // 2
            row = jnp.sum(masked * padded[u, pl.ds(shift, slots), :], axis=0, keepdims=True)
            if u == 0:
                small_sent[0, pl.ds(k, 1), :] = row
            else:
                small_sent[0, pl.ds(k, 1), :] = small_sent[0, pl.ds(k, 1), :] + row
        padded[u, pl.ds(8, slots), :] = masked
        for j in range(width // 128):
            cols = pl.ds(j * 128, 128)
            total = jnp.zeros((slots, 128), F32)
            for k in range(kernel_rows.shape[0]):
                shift = 8 - k + kernel_rows.shape[0] // 2
                total = total + kernel_rows[pl.ds(k, 1), cols] * padded[u, pl.ds(shift, slots), cols]
            stream_one[at, cols] = total * valid
        grad_norm = stream_one[at, :]
        hat, scale = normalise(stream_in[at, :])
        gain_1_total = gain_1_total + jnp.sum(grad_norm * hat, axis=0, keepdims=True)
        bias_1_total = bias_1_total + jnp.sum(grad_norm, axis=0, keepdims=True)
        zero = grad_two[at, :] + normalise_back(grad_norm * gain_1, hat, scale)
        terms[u] = blend[u * slots : (u + 1) * slots] * zero
        stream_one[at, :] = zero - terms[u]
        plan.run_until(plan.now + 1.5)

    last_taps = kernel_rows.shape[0]
    small_sent[0, pl.ds(last_taps, 12 - last_taps), :] = jnp.zeros((12 - last_taps, width), F32)
    for i, row in enumerate((gain_1_total, bias_1_total, gain_2_total, bias_2_total)):
        small_sent[0, pl.ds(12 + i, 1), :] = row
    for k in range(2):
        small_sent[0, pl.ds(16 + k, 1), :] = rate_sums[k]
    small_sent[0, pl.ds(18, 6), :] = jnp.zeros((6, width), F32)
    small_peers = [peer_of[b] for b in low_bits + bits] + [sibling]

    def small_send(step):
        copy = pltpu.make_async_remote_copy(
            src_ref=small_sent.at[step],
            dst_ref=small_arrived.at[step],
            send_sem=r.small_send.at[step],
            recv_sem=r.small_recv.at[step],
            device_id=small_peers[step],
            device_id_type=MESH,
        )
        copy.start()
        return copy

    def small_take(step, copy):
        copy.wait_recv()
        if step + 1 < len(small_peers):
            small_sent[step + 1] = small_sent[step] + small_arrived[step]
        else:
            r.small_out[pl.ds(0, 16), :] = small_sent[step, pl.ds(0, 16), :]
            r.small_out[pl.ds(16, 8), :] = (
                small_sent[step, pl.ds(16, 8), :] + small_arrived[step, pl.ds(16, 8), :]
            )

    small_links = [link_of(b, bits) for b in low_bits + bits] + ["core"]
    plan.post(Chunk([(l, 24 * width * 4) for l in small_links], small_send, small_take))

    features = width // n_dp
    feature_rows = max(features, 8)
    block_rows = term_blocks.shape[1]
    turned = terms[core].T
    id_row = targets[pl.ds(core, 1), :].astype(F32)
    rest = block_rows - features - 1
    for p in range(n_dp):
        term_blocks[p, pl.ds(0, features), :] = turned[p * features : (p + 1) * features]
        term_blocks[p, pl.ds(features, 1), :] = id_row
        term_blocks[p, pl.ds(features + 1, rest), :] = jnp.zeros((rest, slots), F32)

    def term_copy(k):
        there = lax.rem(me + k, n_dp)
        return pltpu.make_async_remote_copy(
            src_ref=term_blocks.at[there],
            dst_ref=term_arrived.at[me],
            send_sem=r.term_send.at[k],
            recv_sem=r.term_recv.at[k],
            device_id={"dp": there},
            device_id_type=MESH,
        )

    def term_start(k, carry):
        term_copy(k).start()
        return carry

    def term_wait(k, carry):
        term_copy(k).wait()
        return carry

    term_arrived[me] = term_blocks[me]
    lax.fori_loop(1, n_dp, term_start, 0)
    stores = []

    def store(source, target):
        copy = pltpu.make_async_copy(source, target, r.store_sem.at[len(stores)])
        copy.start()
        stores.append(copy)

    store(stream_one, r.acoustic_out)
    for u in range(utterances):
        mem_copies[u].wait()
        for i in range(row_chunks):
            for j in range(width // 256):
                index = (u * row_chunks + i) * (width // 256) + j
                first_tile = (core * utterances) * row_chunks * (width // 256)
                mem_arrived[index] = logits[first_tile + index] + mem_arrived[index]
                at = pl.ds(u * frames + i * step_rows, step_rows)
                store(mem_arrived.at[index], r.memory_out.at[at, pl.ds(j * 128, 128)])
    plan.run_until(plan.now + 8.0)
    lax.fori_loop(1, n_dp, term_wait, 0)
    per_piece = 512 // slots
    blocks_hi = table_out.shape[1] // 256
    batch = 4

    def table_piece(p, fresh):
        found = [term_arrived[p * per_piece + i] for i in range(per_piece)]
        values = jnp.concatenate([f[:feature_rows] for f in found], axis=1)
        ids = jnp.concatenate([f[features : features + 1] for f in found], axis=1).astype(jnp.int32)
        low_ids, high_ids = ids & 255, ids >> 8
        onehot_lo[...] = jnp.where(
            lax.broadcasted_iota(jnp.int32, (256, 512), 0) == low_ids, 1.0, 0.0
        ).astype(BF16)
        coarse = values.astype(BF16).astype(F32)
        both = jnp.concatenate([coarse, values - coarse], axis=0)
        for first_hi in range(0, blocks_hi, batch):
            here = range(first_hi, min(first_hi + batch, blocks_hi))
            masked = jnp.concatenate([jnp.where(high_ids == hi, both, 0.0) for hi in here], axis=0)
            product = dot_nt(masked.astype(BF16), onehot_lo[...])
            for i, hi in enumerate(here):
                top_part = product[2 * i * feature_rows : (2 * i + 1) * feature_rows]
                low_part = product[(2 * i + 1) * feature_rows : (2 * i + 2) * feature_rows]
                at = pl.ds(hi * 256, 256)
                if fresh:
                    table_out[:, at] = top_part + low_part
                else:
                    table_out[:, at] = table_out[:, at] + (top_part + low_part)

    pieces = n_dp // per_piece
    table_piece(0, True)
    if pieces <= 4:
        for p in range(1, pieces):
            plan.run_until(plan.now + 1.5)
            table_piece(p, False)
    else:
        lax.fori_loop(1, pieces, lambda p, c: (table_piece(p, False), c)[1], 0)
    table_swap = swap(table_out, table_theirs, sibling)
    plan.run_until(plan.now + 8.0)
    table_swap.wait()
    whole_table = r.whole_table
    whole_table[...] = (
        table_out[pl.ds(0, whole_table.shape[0]), :] + table_theirs[pl.ds(0, whole_table.shape[0]), :]
    )[:, :table_rows]
    store(whole_table, r.table_out)
    plan.finish()
    if not low_bits:
        rest = vocab_here - main
        r.vocab_out[:, pl.ds(main, rest)] = r.rest_out[...][:, :rest]
    for copy in stores:
        copy.wait()


def link_of(bit, bits):
    if bit == bits[-1]:
        return bits[-2]
    return bit


def chunk_list(part_cols, width, bits, low_bits, sizes):
    turned = [bits[1], bits[0]] + bits[2:]
    listing = []
    for start in range(0, part_cols, 256):
        listing.append(("vocab", start, 256, [b for b in bits if b > 1]))
    for start in range(0, sizes.units, 512):
        listing.append(("back", start, 512, turned))
    for start in range(0, sizes.units, 512):
        listing.append(("in", start, 512, bits))
    listing.append(("rest", 0, 128, turned))
    listing.append(("out", 0, sizes.half, turned))
    listing.append(("query", 0, sizes.half, bits))
    for k, start in enumerate(range(0, 2 * sizes.half, 256)):
        listing.append(("kv", start, 256, [bits, turned][k % 2]))
    return listing


def decoder_call(
    acoustic, memory, embedding, w_query, w_key, w_value, w_out, w_in, w_back, w_vocab, norms,
    fsmn_kernel, rate_table, token_lengths, memory_lengths, rate_groups, glance, targets, n_dp,
):
    utterances = token_lengths.shape[0]
    tokens, width = acoustic.shape
    slots = tokens // utterances
    mem_rows = memory.shape[0]
    half = w_query.shape[1]
    heads = half // HD
    frames = mem_rows // utterances
    units = w_in.shape[1]
    vocab_here = w_vocab.shape[1]
    table_rows = embedding.shape[0]
    part_cols = vocab_here // 512 * 128
    all_cols = 4 * part_cols + 128
    w_turned = w_vocab.T
    mains = table_rows // 2048 * 2048
    nbits = n_dp.bit_length() - 1
    steps = nbits
    while width >> steps < 8:
        steps -= 1
    low_bits, bits = list(range(nbits - steps)), list(range(nbits - steps, nbits))
    rows = width >> steps
    features = width // n_dp
    feature_rows = max(features, 8)
    block_rows = feature_rows + 8 if features >= 8 else 8
    blocks_hi = (table_rows + 255) // 256
    sizes = SimpleNamespace(units=units, half=half)
    plane = [b for b in bits if b < 2]
    listing = chunk_list(part_cols, width, bits, low_bits, sizes)
    most = max(len(c[3]) for c in listing)

    f32 = lambda *shape: jax.ShapeDtypeStruct(shape, F32)
    v32 = lambda *shape: pltpu.VMEM(shape, F32)
    v16 = lambda *shape: pltpu.VMEM(shape, BF16)
    dma = lambda *shape: pltpu.SemaphoreType.DMA(shape)
    inputs = dict(
        acoustic=(VMEM, acoustic),
        table_tail=(VMEM, embedding[mains:]),
        memory=(ANY, memory),
        table=(ANY, embedding),
        w_query_hbm=(ANY, w_query),
        w_key_hbm=(ANY, w_key),
        w_value_hbm=(ANY, w_value),
        w_out_hbm=(ANY, w_out),
        w_in_hbm=(ANY, w_in),
        w_back_hbm=(ANY, w_back),
        w_vocab_hbm=(ANY, w_turned),
        gain_one=(VMEM, norms[0][None]),
        bias_one=(VMEM, norms[1][None]),
        gain_two=(VMEM, norms[2][None]),
        bias_two=(VMEM, norms[3][None]),
        kernel_rows=(VMEM, fsmn_kernel),
        rate_table=(VMEM, rate_table),
        token_lengths=(SMEM, token_lengths),
        memory_lengths=(SMEM, memory_lengths),
        rate_groups=(SMEM, rate_groups),
        glance=(VMEM, glance.reshape(utterances, slots)),
        targets=(VMEM, targets.reshape(utterances, slots)),
    )
    outputs = dict(
        loss_out=f32(utterances, slots),
        small_out=f32(24, width),
        vocab_out=f32(2, rows, part_cols) if low_bits else f32(rows, vocab_here),
        rest_out=f32(rows, 128),
        in_out=f32(rows, units),
        back_out=f32(rows, units),
        query_out=f32(rows, half),
        out_out=f32(rows, half),
        key_out=f32(rows, half),
        value_out=f32(rows, half),
        acoustic_out=f32(tokens, width),
        memory_out=f32(mem_rows, width // 2),
        table_out=f32(features, table_rows),
    )
    shape = (2,) * steps + (rows,)
    scratch = dict(
        w_query=v16(width, half),
        w_kv=v16(width, 2 * half),
        w_out=v16(half, width),
        w_in=v16(width, units),
        w_back=v16(units, width),
        w_vocab=v16(vocab_here, width),
        w_rest=v16(128, width),
        mem_low=v16(mem_rows, width),
        kv=v16(mem_rows, 2 * half),
        spare=v16(mem_rows, 2 * half),
        padded=v32(utterances, slots + 16, width),
        stream_in=v32(tokens, width),
        stream_one=v32(tokens, width),
        stream_two=v32(tokens, width),
        stream_three=v32(utterances, slots, width),
        one_low=v16(tokens, width),
        queries=v16(tokens, half),
        probs=v32(utterances, heads, slots, frames),
        mixed=v16(tokens, half),
        norm_low=v16(tokens, width),
        hidden=v16(tokens, units),
        gelu_slope=v32(tokens, units),
        top=v16(4, tokens, width),
        logits=v32(all_cols // 128, tokens, 128),
        grad_logits=v16(tokens, all_cols),
        grad_others=v16(3 * tokens, part_cols),
        top_turned=v16(width, 4 * tokens),
        taken_mine=v32(utterances, slots, width),
        taken_theirs=v32(utterances, slots, width),
        grad_three=v32(utterances, slots, width),
        grad_two=v32(tokens, width),
        branch_low=v16(tokens, width),
        grad_pre=v16(tokens, units),
        att_low=v16(tokens, width),
        grad_queries=v16(tokens, half),
        mem_arrived=v32(mem_rows // 256 * (width // 256), 256, 128),
        meta=v32(4, 8, tokens),
        stats=v32(2, tokens, 128),
        stats_arrived=v32(2, tokens, 128),
        sent=v32(2 * utterances, slots, width),
        arrived=v32(2 * utterances, slots, width),
        gathered=v32(3, 2, slots, width),
        small_sent=v32(nbits + 1, 24, width),
        small_arrived=v32(nbits + 1, 24, width),
        term_blocks=v32(n_dp, block_rows, slots),
        term_arrived=v32(n_dp, block_rows, slots),
        onehot_lo=v16(256, 512),
        table_rest=v16((table_rows - mains + 127) // 128 * 128, width),
        table_theirs=v32(feature_rows, blocks_hi * 256),
        table_mine=v32(feature_rows, blocks_hi * 256),
        src_vocab=v32(*shape, part_cols),
        src_rest=v32(*shape, 128),
        whole_table=v32(features, table_rows),
        src_back=v32(*shape, units),
        vocab_sum=v32(*(2,) * len(plane), rows, part_cols),
        vocab_traded=v32(3, rows, part_cols),
        src_in=v32(*shape, units),
        src_out=v32(*shape, half),
        src_query=v32(*shape, half),
        src_kv=v32(*shape, 2 * half),
        load_sem=dma(24),
        store_sem=dma(24),
        trade_send=dma(part_cols // 128, 3),
        trade_recv=dma(part_cols // 128, 3),
        swap_send=dma(40),
        swap_recv=dma(40),
        scatter_send=dma(len(listing), most),
        scatter_recv=dma(len(listing), most),
        small_send=dma(nbits + 1),
        small_recv=dma(nbits + 1),
        term_send=dma(n_dp),
        term_recv=dma(n_dp),
    )
    landing = [
        [v32(*(2,) * (steps - 1 - s), rows, cols) for s in range(len(order))]
        for _, _, cols, order in listing
    ]
    names = list(inputs) + list(outputs) + list(scratch)
    flat = [ref for chunk in landing for ref in chunk]

    def kernel(*refs):
        named, rest = refs[: len(names)], list(refs[len(names) :])
        lands = [[rest.pop(0) for _ in chunk] for chunk in landing]
        decoder_kernel(
            names + ["landing", "units", "half"], vocab_here, part_cols, table_rows, n_dp, bits,
            low_bits, *named, lands, units, half,
        )

    out = pl.pallas_call(
        kernel,
        out_shape=list(outputs.values()),
        in_specs=[spec for spec, _ in inputs.values()],
        out_specs=[VMEM] * (len(outputs) - 3) + [ANY] * 3,
        scratch_shapes=list(scratch.values()) + flat,
        compiler_params=pltpu.CompilerParams(
            collective_id=1, has_side_effects=True, vmem_limit_bytes=64 << 20
        ),
    )(*[value for _, value in inputs.values()])
    return SimpleNamespace(**dict(zip(outputs, out))), low_bits


def deliver_kernel(n_dp, n_passed, *refs):
    n = n_passed + 2
    sources, targets, held = refs[:n], refs[n : 2 * n + 5], refs[2 * n + 5 : 3 * n + 5]
    sem_in, sem_out = refs[3 * n + 5 :]
    reads, writes = [], []
    for i, (source, buffer) in enumerate(zip(sources, held)):
        reads.append(pltpu.make_async_copy(source, buffer, sem_in.at[i]))
        reads[-1].start()
    for i in range(n_passed):
        reads[i].wait()
        writes.append(pltpu.make_async_copy(held[i], targets[i], sem_out.at[i]))
        writes[-1].start()
    reads[n_passed].wait()
    reads[n_passed + 1].wait()
    loss, small = held[n_passed:]
    loss_to, gain_one_to, bias_one_to, gain_two_to, bias_two_to, taps_to, rate_to = targets[n_passed:]
    slots = loss.shape[1]
    for u in range(loss.shape[0]):
        loss_to[:, pl.ds(u * slots, slots)] = loss[pl.ds(u, 1), :]
    me = lax.axis_index("dp")
    own = small.shape[1] // n_dp
    mine = jnp.zeros((16, own), F32)
    for p in range(n_dp):
        mine = jnp.where(me == p, small[pl.ds(0, 16), p * own : (p + 1) * own], mine)
    taps_to[...] = mine[: taps_to.shape[0]]
    for i, target in enumerate((gain_one_to, bias_one_to, gain_two_to, bias_two_to)):
        target[...] = mine[12 + i : 13 + i]
    rate_to[...] = small[pl.ds(16, 2), :]
    for copy in writes:
        copy.wait()


def per_device(
    acoustic,
    memory,
    embedding,
    w_query,
    w_key,
    w_value,
    w_out,
    w_in,
    w_back,
    w_vocab,
    gain_one,
    bias_one,
    gain_two,
    bias_two,
    fsmn_kernel,
    rate_table,
    token_lengths,
    memory_lengths,
    rate_groups,
    glance_mask,
    targets,
):
    tok_rows, model_width = acoustic.shape
    half = w_query.shape[1]
    n_dp = lax.axis_size("dp")
    result, low_bits = decoder_call(
        acoustic, memory, embedding, w_query, w_key, w_value, w_out, w_in, w_back, w_vocab,
        (gain_one, bias_one, gain_two, bias_two), fsmn_kernel, rate_table,
        token_lengths, memory_lengths, rate_groups, glance_mask, targets, n_dp,
    )
    vocab = result.vocab_out
    summed = [
        result.query_out, result.key_out, result.value_out, result.out_out, result.in_out,
        result.back_out,
    ]
    if low_bits:
        size = 1 << len(low_bits)
        groups = [list(range(g * size, (g + 1) * size)) for g in range(n_dp // size)]
        planes = [list(range(4 * g, 4 * g + 4)) for g in range(n_dp // 4)]
        vocab = lax.all_to_all(
            vocab.reshape(4, model_width // n_dp, -1), "dp", 0, 0, axis_index_groups=planes, tiled=True
        )
        *summed, rest = [
            lax.psum_scatter(s, "dp", scatter_dimension=0, axis_index_groups=groups, tiled=True)
            for s in (*summed, result.rest_out)
        ]
        vocab = jnp.concatenate([*vocab, rest], axis=1)[:, : w_vocab.shape[1]]
    own = model_width // n_dp
    f32 = lambda *shape: jax.ShapeDtypeStruct(shape, F32)
    like = lambda x: jax.ShapeDtypeStruct(x.shape, F32)
    passed = (result.memory_out, result.table_out, result.acoustic_out, vocab, *summed)
    handed = (*passed, result.loss_out, result.small_out)
    (
        grad_memory, grad_table, grad_acoustic, grad_vocab, grad_query, grad_key, grad_value,
        grad_out, grad_in, grad_back, token_loss, gain_1, bias_1, gain_2, bias_2, grad_taps, grad_rate,
    ) = pl.pallas_call(
        partial(deliver_kernel, n_dp, len(passed)),
        out_shape=[
            *[like(x) for x in passed],
            f32(1, tok_rows),
            *[f32(1, own)] * 4,
            f32(fsmn_kernel.shape[0], own),
            f32(2, model_width),
        ],
        in_specs=[ANY] * len(handed),
        out_specs=[ANY] * len(passed) + [VMEM] * 7,
        scratch_shapes=[pltpu.VMEM(x.shape, F32) for x in handed]
        + [pltpu.SemaphoreType.DMA((len(handed),)), pltpu.SemaphoreType.DMA((len(handed),))],
        compiler_params=pltpu.CompilerParams(vmem_limit_bytes=60 << 20),
    )(*handed)
    return (
        token_loss.reshape(tok_rows),
        grad_acoustic,
        grad_memory,
        grad_table.T,
        grad_query,
        grad_key,
        grad_value,
        grad_out.T,
        grad_in,
        grad_back.T,
        grad_vocab,
        gain_1.reshape(own),
        bias_1.reshape(own),
        gain_2.reshape(own),
        bias_2.reshape(own),
        grad_taps,
        grad_rate,
    )


def solution(mesh):
    return jax.shard_map(
        per_device,
        mesh=mesh,
        in_specs=(
            P("dp", None),
            P("dp", None),
            P(),
            P(None, "mp"),
            P(None, "mp"),
            P(None, "mp"),
            P("mp", None),
            P(None, "mp"),
            P("mp", None),
            P(None, "mp"),
            P(),
            P(),
            P(),
            P(),
            P(),
            P(),
            P("dp"),
            P("dp"),
            P("dp"),
            P("dp"),
            P("dp"),
        ),
        out_specs=(
            P("dp"),
            P("dp", None),
            P("dp", "mp"),
            P(None, "dp"),
            P("dp", "mp"),
            P("dp", "mp"),
            P("dp", "mp"),
            P("mp", "dp"),
            P("dp", "mp"),
            P("mp", "dp"),
            P("dp", "mp"),
            P("dp"),
            P("dp"),
            P("dp"),
            P("dp"),
            P(None, "dp"),
            P(),
        ),
        check_vma=False,
    )
```

```python
from functools import partial
import math
from types import SimpleNamespace

import jax
import jax.numpy as jnp
from jax import lax
from jax.experimental import pallas as pl
from jax.experimental.pallas import tpu as pltpu
from jax.sharding import PartitionSpec as P

HD = 128
V = 8404
EPSILON = 1e-05
MESH = pl.DeviceIdType.MESH
VMEM = pl.BlockSpec(memory_space=pltpu.VMEM)
SMEM = pl.BlockSpec(memory_space=pltpu.SMEM)
ANY = pl.BlockSpec(memory_space=pl.ANY)
F32, BF16 = jnp.float32, jnp.bfloat16
NEG = -1e30


def other_core():
    return {"mp": 1 - lax.axis_index("mp")}


def dot_nn(a, b):
    return lax.dot_general(a, b, (((1,), (0,)), ((), ())), preferred_element_type=F32)


def dot_nt(a, b):
    return lax.dot_general(a, b, (((1,), (1,)), ((), ())), preferred_element_type=F32)


def dot_tn(a, b):
    return lax.dot_general(a, b, (((0,), (0,)), ((), ())), preferred_element_type=F32)


def normalise(rows):
    average = jnp.mean(rows, axis=-1, keepdims=True)
    centred = rows - average
    variance = jnp.mean(centred * centred, axis=-1, keepdims=True)
    scale = lax.rsqrt(variance + EPSILON)
    return centred * scale, scale


def normalise_back(grad_hat, hat, scale):
    first = jnp.mean(grad_hat, axis=-1, keepdims=True)
    second = jnp.mean(grad_hat * hat, axis=-1, keepdims=True)
    return scale * (grad_hat - first - hat * second)


def side_by_side(columns):
    lane = lax.broadcasted_iota(jnp.int32, (columns[0].shape[0], 128), 1)
    tile = jnp.zeros(lane.shape, F32)
    for i, column in enumerate(columns):
        tile = jnp.where(lane == i, column, tile)
    return tile


def to_rows(columns):
    return side_by_side(columns).T[:8]


def to_columns(rows):
    return jnp.concatenate([rows] * 16, axis=0).T


class Planner:
    RATE = 0.045e6
    HOP = 1.5
    BACKLOG = 6.0

    def __init__(self):
        self.now = 0.0
        self.free = {}
        self.flying = []
        self.waiting = []
        self.started = []
        self.count = 0

    def launch(self, item, step):
        link, size = item.steps[step]
        begin = max(self.now, self.free.get(link, 0.0))
        self.free[link] = begin + size / self.RATE
        copy = item.send(step)
        self.started.append(copy)
        self.count += 1
        self.flying.append((self.free[link] + self.HOP, self.count, item, step, copy))

    def release(self):
        kept = []
        for item in self.waiting:
            link = item.steps[0][0]
            if self.free.get(link, 0.0) - self.now < self.BACKLOG:
                self.launch(item, 0)
            else:
                kept.append(item)
        self.waiting = kept

    def post(self, *items):
        self.waiting += items
        self.release()

    def run_until(self, time):
        while self.flying or self.waiting:
            if not self.flying:
                self.now = max(self.now, min(self.free[i.steps[0][0]] for i in self.waiting))
                self.release()
                continue
            first = min(self.flying, key=lambda f: f[:2])
            if first[0] > time:
                break
            self.flying.remove(first)
            self.now = max(self.now, first[0])
            _, _, item, step, copy = first
            item.take(step, copy)
            if step + 1 < len(item.steps):
                self.launch(item, step + 1)
            elif item.follow is not None:
                self.launch(item.follow, 0)
            self.release()
        if time != math.inf:
            self.now = max(self.now, time)
        self.release()

    def finish(self):
        self.run_until(math.inf)
        for copy in self.started:
            copy.wait_send()


class Chunk:
    def __init__(self, steps, send, take):
        self.steps, self.send, self.take, self.follow = steps, send, take, None


class Several:
    def __init__(self, copies):
        self.copies = copies

    def wait_recv(self):
        for copy in self.copies:
            copy.wait_recv()

    def wait_send(self):
        for copy in self.copies:
            copy.wait_send()


def decoder_kernel(
    names,
    vocab_here,
    part_cols,
    table_rows,
    n_dp,
    bits,
    low_bits,
    *refs,
):
    r = SimpleNamespace(**dict(zip(names, refs)))
    acoustic, memory, table = r.acoustic, r.memory, r.table
    targets, glance = r.targets, r.glance
    gain_1, bias_1 = r.gain_one[...], r.bias_one[...]
    gain_2, bias_2 = r.gain_two[...], r.bias_two[...]
    kernel_rows, rate_table = r.kernel_rows, r.rate_table
    token_lengths, memory_lengths, rate_groups = r.token_lengths, r.memory_lengths, r.rate_groups
    w_query, w_kv, w_out, w_in, w_back, w_vocab = r.w_query, r.w_kv, r.w_out, r.w_in, r.w_back, r.w_vocab
    mem_low, kv, padded, spare = r.mem_low, r.kv, r.padded, r.spare
    stream_in, stream_one, stream_two, stream_three = r.stream_in, r.stream_one, r.stream_two, r.stream_three
    one_low, queries, probs, mixed = r.one_low, r.queries, r.probs, r.mixed
    norm_low, hidden, gelu_slope, top = r.norm_low, r.hidden, r.gelu_slope, r.top
    logits, grad_logits, grad_others = r.logits, r.grad_logits, r.grad_others
    taken_mine, taken_theirs = r.taken_mine, r.taken_theirs
    grad_three, grad_two, branch_low = r.grad_three, r.grad_two, r.branch_low
    grad_pre, att_low, grad_queries = r.grad_pre, r.att_low, r.grad_queries
    mem_arrived, meta, stats, stats_arrived = r.mem_arrived, r.meta, r.stats, r.stats_arrived
    sent, arrived, gathered = r.sent, r.arrived, r.gathered
    small_sent, small_arrived = r.small_sent, r.small_arrived
    terms, term_blocks, term_arrived = grad_three, r.term_blocks, r.term_arrived
    onehot_lo, table_theirs, table_out = r.onehot_lo, r.table_theirs, r.table_mine
    swap_send, swap_recv, load_sem = r.swap_send, r.swap_recv, r.load_sem

    utterances, slots = targets.shape
    width = acoustic.shape[1]
    frames = memory.shape[0] // utterances
    half = w_query.shape[1]
    heads = half // HD
    tokens = utterances * slots
    me, core = lax.axis_index("dp"), lax.axis_index("mp")
    sibling = {"mp": 1 - core}
    quarter = lax.rem(me, 4)
    flips = [1 - 2 * lax.rem(me, 2), 2 - 4 * lax.rem(me // 2, 2)]
    mate = [me + flips[0] * (j % 2) + flips[1] * (j // 2) for j in range(4)]
    bit_of = {b: lax.rem(me // (1 << b), 2) for b in low_bits + bits}
    peer_of = {b: {"dp": me + (1 - 2 * bit_of[b]) * (1 << b)} for b in low_bits + bits}
    score_scale = 1.0 / math.sqrt(HD)

    loads = []

    def load(source, target):
        copy = pltpu.make_async_copy(source, target, load_sem.at[len(loads)])
        copy.start()
        loads.append(copy)
        return copy

    load_memory = load(memory, mem_low)
    load_kv = [
        load(r.w_key_hbm, w_kv.at[:, pl.ds(0, half)]),
        load(r.w_value_hbm, w_kv.at[:, pl.ds(half, half)]),
    ]
    load_query = load(r.w_query_hbm, w_query)
    load_out = load(r.w_out_hbm, w_out)

    barrier = pltpu.get_barrier_semaphore()

    def greet(k, carry):
        pl.semaphore_signal(
            barrier, inc=1, device_id={"dp": lax.rem(me + k, n_dp)}, device_id_type=MESH
        )
        return carry

    lax.fori_loop(1, n_dp, greet, 0)
    pl.semaphore_signal(barrier, inc=1, device_id=sibling, device_id_type=MESH)

    load_in = load(r.w_in_hbm, w_in)
    load_back = load(r.w_back_hbm, w_back)
    block = 1024
    per_core = table_rows // (2 * block)
    mains = 2 * per_core * block

    def load_table(k):
        at = pl.ds(pl.multiple_of((core * per_core + k) * block, block), block)
        return load(table.at[at, :], spare.at[pl.ds(k % 2 * block, block), :])

    table_loads = [load_table(0), load_table(1)]
    main = 4 * part_cols
    load_vocab = load(r.w_vocab_hbm, w_vocab)
    w_rest = r.w_rest
    w_rest[...] = jnp.zeros(w_rest.shape, BF16)
    r.table_rest[...] = jnp.zeros(r.table_rest.shape, BF16)
    r.table_rest[pl.ds(0, table_rows - mains), :] = r.table_tail[...]

    swaps = []

    def swap(source, target, device):
        k = len(swaps)
        copy = pltpu.make_async_remote_copy(
            src_ref=source,
            dst_ref=target,
            send_sem=swap_send.at[k],
            recv_sem=swap_recv.at[k],
            device_id=device,
            device_id_type=MESH,
        )
        copy.start()
        swaps.append(copy)
        return copy

    lane = lax.broadcasted_iota(jnp.int32, (1, slots), 1)
    row_of = lax.broadcasted_iota(jnp.int32, (8, slots), 0)
    for u in range(utterances):
        target_row = targets[pl.ds(u, 1), :].astype(F32)
        glance_row = glance[pl.ds(u, 1), :].astype(F32)
        valid_row = (lane < token_lengths[u]).astype(F32)
        meta[0, :, pl.ds(u * slots, slots)] = jnp.where(
            row_of == 0, target_row, jnp.where(row_of == 1, valid_row, glance_row)
        )
    own_columns = to_columns(meta[0])
    own_target = own_columns[:, 0:1]
    own_valid = own_columns[:, 1:2]

    def rows(u):
        return pl.ds(u * slots, slots)

    edge = jnp.zeros((8, width), F32)
    for u in range(utterances):
        padded[u, pl.ds(0, 8), :] = edge
        padded[u, pl.ds(8 + slots, 8), :] = edge

    step_rows = 256
    row_chunks = frames // step_rows

    def key_of(u, h):
        return kv[pl.ds(u * frames, frames), pl.ds(h * HD, HD)]

    def value_of(u, h):
        return kv[pl.ds(u * frames, frames), pl.ds(half + h * HD, HD)]

    frame_lane = lax.broadcasted_iota(jnp.int32, (1, frames), 1)

    def look_up(first_row, count, allowed, source):
        ids = first_row + lax.broadcasted_iota(jnp.int32, (1, count), 1)
        local = jnp.where(allowed, own_target.astype(jnp.int32), -1)
        onehot = jnp.where(ids == local, 1.0, 0.0).astype(BF16)
        return dot_nn(onehot, source)

    def look_up_block(k):
        table_loads[k].wait()
        part = look_up(
            (core * per_core + k) * block, block, True, spare[pl.ds(k % 2 * block, block), :]
        )
        for u in range(utterances):
            piece = part[u * slots : (u + 1) * slots]
            taken_mine[u] = piece if k == 0 else taken_mine[u] + piece
        if k + 2 < per_core:
            table_loads.append(load_table(k + 2))

    def look_up_rest():
        part = look_up(mains, r.table_rest.shape[0], core == 0, r.table_rest[...])
        for u in range(utterances):
            taken_mine[u] = taken_mine[u] + part[u * slots : (u + 1) * slots]

    def local_targets(target_column):
        local = target_column.astype(jnp.int32) - core * vocab_here
        return jnp.where((local >= 0) & (local < vocab_here), local, -1)

    def vocab_stats(target):
        tiles = main // 128
        step_tiles = 4

        ids = main + lax.broadcasted_iota(jnp.int32, (1, 128), 1)
        last = jnp.where(ids < vocab_here, dot_nt(top[0], w_rest[...]), NEG)
        logits[tiles] = last
        top_m, picked = last, jnp.where(ids == target, last, 0.0)
        for j in range(tiles // step_tiles):
            col = j * step_tiles * 128
            product = dot_nt(top[0], w_vocab[pl.ds(col, step_tiles * 128), :])
            for i in range(step_tiles):
                tile = product[:, i * 128 : (i + 1) * 128]
                ids = col + i * 128 + lax.broadcasted_iota(jnp.int32, (1, 128), 1)
                logits[j * step_tiles + i] = tile
                top_m = jnp.maximum(top_m, tile)
                picked = picked + jnp.where(ids == target, tile, 0.0)
        top_row = jnp.max(top_m, axis=1, keepdims=True)

        def add(j, total):
            for i in range(3):
                total = total + jnp.exp(logits[3 * j + i] - top_row)
            return total

        total = lax.fori_loop(0, (tiles + 1) // 3, add, jnp.zeros((tokens, 128), F32))
        return (
            top_row,
            jnp.sum(total, axis=1, keepdims=True),
            jnp.sum(picked, axis=1, keepdims=True),
        )

    def join(mine, theirs):
        top_value = jnp.maximum(mine[0], theirs[0])
        total = mine[1] * jnp.exp(mine[0] - top_value) + theirs[1] * jnp.exp(theirs[0] - top_value)
        return top_value + jnp.log(total), mine[2] + theirs[2]

    def memory_block(u):
        at = rows(u)
        valid = own_valid[u * slots : (u + 1) * slots]
        hat, _ = normalise(stream_in[at, :])
        padded[u, pl.ds(8, slots), :] = (hat * gain_1 + bias_1) * valid
        for j in range(width // 128):
            cols = pl.ds(j * 128, 128)
            total = jnp.zeros((slots, 128), F32)
            for k in range(kernel_rows.shape[0]):
                shift = 8 + k - kernel_rows.shape[0] // 2
                total = total + kernel_rows[pl.ds(k, 1), cols] * padded[u, pl.ds(shift, slots), cols]
            stream_one[at, cols] = stream_in[at, cols] + total * valid
        low = stream_one[at, :].astype(BF16)
        one_low[at, :] = low
        queries[at, :] = dot_nn(low, w_query[...]).astype(BF16)

    def forward(second, beside_one=None, beside_two=None):
        copies = []
        for u in range(utterances):
            at = rows(u)
            if second:
                memory_block(u)
            frame_ok = frame_lane < memory_lengths[u]
            for h in range(heads):
                cols = pl.ds(h * HD, HD)
                scores = dot_nt(queries[at, cols], key_of(u, h)) * score_scale
                scores = jnp.where(frame_ok, scores, NEG)
                raised = jnp.exp(scores - jnp.max(scores, axis=-1, keepdims=True))
                prob = raised * (1.0 / jnp.sum(raised, axis=-1, keepdims=True))
                if second:
                    probs[u, h] = prob
                mixed[at, cols] = dot_nn(prob.astype(BF16), value_of(u, h)).astype(BF16)
            sent[u] = dot_nn(mixed[at, :], w_out[...])
            copies.append(swap(sent.at[u], arrived.at[u], sibling))
        if not second:
            beside_one()
            load_in.wait()
            load_back.wait()
        ff_copies = []
        for u in range(utterances):
            at = rows(u)
            copies[u].wait()
            two = stream_one[at, :] + (sent[u] + arrived[u])
            stream_two[at, :] = two
            hat, _ = normalise(two)
            low = (hat * gain_2 + bias_2).astype(BF16)
            norm_low[at, :] = low
            pre = dot_nn(low, w_in[...])
            phi = 0.5 * (1.0 + lax.erf(pre * math.sqrt(0.5)))
            hidden[at, :] = (pre * phi).astype(BF16)
            if second:
                gelu_slope[at, :] = phi + pre * (
                    jnp.exp(-0.5 * pre * pre) * (1.0 / math.sqrt(2.0 * math.pi))
                )
            sent[utterances + u] = dot_nn(hidden[at, :], w_back[...])
            ff_copies.append(swap(sent.at[utterances + u], arrived.at[utterances + u], sibling))
        if not second:
            beside_two()
        for u in range(utterances):
            at = rows(u)
            ff_copies[u].wait()
            three = stream_two[at, :] + (sent[utterances + u] + arrived[utterances + u])
            stream_three[u] = three
            top[0, at, :] = three.astype(BF16)

    stream_in[...] = acoustic[...].astype(F32)

    def beside_one():
        look_up_block(0)
        look_up_block(1)

    def beside_two():
        for k in range(2, per_core):
            look_up_block(k)
        look_up_rest()

    load_query.wait()
    for u in range(utterances):
        memory_block(u)
    load_memory.wait()
    for copy in load_kv:
        copy.wait()
    kv_rows = 512
    kv_chunks = frames // kv_rows

    def kv_step(i, carry):
        at = pl.ds(pl.multiple_of(i * kv_rows, kv_rows), kv_rows)
        group = jnp.zeros((1, width), jnp.int32) + rate_groups[i // kv_chunks]
        rate_row = jnp.where(group == 1, rate_table[pl.ds(1, 1), :], rate_table[pl.ds(0, 1), :])
        low = (mem_low[at, :].astype(F32) + rate_row).astype(BF16)
        mem_low[at, :] = low
        kv[at, :] = dot_nn(low, w_kv[...]).astype(BF16)
        return carry

    lax.fori_loop(0, utterances * kv_chunks, kv_step, 0)

    pl.semaphore_wait(barrier, n_dp)
    load_out.wait()
    forward(False, beside_one, beside_two)
    table_swap = swap(taken_mine, taken_theirs, sibling)
    load_vocab.wait()
    w_rest[pl.ds(0, vocab_here - main), :] = w_vocab[pl.ds(main, vocab_here - main), :]
    own_local = local_targets(own_target)
    mine = vocab_stats(own_local)
    stats[0] = side_by_side(mine)
    first_swap = swap(stats.at[0], stats_arrived.at[0], sibling)
    table_swap.wait()
    first_swap.wait()
    log_total, picked = join(mine, [stats_arrived[0, :, i : i + 1] for i in range(3)])
    first_loss = (log_total - picked) * own_valid
    blend = own_columns[:, 2:3] * own_valid / (1.0 + jnp.exp(math.log(V) - first_loss))
    for u in range(utterances):
        at = rows(u)
        wide_acoustic = acoustic[at, :].astype(F32)
        taken = taken_mine[u] + taken_theirs[u]
        stream_in[at, :] = wide_acoustic + blend[u * slots : (u + 1) * slots] * (taken - wide_acoustic)

    forward(True)
    token_swaps = [
        swap(stream_three.at[core], gathered.at[j - 1, 0], {"dp": mate[j]}) for j in (1, 2)
    ]
    mine = vocab_stats(own_local)
    stats[1] = side_by_side(mine)
    stat_swap = swap(stats.at[1], stats_arrived.at[1], sibling)
    stat_swap.wait()
    log_column, picked = join(mine, [stats_arrived[1, :, i : i + 1] for i in range(3)])

    def slope(j, carry):
        col = pl.multiple_of(j * 128, 128)
        ids = col + lax.broadcasted_iota(jnp.int32, (1, 128), 1)
        onehot = jnp.where(ids == own_local, 1.0, 0.0)
        grad = (jnp.exp(logits[j] - log_column) - onehot) * own_valid
        grad_logits[:, pl.ds(col, 128)] = grad.astype(BF16)
        return carry

    lax.fori_loop(0, main // 128 + 1, slope, 0, unroll=3)
    three_copies = []
    for u in range(utterances):
        sent[u] = dot_nn(grad_logits[rows(u), pl.ds(0, main)], w_vocab[pl.ds(0, main), :]) + dot_nn(
            grad_logits[rows(u), pl.ds(main, 128)], w_rest[...]
        )
        three_copies.append(swap(sent.at[u], arrived.at[u], sibling))
    for copy in token_swaps:
        copy.wait()
    part = slots // 2
    relays = [
        swap(gathered.at[0, 0, pl.ds(0, part)], gathered.at[2, 0, pl.ds(0, part)], {"dp": mate[2]}),
        swap(gathered.at[1, 0, pl.ds(part, part)], gathered.at[2, 0, pl.ds(part, part)], {"dp": mate[1]}),
    ]
    share_swaps = [swap(gathered.at[j, 0], gathered.at[j, 1], sibling) for j in range(2)]
    meta[0] = to_rows([own_target, own_valid, log_column, (log_column - picked) * own_valid])
    meta_swaps = [swap(meta.at[0], meta.at[j], {"dp": mate[j]}) for j in range(1, 4)]
    for u in range(utterances):
        r.loss_out[pl.ds(u, 1), :] = meta[0, 3:4, u * slots : (u + 1) * slots]

    plan = Planner()
    steps_all = len(bits)
    scatter_send, scatter_recv = r.scatter_send, r.scatter_recv

    def make_chunk(index):
        name, start, cols, order = chunk_list(part_cols, width, bits, low_bits, r)[index]
        source, landing = getattr(r, "src_" + name), r.landing[index]
        if name == "kv":
            out, out_start = (r.key_out, r.value_out)[start // cols], 0
        else:
            out = r.vocab_sum if name == "vocab" and not low_bits else getattr(r, name + "_out")
            out_start = start
        rows_here = source.shape[-2]

        def pick(step, which):
            rest = sorted([b for b in bits if b not in order[:step]], reverse=True)
            where = tuple(which if b == order[step] else slice(None) for b in rest)
            if step == 0:
                return source, where + (slice(None), pl.ds(start, cols))
            return landing[step - 1], where + (slice(None), slice(None))

        def send(step):
            b = order[step]
            ref, where = pick(step, 1 - bit_of[b])
            copy = pltpu.make_async_remote_copy(
                src_ref=ref.at[where],
                dst_ref=landing[step],
                send_sem=scatter_send.at[index, step],
                recv_sem=scatter_recv.at[index, step],
                device_id=peer_of[b],
                device_id_type=MESH,
            )
            copy.start()
            return copy

        def take(step, copy):
            copy.wait_recv()
            ref, where = pick(step, bit_of[order[step]])
            got = landing[step]
            at = pl.ds(out_start, cols)
            if step < len(order) - 1:
                got[...] = got[...] + ref[where]
            elif name == "vocab":
                out[..., at] = got[...] + ref[where]
            else:
                out[:, at] = got[...] + ref[where]

        steps = [
            (link_of(b, bits), rows_here * cols * 4 * 2 ** (steps_all - 1 - s))
            for s, b in enumerate(order)
        ]
        return Chunk(steps, send, take)

    def make_trade(start, cols):
        summed, traded = r.vocab_sum, r.vocab_traded
        at = pl.ds(start, cols)

        def send(step):
            copies = []
            for j in range(1, 4):
                to = lax.rem(mate[j], 4)
                copies.append(
                    pltpu.make_async_remote_copy(
                        src_ref=summed.at[to // 2, lax.rem(to, 2), :, at],
                        dst_ref=traded.at[j - 1, :, at],
                        send_sem=r.trade_send.at[start // 128, j - 1],
                        recv_sem=r.trade_recv.at[start // 128, j - 1],
                        device_id={"dp": mate[j]},
                        device_id_type=MESH,
                    )
                )
                copies[-1].start()
            return Several(copies)

        def take(step, copies):
            copies.wait_recv()
            for j in range(1, 4):
                there = pl.multiple_of(lax.rem(mate[j], 4) * part_cols + start, 128)
                r.vocab_out[:, pl.ds(there, cols)] = traded[j - 1, :, at]
            here = pl.multiple_of(base + start, 128)
            r.vocab_out[:, pl.ds(here, cols)] = summed[quarter // 2, lax.rem(quarter, 2), :, at]

        return Chunk([(0, 2 * r.src_vocab.shape[-2] * cols * 4)], send, take)

    chunks = {}
    for index, (name, start, cols, _) in enumerate(chunk_list(part_cols, width, bits, low_bits, r)):
        chunks[name, start] = make_chunk(index)
        if name == "vocab" and not low_bits:
            chunks[name, start].follow = make_trade(start, cols)

    def put(name, at, product):
        source = getattr(r, "src_" + name)
        source[..., at] = product.reshape(source.shape[:-1] + (product.shape[1],))

    copies = []
    for u in range(utterances):
        at = rows(u)
        three_copies[u].wait()
        three = sent[u] + arrived[u]
        grad_three[u] = three
        low = three.astype(BF16)
        branch_low[at, :] = low
        pre = (dot_nt(low, w_back[...]) * gelu_slope[at, :]).astype(BF16)
        grad_pre[at, :] = pre
        sent[utterances + u] = dot_nt(pre, w_in[...])
        copies.append(swap(sent.at[utterances + u], arrived.at[utterances + u], sibling))
    plan.run_until(plan.now + 8.0)
    for name, left, right in (("back", branch_low, hidden), ("in", norm_low, grad_pre)):
        left_turned = left[...].T
        for start in sorted(s for n, s in chunks if n == name):
            at = pl.ds(start, 512)
            put(name, at, dot_nn(left_turned, right[:, at]))
            plan.run_until(plan.now + 0.5)
            plan.post(chunks[name, start])

    at_core = pl.ds(pl.multiple_of(core * slots, slots), slots)
    at_other = pl.ds(pl.multiple_of((1 - core) * slots, slots), slots)
    base = pl.multiple_of(quarter * part_cols, part_cols)
    pieces = [(c, 256) for c in range(0, part_cols, 256)]
    for j in range(1, 4):
        if j == 2:
            for copy in relays:
                copy.wait()
            share_swaps.append(swap(gathered.at[2, 0], gathered.at[2, 1], sibling))
        meta_swaps[j - 1].wait()
        columns = to_columns(meta[j])
        target, valid, log_total = local_targets(columns[:, 0:1]), columns[:, 1:2], columns[:, 2:3]
        top[j, at_core, :] = gathered[j - 1, 0].astype(BF16)
        share_swaps[j - 1].wait()
        top[j, at_other, :] = gathered[j - 1, 1].astype(BF16)
        for col, cols in pieces:
            ids = base + col + lax.broadcasted_iota(jnp.int32, (1, cols), 1)
            tile = dot_nt(top[j], w_vocab[pl.ds(base + col, cols), :])
            grad = (jnp.exp(tile - log_total) - jnp.where(ids == target, 1.0, 0.0)) * valid
            grad_others[pl.ds((j - 1) * tokens, tokens), pl.ds(col, cols)] = grad.astype(BF16)
    top_turned = r.top_turned
    for j in range(4):
        top_turned[:, pl.ds(j * tokens, tokens)] = top[j].T
    plan.run_until(plan.now + 4.0)
    put("rest", slice(None), dot_nn(top_turned[:, pl.ds(0, tokens)], grad_logits[:, pl.ds(main, 128)]))
    starts = sorted(start for name, start in chunks if name == "vocab")
    for start, stop in zip(starts, starts[1:] + [part_cols]):
        for col in range(start, stop, 256):
            cols = min(256, stop - col)
            product = dot_nn(top_turned[:, pl.ds(0, tokens)], grad_logits[:, pl.ds(base + col, cols)])
            product = product + dot_nn(
                top_turned[:, pl.ds(tokens, 3 * tokens)], grad_others[:, pl.ds(col, cols)]
            )
            put("vocab", pl.ds(col, cols), product)
        plan.run_until(plan.now + 0.7)
        plan.post(chunks["vocab", start])
    plan.post(chunks["rest", 0])

    one_copies = []
    gain_2_total, bias_2_total = 0.0, 0.0
    for u in range(utterances):
        at = rows(u)
        copies[u].wait()
        grad_norm = sent[utterances + u] + arrived[utterances + u]
        hat, scale = normalise(stream_two[at, :])
        gain_2_total = gain_2_total + jnp.sum(grad_norm * hat, axis=0, keepdims=True)
        bias_2_total = bias_2_total + jnp.sum(grad_norm, axis=0, keepdims=True)
        two = grad_three[u] + normalise_back(grad_norm * gain_2, hat, scale)
        grad_two[at, :] = two
        low = two.astype(BF16)
        att_low[at, :] = low
        grad_mixed = dot_nt(low, w_out[...]).astype(BF16)
        for h in range(heads):
            cols = pl.ds(h * HD, HD)
            grad_head = grad_mixed[:, h * HD : (h + 1) * HD]
            prob = probs[u, h]
            grad_prob = dot_nt(grad_head, value_of(u, h))
            spare[pl.ds(u * frames, frames), pl.ds(half + h * HD, HD)] = dot_tn(
                prob.astype(BF16), grad_head
            ).astype(BF16)
            inner = jnp.sum(prob * grad_prob, axis=-1, keepdims=True)
            grad_score = (prob * (grad_prob - inner)).astype(BF16)
            grad_queries[at, cols] = (dot_nn(grad_score, key_of(u, h)) * score_scale).astype(BF16)
            spare[pl.ds(u * frames, frames), cols] = (
                dot_tn(grad_score, queries[at, cols]) * score_scale
            ).astype(BF16)
            plan.run_until(plan.now + 1.5)
        sent[u] = dot_nt(grad_queries[at, :], w_query[...])
        one_copies.append(swap(sent.at[u], arrived.at[u], sibling))
    every = slice(None)
    put("out", every, dot_tn(att_low[...], mixed[...]))
    plan.post(chunks["out", 0])
    put("query", every, dot_tn(one_low[...], grad_queries[...]))
    plan.post(chunks["query", 0])
    plan.run_until(plan.now + 1.0)

    mem_copies = []
    rate_sums = [0.0, 0.0]
    for u in range(utterances):
        total = jnp.zeros((1, width), F32)
        for i in range(row_chunks):
            at = pl.ds(u * frames + i * step_rows, step_rows)
            part = dot_nt(spare[at, :], w_kv[...])
            for j in range(width // 128):
                side_of, tile = j // (width // 256), j % (width // 256)
                index = ((side_of * utterances + u) * row_chunks + i) * (width // 256) + tile
                logits[index] = part[:, j * 128 : (j + 1) * 128]
            total = total + jnp.sum(part, axis=0, keepdims=True)
        tiles = row_chunks * (width // 256)
        mem_copies.append(
            swap(
                logits.at[pl.ds(((1 - core) * utterances + u) * tiles, tiles)],
                mem_arrived.at[pl.ds(u * tiles, tiles)],
                sibling,
            )
        )
        group = jnp.zeros((1, width), jnp.int32) + rate_groups[u]
        for k in range(2):
            rate_sums[k] = rate_sums[k] + jnp.where((group == 1) == (k == 1), total, 0.0)
        plan.run_until(plan.now + 1.2)
    span = frames // 2
    for k in range(2 * utterances):
        at = pl.ds(k * span, span)
        product = dot_tn(mem_low[at, :], spare[at, :])
        product = product.reshape(r.src_kv.shape)
        r.src_kv[...] = product if k == 0 else r.src_kv[...] + product
    plan.run_until(plan.now + 2.0)
    plan.post(*[chunks["kv", start] for start in sorted(s for n, s in chunks if n == "kv")])

    gain_1_total, bias_1_total = 0.0, 0.0
    for u in range(utterances):
        at = rows(u)
        valid = own_valid[u * slots : (u + 1) * slots]
        one_copies[u].wait()
        one = grad_two[at, :] + (sent[u] + arrived[u])
        grad_two[at, :] = one
        masked = one * valid
        for k in range(kernel_rows.shape[0]):
            shift = 8 + k - kernel_rows.shape[0] // 2
            row = jnp.sum(masked * padded[u, pl.ds(shift, slots), :], axis=0, keepdims=True)
            if u == 0:
                small_sent[0, pl.ds(k, 1), :] = row
            else:
                small_sent[0, pl.ds(k, 1), :] = small_sent[0, pl.ds(k, 1), :] + row
        padded[u, pl.ds(8, slots), :] = masked
        for j in range(width // 128):
            cols = pl.ds(j * 128, 128)
            total = jnp.zeros((slots, 128), F32)
            for k in range(kernel_rows.shape[0]):
                shift = 8 - k + kernel_rows.shape[0] // 2
                total = total + kernel_rows[pl.ds(k, 1), cols] * padded[u, pl.ds(shift, slots), cols]
            stream_one[at, cols] = total * valid
        grad_norm = stream_one[at, :]
        hat, scale = normalise(stream_in[at, :])
        gain_1_total = gain_1_total + jnp.sum(grad_norm * hat, axis=0, keepdims=True)
        bias_1_total = bias_1_total + jnp.sum(grad_norm, axis=0, keepdims=True)
        zero = grad_two[at, :] + normalise_back(grad_norm * gain_1, hat, scale)
        terms[u] = blend[u * slots : (u + 1) * slots] * zero
        stream_one[at, :] = zero - terms[u]
        plan.run_until(plan.now + 1.5)

    last_taps = kernel_rows.shape[0]
    small_sent[0, pl.ds(last_taps, 12 - last_taps), :] = jnp.zeros((12 - last_taps, width), F32)
    for i, row in enumerate((gain_1_total, bias_1_total, gain_2_total, bias_2_total)):
        small_sent[0, pl.ds(12 + i, 1), :] = row
    for k in range(2):
        small_sent[0, pl.ds(16 + k, 1), :] = rate_sums[k]
    small_sent[0, pl.ds(18, 6), :] = jnp.zeros((6, width), F32)
    small_peers = [peer_of[b] for b in low_bits + bits] + [sibling]

    def small_send(step):
        copy = pltpu.make_async_remote_copy(
            src_ref=small_sent.at[step],
            dst_ref=small_arrived.at[step],
            send_sem=r.small_send.at[step],
            recv_sem=r.small_recv.at[step],
            device_id=small_peers[step],
            device_id_type=MESH,
        )
        copy.start()
        return copy

    def small_take(step, copy):
        copy.wait_recv()
        if step + 1 < len(small_peers):
            small_sent[step + 1] = small_sent[step] + small_arrived[step]
        else:
            r.small_out[pl.ds(0, 16), :] = small_sent[step, pl.ds(0, 16), :]
            r.small_out[pl.ds(16, 8), :] = (
                small_sent[step, pl.ds(16, 8), :] + small_arrived[step, pl.ds(16, 8), :]
            )

    small_links = [link_of(b, bits) for b in low_bits + bits] + ["core"]
    plan.post(Chunk([(l, 24 * width * 4) for l in small_links], small_send, small_take))

    features = width // n_dp
    feature_rows = max(features, 8)
    block_rows = term_blocks.shape[1]
    turned = terms[core].T
    id_row = targets[pl.ds(core, 1), :].astype(F32)
    rest = block_rows - features - 1
    for p in range(n_dp):
        term_blocks[p, pl.ds(0, features), :] = turned[p * features : (p + 1) * features]
        term_blocks[p, pl.ds(features, 1), :] = id_row
        term_blocks[p, pl.ds(features + 1, rest), :] = jnp.zeros((rest, slots), F32)

    def term_copy(k):
        there = lax.rem(me + k, n_dp)
        return pltpu.make_async_remote_copy(
            src_ref=term_blocks.at[there],
            dst_ref=term_arrived.at[me],
            send_sem=r.term_send.at[k],
            recv_sem=r.term_recv.at[k],
            device_id={"dp": there},
            device_id_type=MESH,
        )

    def term_start(k, carry):
        term_copy(k).start()
        return carry

    def term_wait(k, carry):
        term_copy(k).wait()
        return carry

    term_arrived[me] = term_blocks[me]
    lax.fori_loop(1, n_dp, term_start, 0)
    stores = []

    def store(source, target):
        copy = pltpu.make_async_copy(source, target, r.store_sem.at[len(stores)])
        copy.start()
        stores.append(copy)

    store(stream_one, r.acoustic_out)
    for u in range(utterances):
        mem_copies[u].wait()
        for i in range(row_chunks):
            for j in range(width // 256):
                index = (u * row_chunks + i) * (width // 256) + j
                first_tile = (core * utterances) * row_chunks * (width // 256)
                mem_arrived[index] = logits[first_tile + index] + mem_arrived[index]
                at = pl.ds(u * frames + i * step_rows, step_rows)
                store(mem_arrived.at[index], r.memory_out.at[at, pl.ds(j * 128, 128)])
    plan.run_until(plan.now + 8.0)
    lax.fori_loop(1, n_dp, term_wait, 0)
    per_piece = 512 // slots
    blocks_hi = table_out.shape[1] // 256
    batch = 4

    def table_piece(p, fresh):
        found = [term_arrived[p * per_piece + i] for i in range(per_piece)]
        values = jnp.concatenate([f[:feature_rows] for f in found], axis=1)
        ids = jnp.concatenate([f[features : features + 1] for f in found], axis=1).astype(jnp.int32)
        low_ids, high_ids = ids & 255, ids >> 8
        onehot_lo[...] = jnp.where(
            lax.broadcasted_iota(jnp.int32, (256, 512), 0) == low_ids, 1.0, 0.0
        ).astype(BF16)
        coarse = values.astype(BF16).astype(F32)
        both = jnp.concatenate([coarse, values - coarse], axis=0)
        for first_hi in range(0, blocks_hi, batch):
            here = range(first_hi, min(first_hi + batch, blocks_hi))
            masked = jnp.concatenate([jnp.where(high_ids == hi, both, 0.0) for hi in here], axis=0)
            product = dot_nt(masked.astype(BF16), onehot_lo[...])
            for i, hi in enumerate(here):
                top_part = product[2 * i * feature_rows : (2 * i + 1) * feature_rows]
                low_part = product[(2 * i + 1) * feature_rows : (2 * i + 2) * feature_rows]
                at = pl.ds(hi * 256, 256)
                if fresh:
                    table_out[:, at] = top_part + low_part
                else:
                    table_out[:, at] = table_out[:, at] + (top_part + low_part)

    pieces = n_dp // per_piece
    table_piece(0, True)
    if pieces <= 4:
        for p in range(1, pieces):
            plan.run_until(plan.now + 1.5)
            table_piece(p, False)
    else:
        lax.fori_loop(1, pieces, lambda p, c: (table_piece(p, False), c)[1], 0)
    table_swap = swap(table_out, table_theirs, sibling)
    plan.run_until(plan.now + 8.0)
    table_swap.wait()
    whole_table = r.whole_table
    whole_table[...] = (
        table_out[pl.ds(0, whole_table.shape[0]), :] + table_theirs[pl.ds(0, whole_table.shape[0]), :]
    )[:, :table_rows]
    store(whole_table, r.table_out)
    plan.finish()
    if not low_bits:
        rest = vocab_here - main
        r.vocab_out[:, pl.ds(main, rest)] = r.rest_out[...][:, :rest]
    for copy in stores:
        copy.wait()


def link_of(bit, bits):
    if bit == bits[-1]:
        return bits[-2]
    return bit


def chunk_list(part_cols, width, bits, low_bits, sizes):
    turned = [bits[1], bits[0]] + bits[2:]
    listing = []
    for start in range(0, part_cols, 512):
        listing.append(("vocab", start, 512, [b for b in bits if b > 1]))
    for name in ("back", "in"):
        for k, start in enumerate(range(0, sizes.units, 512)):
            listing.append((name, start, 512, [bits, turned][k % 2]))
    listing.append(("rest", 0, 128, turned))
    listing.append(("out", 0, sizes.half, bits))
    listing.append(("query", 0, sizes.half, bits))
    for start in range(0, 2 * sizes.half, 256):
        listing.append(("kv", start, 256, turned))
    return listing


def decoder_call(
    acoustic, memory, embedding, w_query, w_key, w_value, w_out, w_in, w_back, w_vocab, norms,
    fsmn_kernel, rate_table, token_lengths, memory_lengths, rate_groups, glance, targets, n_dp,
):
    utterances = token_lengths.shape[0]
    tokens, width = acoustic.shape
    slots = tokens // utterances
    mem_rows = memory.shape[0]
    half = w_query.shape[1]
    heads = half // HD
    frames = mem_rows // utterances
    units = w_in.shape[1]
    vocab_here = w_vocab.shape[1]
    table_rows = embedding.shape[0]
    part_cols = vocab_here // 512 * 128
    all_cols = 4 * part_cols + 128
    w_turned = w_vocab.T
    mains = table_rows // 2048 * 2048
    nbits = n_dp.bit_length() - 1
    steps = nbits
    while width >> steps < 8:
        steps -= 1
    low_bits, bits = list(range(nbits - steps)), list(range(nbits - steps, nbits))
    rows = width >> steps
    features = width // n_dp
    feature_rows = max(features, 8)
    block_rows = feature_rows + 8 if features >= 8 else 8
    blocks_hi = (table_rows + 255) // 256
    sizes = SimpleNamespace(units=units, half=half)
    plane = [b for b in bits if b < 2]
    listing = chunk_list(part_cols, width, bits, low_bits, sizes)
    most = max(len(c[3]) for c in listing)

    f32 = lambda *shape: jax.ShapeDtypeStruct(shape, F32)
    v32 = lambda *shape: pltpu.VMEM(shape, F32)
    v16 = lambda *shape: pltpu.VMEM(shape, BF16)
    dma = lambda *shape: pltpu.SemaphoreType.DMA(shape)
    inputs = dict(
        acoustic=(VMEM, acoustic),
        table_tail=(VMEM, embedding[mains:]),
        memory=(ANY, memory),
        table=(ANY, embedding),
        w_query_hbm=(ANY, w_query),
        w_key_hbm=(ANY, w_key),
        w_value_hbm=(ANY, w_value),
        w_out_hbm=(ANY, w_out),
        w_in_hbm=(ANY, w_in),
        w_back_hbm=(ANY, w_back),
        w_vocab_hbm=(ANY, w_turned),
        gain_one=(VMEM, norms[0][None]),
        bias_one=(VMEM, norms[1][None]),
        gain_two=(VMEM, norms[2][None]),
        bias_two=(VMEM, norms[3][None]),
        kernel_rows=(VMEM, fsmn_kernel),
        rate_table=(VMEM, rate_table),
        token_lengths=(SMEM, token_lengths),
        memory_lengths=(SMEM, memory_lengths),
        rate_groups=(SMEM, rate_groups),
        glance=(VMEM, glance.reshape(utterances, slots)),
        targets=(VMEM, targets.reshape(utterances, slots)),
    )
    outputs = dict(
        loss_out=f32(utterances, slots),
        small_out=f32(24, width),
        vocab_out=f32(2, rows, part_cols) if low_bits else f32(rows, vocab_here),
        rest_out=f32(rows, 128),
        in_out=f32(rows, units),
        back_out=f32(rows, units),
        query_out=f32(rows, half),
        out_out=f32(rows, half),
        key_out=f32(rows, half),
        value_out=f32(rows, half),
        acoustic_out=f32(tokens, width),
        memory_out=f32(mem_rows, width // 2),
        table_out=f32(features, table_rows),
    )
    shape = (2,) * steps + (rows,)
    scratch = dict(
        w_query=v16(width, half),
        w_kv=v16(width, 2 * half),
        w_out=v16(half, width),
        w_in=v16(width, units),
        w_back=v16(units, width),
        w_vocab=v16(vocab_here, width),
        w_rest=v16(128, width),
        mem_low=v16(mem_rows, width),
        kv=v16(mem_rows, 2 * half),
        spare=v16(mem_rows, 2 * half),
        padded=v32(utterances, slots + 16, width),
        stream_in=v32(tokens, width),
        stream_one=v32(tokens, width),
        stream_two=v32(tokens, width),
        stream_three=v32(utterances, slots, width),
        one_low=v16(tokens, width),
        queries=v16(tokens, half),
        probs=v32(utterances, heads, slots, frames),
        mixed=v16(tokens, half),
        norm_low=v16(tokens, width),
        hidden=v16(tokens, units),
        gelu_slope=v32(tokens, units),
        top=v16(4, tokens, width),
        logits=v32(all_cols // 128, tokens, 128),
        grad_logits=v16(tokens, all_cols),
        grad_others=v16(3 * tokens, part_cols),
        top_turned=v16(width, 4 * tokens),
        taken_mine=v32(utterances, slots, width),
        taken_theirs=v32(utterances, slots, width),
        grad_three=v32(utterances, slots, width),
        grad_two=v32(tokens, width),
        branch_low=v16(tokens, width),
        grad_pre=v16(tokens, units),
        att_low=v16(tokens, width),
        grad_queries=v16(tokens, half),
        mem_arrived=v32(mem_rows // 256 * (width // 256), 256, 128),
        meta=v32(4, 8, tokens),
        stats=v32(2, tokens, 128),
        stats_arrived=v32(2, tokens, 128),
        sent=v32(2 * utterances, slots, width),
        arrived=v32(2 * utterances, slots, width),
        gathered=v32(3, 2, slots, width),
        small_sent=v32(nbits + 1, 24, width),
        small_arrived=v32(nbits + 1, 24, width),
        term_blocks=v32(n_dp, block_rows, slots),
        term_arrived=v32(n_dp, block_rows, slots),
        onehot_lo=v16(256, 512),
        table_rest=v16((table_rows - mains + 127) // 128 * 128, width),
        table_theirs=v32(feature_rows, blocks_hi * 256),
        table_mine=v32(feature_rows, blocks_hi * 256),
        src_vocab=v32(*shape, part_cols),
        src_rest=v32(*shape, 128),
        whole_table=v32(features, table_rows),
        src_back=v32(*shape, units),
        vocab_sum=v32(*(2,) * len(plane), rows, part_cols),
        vocab_traded=v32(3, rows, part_cols),
        src_in=v32(*shape, units),
        src_out=v32(*shape, half),
        src_query=v32(*shape, half),
        src_kv=v32(*shape, 2 * half),
        load_sem=dma(24),
        store_sem=dma(24),
        trade_send=dma(part_cols // 128, 3),
        trade_recv=dma(part_cols // 128, 3),
        swap_send=dma(40),
        swap_recv=dma(40),
        scatter_send=dma(len(listing), most),
        scatter_recv=dma(len(listing), most),
        small_send=dma(nbits + 1),
        small_recv=dma(nbits + 1),
        term_send=dma(n_dp),
        term_recv=dma(n_dp),
    )
    landing = [
        [v32(*(2,) * (steps - 1 - s), rows, cols) for s in range(len(order))]
        for _, _, cols, order in listing
    ]
    names = list(inputs) + list(outputs) + list(scratch)
    flat = [ref for chunk in landing for ref in chunk]

    def kernel(*refs):
        named, rest = refs[: len(names)], list(refs[len(names) :])
        lands = [[rest.pop(0) for _ in chunk] for chunk in landing]
        decoder_kernel(
            names + ["landing", "units", "half"], vocab_here, part_cols, table_rows, n_dp, bits,
            low_bits, *named, lands, units, half,
        )

    out = pl.pallas_call(
        kernel,
        out_shape=list(outputs.values()),
        in_specs=[spec for spec, _ in inputs.values()],
        out_specs=[VMEM] * (len(outputs) - 3) + [ANY] * 3,
        scratch_shapes=list(scratch.values()) + flat,
        compiler_params=pltpu.CompilerParams(
            collective_id=1, has_side_effects=True, vmem_limit_bytes=64 << 20
        ),
    )(*[value for _, value in inputs.values()])
    return SimpleNamespace(**dict(zip(outputs, out))), low_bits


def deliver_kernel(n_dp, n_passed, *refs):
    n = n_passed + 2
    sources, targets, held = refs[:n], refs[n : 2 * n + 5], refs[2 * n + 5 : 3 * n + 5]
    sem_in, sem_out = refs[3 * n + 5 :]
    reads, writes = [], []
    for i, (source, buffer) in enumerate(zip(sources, held)):
        reads.append(pltpu.make_async_copy(source, buffer, sem_in.at[i]))
        reads[-1].start()
    for i in range(n_passed):
        reads[i].wait()
        writes.append(pltpu.make_async_copy(held[i], targets[i], sem_out.at[i]))
        writes[-1].start()
    reads[n_passed].wait()
    reads[n_passed + 1].wait()
    loss, small = held[n_passed:]
    loss_to, gain_one_to, bias_one_to, gain_two_to, bias_two_to, taps_to, rate_to = targets[n_passed:]
    slots = loss.shape[1]
    for u in range(loss.shape[0]):
        loss_to[:, pl.ds(u * slots, slots)] = loss[pl.ds(u, 1), :]
    me = lax.axis_index("dp")
    own = small.shape[1] // n_dp
    mine = jnp.zeros((16, own), F32)
    for p in range(n_dp):
        mine = jnp.where(me == p, small[pl.ds(0, 16), p * own : (p + 1) * own], mine)
    taps_to[...] = mine[: taps_to.shape[0]]
    for i, target in enumerate((gain_one_to, bias_one_to, gain_two_to, bias_two_to)):
        target[...] = mine[12 + i : 13 + i]
    rate_to[...] = small[pl.ds(16, 2), :]
    for copy in writes:
        copy.wait()


def per_device(
    acoustic,
    memory,
    embedding,
    w_query,
    w_key,
    w_value,
    w_out,
    w_in,
    w_back,
    w_vocab,
    gain_one,
    bias_one,
    gain_two,
    bias_two,
    fsmn_kernel,
    rate_table,
    token_lengths,
    memory_lengths,
    rate_groups,
    glance_mask,
    targets,
):
    tok_rows, model_width = acoustic.shape
    half = w_query.shape[1]
    n_dp = lax.axis_size("dp")
    result, low_bits = decoder_call(
        acoustic, memory, embedding, w_query, w_key, w_value, w_out, w_in, w_back, w_vocab,
        (gain_one, bias_one, gain_two, bias_two), fsmn_kernel, rate_table,
        token_lengths, memory_lengths, rate_groups, glance_mask, targets, n_dp,
    )
    vocab = result.vocab_out
    summed = [
        result.query_out, result.key_out, result.value_out, result.out_out, result.in_out,
        result.back_out,
    ]
    if low_bits:
        size = 1 << len(low_bits)
        groups = [list(range(g * size, (g + 1) * size)) for g in range(n_dp // size)]
        planes = [list(range(4 * g, 4 * g + 4)) for g in range(n_dp // 4)]
        vocab = lax.all_to_all(
            vocab.reshape(4, model_width // n_dp, -1), "dp", 0, 0, axis_index_groups=planes, tiled=True
        )
        *summed, rest = [
            lax.psum_scatter(s, "dp", scatter_dimension=0, axis_index_groups=groups, tiled=True)
            for s in (*summed, result.rest_out)
        ]
        vocab = jnp.concatenate([*vocab, rest], axis=1)[:, : w_vocab.shape[1]]
    own = model_width // n_dp
    f32 = lambda *shape: jax.ShapeDtypeStruct(shape, F32)
    like = lambda x: jax.ShapeDtypeStruct(x.shape, F32)
    passed = (result.memory_out, result.table_out, result.acoustic_out, vocab, *summed)
    handed = (*passed, result.loss_out, result.small_out)
    (
        grad_memory, grad_table, grad_acoustic, grad_vocab, grad_query, grad_key, grad_value,
        grad_out, grad_in, grad_back, token_loss, gain_1, bias_1, gain_2, bias_2, grad_taps, grad_rate,
    ) = pl.pallas_call(
        partial(deliver_kernel, n_dp, len(passed)),
        out_shape=[
            *[like(x) for x in passed],
            f32(1, tok_rows),
            *[f32(1, own)] * 4,
            f32(fsmn_kernel.shape[0], own),
            f32(2, model_width),
        ],
        in_specs=[ANY] * len(handed),
        out_specs=[ANY] * len(passed) + [VMEM] * 7,
        scratch_shapes=[pltpu.VMEM(x.shape, F32) for x in handed]
        + [pltpu.SemaphoreType.DMA((len(handed),)), pltpu.SemaphoreType.DMA((len(handed),))],
        compiler_params=pltpu.CompilerParams(vmem_limit_bytes=60 << 20),
    )(*handed)
    return (
        token_loss.reshape(tok_rows),
        grad_acoustic,
        grad_memory,
        grad_table.T,
        grad_query,
        grad_key,
        grad_value,
        grad_out.T,
        grad_in,
        grad_back.T,
        grad_vocab,
        gain_1.reshape(own),
        bias_1.reshape(own),
        gain_2.reshape(own),
        bias_2.reshape(own),
        grad_taps,
        grad_rate,
    )


def solution(mesh):
    return jax.shard_map(
        per_device,
        mesh=mesh,
        in_specs=(
            P("dp", None),
            P("dp", None),
            P(),
            P(None, "mp"),
            P(None, "mp"),
            P(None, "mp"),
            P("mp", None),
            P(None, "mp"),
            P("mp", None),
            P(None, "mp"),
            P(),
            P(),
            P(),
            P(),
            P(),
            P(),
            P("dp"),
            P("dp"),
            P("dp"),
            P("dp"),
            P("dp"),
        ),
        out_specs=(
            P("dp"),
            P("dp", None),
            P("dp", "mp"),
            P(None, "dp"),
            P("dp", "mp"),
            P("dp", "mp"),
            P("dp", "mp"),
            P("mp", "dp"),
            P("dp", "mp"),
            P("mp", "dp"),
            P("dp", "mp"),
            P("dp"),
            P("dp"),
            P("dp"),
            P("dp"),
            P(None, "dp"),
            P(),
        ),
        check_vma=False,
    )
```

```python
from functools import partial
import math
from types import SimpleNamespace

import jax
import jax.numpy as jnp
from jax import lax
from jax.experimental import pallas as pl
from jax.experimental.pallas import tpu as pltpu
from jax.sharding import PartitionSpec as P

HD = 128
V = 8404
EPSILON = 1e-05
MESH = pl.DeviceIdType.MESH
VMEM = pl.BlockSpec(memory_space=pltpu.VMEM)
SMEM = pl.BlockSpec(memory_space=pltpu.SMEM)
ANY = pl.BlockSpec(memory_space=pl.ANY)
F32, BF16 = jnp.float32, jnp.bfloat16
NEG = -1e30


def other_core():
    return {"mp": 1 - lax.axis_index("mp")}


def dot_nn(a, b):
    return lax.dot_general(a, b, (((1,), (0,)), ((), ())), preferred_element_type=F32)


def dot_nt(a, b):
    return lax.dot_general(a, b, (((1,), (1,)), ((), ())), preferred_element_type=F32)


def dot_tn(a, b):
    return lax.dot_general(a, b, (((0,), (0,)), ((), ())), preferred_element_type=F32)


def normalise(rows):
    average = jnp.mean(rows, axis=-1, keepdims=True)
    centred = rows - average
    variance = jnp.mean(centred * centred, axis=-1, keepdims=True)
    scale = lax.rsqrt(variance + EPSILON)
    return centred * scale, scale


def normalise_back(grad_hat, hat, scale):
    first = jnp.mean(grad_hat, axis=-1, keepdims=True)
    second = jnp.mean(grad_hat * hat, axis=-1, keepdims=True)
    return scale * (grad_hat - first - hat * second)


def side_by_side(columns):
    lane = lax.broadcasted_iota(jnp.int32, (columns[0].shape[0], 128), 1)
    tile = jnp.zeros(lane.shape, F32)
    for i, column in enumerate(columns):
        tile = jnp.where(lane == i, column, tile)
    return tile


def to_rows(columns):
    return side_by_side(columns).T[:8]


def to_columns(rows):
    return jnp.concatenate([rows] * 16, axis=0).T


class Planner:
    RATE = 0.045e6
    HOP = 1.5
    BACKLOG = 3.0

    def __init__(self):
        self.now = 0.0
        self.free = {}
        self.flying = []
        self.waiting = []
        self.started = []
        self.count = 0

    def launch(self, item, step):
        link, size = item.steps[step]
        begin = max(self.now, self.free.get(link, 0.0))
        self.free[link] = begin + size / self.RATE
        copy = item.send(step)
        self.started.append(copy)
        self.count += 1
        self.flying.append((self.free[link] + self.HOP, self.count, item, step, copy))

    def release(self):
        kept = []
        for item in self.waiting:
            link = item.steps[0][0]
            if self.free.get(link, 0.0) - self.now < self.BACKLOG:
                self.launch(item, 0)
            else:
                kept.append(item)
        self.waiting = kept

    def post(self, *items):
        self.waiting += items
        self.release()

    def run_until(self, time):
        while self.flying or self.waiting:
            if not self.flying:
                self.now = max(self.now, min(self.free[i.steps[0][0]] for i in self.waiting))
                self.release()
                continue
            first = min(self.flying, key=lambda f: f[:2])
            if first[0] > time:
                break
            self.flying.remove(first)
            self.now = max(self.now, first[0])
            _, _, item, step, copy = first
            item.take(step, copy)
            if step + 1 < len(item.steps):
                self.launch(item, step + 1)
            elif item.follow is not None:
                self.launch(item.follow, 0)
            self.release()
        if time != math.inf:
            self.now = max(self.now, time)
        self.release()

    def finish(self):
        self.run_until(math.inf)
        for copy in self.started:
            copy.wait_send()


class Chunk:
    def __init__(self, steps, send, take):
        self.steps, self.send, self.take, self.follow = steps, send, take, None


class Several:
    def __init__(self, copies):
        self.copies = copies

    def wait_recv(self):
        for copy in self.copies:
            copy.wait_recv()

    def wait_send(self):
        for copy in self.copies:
            copy.wait_send()


def decoder_kernel(
    names,
    vocab_here,
    part_cols,
    table_rows,
    n_dp,
    bits,
    low_bits,
    *refs,
):
    r = SimpleNamespace(**dict(zip(names, refs)))
    acoustic, memory, table = r.acoustic, r.memory, r.table
    targets, glance = r.targets, r.glance
    gain_1, bias_1 = r.gain_one[...], r.bias_one[...]
    gain_2, bias_2 = r.gain_two[...], r.bias_two[...]
    kernel_rows, rate_table = r.kernel_rows, r.rate_table
    token_lengths, memory_lengths, rate_groups = r.token_lengths, r.memory_lengths, r.rate_groups
    w_query, w_kv, w_out, w_in, w_back, w_vocab = r.w_query, r.w_kv, r.w_out, r.w_in, r.w_back, r.w_vocab
    mem_low, kv, padded, spare = r.mem_low, r.kv, r.padded, r.spare
    stream_in, stream_one, stream_two, stream_three = r.stream_in, r.stream_one, r.stream_two, r.stream_three
    one_low, queries, probs, mixed = r.one_low, r.queries, r.probs, r.mixed
    norm_low, hidden, gelu_slope, top = r.norm_low, r.hidden, r.gelu_slope, r.top
    logits, grad_logits, grad_others = r.logits, r.grad_logits, r.grad_others
    taken_mine, taken_theirs = r.grad_three, r.taken_theirs
    grad_three, grad_two, branch_low = r.grad_three, r.grad_two, r.branch_low
    grad_pre, att_low, grad_queries = r.grad_pre, r.att_low, r.grad_queries
    mem_arrived, meta, stats, stats_arrived = r.mem_arrived, r.meta, r.stats, r.stats_arrived
    sent, arrived, gathered = r.sent, r.arrived, r.gathered
    small_sent, small_arrived = r.small_sent, r.small_arrived
    terms, term_blocks, term_arrived = grad_three, r.term_blocks, r.term_arrived
    onehot_lo, table_theirs, whole_table = r.onehot_lo, r.table_theirs, r.whole_table
    swap_send, swap_recv, load_sem = r.swap_send, r.swap_recv, r.load_sem

    utterances, slots = targets.shape
    width = acoustic.shape[1]
    frames = memory.shape[0] // utterances
    half = w_query.shape[1]
    heads = half // HD
    tokens = utterances * slots
    me, core = lax.axis_index("dp"), lax.axis_index("mp")
    sibling = {"mp": 1 - core}
    quarter = lax.rem(me, 4)
    flips = [1 - 2 * lax.rem(me, 2), 2 - 4 * lax.rem(me // 2, 2)]
    mate = [me + flips[0] * (j % 2) + flips[1] * (j // 2) for j in range(4)]
    bit_of = {b: lax.rem(me // (1 << b), 2) for b in low_bits + bits}
    peer_of = {b: {"dp": me + (1 - 2 * bit_of[b]) * (1 << b)} for b in low_bits + bits}
    score_scale = 1.0 / math.sqrt(HD)

    loads = []

    def load(source, target):
        copy = pltpu.make_async_copy(source, target, load_sem.at[len(loads)])
        copy.start()
        loads.append(copy)
        return copy

    load_memory = load(memory, mem_low)
    load_kv = [
        load(r.w_key_hbm, w_kv.at[:, pl.ds(0, half)]),
        load(r.w_value_hbm, w_kv.at[:, pl.ds(half, half)]),
    ]
    load_query = load(r.w_query_hbm, w_query)
    load_out = load(r.w_out_hbm, w_out)

    barrier = pltpu.get_barrier_semaphore()

    def greet(k, carry):
        pl.semaphore_signal(
            barrier, inc=1, device_id={"dp": lax.rem(me + k, n_dp)}, device_id_type=MESH
        )
        return carry

    lax.fori_loop(1, n_dp, greet, 0)
    pl.semaphore_signal(barrier, inc=1, device_id=sibling, device_id_type=MESH)

    load_in = load(r.w_in_hbm, w_in)
    load_back = load(r.w_back_hbm, w_back)
    block = 1024
    per_core = table_rows // (2 * block)
    mains = 2 * per_core * block

    def load_table(k):
        at = pl.ds(pl.multiple_of((core * per_core + k) * block, block), block)
        return load(table.at[at, :], spare.at[pl.ds(k % 2 * block, block), :])

    table_loads = [load_table(0), load_table(1)]
    main = 4 * part_cols
    load_vocab = load(r.w_vocab_hbm, w_vocab)
    w_rest = r.w_rest
    w_rest[...] = jnp.zeros(w_rest.shape, BF16)
    rest_rows = (table_rows - mains) // 16 * 16
    r.table_rest[...] = jnp.zeros(r.table_rest.shape, BF16)
    load_rest = load(table.at[pl.ds(mains, rest_rows), :], r.table_rest.at[pl.ds(0, rest_rows), :])
    r.table_rest[pl.ds(rest_rows, table_rows - mains - rest_rows), :] = r.table_tail[...]

    stores = []

    def store(source, target):
        copy = pltpu.make_async_copy(source, target, r.store_sem.at[len(stores)])
        copy.start()
        stores.append(copy)

    swaps = []

    def swap(source, target, device):
        k = len(swaps)
        copy = pltpu.make_async_remote_copy(
            src_ref=source,
            dst_ref=target,
            send_sem=swap_send.at[k],
            recv_sem=swap_recv.at[k],
            device_id=device,
            device_id_type=MESH,
        )
        copy.start()
        swaps.append(copy)
        return copy

    lane = lax.broadcasted_iota(jnp.int32, (1, slots), 1)
    row_of = lax.broadcasted_iota(jnp.int32, (8, slots), 0)
    for u in range(utterances):
        target_row = targets[pl.ds(u, 1), :].astype(F32)
        glance_row = glance[pl.ds(u, 1), :].astype(F32)
        valid_row = (lane < token_lengths[u]).astype(F32)
        meta[0, :, pl.ds(u * slots, slots)] = jnp.where(
            row_of == 0, target_row, jnp.where(row_of == 1, valid_row, glance_row)
        )
    own_columns = to_columns(meta[0])
    own_target = own_columns[:, 0:1]
    own_valid = own_columns[:, 1:2]

    def rows(u):
        return pl.ds(u * slots, slots)

    edge = jnp.zeros((8, width), F32)
    for u in range(utterances):
        padded[u, pl.ds(0, 8), :] = edge
        padded[u, pl.ds(8 + slots, 8), :] = edge

    step_rows = 256
    row_chunks = frames // step_rows

    def key_of(u, h):
        return kv[pl.ds(u * frames, frames), pl.ds(h * HD, HD)]

    def value_of(u, h):
        return kv[pl.ds(u * frames, frames), pl.ds(half + h * HD, HD)]

    frame_lane = lax.broadcasted_iota(jnp.int32, (1, frames), 1)

    def look_up(first_row, count, allowed, source):
        ids = first_row + lax.broadcasted_iota(jnp.int32, (1, count), 1)
        local = jnp.where(allowed, own_target.astype(jnp.int32), -1)
        onehot = jnp.where(ids == local, 1.0, 0.0).astype(BF16)
        return dot_nn(onehot, source)

    def look_up_block(k):
        table_loads[k].wait()
        part = look_up(
            (core * per_core + k) * block, block, True, spare[pl.ds(k % 2 * block, block), :]
        )
        for u in range(utterances):
            piece = part[u * slots : (u + 1) * slots]
            taken_mine[u] = piece if k == 0 else taken_mine[u] + piece
        if k + 2 < per_core:
            table_loads.append(load_table(k + 2))

    def look_up_rest():
        load_rest.wait()
        part = look_up(mains, r.table_rest.shape[0], core == 0, r.table_rest[...])
        for u in range(utterances):
            taken_mine[u] = taken_mine[u] + part[u * slots : (u + 1) * slots]

    def local_targets(target_column):
        local = target_column.astype(jnp.int32) - core * vocab_here
        return jnp.where((local >= 0) & (local < vocab_here), local, -1)

    def vocab_stats(target, keep=False):
        tiles = main // 128
        step_tiles = 4

        ids = main + lax.broadcasted_iota(jnp.int32, (1, 128), 1)
        last = jnp.where(ids < vocab_here, dot_nt(top[0], w_rest[...]), NEG)
        logits[tiles] = last
        top_m, picked = last, jnp.where(ids == target, last, 0.0)
        for j in range(tiles // step_tiles):
            col = j * step_tiles * 128
            product = dot_nt(top[0], w_vocab[pl.ds(col, step_tiles * 128), :])
            for i in range(step_tiles):
                tile = product[:, i * 128 : (i + 1) * 128]
                ids = col + i * 128 + lax.broadcasted_iota(jnp.int32, (1, 128), 1)
                logits[j * step_tiles + i] = tile
                top_m = jnp.maximum(top_m, tile)
                picked = picked + jnp.where(ids == target, tile, 0.0)
        top_row = jnp.max(top_m, axis=1, keepdims=True)

        def add(j, total):
            for i in range(3):
                raised = jnp.exp(logits[3 * j + i] - top_row)
                if keep:
                    logits[3 * j + i] = raised
                total = total + raised
            return total

        total = lax.fori_loop(0, (tiles + 1) // 3, add, jnp.zeros((tokens, 128), F32))
        return (
            top_row,
            jnp.sum(total, axis=1, keepdims=True),
            jnp.sum(picked, axis=1, keepdims=True),
        )

    def join(mine, theirs):
        top_value = jnp.maximum(mine[0], theirs[0])
        total = mine[1] * jnp.exp(mine[0] - top_value) + theirs[1] * jnp.exp(theirs[0] - top_value)
        return top_value + jnp.log(total), mine[2] + theirs[2]

    def memory_block(u):
        at = rows(u)
        valid = own_valid[u * slots : (u + 1) * slots]
        hat, _ = normalise(stream_in[at, :])
        padded[u, pl.ds(8, slots), :] = (hat * gain_1 + bias_1) * valid
        for j in range(width // 128):
            cols = pl.ds(j * 128, 128)
            total = jnp.zeros((slots, 128), F32)
            for k in range(kernel_rows.shape[0]):
                shift = 8 + k - kernel_rows.shape[0] // 2
                total = total + kernel_rows[pl.ds(k, 1), cols] * padded[u, pl.ds(shift, slots), cols]
            stream_one[at, cols] = stream_in[at, cols] + total * valid
        low = stream_one[at, :].astype(BF16)
        one_low[at, :] = low
        queries[at, :] = dot_nn(low, w_query[...]).astype(BF16)

    def forward(second, beside_one=None, beside_two=None):
        copies = []
        for u in range(utterances):
            at = rows(u)
            if second:
                memory_block(u)
            frame_ok = frame_lane < memory_lengths[u]
            for h in range(heads):
                cols = pl.ds(h * HD, HD)
                scores = dot_nt(queries[at, cols], key_of(u, h)) * score_scale
                scores = jnp.where(frame_ok, scores, NEG)
                raised = jnp.exp(scores - jnp.max(scores, axis=-1, keepdims=True))
                prob = raised * (1.0 / jnp.sum(raised, axis=-1, keepdims=True))
                if second:
                    probs[u, h] = prob
                mixed[at, cols] = dot_nn(prob.astype(BF16), value_of(u, h)).astype(BF16)
            sent[u] = dot_nn(mixed[at, :], w_out[...])
            copies.append(swap(sent.at[u], arrived.at[u], sibling))
        if not second:
            beside_one()
            load_in.wait()
            load_back.wait()
        ff_copies = []
        for u in range(utterances):
            at = rows(u)
            copies[u].wait()
            two = stream_one[at, :] + (sent[u] + arrived[u])
            stream_two[at, :] = two
            hat, _ = normalise(two)
            low = (hat * gain_2 + bias_2).astype(BF16)
            norm_low[at, :] = low
            pre = dot_nn(low, w_in[...])
            phi = 0.5 * (1.0 + lax.erf(pre * math.sqrt(0.5)))
            hidden[at, :] = (pre * phi).astype(BF16)
            if second:
                gelu_slope[at, :] = phi + pre * (
                    jnp.exp(-0.5 * pre * pre) * (1.0 / math.sqrt(2.0 * math.pi))
                )
            sent[utterances + u] = dot_nn(hidden[at, :], w_back[...])
            ff_copies.append(swap(sent.at[utterances + u], arrived.at[utterances + u], sibling))
        if not second:
            beside_two()
        for u in range(utterances):
            at = rows(u)
            ff_copies[u].wait()
            three = stream_two[at, :] + (sent[utterances + u] + arrived[utterances + u])
            stream_three[u] = three
            top[0, at, :] = three.astype(BF16)

    stream_in[...] = acoustic[...].astype(F32)

    def beside_one():
        look_up_block(0)
        look_up_block(1)

    def beside_two():
        for k in range(2, per_core):
            look_up_block(k)
        look_up_rest()

    load_query.wait()
    for u in range(utterances):
        memory_block(u)
    load_memory.wait()
    for copy in load_kv:
        copy.wait()
    kv_rows = 512
    kv_chunks = frames // kv_rows

    def kv_step(i, carry):
        at = pl.ds(pl.multiple_of(i * kv_rows, kv_rows), kv_rows)
        group = jnp.zeros((1, width), jnp.int32) + rate_groups[i // kv_chunks]
        rate_row = jnp.where(group == 1, rate_table[pl.ds(1, 1), :], rate_table[pl.ds(0, 1), :])
        low = (mem_low[at, :].astype(F32) + rate_row).astype(BF16)
        mem_low[at, :] = low
        kv[at, :] = dot_nn(low, w_kv[...]).astype(BF16)
        return carry

    lax.fori_loop(0, utterances * kv_chunks, kv_step, 0)

    pl.semaphore_wait(barrier, n_dp)
    load_out.wait()
    forward(False, beside_one, beside_two)
    table_swap = swap(taken_mine, taken_theirs, sibling)
    load_vocab.wait()
    w_rest[pl.ds(0, vocab_here - main), :] = w_vocab[pl.ds(main, vocab_here - main), :]
    own_local = local_targets(own_target)
    mine = vocab_stats(own_local)
    stats[0] = side_by_side(mine)
    first_swap = swap(stats.at[0], stats_arrived.at[0], sibling)
    table_swap.wait()
    first_swap.wait()
    log_total, picked = join(mine, [stats_arrived[0, :, i : i + 1] for i in range(3)])
    first_loss = (log_total - picked) * own_valid
    blend = own_columns[:, 2:3] * own_valid / (1.0 + jnp.exp(math.log(V) - first_loss))
    for u in range(utterances):
        at = rows(u)
        wide_acoustic = acoustic[at, :].astype(F32)
        taken = taken_mine[u] + taken_theirs[u]
        stream_in[at, :] = wide_acoustic + blend[u * slots : (u + 1) * slots] * (taken - wide_acoustic)

    forward(True)
    token_swaps = [
        swap(stream_three.at[core], gathered.at[j - 1, 0], {"dp": mate[j]}) for j in (1, 2)
    ]
    mine = vocab_stats(own_local, keep=True)
    stats[1] = side_by_side(mine)
    stat_swap = swap(stats.at[1], stats_arrived.at[1], sibling)
    stat_swap.wait()
    log_column, picked = join(mine, [stats_arrived[1, :, i : i + 1] for i in range(3)])

    factor = jnp.exp(mine[0] - log_column) * own_valid
    valid_local = jnp.where(own_valid > 0.0, own_local, -1)

    def slope(j, carry):
        col = pl.multiple_of(j * 128, 128)
        ids = col + lax.broadcasted_iota(jnp.int32, (1, 128), 1)
        grad = logits[j] * factor - jnp.where(ids == valid_local, 1.0, 0.0)
        grad_logits[:, pl.ds(col, 128)] = grad.astype(BF16)
        return carry

    lax.fori_loop(0, main // 128 + 1, slope, 0, unroll=3)
    three_copies = []
    for u in range(utterances):
        sent[u] = dot_nn(grad_logits[rows(u), pl.ds(0, main)], w_vocab[pl.ds(0, main), :]) + dot_nn(
            grad_logits[rows(u), pl.ds(main, 128)], w_rest[...]
        )
        three_copies.append(swap(sent.at[u], arrived.at[u], sibling))
    for copy in token_swaps:
        copy.wait()
    part = slots // 2
    relays = [
        swap(gathered.at[0, 0, pl.ds(0, part)], gathered.at[2, 0, pl.ds(0, part)], {"dp": mate[2]}),
        swap(gathered.at[1, 0, pl.ds(part, part)], gathered.at[2, 0, pl.ds(part, part)], {"dp": mate[1]}),
    ]
    share_swaps = [swap(gathered.at[j, 0], gathered.at[j, 1], sibling) for j in range(2)]
    meta[0] = to_rows([own_target, own_valid, log_column, (log_column - picked) * own_valid])
    meta_swaps = [swap(meta.at[0], meta.at[j], {"dp": mate[j]}) for j in range(1, 4)]
    for u in range(utterances):
        r.loss_sum[pl.ds(u, 1), :] = meta[0, 3:4, u * slots : (u + 1) * slots]
    store(r.loss_sum, r.loss_out)

    plan = Planner()
    steps_all = len(bits)
    scatter_send, scatter_recv = r.scatter_send, r.scatter_recv

    vocab_parts = []

    def vocab_done():
        vocab_parts.append(1)
        if len(vocab_parts) == 1 + part_cols // 512:
            store(r.vocab_whole, r.vocab_out)

    def make_chunk(index):
        name, start, cols, order = chunk_list(part_cols, width, bits, low_bits, r)[index]
        source, landing = getattr(r, "src_" + name), r.landing[index]
        out_start = start
        if name == "kv":
            out, final = ((r.key_sum, r.key_out), (r.value_sum, r.value_out))[start // cols]
            out_start = 0
        else:
            out, final = getattr(r, name + "_sum"), getattr(r, name + "_out")
        rows_here = source.shape[-2]

        def pick(step, which):
            rest = sorted([b for b in bits if b not in order[:step]], reverse=True)
            where = tuple(which if b == order[step] else slice(None) for b in rest)
            if step == 0:
                return source, where + (slice(None), pl.ds(start, cols))
            return landing[step - 1], where + (slice(None), slice(None))

        def send(step):
            b = order[step]
            ref, where = pick(step, 1 - bit_of[b])
            copy = pltpu.make_async_remote_copy(
                src_ref=ref.at[where],
                dst_ref=landing[step],
                send_sem=scatter_send.at[index, step],
                recv_sem=scatter_recv.at[index, step],
                device_id=peer_of[b],
                device_id_type=MESH,
            )
            copy.start()
            return copy

        def take(step, copy):
            copy.wait_recv()
            ref, where = pick(step, bit_of[order[step]])
            got = landing[step]
            at = pl.ds(out_start, cols)
            if step < len(order) - 1:
                got[...] = got[...] + ref[where]
                return
            out[..., at] = got[...] + ref[where]
            if low_bits or name not in ("vocab", "rest"):
                store(out.at[..., at], final.at[..., at])
            elif name == "rest":
                rest = vocab_here - main
                r.vocab_whole[:, pl.ds(main, rest)] = out[...][:, :rest]
                vocab_done()

        steps = [
            (link_of(b, bits), rows_here * cols * 4 * 2 ** (steps_all - 1 - s))
            for s, b in enumerate(order)
        ]
        return Chunk(steps, send, take)

    def make_trade(start, cols):
        summed, traded = r.vocab_sum, r.vocab_traded
        at = pl.ds(start, cols)

        def send(step):
            copies = []
            for j in range(1, 4):
                to = lax.rem(mate[j], 4)
                copies.append(
                    pltpu.make_async_remote_copy(
                        src_ref=summed.at[to // 2, lax.rem(to, 2), :, at],
                        dst_ref=traded.at[j - 1, :, at],
                        send_sem=r.trade_send.at[start // 128, j - 1],
                        recv_sem=r.trade_recv.at[start // 128, j - 1],
                        device_id={"dp": mate[j]},
                        device_id_type=MESH,
                    )
                )
                copies[-1].start()
            return Several(copies)

        def take(step, copies):
            copies.wait_recv()
            for j in range(1, 4):
                there = pl.multiple_of(lax.rem(mate[j], 4) * part_cols + start, 128)
                r.vocab_whole[:, pl.ds(there, cols)] = traded[j - 1, :, at]
            here = pl.multiple_of(base + start, 128)
            r.vocab_whole[:, pl.ds(here, cols)] = summed[quarter // 2, lax.rem(quarter, 2), :, at]
            vocab_done()

        return Chunk([(0, 2 * r.src_vocab.shape[-2] * cols * 4)], send, take)

    chunks = {}
    for index, (name, start, cols, _) in enumerate(chunk_list(part_cols, width, bits, low_bits, r)):
        chunks[name, start] = make_chunk(index)
        if name == "vocab" and not low_bits:
            chunks[name, start].follow = make_trade(start, cols)

    def put(name, at, product):
        source = getattr(r, "src_" + name)
        source[..., at] = product.reshape(source.shape[:-1] + (product.shape[1],))

    copies = []
    for u in range(utterances):
        at = rows(u)
        three_copies[u].wait()
        three = sent[u] + arrived[u]
        grad_three[u] = three
        low = three.astype(BF16)
        branch_low[at, :] = low
        pre = (dot_nt(low, w_back[...]) * gelu_slope[at, :]).astype(BF16)
        grad_pre[at, :] = pre
        sent[utterances + u] = dot_nt(pre, w_in[...])
        copies.append(swap(sent.at[utterances + u], arrived.at[utterances + u], sibling))
    plan.run_until(plan.now + 8.0)
    for name, left, right in (("back", branch_low, hidden), ("in", norm_low, grad_pre)):
        left_turned = left[...].T
        for start in sorted(s for n, s in chunks if n == name):
            at = pl.ds(start, 512)
            put(name, at, dot_nn(left_turned, right[:, at]))
            plan.run_until(plan.now + 0.5)
            plan.post(chunks[name, start])

    at_core = pl.ds(pl.multiple_of(core * slots, slots), slots)
    at_other = pl.ds(pl.multiple_of((1 - core) * slots, slots), slots)
    base = pl.multiple_of(quarter * part_cols, part_cols)
    pieces = [(c, 256) for c in range(0, part_cols, 256)]
    for j in range(1, 4):
        if j == 2:
            for copy in relays:
                copy.wait()
            share_swaps.append(swap(gathered.at[2, 0], gathered.at[2, 1], sibling))
        meta_swaps[j - 1].wait()
        columns = to_columns(meta[j])
        valid = columns[:, 1:2] > 0.0
        target = jnp.where(valid, local_targets(columns[:, 0:1]), -1)
        log_total = jnp.where(valid, columns[:, 2:3], -NEG)
        top[j, at_core, :] = gathered[j - 1, 0].astype(BF16)
        share_swaps[j - 1].wait()
        top[j, at_other, :] = gathered[j - 1, 1].astype(BF16)
        for col, cols in pieces:
            ids = base + col + lax.broadcasted_iota(jnp.int32, (1, cols), 1)
            tile = dot_nt(top[j], w_vocab[pl.ds(base + col, cols), :])
            grad = jnp.exp(tile - log_total) - jnp.where(ids == target, 1.0, 0.0)
            grad_others[pl.ds((j - 1) * tokens, tokens), pl.ds(col, cols)] = grad.astype(BF16)
    top_turned = r.top_turned
    for j in range(4):
        top_turned[:, pl.ds(j * tokens, tokens)] = top[j].T
    plan.run_until(plan.now + 4.0)
    put("rest", slice(None), dot_nn(top_turned[:, pl.ds(0, tokens)], grad_logits[:, pl.ds(main, 128)]))
    starts = sorted(start for name, start in chunks if name == "vocab")
    for start, stop in zip(starts, starts[1:] + [part_cols]):
        for col in range(start, stop, 256):
            cols = min(256, stop - col)
            product = dot_nn(top_turned[:, pl.ds(0, tokens)], grad_logits[:, pl.ds(base + col, cols)])
            product = product + dot_nn(
                top_turned[:, pl.ds(tokens, 3 * tokens)], grad_others[:, pl.ds(col, cols)]
            )
            put("vocab", pl.ds(col, cols), product)
        plan.run_until(plan.now + 0.7)
        plan.post(chunks["vocab", start])
    plan.post(chunks["rest", 0])

    one_copies = []
    gain_2_total, bias_2_total = 0.0, 0.0
    for u in range(utterances):
        at = rows(u)
        copies[u].wait()
        grad_norm = sent[utterances + u] + arrived[utterances + u]
        hat, scale = normalise(stream_two[at, :])
        gain_2_total = gain_2_total + jnp.sum(grad_norm * hat, axis=0, keepdims=True)
        bias_2_total = bias_2_total + jnp.sum(grad_norm, axis=0, keepdims=True)
        two = grad_three[u] + normalise_back(grad_norm * gain_2, hat, scale)
        grad_two[at, :] = two
        low = two.astype(BF16)
        att_low[at, :] = low
        grad_mixed = dot_nt(low, w_out[...]).astype(BF16)
        for h in range(heads):
            cols = pl.ds(h * HD, HD)
            grad_head = grad_mixed[:, h * HD : (h + 1) * HD]
            prob = probs[u, h]
            grad_prob = dot_nt(grad_head, value_of(u, h))
            spare[pl.ds(u * frames, frames), pl.ds(half + h * HD, HD)] = dot_tn(
                prob.astype(BF16), grad_head
            ).astype(BF16)
            inner = jnp.sum(prob * grad_prob, axis=-1, keepdims=True)
            grad_score = (prob * (grad_prob - inner)).astype(BF16)
            grad_queries[at, cols] = (dot_nn(grad_score, key_of(u, h)) * score_scale).astype(BF16)
            spare[pl.ds(u * frames, frames), cols] = (
                dot_tn(grad_score, queries[at, cols]) * score_scale
            ).astype(BF16)
            plan.run_until(plan.now + 1.5)
        sent[u] = dot_nt(grad_queries[at, :], w_query[...])
        one_copies.append(swap(sent.at[u], arrived.at[u], sibling))
    every = slice(None)
    put("out", every, dot_tn(att_low[...], mixed[...]))
    plan.post(chunks["out", 0])
    put("query", every, dot_tn(one_low[...], grad_queries[...]))
    plan.post(chunks["query", 0])
    plan.run_until(plan.now + 1.0)

    mem_copies = []
    rate_sums = [0.0, 0.0]
    for u in range(utterances):
        total = jnp.zeros((1, width), F32)
        for i in range(row_chunks):
            at = pl.ds(u * frames + i * step_rows, step_rows)
            part = dot_nt(spare[at, :], w_kv[...])
            for j in range(width // 128):
                side_of, tile = j // (width // 256), j % (width // 256)
                index = ((side_of * utterances + u) * row_chunks + i) * (width // 256) + tile
                logits[index] = part[:, j * 128 : (j + 1) * 128]
            total = total + jnp.sum(part, axis=0, keepdims=True)
        tiles = row_chunks * (width // 256)
        mem_copies.append(
            swap(
                logits.at[pl.ds(((1 - core) * utterances + u) * tiles, tiles)],
                mem_arrived.at[pl.ds(u * tiles, tiles)],
                sibling,
            )
        )
        group = jnp.zeros((1, width), jnp.int32) + rate_groups[u]
        for k in range(2):
            rate_sums[k] = rate_sums[k] + jnp.where((group == 1) == (k == 1), total, 0.0)
        plan.run_until(plan.now + 1.2)
    span = frames // 2
    for k in range(2 * utterances):
        at = pl.ds(k * span, span)
        product = dot_tn(mem_low[at, :], spare[at, :])
        product = product.reshape(r.src_kv.shape)
        r.src_kv[...] = product if k == 0 else r.src_kv[...] + product
    plan.run_until(plan.now + 2.0)
    plan.post(*[chunks["kv", start] for start in sorted(s for n, s in chunks if n == "kv")])

    gain_1_total, bias_1_total = 0.0, 0.0
    for u in range(utterances):
        at = rows(u)
        valid = own_valid[u * slots : (u + 1) * slots]
        one_copies[u].wait()
        one = grad_two[at, :] + (sent[u] + arrived[u])
        grad_two[at, :] = one
        masked = one * valid
        for k in range(kernel_rows.shape[0]):
            shift = 8 + k - kernel_rows.shape[0] // 2
            row = jnp.sum(masked * padded[u, pl.ds(shift, slots), :], axis=0, keepdims=True)
            if u == 0:
                small_sent[0, pl.ds(k, 1), :] = row
            else:
                small_sent[0, pl.ds(k, 1), :] = small_sent[0, pl.ds(k, 1), :] + row
        padded[u, pl.ds(8, slots), :] = masked
        for j in range(width // 128):
            cols = pl.ds(j * 128, 128)
            total = jnp.zeros((slots, 128), F32)
            for k in range(kernel_rows.shape[0]):
                shift = 8 - k + kernel_rows.shape[0] // 2
                total = total + kernel_rows[pl.ds(k, 1), cols] * padded[u, pl.ds(shift, slots), cols]
            stream_one[at, cols] = total * valid
        grad_norm = stream_one[at, :]
        hat, scale = normalise(stream_in[at, :])
        gain_1_total = gain_1_total + jnp.sum(grad_norm * hat, axis=0, keepdims=True)
        bias_1_total = bias_1_total + jnp.sum(grad_norm, axis=0, keepdims=True)
        zero = grad_two[at, :] + normalise_back(grad_norm * gain_1, hat, scale)
        terms[u] = blend[u * slots : (u + 1) * slots] * zero
        stream_one[at, :] = zero - terms[u]
        plan.run_until(plan.now + 1.5)

    last_taps = kernel_rows.shape[0]
    small_sent[0, pl.ds(last_taps, 12 - last_taps), :] = jnp.zeros((12 - last_taps, width), F32)
    for i, row in enumerate((gain_1_total, bias_1_total, gain_2_total, bias_2_total)):
        small_sent[0, pl.ds(12 + i, 1), :] = row
    for k in range(2):
        small_sent[0, pl.ds(16 + k, 1), :] = rate_sums[k]
    small_sent[0, pl.ds(18, 6), :] = jnp.zeros((6, width), F32)
    small_peers = [peer_of[b] for b in low_bits + bits] + [sibling]

    def small_send(step):
        copy = pltpu.make_async_remote_copy(
            src_ref=small_sent.at[step],
            dst_ref=small_arrived.at[step],
            send_sem=r.small_send.at[step],
            recv_sem=r.small_recv.at[step],
            device_id=small_peers[step],
            device_id_type=MESH,
        )
        copy.start()
        return copy

    def small_take(step, copy):
        copy.wait_recv()
        if step + 1 == len(small_peers):
            copy.wait_send()
            plan.started = [c for c in plan.started if c is not copy]
        if step + 1 < len(small_peers):
            small_sent[step + 1] = small_sent[step] + small_arrived[step]
        else:
            small_sent[step, pl.ds(16, 8), :] = (
                small_sent[step, pl.ds(16, 8), :] + small_arrived[step, pl.ds(16, 8), :]
            )
            store(small_sent.at[step], r.small_out)

    small_links = [link_of(b, bits) for b in low_bits + bits] + ["core"]
    plan.post(Chunk([(l, 24 * width * 4) for l in small_links], small_send, small_take))

    features = width // n_dp
    feature_rows = max(features, 8)
    block_rows = term_blocks.shape[1]
    turned = terms[core].T
    id_row = targets[pl.ds(core, 1), :].astype(F32)
    rest = block_rows - features - 1
    for p in range(n_dp):
        term_blocks[p, pl.ds(0, features), :] = turned[p * features : (p + 1) * features]
        term_blocks[p, pl.ds(features, 1), :] = id_row
        term_blocks[p, pl.ds(features + 1, rest), :] = jnp.zeros((rest, slots), F32)

    def term_copy(k):
        there = lax.rem(me + k, n_dp)
        return pltpu.make_async_remote_copy(
            src_ref=term_blocks.at[there],
            dst_ref=term_arrived.at[me],
            send_sem=r.term_send.at[k],
            recv_sem=r.term_recv.at[k],
            device_id={"dp": there},
            device_id_type=MESH,
        )

    def term_start(k, carry):
        term_copy(k).start()
        return carry

    def term_wait(k, carry):
        term_copy(k).wait()
        return carry

    term_arrived[me] = term_blocks[me]
    lax.fori_loop(1, n_dp, term_start, 0)
    store(stream_one, r.acoustic_out)
    for u in range(utterances):
        mem_copies[u].wait()
        for i in range(row_chunks):
            for j in range(width // 256):
                index = (u * row_chunks + i) * (width // 256) + j
                first_tile = (core * utterances) * row_chunks * (width // 256)
                mem_arrived[index] = logits[first_tile + index] + mem_arrived[index]
                at = pl.ds(u * frames + i * step_rows, step_rows)
                store(mem_arrived.at[index], r.memory_out.at[at, pl.ds(j * 128, 128)])
    plan.run_until(plan.now + 8.0)
    lax.fori_loop(1, n_dp, term_wait, 0)
    per_piece = 512 // slots
    blocks_hi = (table_rows + 255) // 256
    batch = 4

    def table_piece(p, fresh):
        found = [term_arrived[p * per_piece + i] for i in range(per_piece)]
        values = jnp.concatenate([f[:feature_rows] for f in found], axis=1)
        ids = jnp.concatenate([f[features : features + 1] for f in found], axis=1).astype(jnp.int32)
        low_ids, high_ids = ids & 255, ids >> 8
        onehot_lo[...] = jnp.where(
            lax.broadcasted_iota(jnp.int32, (256, 512), 0) == low_ids, 1.0, 0.0
        ).astype(BF16)
        coarse = values.astype(BF16).astype(F32)
        both = jnp.concatenate([coarse, values - coarse], axis=0)
        for first_hi in range(0, blocks_hi, batch):
            here = range(first_hi, min(first_hi + batch, blocks_hi))
            masked = jnp.concatenate([jnp.where(high_ids == hi, both, 0.0) for hi in here], axis=0)
            product = dot_nt(masked.astype(BF16), onehot_lo[...])
            for i, hi in enumerate(here):
                top_part = product[2 * i * feature_rows : (2 * i + 1) * feature_rows]
                low_part = product[(2 * i + 1) * feature_rows : (2 * i + 2) * feature_rows]
                cols = min(256, table_rows - hi * 256)
                at = pl.ds(hi * 256, cols)
                found = (top_part + low_part)[:features, :cols]
                whole_table[:, at] = found if fresh else whole_table[:, at] + found

    pieces = n_dp // per_piece
    table_piece(0, True)
    if pieces <= 4:
        for p in range(1, pieces):
            plan.run_until(plan.now + 1.5)
            table_piece(p, False)
    else:
        lax.fori_loop(1, pieces, lambda p, c: (table_piece(p, False), c)[1], 0)
    table_swap = swap(whole_table, table_theirs, sibling)
    plan.run_until(plan.now + 8.0)
    table_swap.wait()
    whole_table[...] = whole_table[...] + table_theirs[...]
    store(whole_table, r.table_out)
    plan.finish()
    for copy in stores:
        copy.wait()


def link_of(bit, bits):
    if bit == bits[-1]:
        return bits[-2]
    return bit


def chunk_list(part_cols, width, bits, low_bits, sizes):
    turned = [bits[1], bits[0]] + bits[2:]
    listing = []
    for start in range(0, part_cols, 512):
        listing.append(("vocab", start, 512, [b for b in bits if b > 1]))
    listing.append(("rest", 0, 128, bits))
    for name, order in (("back", turned), ("in", bits)):
        for start in range(0, sizes.units, 512):
            if name == "in" and start:
                order = [bits[2], bits[0], bits[1]] + bits[3:]
            listing.append((name, start, 512, order))
    listing.append(("out", 0, sizes.half, turned))
    listing.append(("query", 0, sizes.half, bits))
    for k, start in enumerate(range(0, 2 * sizes.half, 256)):
        listing.append(("kv", start, 256, [bits, turned][k % 2]))
    return listing


def decoder_call(
    acoustic, memory, embedding, w_query, w_key, w_value, w_out, w_in, w_back, w_vocab, norms,
    fsmn_kernel, rate_table, token_lengths, memory_lengths, rate_groups, glance, targets, n_dp,
):
    utterances = token_lengths.shape[0]
    tokens, width = acoustic.shape
    slots = tokens // utterances
    mem_rows = memory.shape[0]
    half = w_query.shape[1]
    heads = half // HD
    frames = mem_rows // utterances
    units = w_in.shape[1]
    vocab_here = w_vocab.shape[1]
    table_rows = embedding.shape[0]
    part_cols = vocab_here // 512 * 128
    all_cols = 4 * part_cols + 128
    w_turned = w_vocab.T
    mains = table_rows // 2048 * 2048
    nbits = n_dp.bit_length() - 1
    steps = nbits
    while width >> steps < 8:
        steps -= 1
    low_bits, bits = list(range(nbits - steps)), list(range(nbits - steps, nbits))
    rows = width >> steps
    features = width // n_dp
    feature_rows = max(features, 8)
    block_rows = feature_rows + 8 if features >= 8 else 8
    blocks_hi = (table_rows + 255) // 256
    sizes = SimpleNamespace(units=units, half=half)
    plane = [b for b in bits if b < 2]
    listing = chunk_list(part_cols, width, bits, low_bits, sizes)
    most = max(len(c[3]) for c in listing)

    f32 = lambda *shape: jax.ShapeDtypeStruct(shape, F32)
    v32 = lambda *shape: pltpu.VMEM(shape, F32)
    v16 = lambda *shape: pltpu.VMEM(shape, BF16)
    dma = lambda *shape: pltpu.SemaphoreType.DMA(shape)
    inputs = dict(
        acoustic=(VMEM, acoustic),
        table_tail=(VMEM, embedding[mains + (table_rows - mains) // 16 * 16 :]),
        memory=(ANY, memory),
        table=(ANY, embedding),
        w_query_hbm=(ANY, w_query),
        w_key_hbm=(ANY, w_key),
        w_value_hbm=(ANY, w_value),
        w_out_hbm=(ANY, w_out),
        w_in_hbm=(ANY, w_in),
        w_back_hbm=(ANY, w_back),
        w_vocab_hbm=(ANY, w_turned),
        gain_one=(VMEM, norms[0][None]),
        bias_one=(VMEM, norms[1][None]),
        gain_two=(VMEM, norms[2][None]),
        bias_two=(VMEM, norms[3][None]),
        kernel_rows=(VMEM, fsmn_kernel),
        rate_table=(VMEM, rate_table),
        token_lengths=(SMEM, token_lengths),
        memory_lengths=(SMEM, memory_lengths),
        rate_groups=(SMEM, rate_groups),
        glance=(VMEM, glance.reshape(utterances, slots)),
        targets=(VMEM, targets.reshape(utterances, slots)),
    )
    outputs = dict(
        loss_out=f32(utterances, slots),
        small_out=f32(24, width),
        vocab_out=f32(2, rows, part_cols) if low_bits else f32(rows, vocab_here),
        rest_out=f32(rows, 128),
        in_out=f32(rows, units),
        back_out=f32(rows, units),
        query_out=f32(rows, half),
        out_out=f32(rows, half),
        key_out=f32(rows, half),
        value_out=f32(rows, half),
        acoustic_out=f32(tokens, width),
        memory_out=f32(mem_rows, width // 2),
        table_out=f32(features, table_rows),
    )
    shape = (2,) * steps + (rows,)
    scratch = dict(
        w_query=v16(width, half),
        w_kv=v16(width, 2 * half),
        w_out=v16(half, width),
        w_in=v16(width, units),
        w_back=v16(units, width),
        w_vocab=v16(vocab_here, width),
        w_rest=v16(128, width),
        mem_low=v16(mem_rows, width),
        kv=v16(mem_rows, 2 * half),
        spare=v16(mem_rows, 2 * half),
        padded=v32(utterances, slots + 16, width),
        stream_in=v32(tokens, width),
        stream_one=v32(tokens, width),
        stream_two=v32(tokens, width),
        stream_three=v32(utterances, slots, width),
        one_low=v16(tokens, width),
        queries=v16(tokens, half),
        probs=v32(utterances, heads, slots, frames),
        mixed=v16(tokens, half),
        norm_low=v16(tokens, width),
        hidden=v16(tokens, units),
        gelu_slope=v32(tokens, units),
        top=v16(4, tokens, width),
        logits=v32(all_cols // 128, tokens, 128),
        grad_logits=v16(tokens, all_cols),
        grad_others=v16(3 * tokens, part_cols),
        top_turned=v16(width, 4 * tokens),
        taken_theirs=v32(utterances, slots, width),
        grad_three=v32(utterances, slots, width),
        grad_two=v32(tokens, width),
        branch_low=v16(tokens, width),
        grad_pre=v16(tokens, units),
        att_low=v16(tokens, width),
        grad_queries=v16(tokens, half),
        mem_arrived=v32(mem_rows // 256 * (width // 256), 256, 128),
        meta=v32(4, 8, tokens),
        stats=v32(2, tokens, 128),
        stats_arrived=v32(2, tokens, 128),
        sent=v32(2 * utterances, slots, width),
        arrived=v32(2 * utterances, slots, width),
        gathered=v32(3, 2, slots, width),
        small_sent=v32(nbits + 1, 24, width),
        small_arrived=v32(nbits + 1, 24, width),
        term_blocks=v32(n_dp, block_rows, slots),
        term_arrived=v32(n_dp, block_rows, slots),
        onehot_lo=v16(256, 512),
        table_rest=v16((table_rows - mains + 127) // 128 * 128, width),
        table_theirs=v32(features, table_rows),
        src_vocab=v32(*shape, part_cols),
        src_rest=v32(*shape, 128),
        whole_table=v32(features, table_rows),
        src_back=v32(*shape, units),
        vocab_sum=v32(*(2,) * len(plane), rows, part_cols),
        rest_sum=v32(rows, 128),
        vocab_whole=v32(rows, vocab_here),
        in_sum=v32(rows, units),
        back_sum=v32(rows, units),
        query_sum=v32(rows, half),
        out_sum=v32(rows, half),
        key_sum=v32(rows, half),
        value_sum=v32(rows, half),
        loss_sum=v32(utterances, slots),
        vocab_traded=v32(3, rows, part_cols),
        src_in=v32(*shape, units),
        src_out=v32(*shape, half),
        src_query=v32(*shape, half),
        src_kv=v32(*shape, 2 * half),
        load_sem=dma(24),
        store_sem=dma(48),
        trade_send=dma(part_cols // 128, 3),
        trade_recv=dma(part_cols // 128, 3),
        swap_send=dma(40),
        swap_recv=dma(40),
        scatter_send=dma(len(listing), most),
        scatter_recv=dma(len(listing), most),
        small_send=dma(nbits + 1),
        small_recv=dma(nbits + 1),
        term_send=dma(n_dp),
        term_recv=dma(n_dp),
    )
    landing = [
        [v32(*(2,) * (steps - 1 - s), rows, cols) for s in range(len(order))]
        for _, _, cols, order in listing
    ]
    names = list(inputs) + list(outputs) + list(scratch)
    flat = [ref for chunk in landing for ref in chunk]

    def kernel(*refs):
        named, rest = refs[: len(names)], list(refs[len(names) :])
        lands = [[rest.pop(0) for _ in chunk] for chunk in landing]
        decoder_kernel(
            names + ["landing", "units", "half"], vocab_here, part_cols, table_rows, n_dp, bits,
            low_bits, *named, lands, units, half,
        )

    out = pl.pallas_call(
        kernel,
        out_shape=list(outputs.values()),
        in_specs=[spec for spec, _ in inputs.values()],
        out_specs=[ANY] * len(outputs),
        scratch_shapes=list(scratch.values()) + flat,
        compiler_params=pltpu.CompilerParams(
            collective_id=1, has_side_effects=True, vmem_limit_bytes=64 << 20
        ),
    )(*[value for _, value in inputs.values()])
    return SimpleNamespace(**dict(zip(outputs, out))), low_bits


def deliver_kernel(n_dp, n_passed, *refs):
    n = n_passed + 2
    sources, targets, held = refs[:n], refs[n : 2 * n + 5], refs[2 * n + 5 : 3 * n + 5]
    shaped, (sem_in, sem_out) = refs[3 * n + 5 : 3 * n + 12], refs[3 * n + 12 :]
    reads, writes = [], []
    for i, (source, buffer) in enumerate(zip(sources, held)):
        reads.append(pltpu.make_async_copy(source, buffer, sem_in.at[i]))
        reads[-1].start()
    for i in range(n_passed):
        reads[i].wait()
        writes.append(pltpu.make_async_copy(held[i], targets[i], sem_out.at[i]))
        writes[-1].start()
    reads[n_passed].wait()
    reads[n_passed + 1].wait()
    loss, small = held[n_passed:]
    loss_at, gain_one_at, bias_one_at, gain_two_at, bias_two_at, taps_at, rate_at = shaped
    slots = loss.shape[1]
    for u in range(loss.shape[0]):
        loss_at[:, pl.ds(u * slots, slots)] = loss[pl.ds(u, 1), :]
    me = lax.axis_index("dp")
    own = small.shape[1] // n_dp
    mine = jnp.zeros((16, own), F32)
    for p in range(n_dp):
        mine = jnp.where(me == p, small[pl.ds(0, 16), p * own : (p + 1) * own], mine)
    taps_at[...] = mine[: taps_at.shape[0]]
    for i, target in enumerate((gain_one_at, bias_one_at, gain_two_at, bias_two_at)):
        target[...] = mine[12 + i : 13 + i]
    rate_at[...] = small[pl.ds(16, 2), :]
    for i, source in enumerate(shaped):
        writes.append(pltpu.make_async_copy(source, targets[n_passed + i], sem_out.at[n_passed + i]))
        writes[-1].start()
    for copy in writes:
        copy.wait()


def per_device(
    acoustic,
    memory,
    embedding,
    w_query,
    w_key,
    w_value,
    w_out,
    w_in,
    w_back,
    w_vocab,
    gain_one,
    bias_one,
    gain_two,
    bias_two,
    fsmn_kernel,
    rate_table,
    token_lengths,
    memory_lengths,
    rate_groups,
    glance_mask,
    targets,
):
    tok_rows, model_width = acoustic.shape
    half = w_query.shape[1]
    n_dp = lax.axis_size("dp")
    result, low_bits = decoder_call(
        acoustic, memory, embedding, w_query, w_key, w_value, w_out, w_in, w_back, w_vocab,
        (gain_one, bias_one, gain_two, bias_two), fsmn_kernel, rate_table,
        token_lengths, memory_lengths, rate_groups, glance_mask, targets, n_dp,
    )
    vocab = result.vocab_out
    summed = [
        result.query_out, result.key_out, result.value_out, result.out_out, result.in_out,
        result.back_out,
    ]
    if low_bits:
        size = 1 << len(low_bits)
        groups = [list(range(g * size, (g + 1) * size)) for g in range(n_dp // size)]
        planes = [list(range(4 * g, 4 * g + 4)) for g in range(n_dp // 4)]
        vocab = lax.all_to_all(
            vocab.reshape(4, model_width // n_dp, -1), "dp", 0, 0, axis_index_groups=planes, tiled=True
        )
        *summed, rest = [
            lax.psum_scatter(s, "dp", scatter_dimension=0, axis_index_groups=groups, tiled=True)
            for s in (*summed, result.rest_out)
        ]
        vocab = jnp.concatenate([*vocab, rest], axis=1)[:, : w_vocab.shape[1]]
    own = model_width // n_dp
    f32 = lambda *shape: jax.ShapeDtypeStruct(shape, F32)
    like = lambda x: jax.ShapeDtypeStruct(x.shape, F32)
    passed = (result.memory_out, result.table_out, result.acoustic_out, vocab, *summed)
    handed = (*passed, result.loss_out, result.small_out)
    small_shapes = [
        f32(1, tok_rows), *[f32(1, own)] * 4, f32(fsmn_kernel.shape[0], own), f32(2, model_width)
    ]
    (
        grad_memory, grad_table, grad_acoustic, grad_vocab, grad_query, grad_key, grad_value,
        grad_out, grad_in, grad_back, token_loss, gain_1, bias_1, gain_2, bias_2, grad_taps, grad_rate,
    ) = pl.pallas_call(
        partial(deliver_kernel, n_dp, len(passed)),
        out_shape=[*[like(x) for x in passed], *small_shapes],
        in_specs=[ANY] * len(handed),
        out_specs=[ANY] * (len(passed) + 7),
        scratch_shapes=[pltpu.VMEM(x.shape, F32) for x in (*handed, *small_shapes)]
        + [pltpu.SemaphoreType.DMA((len(handed),)), pltpu.SemaphoreType.DMA((len(passed) + 7,))],
        compiler_params=pltpu.CompilerParams(vmem_limit_bytes=60 << 20),
    )(*handed)
    return (
        token_loss.reshape(tok_rows),
        grad_acoustic,
        grad_memory,
        grad_table.T,
        grad_query,
        grad_key,
        grad_value,
        grad_out.T,
        grad_in,
        grad_back.T,
        grad_vocab,
        gain_1.reshape(own),
        bias_1.reshape(own),
        gain_2.reshape(own),
        bias_2.reshape(own),
        grad_taps,
        grad_rate,
    )


def solution(mesh):
    return jax.shard_map(
        per_device,
        mesh=mesh,
        in_specs=(
            P("dp", None),
            P("dp", None),
            P(),
            P(None, "mp"),
            P(None, "mp"),
            P(None, "mp"),
            P("mp", None),
            P(None, "mp"),
            P("mp", None),
            P(None, "mp"),
            P(),
            P(),
            P(),
            P(),
            P(),
            P(),
            P("dp"),
            P("dp"),
            P("dp"),
            P("dp"),
            P("dp"),
        ),
        out_specs=(
            P("dp"),
            P("dp", None),
            P("dp", "mp"),
            P(None, "dp"),
            P("dp", "mp"),
            P("dp", "mp"),
            P("dp", "mp"),
            P("mp", "dp"),
            P("dp", "mp"),
            P("mp", "dp"),
            P("dp", "mp"),
            P("dp"),
            P("dp"),
            P("dp"),
            P("dp"),
            P(None, "dp"),
            P(),
        ),
        check_vma=False,
    )
```

```python
from functools import partial
import math
from types import SimpleNamespace

import jax
import jax.numpy as jnp
from jax import lax
from jax.experimental import pallas as pl
from jax.experimental.pallas import tpu as pltpu
from jax.sharding import PartitionSpec as P

HD = 128
V = 8404
EPSILON = 1e-05
MESH = pl.DeviceIdType.MESH
VMEM = pl.BlockSpec(memory_space=pltpu.VMEM)
SMEM = pl.BlockSpec(memory_space=pltpu.SMEM)
ANY = pl.BlockSpec(memory_space=pl.ANY)
F32, BF16 = jnp.float32, jnp.bfloat16
NEG = -1e30


def other_core():
    return {"mp": 1 - lax.axis_index("mp")}


def dot_nn(a, b):
    return lax.dot_general(a, b, (((1,), (0,)), ((), ())), preferred_element_type=F32)


def dot_nt(a, b):
    return lax.dot_general(a, b, (((1,), (1,)), ((), ())), preferred_element_type=F32)


def dot_tn(a, b):
    return lax.dot_general(a, b, (((0,), (0,)), ((), ())), preferred_element_type=F32)


def normalise(rows):
    average = jnp.mean(rows, axis=-1, keepdims=True)
    centred = rows - average
    variance = jnp.mean(centred * centred, axis=-1, keepdims=True)
    scale = lax.rsqrt(variance + EPSILON)
    return centred * scale, scale


def normalise_back(grad_hat, hat, scale):
    first = jnp.mean(grad_hat, axis=-1, keepdims=True)
    second = jnp.mean(grad_hat * hat, axis=-1, keepdims=True)
    return scale * (grad_hat - first - hat * second)


def side_by_side(columns):
    lane = lax.broadcasted_iota(jnp.int32, (columns[0].shape[0], 128), 1)
    tile = jnp.zeros(lane.shape, F32)
    for i, column in enumerate(columns):
        tile = jnp.where(lane == i, column, tile)
    return tile


def to_rows(columns):
    return side_by_side(columns).T[:8]


def to_columns(rows):
    return jnp.concatenate([rows] * 16, axis=0).T


class Planner:
    RATE = 0.045e6
    HOP = 1.5
    BACKLOG = 4.0

    def __init__(self):
        self.now = 0.0
        self.free = {}
        self.flying = []
        self.waiting = []
        self.started = []
        self.count = 0

    def launch(self, item, step):
        link, size = item.steps[step]
        begin = max(self.now, self.free.get(link, 0.0))
        self.free[link] = begin + size / self.RATE
        copy = item.send(step)
        self.started.append(copy)
        self.count += 1
        self.flying.append((self.free[link] + self.HOP, self.count, item, step, copy))

    def release(self):
        kept = []
        for item in self.waiting:
            link = item.steps[0][0]
            if self.free.get(link, 0.0) - self.now < self.BACKLOG:
                self.launch(item, 0)
            else:
                kept.append(item)
        self.waiting = kept

    def post(self, *items):
        self.waiting += items
        self.release()

    def run_until(self, time):
        while self.flying or self.waiting:
            if not self.flying:
                self.now = max(self.now, min(self.free[i.steps[0][0]] for i in self.waiting))
                self.release()
                continue
            first = min(self.flying, key=lambda f: f[:2])
            if first[0] > time:
                break
            self.flying.remove(first)
            self.now = max(self.now, first[0])
            _, _, item, step, copy = first
            item.take(step, copy)
            if step + 1 < len(item.steps):
                self.launch(item, step + 1)
            elif item.follow is not None:
                self.launch(item.follow, 0)
            self.release()
        if time != math.inf:
            self.now = max(self.now, time)
        self.release()

    def finish(self):
        self.run_until(math.inf)
        for copy in self.started:
            copy.wait_send()


class Chunk:
    def __init__(self, steps, send, take):
        self.steps, self.send, self.take, self.follow = steps, send, take, None


class Several:
    def __init__(self, copies):
        self.copies = copies

    def wait_recv(self):
        for copy in self.copies:
            copy.wait_recv()

    def wait_send(self):
        for copy in self.copies:
            copy.wait_send()


def decoder_kernel(
    names,
    vocab_here,
    part_cols,
    table_rows,
    n_dp,
    bits,
    low_bits,
    *refs,
):
    r = SimpleNamespace(**dict(zip(names, refs)))
    acoustic, memory, table = r.acoustic, r.memory, r.table
    targets, glance = r.targets, r.glance
    gain_1, bias_1 = r.gain_one[...], r.bias_one[...]
    gain_2, bias_2 = r.gain_two[...], r.bias_two[...]
    kernel_rows, rate_table = r.kernel_rows, r.rate_table
    token_lengths, memory_lengths, rate_groups = r.token_lengths, r.memory_lengths, r.rate_groups
    w_query, w_kv, w_out, w_in, w_back, w_vocab = r.w_query, r.w_kv, r.w_out, r.w_in, r.w_back, r.w_vocab
    mem_low, kv, padded, spare = r.mem_low, r.kv, r.padded, r.spare
    stream_in, stream_one, stream_two, stream_three = r.stream_in, r.stream_one, r.stream_two, r.stream_three
    one_low, queries, probs, mixed = r.one_low, r.queries, r.probs, r.mixed
    norm_low, hidden, gelu_slope, top = r.norm_low, r.hidden, r.gelu_slope, r.top
    logits, grad_logits, grad_others = r.logits, r.grad_logits, r.grad_others
    taken_mine, taken_theirs = r.grad_three, r.taken_theirs
    grad_three, grad_two, branch_low = r.grad_three, r.grad_two, r.branch_low
    grad_pre, att_low, grad_queries = r.grad_pre, r.att_low, r.grad_queries
    mem_arrived, meta, stats, stats_arrived = r.mem_arrived, r.meta, r.stats, r.stats_arrived
    sent, arrived, gathered = r.sent, r.arrived, r.gathered
    small_sent, small_arrived = r.small_sent, r.small_arrived
    terms, term_blocks, term_arrived = grad_three, r.term_blocks, r.term_arrived
    onehot_lo, table_theirs, whole_table = r.onehot_lo, r.table_theirs, r.whole_table
    swap_send, swap_recv, load_sem = r.swap_send, r.swap_recv, r.load_sem

    utterances, slots = targets.shape
    width = acoustic.shape[1]
    frames = memory.shape[0] // utterances
    half = w_query.shape[1]
    heads = half // HD
    tokens = utterances * slots
    me, core = lax.axis_index("dp"), lax.axis_index("mp")
    sibling = {"mp": 1 - core}
    quarter = lax.rem(me, 4)
    bit_0 = lax.rem(me, 2)
    flips = [1 - 2 * lax.rem(me, 2), 2 - 4 * lax.rem(me // 2, 2)]
    mate = [me + flips[0] * (j % 2) + flips[1] * (j // 2) for j in range(4)]
    bit_of = {b: lax.rem(me // (1 << b), 2) for b in low_bits + bits}
    peer_of = {b: {"dp": me + (1 - 2 * bit_of[b]) * (1 << b)} for b in low_bits + bits}
    score_scale = 1.0 / math.sqrt(HD)

    loads = []

    def load(source, target):
        copy = pltpu.make_async_copy(source, target, load_sem.at[len(loads)])
        copy.start()
        loads.append(copy)
        return copy

    load_memory = load(memory, mem_low)
    load_kv = [
        load(r.w_key_hbm, w_kv.at[:, pl.ds(0, half)]),
        load(r.w_value_hbm, w_kv.at[:, pl.ds(half, half)]),
    ]
    load_query = load(r.w_query_hbm, w_query)
    load_out = load(r.w_out_hbm, w_out)

    barrier = pltpu.get_barrier_semaphore()

    def greet(k, carry):
        pl.semaphore_signal(
            barrier, inc=1, device_id={"dp": lax.rem(me + k, n_dp)}, device_id_type=MESH
        )
        return carry

    lax.fori_loop(1, n_dp, greet, 0)
    pl.semaphore_signal(barrier, inc=1, device_id=sibling, device_id_type=MESH)

    load_in = load(r.w_in_hbm, w_in)
    load_back = load(r.w_back_hbm, w_back)
    block = 1024
    per_core = table_rows // (2 * block)
    mains = 2 * per_core * block

    def load_table(k):
        at = pl.ds(pl.multiple_of((core * per_core + k) * block, block), block)
        return load(table.at[at, :], spare.at[pl.ds(k % 2 * block, block), :])

    table_loads = [load_table(0), load_table(1)]
    main = 4 * part_cols
    load_vocab = load(r.w_vocab_hbm, w_vocab)
    w_rest = r.w_rest
    w_rest[...] = jnp.zeros(w_rest.shape, BF16)
    rest_rows = (table_rows - mains) // 16 * 16
    r.table_rest[...] = jnp.zeros(r.table_rest.shape, BF16)
    load_rest = load(table.at[pl.ds(mains, rest_rows), :], r.table_rest.at[pl.ds(0, rest_rows), :])
    r.table_rest[pl.ds(rest_rows, table_rows - mains - rest_rows), :] = r.table_tail[...]

    stores = []

    def store(source, target):
        copy = pltpu.make_async_copy(source, target, r.store_sem.at[len(stores)])
        copy.start()
        stores.append(copy)

    swaps = []

    def swap(source, target, device):
        k = len(swaps)
        copy = pltpu.make_async_remote_copy(
            src_ref=source,
            dst_ref=target,
            send_sem=swap_send.at[k],
            recv_sem=swap_recv.at[k],
            device_id=device,
            device_id_type=MESH,
        )
        copy.start()
        swaps.append(copy)
        return copy

    lane = lax.broadcasted_iota(jnp.int32, (1, slots), 1)
    row_of = lax.broadcasted_iota(jnp.int32, (8, slots), 0)
    for u in range(utterances):
        target_row = targets[pl.ds(u, 1), :].astype(F32)
        glance_row = glance[pl.ds(u, 1), :].astype(F32)
        valid_row = (lane < token_lengths[u]).astype(F32)
        meta[0, :, pl.ds(u * slots, slots)] = jnp.where(
            row_of == 0, target_row, jnp.where(row_of == 1, valid_row, glance_row)
        )
    own_columns = to_columns(meta[0])
    own_target = own_columns[:, 0:1]
    own_valid = own_columns[:, 1:2]

    def rows(u):
        return pl.ds(u * slots, slots)

    edge = jnp.zeros((8, width), F32)
    for u in range(utterances):
        padded[u, pl.ds(0, 8), :] = edge
        padded[u, pl.ds(8 + slots, 8), :] = edge

    step_rows = 256
    row_chunks = frames // step_rows

    def key_of(u, h):
        return kv[pl.ds(u * frames, frames), pl.ds(h * HD, HD)]

    def value_of(u, h):
        return kv[pl.ds(u * frames, frames), pl.ds(half + h * HD, HD)]

    frame_lane = lax.broadcasted_iota(jnp.int32, (1, frames), 1)

    def look_up(first_row, count, allowed, source):
        ids = first_row + lax.broadcasted_iota(jnp.int32, (1, count), 1)
        local = jnp.where(allowed, own_target.astype(jnp.int32), -1)
        onehot = jnp.where(ids == local, 1.0, 0.0).astype(BF16)
        return dot_nn(onehot, source)

    def look_up_block(k):
        table_loads[k].wait()
        part = look_up(
            (core * per_core + k) * block, block, True, spare[pl.ds(k % 2 * block, block), :]
        )
        for u in range(utterances):
            piece = part[u * slots : (u + 1) * slots]
            taken_mine[u] = piece if k == 0 else taken_mine[u] + piece
        if k + 2 < per_core:
            table_loads.append(load_table(k + 2))

    def look_up_rest():
        load_rest.wait()
        part = look_up(mains, r.table_rest.shape[0], core == 0, r.table_rest[...])
        for u in range(utterances):
            taken_mine[u] = taken_mine[u] + part[u * slots : (u + 1) * slots]

    def local_targets(target_column):
        local = target_column.astype(jnp.int32) - core * vocab_here
        return jnp.where((local >= 0) & (local < vocab_here), local, -1)

    def vocab_stats(target, keep=False):
        tiles = main // 128
        step_tiles = 4

        ids = main + lax.broadcasted_iota(jnp.int32, (1, 128), 1)
        last = jnp.where(ids < vocab_here, dot_nt(top[0], w_rest[...]), NEG)
        logits[tiles] = last
        top_m, picked = last, jnp.where(ids == target, last, 0.0)
        for j in range(tiles // step_tiles):
            col = j * step_tiles * 128
            product = dot_nt(top[0], w_vocab[pl.ds(col, step_tiles * 128), :])
            for i in range(step_tiles):
                tile = product[:, i * 128 : (i + 1) * 128]
                ids = col + i * 128 + lax.broadcasted_iota(jnp.int32, (1, 128), 1)
                logits[j * step_tiles + i] = tile
                top_m = jnp.maximum(top_m, tile)
                picked = picked + jnp.where(ids == target, tile, 0.0)
        top_row = jnp.max(top_m, axis=1, keepdims=True)

        def add(j, total):
            for i in range(3):
                raised = jnp.exp(logits[3 * j + i] - top_row)
                if keep:
                    logits[3 * j + i] = raised
                total = total + raised
            return total

        total = lax.fori_loop(0, (tiles + 1) // 3, add, jnp.zeros((tokens, 128), F32))
        return (
            top_row,
            jnp.sum(total, axis=1, keepdims=True),
            jnp.sum(picked, axis=1, keepdims=True),
        )

    def join(mine, theirs):
        top_value = jnp.maximum(mine[0], theirs[0])
        total = mine[1] * jnp.exp(mine[0] - top_value) + theirs[1] * jnp.exp(theirs[0] - top_value)
        return top_value + jnp.log(total), mine[2] + theirs[2]

    def memory_block(u):
        at = rows(u)
        valid = own_valid[u * slots : (u + 1) * slots]
        hat, _ = normalise(stream_in[at, :])
        padded[u, pl.ds(8, slots), :] = (hat * gain_1 + bias_1) * valid
        for j in range(width // 128):
            cols = pl.ds(j * 128, 128)
            total = jnp.zeros((slots, 128), F32)
            for k in range(kernel_rows.shape[0]):
                shift = 8 + k - kernel_rows.shape[0] // 2
                total = total + kernel_rows[pl.ds(k, 1), cols] * padded[u, pl.ds(shift, slots), cols]
            stream_one[at, cols] = stream_in[at, cols] + total * valid
        low = stream_one[at, :].astype(BF16)
        one_low[at, :] = low
        queries[at, :] = dot_nn(low, w_query[...]).astype(BF16)

    def forward(second, beside_one=None, beside_two=None):
        copies = []
        for u in range(utterances):
            at = rows(u)
            if second:
                memory_block(u)
            frame_ok = frame_lane < memory_lengths[u]
            for h in range(heads):
                cols = pl.ds(h * HD, HD)
                scores = dot_nt(queries[at, cols], key_of(u, h)) * score_scale
                scores = jnp.where(frame_ok, scores, NEG)
                raised = jnp.exp(scores - jnp.max(scores, axis=-1, keepdims=True))
                prob = raised * (1.0 / jnp.sum(raised, axis=-1, keepdims=True))
                if second:
                    probs[u, h] = prob
                mixed[at, cols] = dot_nn(prob.astype(BF16), value_of(u, h)).astype(BF16)
            sent[u] = dot_nn(mixed[at, :], w_out[...])
            copies.append(swap(sent.at[u], arrived.at[u], sibling))
        if not second:
            beside_one()
            load_in.wait()
            load_back.wait()
        ff_copies = []
        for u in range(utterances):
            at = rows(u)
            copies[u].wait()
            two = stream_one[at, :] + (sent[u] + arrived[u])
            stream_two[at, :] = two
            hat, _ = normalise(two)
            norm = hat * gain_2 + bias_2
            low = norm.astype(BF16)
            norm_low[at, :] = low
            if second:
                r.norm_wide[u] = norm
                if u == utterances - 1:
                    norm_swap = swap(r.norm_wide.at[core], r.norm_got.at[0], {"dp": mate[1]})
            pre = dot_nn(low, w_in[...])
            phi = 0.5 * (1.0 + lax.erf(pre * math.sqrt(0.5)))
            hidden[at, :] = (pre * phi).astype(BF16)
            if second:
                gelu_slope[at, :] = phi + pre * (
                    jnp.exp(-0.5 * pre * pre) * (1.0 / math.sqrt(2.0 * math.pi))
                )
            sent[utterances + u] = dot_nn(hidden[at, :], w_back[...])
            ff_copies.append(swap(sent.at[utterances + u], arrived.at[utterances + u], sibling))
        if not second:
            beside_two()
        for u in range(utterances):
            at = rows(u)
            ff_copies[u].wait()
            three = stream_two[at, :] + (sent[utterances + u] + arrived[utterances + u])
            stream_three[u] = three
            top[0, at, :] = three.astype(BF16)
        return norm_swap if second else None

    stream_in[...] = acoustic[...].astype(F32)

    def beside_one():
        look_up_block(0)
        look_up_block(1)

    def beside_two():
        for k in range(2, per_core):
            look_up_block(k)
        look_up_rest()

    load_query.wait()
    for u in range(utterances):
        memory_block(u)
    load_memory.wait()
    for copy in load_kv:
        copy.wait()
    kv_rows = 512
    kv_chunks = frames // kv_rows

    def kv_step(i, carry):
        at = pl.ds(pl.multiple_of(i * kv_rows, kv_rows), kv_rows)
        group = jnp.zeros((1, width), jnp.int32) + rate_groups[i // kv_chunks]
        rate_row = jnp.where(group == 1, rate_table[pl.ds(1, 1), :], rate_table[pl.ds(0, 1), :])
        low = (mem_low[at, :].astype(F32) + rate_row).astype(BF16)
        mem_low[at, :] = low
        kv[at, :] = dot_nn(low, w_kv[...]).astype(BF16)
        return carry

    lax.fori_loop(0, utterances * kv_chunks, kv_step, 0)

    pl.semaphore_wait(barrier, n_dp)
    load_out.wait()
    forward(False, beside_one, beside_two)
    table_swap = swap(taken_mine, taken_theirs, sibling)
    load_vocab.wait()
    w_rest[pl.ds(0, vocab_here - main), :] = w_vocab[pl.ds(main, vocab_here - main), :]
    own_local = local_targets(own_target)
    mine = vocab_stats(own_local)
    stats[0] = side_by_side(mine)
    first_swap = swap(stats.at[0], stats_arrived.at[0], sibling)
    table_swap.wait()
    first_swap.wait()
    log_total, picked = join(mine, [stats_arrived[0, :, i : i + 1] for i in range(3)])
    first_loss = (log_total - picked) * own_valid
    blend = own_columns[:, 2:3] * own_valid / (1.0 + jnp.exp(math.log(V) - first_loss))
    for u in range(utterances):
        at = rows(u)
        wide_acoustic = acoustic[at, :].astype(F32)
        taken = taken_mine[u] + taken_theirs[u]
        stream_in[at, :] = wide_acoustic + blend[u * slots : (u + 1) * slots] * (taken - wide_acoustic)

    norm_swap = forward(True)
    token_swaps = [
        swap(stream_three.at[core], gathered.at[j - 1, 0], {"dp": mate[j]}) for j in (1, 2)
    ]
    mine = vocab_stats(own_local, keep=True)
    stats[1] = side_by_side(mine)
    stat_swap = swap(stats.at[1], stats_arrived.at[1], sibling)
    stat_swap.wait()
    log_column, picked = join(mine, [stats_arrived[1, :, i : i + 1] for i in range(3)])

    factor = jnp.exp(mine[0] - log_column) * own_valid
    valid_local = jnp.where(own_valid > 0.0, own_local, -1)

    def slope(j, carry):
        col = pl.multiple_of(j * 128, 128)
        ids = col + lax.broadcasted_iota(jnp.int32, (1, 128), 1)
        grad = logits[j] * factor - jnp.where(ids == valid_local, 1.0, 0.0)
        grad_logits[:, pl.ds(col, 128)] = grad.astype(BF16)
        return carry

    lax.fori_loop(0, main // 128 + 1, slope, 0, unroll=3)
    three_copies = []
    for u in range(utterances):
        sent[u] = dot_nn(grad_logits[rows(u), pl.ds(0, main)], w_vocab[pl.ds(0, main), :]) + dot_nn(
            grad_logits[rows(u), pl.ds(main, 128)], w_rest[...]
        )
        three_copies.append(swap(sent.at[u], arrived.at[u], sibling))
    for copy in token_swaps:
        copy.wait()
    part = slots // 2
    relays = [
        swap(gathered.at[0, 0, pl.ds(0, part)], gathered.at[2, 0, pl.ds(0, part)], {"dp": mate[2]}),
        swap(gathered.at[1, 0, pl.ds(part, part)], gathered.at[2, 0, pl.ds(part, part)], {"dp": mate[1]}),
    ]
    share_swaps = [swap(gathered.at[j, 0], gathered.at[j, 1], sibling) for j in range(2)]
    meta[0] = to_rows([own_target, own_valid, log_column, (log_column - picked) * own_valid])
    meta_swaps = [swap(meta.at[0], meta.at[j], {"dp": mate[j]}) for j in range(1, 4)]
    for u in range(utterances):
        r.loss_sum[pl.ds(u, 1), :] = meta[0, 3:4, u * slots : (u + 1) * slots]
    store(r.loss_sum, r.loss_out)

    plan = Planner()
    steps_all = len(bits)
    scatter_send, scatter_recv = r.scatter_send, r.scatter_recv

    vocab_parts = []

    def vocab_done():
        vocab_parts.append(1)
        if len(vocab_parts) == 1 + part_cols // 512:
            store(r.vocab_whole, r.vocab_out)

    def make_chunk(index):
        name, start, cols, order = chunk_list(part_cols, width, bits, low_bits, r)[index]
        source, landing = getattr(r, "src_" + name), r.landing[index]
        out_start = start
        if name == "kv":
            out, final = ((r.key_sum, r.key_out), (r.value_sum, r.value_out))[start // cols]
            out_start = 0
        else:
            out, final = getattr(r, name + "_sum"), getattr(r, name + "_out")
        rows_here = source.shape[-2]

        def pick(step, which):
            rest = sorted([b for b in bits if b not in order[:step]], reverse=True)
            where = tuple(which if b == order[step] else slice(None) for b in rest)
            if step == 0:
                return source, where + (slice(None), pl.ds(start, cols))
            return landing[step - 1], where + (slice(None), slice(None))

        def send(step):
            b = order[step]
            ref, where = pick(step, 1 - bit_of[b])
            copy = pltpu.make_async_remote_copy(
                src_ref=ref.at[where],
                dst_ref=landing[step],
                send_sem=scatter_send.at[index, step],
                recv_sem=scatter_recv.at[index, step],
                device_id=peer_of[b],
                device_id_type=MESH,
            )
            copy.start()
            return copy

        def take(step, copy):
            copy.wait_recv()
            ref, where = pick(step, bit_of[order[step]])
            got = landing[step]
            at = pl.ds(out_start, cols)
            if step < len(order) - 1:
                got[...] = got[...] + ref[where]
                return
            if name in ("back", "in") and not low_bits:
                here = pl.multiple_of(bit_0 * cols, cols)
                there = pl.multiple_of((1 - bit_0) * cols, cols)
                out[:, pl.ds(here, cols)] = ref[where]
                out[:, pl.ds(there, cols)] = got[...]
                store(out, final)
                return
            out[..., at] = got[...] + ref[where]
            if low_bits or name not in ("vocab", "rest"):
                store(out.at[..., at], final.at[..., at])
            elif name == "rest":
                rest = vocab_here - main
                r.vocab_whole[:, pl.ds(main, rest)] = out[...][:, :rest]
                vocab_done()

        steps = [
            (link_of(b, bits), rows_here * cols * 4 * 2 ** (steps_all - 1 - s))
            for s, b in enumerate(order)
        ]
        return Chunk(steps, send, take)

    def make_trade(start, cols):
        summed, traded = r.vocab_sum, r.vocab_traded
        at = pl.ds(start, cols)

        def send(step):
            copies = []
            for j in range(1, 4):
                to = lax.rem(mate[j], 4)
                copies.append(
                    pltpu.make_async_remote_copy(
                        src_ref=summed.at[to // 2, lax.rem(to, 2), :, at],
                        dst_ref=traded.at[j - 1, :, at],
                        send_sem=r.trade_send.at[start // 128, j - 1],
                        recv_sem=r.trade_recv.at[start // 128, j - 1],
                        device_id={"dp": mate[j]},
                        device_id_type=MESH,
                    )
                )
                copies[-1].start()
            return Several(copies)

        def take(step, copies):
            copies.wait_recv()
            for j in range(1, 4):
                there = pl.multiple_of(lax.rem(mate[j], 4) * part_cols + start, 128)
                r.vocab_whole[:, pl.ds(there, cols)] = traded[j - 1, :, at]
            here = pl.multiple_of(base + start, 128)
            r.vocab_whole[:, pl.ds(here, cols)] = summed[quarter // 2, lax.rem(quarter, 2), :, at]
            vocab_done()

        return Chunk([(0, 2 * r.src_vocab.shape[-2] * cols * 4)], send, take)

    chunks = {}
    for index, (name, start, cols, _) in enumerate(chunk_list(part_cols, width, bits, low_bits, r)):
        chunks[name, start] = make_chunk(index)
        if name == "vocab" and not low_bits:
            chunks[name, start].follow = make_trade(start, cols)

    def put(name, at, product):
        source = getattr(r, "src_" + name)
        source[..., at] = product.reshape(source.shape[:-1] + (product.shape[1],))

    for u in range(utterances):
        three_copies[u].wait()
        three = sent[u] + arrived[u]
        grad_three[u] = three
        branch_low[rows(u), :] = three.astype(BF16)
    pair_swap = swap(grad_three.at[core], r.three_got.at[0], {"dp": mate[1]})
    norm_swap.wait()
    share_norm = swap(r.norm_got.at[0], r.norm_got.at[1], sibling)

    at_core = pl.ds(pl.multiple_of(core * slots, slots), slots)
    at_other = pl.ds(pl.multiple_of((1 - core) * slots, slots), slots)
    base = pl.multiple_of(quarter * part_cols, part_cols)
    pieces = [(c, 256) for c in range(0, part_cols, 256)]
    for j in range(1, 4):
        if j == 2:
            for copy in relays:
                copy.wait()
            share_swaps.append(swap(gathered.at[2, 0], gathered.at[2, 1], sibling))
        meta_swaps[j - 1].wait()
        columns = to_columns(meta[j])
        valid = columns[:, 1:2] > 0.0
        target = jnp.where(valid, local_targets(columns[:, 0:1]), -1)
        log_total = jnp.where(valid, columns[:, 2:3], -NEG)
        top[j, at_core, :] = gathered[j - 1, 0].astype(BF16)
        share_swaps[j - 1].wait()
        top[j, at_other, :] = gathered[j - 1, 1].astype(BF16)
        for col, cols in pieces:
            ids = base + col + lax.broadcasted_iota(jnp.int32, (1, cols), 1)
            tile = dot_nt(top[j], w_vocab[pl.ds(base + col, cols), :])
            grad = jnp.exp(tile - log_total) - jnp.where(ids == target, 1.0, 0.0)
            grad_others[pl.ds((j - 1) * tokens, tokens), pl.ds(col, cols)] = grad.astype(BF16)
    top_turned = r.top_turned
    for j in range(4):
        top_turned[:, pl.ds(j * tokens, tokens)] = top[j].T
    plan.free[link_of(0, bits)] = 11.0
    plan.free[link_of(1, bits)] = 6.0
    plan.run_until(9.0)
    put("rest", slice(None), dot_nn(top_turned[:, pl.ds(0, tokens)], grad_logits[:, pl.ds(main, 128)]))
    starts = sorted(start for name, start in chunks if name == "vocab")
    for start, stop in zip(starts, starts[1:] + [part_cols]):
        for col in range(start, stop, 256):
            cols = min(256, stop - col)
            product = dot_nn(top_turned[:, pl.ds(0, tokens)], grad_logits[:, pl.ds(base + col, cols)])
            product = product + dot_nn(
                top_turned[:, pl.ds(tokens, 3 * tokens)], grad_others[:, pl.ds(col, cols)]
            )
            put("vocab", pl.ds(col, cols), product)
        plan.run_until(plan.now + 0.7)
        plan.post(chunks["vocab", start])
    plan.post(chunks["rest", 0])

    copies = []
    for u in range(utterances):
        at = rows(u)
        low = branch_low[at, :]
        pre = (dot_nt(low, w_back[...]) * gelu_slope[at, :]).astype(BF16)
        grad_pre[at, :] = pre
        sent[utterances + u] = dot_nt(pre, w_in[...])
        copies.append(swap(sent.at[utterances + u], arrived.at[utterances + u], sibling))
    plan.run_until(plan.now + 3.0)
    pair_swap.wait()
    share_three = swap(r.three_got.at[0], r.three_got.at[1], sibling)
    units_half = w_in.shape[1] // 2
    mine = pl.ds(pl.multiple_of(bit_0 * units_half, units_half), units_half)
    norm_mate, three_mate = r.norm_mate, r.three_mate
    share_norm.wait()
    norm_mate[at_core, :] = r.norm_got[0].astype(BF16)
    norm_mate[at_other, :] = r.norm_got[1].astype(BF16)
    pre = dot_nn(norm_mate[...], w_in[:, mine])
    phi = 0.5 * (1.0 + lax.erf(pre * math.sqrt(0.5)))
    r.hidden_mate[...] = (pre * phi).astype(BF16)
    slope_mate = phi + pre * (jnp.exp(-0.5 * pre * pre) * (1.0 / math.sqrt(2.0 * math.pi)))
    three_mate[at_core, :] = r.three_got[0].astype(BF16)
    share_three.wait()
    three_mate[at_other, :] = r.three_got[1].astype(BF16)
    r.pre_mate[...] = (dot_nt(three_mate[...], w_back[mine, :]) * slope_mate).astype(BF16)
    plan.run_until(plan.now + 2.0)
    for name, left, right, left_mate, right_mate in (
        ("back", branch_low, hidden, three_mate, r.hidden_mate),
        ("in", norm_low, grad_pre, norm_mate, r.pre_mate),
    ):
        put(
            name,
            slice(None),
            dot_nn(left[...].T, right[:, mine]) + dot_nn(left_mate[...].T, right_mate[...]),
        )
        plan.run_until(plan.now + 0.8)
        plan.post(chunks[name, 0])

    one_copies = []
    gain_2_total, bias_2_total = 0.0, 0.0
    for u in range(utterances):
        at = rows(u)
        copies[u].wait()
        grad_norm = sent[utterances + u] + arrived[utterances + u]
        hat, scale = normalise(stream_two[at, :])
        gain_2_total = gain_2_total + jnp.sum(grad_norm * hat, axis=0, keepdims=True)
        bias_2_total = bias_2_total + jnp.sum(grad_norm, axis=0, keepdims=True)
        two = grad_three[u] + normalise_back(grad_norm * gain_2, hat, scale)
        grad_two[at, :] = two
        low = two.astype(BF16)
        att_low[at, :] = low
        grad_mixed = dot_nt(low, w_out[...]).astype(BF16)
        for h in range(heads):
            cols = pl.ds(h * HD, HD)
            grad_head = grad_mixed[:, h * HD : (h + 1) * HD]
            prob = probs[u, h]
            grad_prob = dot_nt(grad_head, value_of(u, h))
            spare[pl.ds(u * frames, frames), pl.ds(half + h * HD, HD)] = dot_tn(
                prob.astype(BF16), grad_head
            ).astype(BF16)
            inner = jnp.sum(prob * grad_prob, axis=-1, keepdims=True)
            grad_score = (prob * (grad_prob - inner)).astype(BF16)
            grad_queries[at, cols] = (dot_nn(grad_score, key_of(u, h)) * score_scale).astype(BF16)
            spare[pl.ds(u * frames, frames), cols] = (
                dot_tn(grad_score, queries[at, cols]) * score_scale
            ).astype(BF16)
            plan.run_until(plan.now + 1.5)
        sent[u] = dot_nt(grad_queries[at, :], w_query[...])
        one_copies.append(swap(sent.at[u], arrived.at[u], sibling))
    every = slice(None)
    put("out", every, dot_tn(att_low[...], mixed[...]))
    plan.post(chunks["out", 0])
    put("query", every, dot_tn(one_low[...], grad_queries[...]))
    plan.post(chunks["query", 0])
    plan.run_until(plan.now + 1.0)

    mem_copies = []
    rate_sums = [0.0, 0.0]
    for u in range(utterances):
        total = jnp.zeros((1, width), F32)
        for i in range(row_chunks):
            at = pl.ds(u * frames + i * step_rows, step_rows)
            part = dot_nt(spare[at, :], w_kv[...])
            for j in range(width // 128):
                side_of, tile = j // (width // 256), j % (width // 256)
                index = ((side_of * utterances + u) * row_chunks + i) * (width // 256) + tile
                logits[index] = part[:, j * 128 : (j + 1) * 128]
            total = total + jnp.sum(part, axis=0, keepdims=True)
        tiles = row_chunks * (width // 256)
        mem_copies.append(
            swap(
                logits.at[pl.ds(((1 - core) * utterances + u) * tiles, tiles)],
                mem_arrived.at[pl.ds(u * tiles, tiles)],
                sibling,
            )
        )
        group = jnp.zeros((1, width), jnp.int32) + rate_groups[u]
        for k in range(2):
            rate_sums[k] = rate_sums[k] + jnp.where((group == 1) == (k == 1), total, 0.0)
        plan.run_until(plan.now + 1.2)
    span = frames // 2
    for k in range(2 * utterances):
        at = pl.ds(k * span, span)
        product = dot_tn(mem_low[at, :], spare[at, :])
        product = product.reshape(r.src_kv.shape)
        r.src_kv[...] = product if k == 0 else r.src_kv[...] + product
    plan.run_until(plan.now + 2.0)
    plan.post(*[chunks["kv", start] for start in sorted(s for n, s in chunks if n == "kv")])

    gain_1_total, bias_1_total = 0.0, 0.0
    for u in range(utterances):
        at = rows(u)
        valid = own_valid[u * slots : (u + 1) * slots]
        one_copies[u].wait()
        one = grad_two[at, :] + (sent[u] + arrived[u])
        grad_two[at, :] = one
        masked = one * valid
        for k in range(kernel_rows.shape[0]):
            shift = 8 + k - kernel_rows.shape[0] // 2
            row = jnp.sum(masked * padded[u, pl.ds(shift, slots), :], axis=0, keepdims=True)
            if u == 0:
                small_sent[0, pl.ds(k, 1), :] = row
            else:
                small_sent[0, pl.ds(k, 1), :] = small_sent[0, pl.ds(k, 1), :] + row
        padded[u, pl.ds(8, slots), :] = masked
        for j in range(width // 128):
            cols = pl.ds(j * 128, 128)
            total = jnp.zeros((slots, 128), F32)
            for k in range(kernel_rows.shape[0]):
                shift = 8 - k + kernel_rows.shape[0] // 2
                total = total + kernel_rows[pl.ds(k, 1), cols] * padded[u, pl.ds(shift, slots), cols]
            stream_one[at, cols] = total * valid
        grad_norm = stream_one[at, :]
        hat, scale = normalise(stream_in[at, :])
        gain_1_total = gain_1_total + jnp.sum(grad_norm * hat, axis=0, keepdims=True)
        bias_1_total = bias_1_total + jnp.sum(grad_norm, axis=0, keepdims=True)
        zero = grad_two[at, :] + normalise_back(grad_norm * gain_1, hat, scale)
        terms[u] = blend[u * slots : (u + 1) * slots] * zero
        stream_one[at, :] = zero - terms[u]
        plan.run_until(plan.now + 1.5)

    last_taps = kernel_rows.shape[0]
    small_sent[0, pl.ds(last_taps, 12 - last_taps), :] = jnp.zeros((12 - last_taps, width), F32)
    for i, row in enumerate((gain_1_total, bias_1_total, gain_2_total, bias_2_total)):
        small_sent[0, pl.ds(12 + i, 1), :] = row
    for k in range(2):
        small_sent[0, pl.ds(16 + k, 1), :] = rate_sums[k]
    small_sent[0, pl.ds(18, 6), :] = jnp.zeros((6, width), F32)
    small_peers = [peer_of[b] for b in low_bits + bits] + [sibling]

    def small_send(step):
        copy = pltpu.make_async_remote_copy(
            src_ref=small_sent.at[step],
            dst_ref=small_arrived.at[step],
            send_sem=r.small_send.at[step],
            recv_sem=r.small_recv.at[step],
            device_id=small_peers[step],
            device_id_type=MESH,
        )
        copy.start()
        return copy

    def small_take(step, copy):
        copy.wait_recv()
        if step + 1 == len(small_peers):
            copy.wait_send()
            plan.started = [c for c in plan.started if c is not copy]
        if step + 1 < len(small_peers):
            small_sent[step + 1] = small_sent[step] + small_arrived[step]
        else:
            small_sent[step, pl.ds(16, 8), :] = (
                small_sent[step, pl.ds(16, 8), :] + small_arrived[step, pl.ds(16, 8), :]
            )
            store(small_sent.at[step], r.small_out)

    small_links = [link_of(b, bits) for b in low_bits + bits] + ["core"]
    plan.post(Chunk([(l, 24 * width * 4) for l in small_links], small_send, small_take))

    features = width // n_dp
    feature_rows = max(features, 8)
    block_rows = term_blocks.shape[1]
    turned = terms[core].T
    id_row = targets[pl.ds(core, 1), :].astype(F32)
    rest = block_rows - features - 1
    for p in range(n_dp):
        term_blocks[p, pl.ds(0, features), :] = turned[p * features : (p + 1) * features]
        term_blocks[p, pl.ds(features, 1), :] = id_row
        term_blocks[p, pl.ds(features + 1, rest), :] = jnp.zeros((rest, slots), F32)

    def term_copy(k):
        there = lax.rem(me + k, n_dp)
        return pltpu.make_async_remote_copy(
            src_ref=term_blocks.at[there],
            dst_ref=term_arrived.at[me],
            send_sem=r.term_send.at[k],
            recv_sem=r.term_recv.at[k],
            device_id={"dp": there},
            device_id_type=MESH,
        )

    def term_start(k, carry):
        term_copy(k).start()
        return carry

    def term_wait(k, carry):
        term_copy(k).wait()
        return carry

    term_arrived[me] = term_blocks[me]
    lax.fori_loop(1, n_dp, term_start, 0)
    store(stream_one, r.acoustic_out)
    for u in range(utterances):
        mem_copies[u].wait()
        for i in range(row_chunks):
            for j in range(width // 256):
                index = (u * row_chunks + i) * (width // 256) + j
                first_tile = (core * utterances) * row_chunks * (width // 256)
                mem_arrived[index] = logits[first_tile + index] + mem_arrived[index]
                at = pl.ds(u * frames + i * step_rows, step_rows)
                store(mem_arrived.at[index], r.memory_out.at[at, pl.ds(j * 128, 128)])
    plan.run_until(plan.now + 8.0)
    lax.fori_loop(1, n_dp, term_wait, 0)
    per_piece = 512 // slots
    blocks_hi = (table_rows + 255) // 256
    batch = 4

    def table_piece(p, fresh):
        found = [term_arrived[p * per_piece + i] for i in range(per_piece)]
        values = jnp.concatenate([f[:feature_rows] for f in found], axis=1)
        ids = jnp.concatenate([f[features : features + 1] for f in found], axis=1).astype(jnp.int32)
        low_ids, high_ids = ids & 255, ids >> 8
        onehot_lo[...] = jnp.where(
            lax.broadcasted_iota(jnp.int32, (256, 512), 0) == low_ids, 1.0, 0.0
        ).astype(BF16)
        coarse = values.astype(BF16).astype(F32)
        both = jnp.concatenate([coarse, values - coarse], axis=0)
        for first_hi in range(0, blocks_hi, batch):
            here = range(first_hi, min(first_hi + batch, blocks_hi))
            masked = jnp.concatenate([jnp.where(high_ids == hi, both, 0.0) for hi in here], axis=0)
            product = dot_nt(masked.astype(BF16), onehot_lo[...])
            for i, hi in enumerate(here):
                top_part = product[2 * i * feature_rows : (2 * i + 1) * feature_rows]
                low_part = product[(2 * i + 1) * feature_rows : (2 * i + 2) * feature_rows]
                cols = min(256, table_rows - hi * 256)
                at = pl.ds(hi * 256, cols)
                found = (top_part + low_part)[:features, :cols]
                whole_table[:, at] = found if fresh else whole_table[:, at] + found

    pieces = n_dp // per_piece
    table_piece(0, True)
    if pieces <= 4:
        for p in range(1, pieces):
            plan.run_until(plan.now + 1.5)
            table_piece(p, False)
    else:
        lax.fori_loop(1, pieces, lambda p, c: (table_piece(p, False), c)[1], 0)
    table_swap = swap(whole_table, table_theirs, sibling)
    plan.run_until(plan.now + 8.0)
    table_swap.wait()
    whole_table[...] = whole_table[...] + table_theirs[...]
    store(whole_table, r.table_out)
    plan.finish()
    for copy in stores:
        copy.wait()


def link_of(bit, bits):
    if bit == bits[-1]:
        return bits[-2]
    return bit


def chunk_list(part_cols, width, bits, low_bits, sizes):
    turned = [bits[1], bits[0]] + bits[2:]
    listing = []
    for start in range(0, part_cols, 512):
        listing.append(("vocab", start, 512, [b for b in bits if b > 1]))
    last = [] if low_bits else [0]
    for name in ("back", "in"):
        listing.append((name, 0, sizes.units // 2, [b for b in bits if b > 0] + last))
    listing.append(("rest", 0, 128, bits))
    listing.append(("out", 0, sizes.half, bits))
    listing.append(("query", 0, sizes.half, bits))
    for k, start in enumerate(range(0, 2 * sizes.half, 256)):
        listing.append(("kv", start, 256, [bits, turned][k % 2]))
    return listing


def decoder_call(
    acoustic, memory, embedding, w_query, w_key, w_value, w_out, w_in, w_back, w_vocab, norms,
    fsmn_kernel, rate_table, token_lengths, memory_lengths, rate_groups, glance, targets, n_dp,
):
    utterances = token_lengths.shape[0]
    tokens, width = acoustic.shape
    slots = tokens // utterances
    mem_rows = memory.shape[0]
    half = w_query.shape[1]
    heads = half // HD
    frames = mem_rows // utterances
    units = w_in.shape[1]
    vocab_here = w_vocab.shape[1]
    table_rows = embedding.shape[0]
    part_cols = vocab_here // 512 * 128
    all_cols = 4 * part_cols + 128
    w_turned = w_vocab.T
    mains = table_rows // 2048 * 2048
    nbits = n_dp.bit_length() - 1
    steps = nbits
    while width >> steps < 8:
        steps -= 1
    low_bits, bits = list(range(nbits - steps)), list(range(nbits - steps, nbits))
    rows = width >> steps
    unit_cols = units // 2 if low_bits else units
    features = width // n_dp
    feature_rows = max(features, 8)
    block_rows = feature_rows + 8 if features >= 8 else 8
    blocks_hi = (table_rows + 255) // 256
    sizes = SimpleNamespace(units=units, half=half)
    plane = [b for b in bits if b < 2]
    listing = chunk_list(part_cols, width, bits, low_bits, sizes)
    most = max(len(c[3]) for c in listing)

    f32 = lambda *shape: jax.ShapeDtypeStruct(shape, F32)
    v32 = lambda *shape: pltpu.VMEM(shape, F32)
    v16 = lambda *shape: pltpu.VMEM(shape, BF16)
    dma = lambda *shape: pltpu.SemaphoreType.DMA(shape)
    inputs = dict(
        acoustic=(VMEM, acoustic),
        table_tail=(VMEM, embedding[mains + (table_rows - mains) // 16 * 16 :]),
        memory=(ANY, memory),
        table=(ANY, embedding),
        w_query_hbm=(ANY, w_query),
        w_key_hbm=(ANY, w_key),
        w_value_hbm=(ANY, w_value),
        w_out_hbm=(ANY, w_out),
        w_in_hbm=(ANY, w_in),
        w_back_hbm=(ANY, w_back),
        w_vocab_hbm=(ANY, w_turned),
        gain_one=(VMEM, norms[0][None]),
        bias_one=(VMEM, norms[1][None]),
        gain_two=(VMEM, norms[2][None]),
        bias_two=(VMEM, norms[3][None]),
        kernel_rows=(VMEM, fsmn_kernel),
        rate_table=(VMEM, rate_table),
        token_lengths=(SMEM, token_lengths),
        memory_lengths=(SMEM, memory_lengths),
        rate_groups=(SMEM, rate_groups),
        glance=(VMEM, glance.reshape(utterances, slots)),
        targets=(VMEM, targets.reshape(utterances, slots)),
    )
    outputs = dict(
        loss_out=f32(utterances, slots),
        small_out=f32(24, width),
        vocab_out=f32(2, rows, part_cols) if low_bits else f32(rows, vocab_here),
        rest_out=f32(rows, 128),
        in_out=f32(rows, unit_cols),
        back_out=f32(rows, unit_cols),
        query_out=f32(rows, half),
        out_out=f32(rows, half),
        key_out=f32(rows, half),
        value_out=f32(rows, half),
        acoustic_out=f32(tokens, width),
        memory_out=f32(mem_rows, width // 2),
        table_out=f32(features, table_rows),
    )
    shape = (2,) * steps + (rows,)
    scratch = dict(
        w_query=v16(width, half),
        w_kv=v16(width, 2 * half),
        w_out=v16(half, width),
        w_in=v16(width, units),
        w_back=v16(units, width),
        w_vocab=v16(vocab_here, width),
        w_rest=v16(128, width),
        mem_low=v16(mem_rows, width),
        kv=v16(mem_rows, 2 * half),
        spare=v16(mem_rows, 2 * half),
        padded=v32(utterances, slots + 16, width),
        stream_in=v32(tokens, width),
        stream_one=v32(tokens, width),
        stream_two=v32(tokens, width),
        stream_three=v32(utterances, slots, width),
        one_low=v16(tokens, width),
        queries=v16(tokens, half),
        probs=v32(utterances, heads, slots, frames),
        mixed=v16(tokens, half),
        norm_low=v16(tokens, width),
        hidden=v16(tokens, units),
        gelu_slope=v32(tokens, units),
        top=v16(4, tokens, width),
        logits=v32(all_cols // 128, tokens, 128),
        grad_logits=v16(tokens, all_cols),
        grad_others=v16(3 * tokens, part_cols),
        top_turned=v16(width, 4 * tokens),
        taken_theirs=v32(utterances, slots, width),
        grad_three=v32(utterances, slots, width),
        grad_two=v32(tokens, width),
        branch_low=v16(tokens, width),
        grad_pre=v16(tokens, units),
        att_low=v16(tokens, width),
        grad_queries=v16(tokens, half),
        mem_arrived=v32(mem_rows // 256 * (width // 256), 256, 128),
        meta=v32(4, 8, tokens),
        stats=v32(2, tokens, 128),
        stats_arrived=v32(2, tokens, 128),
        sent=v32(2 * utterances, slots, width),
        arrived=v32(2 * utterances, slots, width),
        gathered=v32(3, 2, slots, width),
        small_sent=v32(nbits + 1, 24, width),
        small_arrived=v32(nbits + 1, 24, width),
        term_blocks=v32(n_dp, block_rows, slots),
        term_arrived=v32(n_dp, block_rows, slots),
        onehot_lo=v16(256, 512),
        table_rest=v16((table_rows - mains + 127) // 128 * 128, width),
        table_theirs=v32(features, table_rows),
        src_vocab=v32(*shape, part_cols),
        src_rest=v32(*shape, 128),
        whole_table=v32(features, table_rows),
        src_back=v32(*shape, units // 2),
        vocab_sum=v32(*(2,) * len(plane), rows, part_cols),
        rest_sum=v32(rows, 128),
        vocab_whole=v32(rows, vocab_here),
        in_sum=v32(rows, unit_cols),
        back_sum=v32(rows, unit_cols),
        query_sum=v32(rows, half),
        out_sum=v32(rows, half),
        key_sum=v32(rows, half),
        value_sum=v32(rows, half),
        loss_sum=v32(utterances, slots),
        vocab_traded=v32(3, rows, part_cols),
        src_in=v32(*shape, units // 2),
        norm_wide=v32(utterances, slots, width),
        norm_got=v32(2, slots, width),
        three_got=v32(2, slots, width),
        norm_mate=v16(tokens, width),
        three_mate=v16(tokens, width),
        hidden_mate=v16(tokens, units // 2),
        pre_mate=v16(tokens, units // 2),
        src_out=v32(*shape, half),
        src_query=v32(*shape, half),
        src_kv=v32(*shape, 2 * half),
        load_sem=dma(24),
        store_sem=dma(48),
        trade_send=dma(part_cols // 128, 3),
        trade_recv=dma(part_cols // 128, 3),
        swap_send=dma(40),
        swap_recv=dma(40),
        scatter_send=dma(len(listing), most),
        scatter_recv=dma(len(listing), most),
        small_send=dma(nbits + 1),
        small_recv=dma(nbits + 1),
        term_send=dma(n_dp),
        term_recv=dma(n_dp),
    )
    landing = [
        [v32(*(2,) * (steps - 1 - s), rows, cols) for s in range(len(order))]
        for _, _, cols, order in listing
    ]
    names = list(inputs) + list(outputs) + list(scratch)
    flat = [ref for chunk in landing for ref in chunk]

    def kernel(*refs):
        named, rest = refs[: len(names)], list(refs[len(names) :])
        lands = [[rest.pop(0) for _ in chunk] for chunk in landing]
        decoder_kernel(
            names + ["landing", "units", "half"], vocab_here, part_cols, table_rows, n_dp, bits,
            low_bits, *named, lands, units, half,
        )

    out = pl.pallas_call(
        kernel,
        out_shape=list(outputs.values()),
        in_specs=[spec for spec, _ in inputs.values()],
        out_specs=[ANY] * len(outputs),
        scratch_shapes=list(scratch.values()) + flat,
        compiler_params=pltpu.CompilerParams(
            collective_id=1, has_side_effects=True, vmem_limit_bytes=64 << 20
        ),
    )(*[value for _, value in inputs.values()])
    return SimpleNamespace(**dict(zip(outputs, out))), low_bits


def deliver_kernel(n_dp, n_passed, *refs):
    n = n_passed + 2
    sources, targets, held = refs[:n], refs[n : 2 * n + 5], refs[2 * n + 5 : 3 * n + 5]
    shaped, (sem_in, sem_out) = refs[3 * n + 5 : 3 * n + 12], refs[3 * n + 12 :]
    reads, writes = [], []
    for i, (source, buffer) in enumerate(zip(sources, held)):
        reads.append(pltpu.make_async_copy(source, buffer, sem_in.at[i]))
        reads[-1].start()
    for i in range(n_passed):
        reads[i].wait()
        writes.append(pltpu.make_async_copy(held[i], targets[i], sem_out.at[i]))
        writes[-1].start()
    reads[n_passed].wait()
    reads[n_passed + 1].wait()
    loss, small = held[n_passed:]
    loss_at, gain_one_at, bias_one_at, gain_two_at, bias_two_at, taps_at, rate_at = shaped
    slots = loss.shape[1]
    for u in range(loss.shape[0]):
        loss_at[:, pl.ds(u * slots, slots)] = loss[pl.ds(u, 1), :]
    me = lax.axis_index("dp")
    own = small.shape[1] // n_dp
    mine = jnp.zeros((16, own), F32)
    for p in range(n_dp):
        mine = jnp.where(me == p, small[pl.ds(0, 16), p * own : (p + 1) * own], mine)
    taps_at[...] = mine[: taps_at.shape[0]]
    for i, target in enumerate((gain_one_at, bias_one_at, gain_two_at, bias_two_at)):
        target[...] = mine[12 + i : 13 + i]
    rate_at[...] = small[pl.ds(16, 2), :]
    for i, source in enumerate(shaped):
        writes.append(pltpu.make_async_copy(source, targets[n_passed + i], sem_out.at[n_passed + i]))
        writes[-1].start()
    for copy in writes:
        copy.wait()


def per_device(
    acoustic,
    memory,
    embedding,
    w_query,
    w_key,
    w_value,
    w_out,
    w_in,
    w_back,
    w_vocab,
    gain_one,
    bias_one,
    gain_two,
    bias_two,
    fsmn_kernel,
    rate_table,
    token_lengths,
    memory_lengths,
    rate_groups,
    glance_mask,
    targets,
):
    tok_rows, model_width = acoustic.shape
    half = w_query.shape[1]
    n_dp = lax.axis_size("dp")
    result, low_bits = decoder_call(
        acoustic, memory, embedding, w_query, w_key, w_value, w_out, w_in, w_back, w_vocab,
        (gain_one, bias_one, gain_two, bias_two), fsmn_kernel, rate_table,
        token_lengths, memory_lengths, rate_groups, glance_mask, targets, n_dp,
    )
    vocab = result.vocab_out
    summed = [result.query_out, result.key_out, result.value_out, result.out_out]
    halves = [result.in_out, result.back_out]
    if low_bits:
        size = 1 << len(low_bits)
        groups = [list(range(g * size, (g + 1) * size)) for g in range(n_dp // size)]
        planes = [list(range(4 * g, 4 * g + 4)) for g in range(n_dp // 4)]
        vocab = lax.all_to_all(
            vocab.reshape(4, model_width // n_dp, -1), "dp", 0, 0, axis_index_groups=planes, tiled=True
        )
        *summed, rest = [
            lax.psum_scatter(s, "dp", scatter_dimension=0, axis_index_groups=groups, tiled=True)
            for s in (*summed, result.rest_out)
        ]
        vocab = jnp.concatenate([*vocab, rest], axis=1)[:, : w_vocab.shape[1]]
        pairs = [[2 * g, 2 * g + 1] for g in range(n_dp // 2)]
        halves = [
            jnp.concatenate(
                [
                    *lax.all_to_all(
                        h.reshape(2, model_width // n_dp, -1), "dp", 0, 0, axis_index_groups=pairs,
                        tiled=True,
                    )
                ],
                axis=1,
            )
            for h in halves
        ]
    own = model_width // n_dp
    f32 = lambda *shape: jax.ShapeDtypeStruct(shape, F32)
    like = lambda x: jax.ShapeDtypeStruct(x.shape, F32)
    passed = (result.memory_out, result.table_out, result.acoustic_out, vocab, *summed, *halves)
    handed = (*passed, result.loss_out, result.small_out)
    small_shapes = [
        f32(1, tok_rows), *[f32(1, own)] * 4, f32(fsmn_kernel.shape[0], own), f32(2, model_width)
    ]
    (
        grad_memory, grad_table, grad_acoustic, grad_vocab, grad_query, grad_key, grad_value,
        grad_out, grad_in, grad_back, token_loss, gain_1, bias_1, gain_2, bias_2, grad_taps, grad_rate,
    ) = pl.pallas_call(
        partial(deliver_kernel, n_dp, len(passed)),
        out_shape=[*[like(x) for x in passed], *small_shapes],
        in_specs=[ANY] * len(handed),
        out_specs=[ANY] * (len(passed) + 7),
        scratch_shapes=[pltpu.VMEM(x.shape, F32) for x in (*handed, *small_shapes)]
        + [pltpu.SemaphoreType.DMA((len(handed),)), pltpu.SemaphoreType.DMA((len(passed) + 7,))],
        compiler_params=pltpu.CompilerParams(vmem_limit_bytes=60 << 20),
    )(*handed)
    return (
        token_loss.reshape(tok_rows),
        grad_acoustic,
        grad_memory,
        grad_table.T,
        grad_query,
        grad_key,
        grad_value,
        grad_out.T,
        grad_in,
        grad_back.T,
        grad_vocab,
        gain_1.reshape(own),
        bias_1.reshape(own),
        gain_2.reshape(own),
        bias_2.reshape(own),
        grad_taps,
        grad_rate,
    )


def solution(mesh):
    return jax.shard_map(
        per_device,
        mesh=mesh,
        in_specs=(
            P("dp", None),
            P("dp", None),
            P(),
            P(None, "mp"),
            P(None, "mp"),
            P(None, "mp"),
            P("mp", None),
            P(None, "mp"),
            P("mp", None),
            P(None, "mp"),
            P(),
            P(),
            P(),
            P(),
            P(),
            P(),
            P("dp"),
            P("dp"),
            P("dp"),
            P("dp"),
            P("dp"),
        ),
        out_specs=(
            P("dp"),
            P("dp", None),
            P("dp", "mp"),
            P(None, "dp"),
            P("dp", "mp"),
            P("dp", "mp"),
            P("dp", "mp"),
            P("mp", "dp"),
            P("dp", "mp"),
            P("mp", "dp"),
            P("dp", "mp"),
            P("dp"),
            P("dp"),
            P("dp"),
            P("dp"),
            P(None, "dp"),
            P(),
        ),
        check_vma=False,
    )
```

```python
from functools import partial
import math
from types import SimpleNamespace

import jax
import jax.numpy as jnp
from jax import lax
from jax.experimental import pallas as pl
from jax.experimental.pallas import tpu as pltpu
from jax.sharding import PartitionSpec as P

HD = 128
V = 8404
EPSILON = 1e-05
MESH = pl.DeviceIdType.MESH
VMEM = pl.BlockSpec(memory_space=pltpu.VMEM)
SMEM = pl.BlockSpec(memory_space=pltpu.SMEM)
ANY = pl.BlockSpec(memory_space=pl.ANY)
F32, BF16 = jnp.float32, jnp.bfloat16
NEG = -1e30


def other_core():
    return {"mp": 1 - lax.axis_index("mp")}


def dot_nn(a, b):
    return lax.dot_general(a, b, (((1,), (0,)), ((), ())), preferred_element_type=F32)


def dot_nt(a, b):
    return lax.dot_general(a, b, (((1,), (1,)), ((), ())), preferred_element_type=F32)


def dot_tn(a, b):
    return lax.dot_general(a, b, (((0,), (0,)), ((), ())), preferred_element_type=F32)


def normalise(rows):
    average = jnp.mean(rows, axis=-1, keepdims=True)
    centred = rows - average
    variance = jnp.mean(centred * centred, axis=-1, keepdims=True)
    scale = lax.rsqrt(variance + EPSILON)
    return centred * scale, scale


def normalise_back(grad_hat, hat, scale):
    first = jnp.mean(grad_hat, axis=-1, keepdims=True)
    second = jnp.mean(grad_hat * hat, axis=-1, keepdims=True)
    return scale * (grad_hat - first - hat * second)


def side_by_side(columns):
    lane = lax.broadcasted_iota(jnp.int32, (columns[0].shape[0], 128), 1)
    tile = jnp.zeros(lane.shape, F32)
    for i, column in enumerate(columns):
        tile = jnp.where(lane == i, column, tile)
    return tile


def to_rows(columns):
    return side_by_side(columns).T[:8]


def to_columns(rows):
    return jnp.concatenate([rows] * 16, axis=0).T


class Planner:
    RATE = 0.045e6
    HOP = 4.0
    BACKLOG = 6.0

    def __init__(self):
        self.now = 0.0
        self.free = {}
        self.flying = []
        self.waiting = []
        self.started = []
        self.count = 0

    def launch(self, item, step):
        link, size = item.steps[step]
        begin = max(self.now, self.free.get(link, 0.0))
        self.free[link] = begin + size / self.RATE
        copy = item.send(step)
        self.started.append(copy)
        self.count += 1
        self.flying.append((self.free[link] + self.HOP, self.count, item, step, copy))

    def release(self):
        kept = []
        for item in self.waiting:
            link = item.steps[0][0]
            if self.free.get(link, 0.0) - self.now < self.BACKLOG:
                self.launch(item, 0)
            else:
                kept.append(item)
        self.waiting = kept

    def post(self, *items):
        self.waiting += items
        self.release()

    def run_until(self, time):
        while self.flying or self.waiting:
            if not self.flying:
                self.now = max(self.now, min(self.free[i.steps[0][0]] for i in self.waiting))
                self.release()
                continue
            first = min(self.flying, key=lambda f: f[:2])
            if first[0] > time:
                break
            self.flying.remove(first)
            self.now = max(self.now, first[0])
            _, _, item, step, copy = first
            item.take(step, copy)
            if step + 1 < len(item.steps):
                self.launch(item, step + 1)
            elif item.follow is not None:
                self.launch(item.follow, 0)
            self.release()
        if time != math.inf:
            self.now = max(self.now, time)
        self.release()

    def finish(self):
        self.run_until(math.inf)
        for copy in self.started:
            copy.wait_send()


class Chunk:
    def __init__(self, steps, send, take):
        self.steps, self.send, self.take, self.follow = steps, send, take, None


class Several:
    def __init__(self, copies):
        self.copies = copies

    def wait_recv(self):
        for copy in self.copies:
            copy.wait_recv()

    def wait_send(self):
        for copy in self.copies:
            copy.wait_send()


def decoder_kernel(
    names,
    vocab_here,
    part_cols,
    table_rows,
    n_dp,
    bits,
    low_bits,
    *refs,
):
    r = SimpleNamespace(**dict(zip(names, refs)))
    acoustic, memory, table = r.acoustic, r.memory, r.table
    targets, glance = r.targets, r.glance
    gain_1, bias_1 = r.gain_one[...], r.bias_one[...]
    gain_2, bias_2 = r.gain_two[...], r.bias_two[...]
    kernel_rows, rate_table = r.kernel_rows, r.rate_table
    token_lengths, memory_lengths, rate_groups = r.token_lengths, r.memory_lengths, r.rate_groups
    w_query, w_kv, w_out, w_in, w_back, w_vocab = r.w_query, r.w_kv, r.w_out, r.w_in, r.w_back, r.w_vocab
    mem_low, kv, padded, spare = r.mem_low, r.kv, r.padded, r.spare
    stream_in, stream_one, stream_two, stream_three = r.stream_in, r.stream_one, r.stream_two, r.stream_three
    one_low, queries, probs, mixed = r.one_low, r.queries, r.probs, r.mixed
    norm_low, hidden, gelu_slope, top = r.norm_low, r.hidden, r.gelu_slope, r.top
    logits, grad_logits, grad_others = r.logits, r.grad_logits, r.grad_others
    taken_mine, taken_theirs = r.grad_three, r.taken_theirs
    grad_three, grad_two, branch_low = r.grad_three, r.grad_two, r.branch_low
    grad_pre, att_low, grad_queries = r.grad_pre, r.att_low, r.grad_queries
    mem_arrived, meta, stats, stats_arrived = r.mem_arrived, r.meta, r.stats, r.stats_arrived
    sent, arrived, gathered = r.sent, r.arrived, r.gathered
    small_sent, small_arrived = r.small_sent, r.small_arrived
    terms, term_blocks, term_arrived = grad_three, r.term_blocks, r.term_arrived
    onehot_lo, table_theirs, whole_table = r.onehot_lo, r.table_theirs, r.whole_table
    swap_send, swap_recv, load_sem = r.swap_send, r.swap_recv, r.load_sem

    utterances, slots = targets.shape
    width = acoustic.shape[1]
    frames = memory.shape[0] // utterances
    half = w_query.shape[1]
    heads = half // HD
    tokens = utterances * slots
    me, core = lax.axis_index("dp"), lax.axis_index("mp")
    sibling = {"mp": 1 - core}
    quarter = lax.rem(me, 4)
    flips = [1 - 2 * lax.rem(me, 2), 2 - 4 * lax.rem(me // 2, 2)]
    mate = [me + flips[0] * (j % 2) + flips[1] * (j // 2) for j in range(4)]
    bit_of = {b: lax.rem(me // (1 << b), 2) for b in low_bits + bits}
    peer_of = {b: {"dp": me + (1 - 2 * bit_of[b]) * (1 << b)} for b in low_bits + bits}
    score_scale = 1.0 / math.sqrt(HD)

    loads = []

    def load(source, target):
        copy = pltpu.make_async_copy(source, target, load_sem.at[len(loads)])
        copy.start()
        loads.append(copy)
        return copy

    load_memory = load(memory, mem_low)
    load_kv = [
        load(r.w_key_hbm, w_kv.at[:, pl.ds(0, half)]),
        load(r.w_value_hbm, w_kv.at[:, pl.ds(half, half)]),
    ]
    load_query = load(r.w_query_hbm, w_query)
    load_out = load(r.w_out_hbm, w_out)

    barrier = pltpu.get_barrier_semaphore()

    def greet(k, carry):
        pl.semaphore_signal(
            barrier, inc=1, device_id={"dp": lax.rem(me + k, n_dp)}, device_id_type=MESH
        )
        return carry

    lax.fori_loop(1, n_dp, greet, 0)
    pl.semaphore_signal(barrier, inc=1, device_id=sibling, device_id_type=MESH)

    load_in = load(r.w_in_hbm, w_in)
    load_back = load(r.w_back_hbm, w_back)
    block = 1024
    per_core = table_rows // (2 * block)
    mains = 2 * per_core * block

    def load_table(k):
        at = pl.ds(pl.multiple_of((core * per_core + k) * block, block), block)
        return load(table.at[at, :], spare.at[pl.ds(k % 2 * block, block), :])

    table_loads = [load_table(0), load_table(1)]
    main = 4 * part_cols
    load_vocab = load(r.w_vocab_hbm, w_vocab)
    w_rest = r.w_rest
    w_rest[...] = jnp.zeros(w_rest.shape, BF16)
    rest_rows = (table_rows - mains) // 16 * 16
    r.table_rest[...] = jnp.zeros(r.table_rest.shape, BF16)
    load_rest = load(table.at[pl.ds(mains, rest_rows), :], r.table_rest.at[pl.ds(0, rest_rows), :])
    r.table_rest[pl.ds(rest_rows, table_rows - mains - rest_rows), :] = r.table_tail[...]

    stores = []

    def store(source, target):
        copy = pltpu.make_async_copy(source, target, r.store_sem.at[len(stores)])
        copy.start()
        stores.append(copy)

    swaps = []

    def swap(source, target, device):
        k = len(swaps)
        copy = pltpu.make_async_remote_copy(
            src_ref=source,
            dst_ref=target,
            send_sem=swap_send.at[k],
            recv_sem=swap_recv.at[k],
            device_id=device,
            device_id_type=MESH,
        )
        copy.start()
        swaps.append(copy)
        return copy

    lane = lax.broadcasted_iota(jnp.int32, (1, slots), 1)
    row_of = lax.broadcasted_iota(jnp.int32, (8, slots), 0)
    for u in range(utterances):
        target_row = targets[pl.ds(u, 1), :].astype(F32)
        glance_row = glance[pl.ds(u, 1), :].astype(F32)
        valid_row = (lane < token_lengths[u]).astype(F32)
        meta[0, :, pl.ds(u * slots, slots)] = jnp.where(
            row_of == 0, target_row, jnp.where(row_of == 1, valid_row, glance_row)
        )
    own_columns = to_columns(meta[0])
    own_target = own_columns[:, 0:1]
    own_valid = own_columns[:, 1:2]

    def rows(u):
        return pl.ds(u * slots, slots)

    edge = jnp.zeros((8, width), F32)
    for u in range(utterances):
        padded[u, pl.ds(0, 8), :] = edge
        padded[u, pl.ds(8 + slots, 8), :] = edge

    step_rows = 256
    row_chunks = frames // step_rows

    def key_of(u, h):
        return kv[pl.ds(u * frames, frames), pl.ds(h * HD, HD)]

    def value_of(u, h):
        return kv[pl.ds(u * frames, frames), pl.ds(half + h * HD, HD)]

    frame_lane = lax.broadcasted_iota(jnp.int32, (1, frames), 1)

    def look_up(first_row, count, allowed, source):
        ids = first_row + lax.broadcasted_iota(jnp.int32, (1, count), 1)
        local = jnp.where(allowed, own_target.astype(jnp.int32), -1)
        onehot = jnp.where(ids == local, 1.0, 0.0).astype(BF16)
        return dot_nn(onehot, source)

    def look_up_block(k):
        table_loads[k].wait()
        part = look_up(
            (core * per_core + k) * block, block, True, spare[pl.ds(k % 2 * block, block), :]
        )
        for u in range(utterances):
            piece = part[u * slots : (u + 1) * slots]
            taken_mine[u] = piece if k == 0 else taken_mine[u] + piece
        if k + 2 < per_core:
            table_loads.append(load_table(k + 2))

    def look_up_rest():
        load_rest.wait()
        part = look_up(mains, r.table_rest.shape[0], core == 0, r.table_rest[...])
        for u in range(utterances):
            taken_mine[u] = taken_mine[u] + part[u * slots : (u + 1) * slots]

    def local_targets(target_column):
        local = target_column.astype(jnp.int32) - core * vocab_here
        return jnp.where((local >= 0) & (local < vocab_here), local, -1)

    def vocab_stats(target, keep=False):
        tiles = main // 128
        step_tiles = 4

        ids = main + lax.broadcasted_iota(jnp.int32, (1, 128), 1)
        last = jnp.where(ids < vocab_here, dot_nt(top[0], w_rest[...]), NEG)
        logits[tiles] = last
        top_m, picked = last, jnp.where(ids == target, last, 0.0)
        for j in range(tiles // step_tiles):
            col = j * step_tiles * 128
            product = dot_nt(top[0], w_vocab[pl.ds(col, step_tiles * 128), :])
            for i in range(step_tiles):
                tile = product[:, i * 128 : (i + 1) * 128]
                ids = col + i * 128 + lax.broadcasted_iota(jnp.int32, (1, 128), 1)
                logits[j * step_tiles + i] = tile
                top_m = jnp.maximum(top_m, tile)
                picked = picked + jnp.where(ids == target, tile, 0.0)
        top_row = jnp.max(top_m, axis=1, keepdims=True)

        def add(j, total):
            for i in range(3):
                raised = jnp.exp(logits[3 * j + i] - top_row)
                if keep:
                    logits[3 * j + i] = raised
                total = total + raised
            return total

        total = lax.fori_loop(0, (tiles + 1) // 3, add, jnp.zeros((tokens, 128), F32))
        return (
            top_row,
            jnp.sum(total, axis=1, keepdims=True),
            jnp.sum(picked, axis=1, keepdims=True),
        )

    def join(mine, theirs):
        top_value = jnp.maximum(mine[0], theirs[0])
        total = mine[1] * jnp.exp(mine[0] - top_value) + theirs[1] * jnp.exp(theirs[0] - top_value)
        return top_value + jnp.log(total), mine[2] + theirs[2]

    def memory_block(u):
        at = rows(u)
        valid = own_valid[u * slots : (u + 1) * slots]
        hat, _ = normalise(stream_in[at, :])
        padded[u, pl.ds(8, slots), :] = (hat * gain_1 + bias_1) * valid
        for j in range(width // 128):
            cols = pl.ds(j * 128, 128)
            total = jnp.zeros((slots, 128), F32)
            for k in range(kernel_rows.shape[0]):
                shift = 8 + k - kernel_rows.shape[0] // 2
                total = total + kernel_rows[pl.ds(k, 1), cols] * padded[u, pl.ds(shift, slots), cols]
            stream_one[at, cols] = stream_in[at, cols] + total * valid
        low = stream_one[at, :].astype(BF16)
        one_low[at, :] = low
        queries[at, :] = dot_nn(low, w_query[...]).astype(BF16)

    def forward(second, beside_one=None, beside_two=None):
        copies = []
        for u in range(utterances):
            at = rows(u)
            if second:
                memory_block(u)
            frame_ok = frame_lane < memory_lengths[u]
            for h in range(heads):
                cols = pl.ds(h * HD, HD)
                scores = dot_nt(queries[at, cols], key_of(u, h)) * score_scale
                scores = jnp.where(frame_ok, scores, NEG)
                raised = jnp.exp(scores - jnp.max(scores, axis=-1, keepdims=True))
                prob = raised * (1.0 / jnp.sum(raised, axis=-1, keepdims=True))
                if second:
                    probs[u, h] = prob
                mixed[at, cols] = dot_nn(prob.astype(BF16), value_of(u, h)).astype(BF16)
            sent[u] = dot_nn(mixed[at, :], w_out[...])
            copies.append(swap(sent.at[u], arrived.at[u], sibling))
        if not second:
            beside_one()
            load_in.wait()
            load_back.wait()
        ff_copies = []
        for u in range(utterances):
            at = rows(u)
            copies[u].wait()
            two = stream_one[at, :] + (sent[u] + arrived[u])
            stream_two[at, :] = two
            hat, _ = normalise(two)
            low = (hat * gain_2 + bias_2).astype(BF16)
            norm_low[at, :] = low
            pre = dot_nn(low, w_in[...])
            phi = 0.5 * (1.0 + lax.erf(pre * math.sqrt(0.5)))
            hidden[at, :] = (pre * phi).astype(BF16)
            if second:
                gelu_slope[at, :] = phi + pre * (
                    jnp.exp(-0.5 * pre * pre) * (1.0 / math.sqrt(2.0 * math.pi))
                )
            sent[utterances + u] = dot_nn(hidden[at, :], w_back[...])
            ff_copies.append(swap(sent.at[utterances + u], arrived.at[utterances + u], sibling))
        if not second:
            beside_two()
        for u in range(utterances):
            at = rows(u)
            ff_copies[u].wait()
            three = stream_two[at, :] + (sent[utterances + u] + arrived[utterances + u])
            stream_three[u] = three
            top[0, at, :] = three.astype(BF16)

    stream_in[...] = acoustic[...].astype(F32)

    def beside_one():
        look_up_block(0)
        look_up_block(1)

    def beside_two():
        for k in range(2, per_core):
            look_up_block(k)
        look_up_rest()

    load_query.wait()
    for u in range(utterances):
        memory_block(u)
    load_memory.wait()
    for copy in load_kv:
        copy.wait()
    kv_rows = 512
    kv_chunks = frames // kv_rows

    def kv_step(i, carry):
        at = pl.ds(pl.multiple_of(i * kv_rows, kv_rows), kv_rows)
        group = jnp.zeros((1, width), jnp.int32) + rate_groups[i // kv_chunks]
        rate_row = jnp.where(group == 1, rate_table[pl.ds(1, 1), :], rate_table[pl.ds(0, 1), :])
        low = (mem_low[at, :].astype(F32) + rate_row).astype(BF16)
        mem_low[at, :] = low
        kv[at, :] = dot_nn(low, w_kv[...]).astype(BF16)
        return carry

    lax.fori_loop(0, utterances * kv_chunks, kv_step, 0)

    pl.semaphore_wait(barrier, n_dp)
    load_out.wait()
    forward(False, beside_one, beside_two)
    table_swap = swap(taken_mine, taken_theirs, sibling)
    load_vocab.wait()
    w_rest[pl.ds(0, vocab_here - main), :] = w_vocab[pl.ds(main, vocab_here - main), :]
    own_local = local_targets(own_target)
    mine = vocab_stats(own_local)
    stats[0] = side_by_side(mine)
    first_swap = swap(stats.at[0], stats_arrived.at[0], sibling)
    table_swap.wait()
    first_swap.wait()
    log_total, picked = join(mine, [stats_arrived[0, :, i : i + 1] for i in range(3)])
    first_loss = (log_total - picked) * own_valid
    blend = own_columns[:, 2:3] * own_valid / (1.0 + jnp.exp(math.log(V) - first_loss))
    for u in range(utterances):
        at = rows(u)
        wide_acoustic = acoustic[at, :].astype(F32)
        taken = taken_mine[u] + taken_theirs[u]
        stream_in[at, :] = wide_acoustic + blend[u * slots : (u + 1) * slots] * (taken - wide_acoustic)

    forward(True)
    token_swaps = [
        swap(stream_three.at[core], gathered.at[j - 1, 0], {"dp": mate[j]}) for j in (1, 2)
    ]
    mine = vocab_stats(own_local, keep=True)
    stats[1] = side_by_side(mine)
    stat_swap = swap(stats.at[1], stats_arrived.at[1], sibling)
    stat_swap.wait()
    log_column, picked = join(mine, [stats_arrived[1, :, i : i + 1] for i in range(3)])

    factor = jnp.exp(mine[0] - log_column) * own_valid
    valid_local = jnp.where(own_valid > 0.0, own_local, -1)

    def slope(j, carry):
        col = pl.multiple_of(j * 128, 128)
        ids = col + lax.broadcasted_iota(jnp.int32, (1, 128), 1)
        grad = logits[j] * factor - jnp.where(ids == valid_local, 1.0, 0.0)
        grad_logits[:, pl.ds(col, 128)] = grad.astype(BF16)
        return carry

    lax.fori_loop(0, main // 128 + 1, slope, 0, unroll=3)
    three_copies = []
    for u in range(utterances):
        sent[u] = dot_nn(grad_logits[rows(u), pl.ds(0, main)], w_vocab[pl.ds(0, main), :]) + dot_nn(
            grad_logits[rows(u), pl.ds(main, 128)], w_rest[...]
        )
        three_copies.append(swap(sent.at[u], arrived.at[u], sibling))
    for copy in token_swaps:
        copy.wait()
    part = slots // 2
    relays = [
        swap(gathered.at[0, 0, pl.ds(0, part)], gathered.at[2, 0, pl.ds(0, part)], {"dp": mate[2]}),
        swap(gathered.at[1, 0, pl.ds(part, part)], gathered.at[2, 0, pl.ds(part, part)], {"dp": mate[1]}),
    ]
    share_swaps = [swap(gathered.at[j, 0], gathered.at[j, 1], sibling) for j in range(2)]
    meta[0] = to_rows([own_target, own_valid, log_column, (log_column - picked) * own_valid])
    meta_swaps = [swap(meta.at[0], meta.at[j], {"dp": mate[j]}) for j in range(1, 4)]
    for u in range(utterances):
        r.loss_sum[pl.ds(u, 1), :] = meta[0, 3:4, u * slots : (u + 1) * slots]
    store(r.loss_sum, r.loss_out)

    plan = Planner()
    steps_all = len(bits)
    scatter_send, scatter_recv = r.scatter_send, r.scatter_recv

    vocab_parts = []

    def vocab_done():
        vocab_parts.append(1)
        if len(vocab_parts) == 1 + part_cols // 512:
            store(r.vocab_whole, r.vocab_out)

    def make_chunk(index):
        name, start, cols, order = chunk_list(part_cols, width, bits, low_bits, r)[index]
        source, landing = getattr(r, "src_" + name), r.landing[index]
        out_start = start
        if name == "kv":
            out, final = ((r.key_sum, r.key_out), (r.value_sum, r.value_out))[start // cols]
            out_start = 0
        else:
            out, final = getattr(r, name + "_sum"), getattr(r, name + "_out")
        rows_here = source.shape[-2]

        def pick(step, which):
            rest = sorted([b for b in bits if b not in order[:step]], reverse=True)
            where = tuple(which if b == order[step] else slice(None) for b in rest)
            if step == 0:
                return source, where + (slice(None), pl.ds(start, cols))
            return landing[step - 1], where + (slice(None), slice(None))

        def send(step):
            b = order[step]
            ref, where = pick(step, 1 - bit_of[b])
            copy = pltpu.make_async_remote_copy(
                src_ref=ref.at[where],
                dst_ref=landing[step],
                send_sem=scatter_send.at[index, step],
                recv_sem=scatter_recv.at[index, step],
                device_id=peer_of[b],
                device_id_type=MESH,
            )
            copy.start()
            return copy

        def take(step, copy):
            copy.wait_recv()
            ref, where = pick(step, bit_of[order[step]])
            got = landing[step]
            at = pl.ds(out_start, cols)
            if step < len(order) - 1:
                got[...] = got[...] + ref[where]
                return
            out[..., at] = got[...] + ref[where]
            if low_bits or name not in ("vocab", "rest"):
                store(out.at[..., at], final.at[..., at])
            elif name == "rest":
                rest = vocab_here - main
                r.vocab_whole[:, pl.ds(main, rest)] = out[...][:, :rest]
                vocab_done()

        steps = [
            (link_of(b, bits), rows_here * cols * 4 * 2 ** (steps_all - 1 - s))
            for s, b in enumerate(order)
        ]
        return Chunk(steps, send, take)

    def make_trade(start, cols):
        summed, traded = r.vocab_sum, r.vocab_traded
        at = pl.ds(start, cols)

        def send(step):
            copies = []
            for j in range(1, 4):
                to = lax.rem(mate[j], 4)
                copies.append(
                    pltpu.make_async_remote_copy(
                        src_ref=summed.at[to // 2, lax.rem(to, 2), :, at],
                        dst_ref=traded.at[j - 1, :, at],
                        send_sem=r.trade_send.at[start // 128, j - 1],
                        recv_sem=r.trade_recv.at[start // 128, j - 1],
                        device_id={"dp": mate[j]},
                        device_id_type=MESH,
                    )
                )
                copies[-1].start()
            return Several(copies)

        def take(step, copies):
            copies.wait_recv()
            for j in range(1, 4):
                there = pl.multiple_of(lax.rem(mate[j], 4) * part_cols + start, 128)
                r.vocab_whole[:, pl.ds(there, cols)] = traded[j - 1, :, at]
            here = pl.multiple_of(base + start, 128)
            r.vocab_whole[:, pl.ds(here, cols)] = summed[quarter // 2, lax.rem(quarter, 2), :, at]
            vocab_done()

        return Chunk([(0, 2 * r.src_vocab.shape[-2] * cols * 4)], send, take)

    chunks = {}
    for index, (name, start, cols, _) in enumerate(chunk_list(part_cols, width, bits, low_bits, r)):
        chunks[name, start] = make_chunk(index)
        if name == "vocab" and not low_bits:
            chunks[name, start].follow = make_trade(start, cols)

    def put(name, at, product):
        source = getattr(r, "src_" + name)
        source[..., at] = product.reshape(source.shape[:-1] + (product.shape[1],))

    copies = []
    for u in range(utterances):
        at = rows(u)
        three_copies[u].wait()
        three = sent[u] + arrived[u]
        grad_three[u] = three
        low = three.astype(BF16)
        branch_low[at, :] = low
        pre = (dot_nt(low, w_back[...]) * gelu_slope[at, :]).astype(BF16)
        grad_pre[at, :] = pre
        sent[utterances + u] = dot_nt(pre, w_in[...])
        copies.append(swap(sent.at[utterances + u], arrived.at[utterances + u], sibling))
    plan.run_until(plan.now + 8.0)
    for name, left, right in (("back", branch_low, hidden), ("in", norm_low, grad_pre)):
        left_turned = left[...].T
        for start in sorted(s for n, s in chunks if n == name):
            at = pl.ds(start, 512)
            put(name, at, dot_nn(left_turned, right[:, at]))
            plan.run_until(plan.now + 0.5)
            plan.post(chunks[name, start])

    at_core = pl.ds(pl.multiple_of(core * slots, slots), slots)
    at_other = pl.ds(pl.multiple_of((1 - core) * slots, slots), slots)
    base = pl.multiple_of(quarter * part_cols, part_cols)
    pieces = [(c, 256) for c in range(0, part_cols, 256)]
    for j in range(1, 4):
        if j == 2:
            for copy in relays:
                copy.wait()
            share_swaps.append(swap(gathered.at[2, 0], gathered.at[2, 1], sibling))
        meta_swaps[j - 1].wait()
        columns = to_columns(meta[j])
        valid = columns[:, 1:2] > 0.0
        target = jnp.where(valid, local_targets(columns[:, 0:1]), -1)
        log_total = jnp.where(valid, columns[:, 2:3], -NEG)
        top[j, at_core, :] = gathered[j - 1, 0].astype(BF16)
        share_swaps[j - 1].wait()
        top[j, at_other, :] = gathered[j - 1, 1].astype(BF16)
        for col, cols in pieces:
            ids = base + col + lax.broadcasted_iota(jnp.int32, (1, cols), 1)
            tile = dot_nt(top[j], w_vocab[pl.ds(base + col, cols), :])
            grad = jnp.exp(tile - log_total) - jnp.where(ids == target, 1.0, 0.0)
            grad_others[pl.ds((j - 1) * tokens, tokens), pl.ds(col, cols)] = grad.astype(BF16)
    top_turned = r.top_turned
    for j in range(4):
        top_turned[:, pl.ds(j * tokens, tokens)] = top[j].T
    plan.run_until(plan.now + 4.0)
    put("rest", slice(None), dot_nn(top_turned[:, pl.ds(0, tokens)], grad_logits[:, pl.ds(main, 128)]))
    starts = sorted(start for name, start in chunks if name == "vocab")
    for start, stop in zip(starts, starts[1:] + [part_cols]):
        for col in range(start, stop, 256):
            cols = min(256, stop - col)
            product = dot_nn(top_turned[:, pl.ds(0, tokens)], grad_logits[:, pl.ds(base + col, cols)])
            product = product + dot_nn(
                top_turned[:, pl.ds(tokens, 3 * tokens)], grad_others[:, pl.ds(col, cols)]
            )
            put("vocab", pl.ds(col, cols), product)
        plan.run_until(plan.now + 0.7)
        plan.post(chunks["vocab", start])
    plan.post(chunks["rest", 0])

    one_copies = []
    gain_2_total, bias_2_total = 0.0, 0.0
    for u in range(utterances):
        at = rows(u)
        copies[u].wait()
        grad_norm = sent[utterances + u] + arrived[utterances + u]
        hat, scale = normalise(stream_two[at, :])
        gain_2_total = gain_2_total + jnp.sum(grad_norm * hat, axis=0, keepdims=True)
        bias_2_total = bias_2_total + jnp.sum(grad_norm, axis=0, keepdims=True)
        two = grad_three[u] + normalise_back(grad_norm * gain_2, hat, scale)
        grad_two[at, :] = two
        low = two.astype(BF16)
        att_low[at, :] = low
        grad_mixed = dot_nt(low, w_out[...]).astype(BF16)
        for h in range(heads):
            cols = pl.ds(h * HD, HD)
            grad_head = grad_mixed[:, h * HD : (h + 1) * HD]
            prob = probs[u, h]
            grad_prob = dot_nt(grad_head, value_of(u, h))
            spare[pl.ds(u * frames, frames), pl.ds(half + h * HD, HD)] = dot_tn(
                prob.astype(BF16), grad_head
            ).astype(BF16)
            inner = jnp.sum(prob * grad_prob, axis=-1, keepdims=True)
            grad_score = (prob * (grad_prob - inner)).astype(BF16)
            grad_queries[at, cols] = (dot_nn(grad_score, key_of(u, h)) * score_scale).astype(BF16)
            spare[pl.ds(u * frames, frames), cols] = (
                dot_tn(grad_score, queries[at, cols]) * score_scale
            ).astype(BF16)
            plan.run_until(plan.now + 1.5)
        sent[u] = dot_nt(grad_queries[at, :], w_query[...])
        one_copies.append(swap(sent.at[u], arrived.at[u], sibling))
    every = slice(None)
    put("out", every, dot_tn(att_low[...], mixed[...]))
    plan.post(chunks["out", 0])
    put("query", every, dot_tn(one_low[...], grad_queries[...]))
    plan.post(chunks["query", 0])
    plan.run_until(plan.now + 1.0)

    mem_copies = []
    rate_sums = [0.0, 0.0]
    for u in range(utterances):
        total = jnp.zeros((1, width), F32)
        for i in range(row_chunks):
            at = pl.ds(u * frames + i * step_rows, step_rows)
            part = dot_nt(spare[at, :], w_kv[...])
            for j in range(width // 128):
                side_of, tile = j // (width // 256), j % (width // 256)
                index = ((side_of * utterances + u) * row_chunks + i) * (width // 256) + tile
                logits[index] = part[:, j * 128 : (j + 1) * 128]
            total = total + jnp.sum(part, axis=0, keepdims=True)
        tiles = row_chunks * (width // 256)
        mem_copies.append(
            swap(
                logits.at[pl.ds(((1 - core) * utterances + u) * tiles, tiles)],
                mem_arrived.at[pl.ds(u * tiles, tiles)],
                sibling,
            )
        )
        group = jnp.zeros((1, width), jnp.int32) + rate_groups[u]
        for k in range(2):
            rate_sums[k] = rate_sums[k] + jnp.where((group == 1) == (k == 1), total, 0.0)
        plan.run_until(plan.now + 1.2)
    span = frames // 2
    for k in range(2 * utterances):
        at = pl.ds(k * span, span)
        product = dot_tn(mem_low[at, :], spare[at, :])
        product = product.reshape(r.src_kv.shape)
        r.src_kv[...] = product if k == 0 else r.src_kv[...] + product
    plan.run_until(plan.now + 2.0)
    plan.post(*[chunks["kv", start] for start in sorted(s for n, s in chunks if n == "kv")])

    gain_1_total, bias_1_total = 0.0, 0.0
    for u in range(utterances):
        at = rows(u)
        valid = own_valid[u * slots : (u + 1) * slots]
        one_copies[u].wait()
        one = grad_two[at, :] + (sent[u] + arrived[u])
        grad_two[at, :] = one
        masked = one * valid
        for k in range(kernel_rows.shape[0]):
            shift = 8 + k - kernel_rows.shape[0] // 2
            row = jnp.sum(masked * padded[u, pl.ds(shift, slots), :], axis=0, keepdims=True)
            if u == 0:
                small_sent[0, pl.ds(k, 1), :] = row
            else:
                small_sent[0, pl.ds(k, 1), :] = small_sent[0, pl.ds(k, 1), :] + row
        padded[u, pl.ds(8, slots), :] = masked
        for j in range(width // 128):
            cols = pl.ds(j * 128, 128)
            total = jnp.zeros((slots, 128), F32)
            for k in range(kernel_rows.shape[0]):
                shift = 8 - k + kernel_rows.shape[0] // 2
                total = total + kernel_rows[pl.ds(k, 1), cols] * padded[u, pl.ds(shift, slots), cols]
            stream_one[at, cols] = total * valid
        grad_norm = stream_one[at, :]
        hat, scale = normalise(stream_in[at, :])
        gain_1_total = gain_1_total + jnp.sum(grad_norm * hat, axis=0, keepdims=True)
        bias_1_total = bias_1_total + jnp.sum(grad_norm, axis=0, keepdims=True)
        zero = grad_two[at, :] + normalise_back(grad_norm * gain_1, hat, scale)
        terms[u] = blend[u * slots : (u + 1) * slots] * zero
        stream_one[at, :] = zero - terms[u]
        plan.run_until(plan.now + 1.5)

    last_taps = kernel_rows.shape[0]
    small_sent[0, pl.ds(last_taps, 12 - last_taps), :] = jnp.zeros((12 - last_taps, width), F32)
    for i, row in enumerate((gain_1_total, bias_1_total, gain_2_total, bias_2_total)):
        small_sent[0, pl.ds(12 + i, 1), :] = row
    for k in range(2):
        small_sent[0, pl.ds(16 + k, 1), :] = rate_sums[k]
    small_sent[0, pl.ds(18, 6), :] = jnp.zeros((6, width), F32)
    small_peers = [peer_of[b] for b in low_bits + bits] + [sibling]

    def small_send(step):
        copy = pltpu.make_async_remote_copy(
            src_ref=small_sent.at[step],
            dst_ref=small_arrived.at[step],
            send_sem=r.small_send.at[step],
            recv_sem=r.small_recv.at[step],
            device_id=small_peers[step],
            device_id_type=MESH,
        )
        copy.start()
        return copy

    def small_take(step, copy):
        copy.wait_recv()
        if step + 1 == len(small_peers):
            copy.wait_send()
            plan.started = [c for c in plan.started if c is not copy]
        if step + 1 < len(small_peers):
            small_sent[step + 1] = small_sent[step] + small_arrived[step]
        else:
            small_sent[step, pl.ds(16, 8), :] = (
                small_sent[step, pl.ds(16, 8), :] + small_arrived[step, pl.ds(16, 8), :]
            )
            store(small_sent.at[step], r.small_out)

    small_links = [link_of(b, bits) for b in low_bits + bits] + ["core"]
    plan.post(Chunk([(l, 24 * width * 4) for l in small_links], small_send, small_take))

    features = width // n_dp
    feature_rows = max(features, 8)
    block_rows = term_blocks.shape[1]
    turned = terms[core].T
    id_row = targets[pl.ds(core, 1), :].astype(F32)
    rest = block_rows - features - 1
    for p in range(n_dp):
        term_blocks[p, pl.ds(0, features), :] = turned[p * features : (p + 1) * features]
        term_blocks[p, pl.ds(features, 1), :] = id_row
        term_blocks[p, pl.ds(features + 1, rest), :] = jnp.zeros((rest, slots), F32)

    def term_copy(k):
        there = lax.rem(me + k, n_dp)
        return pltpu.make_async_remote_copy(
            src_ref=term_blocks.at[there],
            dst_ref=term_arrived.at[me],
            send_sem=r.term_send.at[k],
            recv_sem=r.term_recv.at[k],
            device_id={"dp": there},
            device_id_type=MESH,
        )

    def term_start(k, carry):
        term_copy(k).start()
        return carry

    def term_wait(k, carry):
        term_copy(k).wait()
        return carry

    term_arrived[me] = term_blocks[me]
    lax.fori_loop(1, n_dp, term_start, 0)
    store(stream_one, r.acoustic_out)
    for u in range(utterances):
        mem_copies[u].wait()
        for i in range(row_chunks):
            for j in range(width // 256):
                index = (u * row_chunks + i) * (width // 256) + j
                first_tile = (core * utterances) * row_chunks * (width // 256)
                mem_arrived[index] = logits[first_tile + index] + mem_arrived[index]
                at = pl.ds(u * frames + i * step_rows, step_rows)
                store(mem_arrived.at[index], r.memory_out.at[at, pl.ds(j * 128, 128)])
    plan.run_until(plan.now + 8.0)
    lax.fori_loop(1, n_dp, term_wait, 0)
    per_piece = 512 // slots
    blocks_hi = (table_rows + 255) // 256
    batch = 4

    def table_piece(p, fresh):
        found = [term_arrived[p * per_piece + i] for i in range(per_piece)]
        values = jnp.concatenate([f[:feature_rows] for f in found], axis=1)
        ids = jnp.concatenate([f[features : features + 1] for f in found], axis=1).astype(jnp.int32)
        low_ids, high_ids = ids & 255, ids >> 8
        onehot_lo[...] = jnp.where(
            lax.broadcasted_iota(jnp.int32, (256, 512), 0) == low_ids, 1.0, 0.0
        ).astype(BF16)
        coarse = values.astype(BF16).astype(F32)
        both = jnp.concatenate([coarse, values - coarse], axis=0)
        for first_hi in range(0, blocks_hi, batch):
            here = range(first_hi, min(first_hi + batch, blocks_hi))
            masked = jnp.concatenate([jnp.where(high_ids == hi, both, 0.0) for hi in here], axis=0)
            product = dot_nt(masked.astype(BF16), onehot_lo[...])
            for i, hi in enumerate(here):
                top_part = product[2 * i * feature_rows : (2 * i + 1) * feature_rows]
                low_part = product[(2 * i + 1) * feature_rows : (2 * i + 2) * feature_rows]
                cols = min(256, table_rows - hi * 256)
                at = pl.ds(hi * 256, cols)
                found = (top_part + low_part)[:features, :cols]
                whole_table[:, at] = found if fresh else whole_table[:, at] + found

    pieces = n_dp // per_piece
    table_piece(0, True)
    if pieces <= 4:
        for p in range(1, pieces):
            plan.run_until(plan.now + 1.5)
            table_piece(p, False)
    else:
        lax.fori_loop(1, pieces, lambda p, c: (table_piece(p, False), c)[1], 0)
    table_swap = swap(whole_table, table_theirs, sibling)
    plan.run_until(plan.now + 8.0)
    table_swap.wait()
    whole_table[...] = whole_table[...] + table_theirs[...]
    store(whole_table, r.table_out)
    plan.finish()
    for copy in stores:
        copy.wait()


def link_of(bit, bits):
    if bit == bits[-1]:
        return bits[-2]
    return bit


def chunk_list(part_cols, width, bits, low_bits, sizes):
    turned = [bits[1], bits[0]] + bits[2:]
    listing = []
    for start in range(0, part_cols, 512):
        listing.append(("vocab", start, 512, [b for b in bits if b > 1]))
    listing.append(("rest", 0, 128, bits))
    for name, order in (("back", turned), ("in", bits)):
        for start in range(0, sizes.units, 512):
            if name == "in" and start:
                order = [bits[2], bits[0], bits[1]] + bits[3:]
            listing.append((name, start, 512, order))
    listing.append(("out", 0, sizes.half, turned))
    listing.append(("query", 0, sizes.half, bits))
    for k, start in enumerate(range(0, 2 * sizes.half, 256)):
        listing.append(("kv", start, 256, [bits, turned][k % 2]))
    return listing


def decoder_call(
    acoustic, memory, embedding, w_query, w_key, w_value, w_out, w_in, w_back, w_vocab, norms,
    fsmn_kernel, rate_table, token_lengths, memory_lengths, rate_groups, glance, targets, n_dp,
):
    utterances = token_lengths.shape[0]
    tokens, width = acoustic.shape
    slots = tokens // utterances
    mem_rows = memory.shape[0]
    half = w_query.shape[1]
    heads = half // HD
    frames = mem_rows // utterances
    units = w_in.shape[1]
    vocab_here = w_vocab.shape[1]
    table_rows = embedding.shape[0]
    part_cols = vocab_here // 512 * 128
    all_cols = 4 * part_cols + 128
    w_turned = w_vocab.T
    mains = table_rows // 2048 * 2048
    nbits = n_dp.bit_length() - 1
    steps = nbits
    while width >> steps < 8:
        steps -= 1
    low_bits, bits = list(range(nbits - steps)), list(range(nbits - steps, nbits))
    rows = width >> steps
    features = width // n_dp
    feature_rows = max(features, 8)
    block_rows = feature_rows + 8 if features >= 8 else 8
    blocks_hi = (table_rows + 255) // 256
    sizes = SimpleNamespace(units=units, half=half)
    plane = [b for b in bits if b < 2]
    listing = chunk_list(part_cols, width, bits, low_bits, sizes)
    most = max(len(c[3]) for c in listing)

    f32 = lambda *shape: jax.ShapeDtypeStruct(shape, F32)
    v32 = lambda *shape: pltpu.VMEM(shape, F32)
    v16 = lambda *shape: pltpu.VMEM(shape, BF16)
    dma = lambda *shape: pltpu.SemaphoreType.DMA(shape)
    inputs = dict(
        acoustic=(VMEM, acoustic),
        table_tail=(VMEM, embedding[mains + (table_rows - mains) // 16 * 16 :]),
        memory=(ANY, memory),
        table=(ANY, embedding),
        w_query_hbm=(ANY, w_query),
        w_key_hbm=(ANY, w_key),
        w_value_hbm=(ANY, w_value),
        w_out_hbm=(ANY, w_out),
        w_in_hbm=(ANY, w_in),
        w_back_hbm=(ANY, w_back),
        w_vocab_hbm=(ANY, w_turned),
        gain_one=(VMEM, norms[0][None]),
        bias_one=(VMEM, norms[1][None]),
        gain_two=(VMEM, norms[2][None]),
        bias_two=(VMEM, norms[3][None]),
        kernel_rows=(VMEM, fsmn_kernel),
        rate_table=(VMEM, rate_table),
        token_lengths=(SMEM, token_lengths),
        memory_lengths=(SMEM, memory_lengths),
        rate_groups=(SMEM, rate_groups),
        glance=(VMEM, glance.reshape(utterances, slots)),
        targets=(VMEM, targets.reshape(utterances, slots)),
    )
    outputs = dict(
        loss_out=f32(utterances, slots),
        small_out=f32(24, width),
        vocab_out=f32(2, rows, part_cols) if low_bits else f32(rows, vocab_here),
        rest_out=f32(rows, 128),
        in_out=f32(rows, units),
        back_out=f32(rows, units),
        query_out=f32(rows, half),
        out_out=f32(rows, half),
        key_out=f32(rows, half),
        value_out=f32(rows, half),
        acoustic_out=f32(tokens, width),
        memory_out=f32(mem_rows, width // 2),
        table_out=f32(features, table_rows),
    )
    shape = (2,) * steps + (rows,)
    scratch = dict(
        w_query=v16(width, half),
        w_kv=v16(width, 2 * half),
        w_out=v16(half, width),
        w_in=v16(width, units),
        w_back=v16(units, width),
        w_vocab=v16(vocab_here, width),
        w_rest=v16(128, width),
        mem_low=v16(mem_rows, width),
        kv=v16(mem_rows, 2 * half),
        spare=v16(mem_rows, 2 * half),
        padded=v32(utterances, slots + 16, width),
        stream_in=v32(tokens, width),
        stream_one=v32(tokens, width),
        stream_two=v32(tokens, width),
        stream_three=v32(utterances, slots, width),
        one_low=v16(tokens, width),
        queries=v16(tokens, half),
        probs=v32(utterances, heads, slots, frames),
        mixed=v16(tokens, half),
        norm_low=v16(tokens, width),
        hidden=v16(tokens, units),
        gelu_slope=v32(tokens, units),
        top=v16(4, tokens, width),
        logits=v32(all_cols // 128, tokens, 128),
        grad_logits=v16(tokens, all_cols),
        grad_others=v16(3 * tokens, part_cols),
        top_turned=v16(width, 4 * tokens),
        taken_theirs=v32(utterances, slots, width),
        grad_three=v32(utterances, slots, width),
        grad_two=v32(tokens, width),
        branch_low=v16(tokens, width),
        grad_pre=v16(tokens, units),
        att_low=v16(tokens, width),
        grad_queries=v16(tokens, half),
        mem_arrived=v32(mem_rows // 256 * (width // 256), 256, 128),
        meta=v32(4, 8, tokens),
        stats=v32(2, tokens, 128),
        stats_arrived=v32(2, tokens, 128),
        sent=v32(2 * utterances, slots, width),
        arrived=v32(2 * utterances, slots, width),
        gathered=v32(3, 2, slots, width),
        small_sent=v32(nbits + 1, 24, width),
        small_arrived=v32(nbits + 1, 24, width),
        term_blocks=v32(n_dp, block_rows, slots),
        term_arrived=v32(n_dp, block_rows, slots),
        onehot_lo=v16(256, 512),
        table_rest=v16((table_rows - mains + 127) // 128 * 128, width),
        table_theirs=v32(features, table_rows),
        src_vocab=v32(*shape, part_cols),
        src_rest=v32(*shape, 128),
        whole_table=v32(features, table_rows),
        src_back=v32(*shape, units),
        vocab_sum=v32(*(2,) * len(plane), rows, part_cols),
        rest_sum=v32(rows, 128),
        vocab_whole=v32(rows, vocab_here),
        in_sum=v32(rows, units),
        back_sum=v32(rows, units),
        query_sum=v32(rows, half),
        out_sum=v32(rows, half),
        key_sum=v32(rows, half),
        value_sum=v32(rows, half),
        loss_sum=v32(utterances, slots),
        vocab_traded=v32(3, rows, part_cols),
        src_in=v32(*shape, units),
        src_out=v32(*shape, half),
        src_query=v32(*shape, half),
        src_kv=v32(*shape, 2 * half),
        load_sem=dma(24),
        store_sem=dma(48),
        trade_send=dma(part_cols // 128, 3),
        trade_recv=dma(part_cols // 128, 3),
        swap_send=dma(40),
        swap_recv=dma(40),
        scatter_send=dma(len(listing), most),
        scatter_recv=dma(len(listing), most),
        small_send=dma(nbits + 1),
        small_recv=dma(nbits + 1),
        term_send=dma(n_dp),
        term_recv=dma(n_dp),
    )
    landing = [
        [v32(*(2,) * (steps - 1 - s), rows, cols) for s in range(len(order))]
        for _, _, cols, order in listing
    ]
    names = list(inputs) + list(outputs) + list(scratch)
    flat = [ref for chunk in landing for ref in chunk]

    def kernel(*refs):
        named, rest = refs[: len(names)], list(refs[len(names) :])
        lands = [[rest.pop(0) for _ in chunk] for chunk in landing]
        decoder_kernel(
            names + ["landing", "units", "half"], vocab_here, part_cols, table_rows, n_dp, bits,
            low_bits, *named, lands, units, half,
        )

    out = pl.pallas_call(
        kernel,
        out_shape=list(outputs.values()),
        in_specs=[spec for spec, _ in inputs.values()],
        out_specs=[ANY] * len(outputs),
        scratch_shapes=list(scratch.values()) + flat,
        compiler_params=pltpu.CompilerParams(
            collective_id=1, has_side_effects=True, vmem_limit_bytes=64 << 20
        ),
    )(*[value for _, value in inputs.values()])
    return SimpleNamespace(**dict(zip(outputs, out))), low_bits


def deliver_kernel(n_dp, n_passed, *refs):
    n = n_passed + 2
    sources, targets, held = refs[:n], refs[n : 2 * n + 5], refs[2 * n + 5 : 3 * n + 5]
    shaped, (sem_in, sem_out) = refs[3 * n + 5 : 3 * n + 12], refs[3 * n + 12 :]
    reads, writes = [], []
    for i, (source, buffer) in enumerate(zip(sources, held)):
        reads.append(pltpu.make_async_copy(source, buffer, sem_in.at[i]))
        reads[-1].start()
    for i in range(n_passed):
        reads[i].wait()
        writes.append(pltpu.make_async_copy(held[i], targets[i], sem_out.at[i]))
        writes[-1].start()
    reads[n_passed].wait()
    reads[n_passed + 1].wait()
    loss, small = held[n_passed:]
    loss_at, gain_one_at, bias_one_at, gain_two_at, bias_two_at, taps_at, rate_at = shaped
    slots = loss.shape[1]
    for u in range(loss.shape[0]):
        loss_at[:, pl.ds(u * slots, slots)] = loss[pl.ds(u, 1), :]
    me = lax.axis_index("dp")
    own = small.shape[1] // n_dp
    mine = jnp.zeros((16, own), F32)
    for p in range(n_dp):
        mine = jnp.where(me == p, small[pl.ds(0, 16), p * own : (p + 1) * own], mine)
    taps_at[...] = mine[: taps_at.shape[0]]
    for i, target in enumerate((gain_one_at, bias_one_at, gain_two_at, bias_two_at)):
        target[...] = mine[12 + i : 13 + i]
    rate_at[...] = small[pl.ds(16, 2), :]
    for i, source in enumerate(shaped):
        writes.append(pltpu.make_async_copy(source, targets[n_passed + i], sem_out.at[n_passed + i]))
        writes[-1].start()
    for copy in writes:
        copy.wait()


def per_device(
    acoustic,
    memory,
    embedding,
    w_query,
    w_key,
    w_value,
    w_out,
    w_in,
    w_back,
    w_vocab,
    gain_one,
    bias_one,
    gain_two,
    bias_two,
    fsmn_kernel,
    rate_table,
    token_lengths,
    memory_lengths,
    rate_groups,
    glance_mask,
    targets,
):
    tok_rows, model_width = acoustic.shape
    half = w_query.shape[1]
    n_dp = lax.axis_size("dp")
    result, low_bits = decoder_call(
        acoustic, memory, embedding, w_query, w_key, w_value, w_out, w_in, w_back, w_vocab,
        (gain_one, bias_one, gain_two, bias_two), fsmn_kernel, rate_table,
        token_lengths, memory_lengths, rate_groups, glance_mask, targets, n_dp,
    )
    vocab = result.vocab_out
    summed = [
        result.query_out, result.key_out, result.value_out, result.out_out, result.in_out,
        result.back_out,
    ]
    if low_bits:
        size = 1 << len(low_bits)
        groups = [list(range(g * size, (g + 1) * size)) for g in range(n_dp // size)]
        planes = [list(range(4 * g, 4 * g + 4)) for g in range(n_dp // 4)]
        vocab = lax.all_to_all(
            vocab.reshape(4, model_width // n_dp, -1), "dp", 0, 0, axis_index_groups=planes, tiled=True
        )
        *summed, rest = [
            lax.psum_scatter(s, "dp", scatter_dimension=0, axis_index_groups=groups, tiled=True)
            for s in (*summed, result.rest_out)
        ]
        vocab = jnp.concatenate([*vocab, rest], axis=1)[:, : w_vocab.shape[1]]
    own = model_width // n_dp
    f32 = lambda *shape: jax.ShapeDtypeStruct(shape, F32)
    like = lambda x: jax.ShapeDtypeStruct(x.shape, F32)
    passed = (result.memory_out, result.table_out, result.acoustic_out, vocab, *summed)
    handed = (*passed, result.loss_out, result.small_out)
    small_shapes = [
        f32(1, tok_rows), *[f32(1, own)] * 4, f32(fsmn_kernel.shape[0], own), f32(2, model_width)
    ]
    (
        grad_memory, grad_table, grad_acoustic, grad_vocab, grad_query, grad_key, grad_value,
        grad_out, grad_in, grad_back, token_loss, gain_1, bias_1, gain_2, bias_2, grad_taps, grad_rate,
    ) = pl.pallas_call(
        partial(deliver_kernel, n_dp, len(passed)),
        out_shape=[*[like(x) for x in passed], *small_shapes],
        in_specs=[ANY] * len(handed),
        out_specs=[ANY] * (len(passed) + 7),
        scratch_shapes=[pltpu.VMEM(x.shape, F32) for x in (*handed, *small_shapes)]
        + [pltpu.SemaphoreType.DMA((len(handed),)), pltpu.SemaphoreType.DMA((len(passed) + 7,))],
        compiler_params=pltpu.CompilerParams(vmem_limit_bytes=60 << 20),
    )(*handed)
    return (
        token_loss.reshape(tok_rows),
        grad_acoustic,
        grad_memory,
        grad_table.T,
        grad_query,
        grad_key,
        grad_value,
        grad_out.T,
        grad_in,
        grad_back.T,
        grad_vocab,
        gain_1.reshape(own),
        bias_1.reshape(own),
        gain_2.reshape(own),
        bias_2.reshape(own),
        grad_taps,
        grad_rate,
    )


def solution(mesh):
    return jax.shard_map(
        per_device,
        mesh=mesh,
        in_specs=(
            P("dp", None),
            P("dp", None),
            P(),
            P(None, "mp"),
            P(None, "mp"),
            P(None, "mp"),
            P("mp", None),
            P(None, "mp"),
            P("mp", None),
            P(None, "mp"),
            P(),
            P(),
            P(),
            P(),
            P(),
            P(),
            P("dp"),
            P("dp"),
            P("dp"),
            P("dp"),
            P("dp"),
        ),
        out_specs=(
            P("dp"),
            P("dp", None),
            P("dp", "mp"),
            P(None, "dp"),
            P("dp", "mp"),
            P("dp", "mp"),
            P("dp", "mp"),
            P("mp", "dp"),
            P("dp", "mp"),
            P("mp", "dp"),
            P("dp", "mp"),
            P("dp"),
            P("dp"),
            P("dp"),
            P("dp"),
            P(None, "dp"),
            P(),
        ),
        check_vma=False,
    )
```

```python
from functools import partial
import math
from types import SimpleNamespace

import jax
import jax.numpy as jnp
from jax import lax
from jax.experimental import pallas as pl
from jax.experimental.pallas import tpu as pltpu
from jax.sharding import PartitionSpec as P

HD = 128
V = 8404
EPSILON = 1e-05
MESH = pl.DeviceIdType.MESH
VMEM = pl.BlockSpec(memory_space=pltpu.VMEM)
SMEM = pl.BlockSpec(memory_space=pltpu.SMEM)
ANY = pl.BlockSpec(memory_space=pl.ANY)
F32, BF16 = jnp.float32, jnp.bfloat16
NEG = -1e30


def other_core():
    return {"mp": 1 - lax.axis_index("mp")}


def dot_nn(a, b):
    return lax.dot_general(a, b, (((1,), (0,)), ((), ())), preferred_element_type=F32)


def dot_nt(a, b):
    return lax.dot_general(a, b, (((1,), (1,)), ((), ())), preferred_element_type=F32)


def dot_tn(a, b):
    return lax.dot_general(a, b, (((0,), (0,)), ((), ())), preferred_element_type=F32)


def normalise(rows):
    average = jnp.mean(rows, axis=-1, keepdims=True)
    centred = rows - average
    variance = jnp.mean(centred * centred, axis=-1, keepdims=True)
    scale = lax.rsqrt(variance + EPSILON)
    return centred * scale, scale


def normalise_back(grad_hat, hat, scale):
    first = jnp.mean(grad_hat, axis=-1, keepdims=True)
    second = jnp.mean(grad_hat * hat, axis=-1, keepdims=True)
    return scale * (grad_hat - first - hat * second)


def side_by_side(columns):
    lane = lax.broadcasted_iota(jnp.int32, (columns[0].shape[0], 128), 1)
    tile = jnp.zeros(lane.shape, F32)
    for i, column in enumerate(columns):
        tile = jnp.where(lane == i, column, tile)
    return tile


def to_rows(columns):
    return side_by_side(columns).T[:8]


def to_columns(rows):
    return jnp.concatenate([rows] * 16, axis=0).T


class Planner:
    RATE = 0.045e6
    HOP = 1.5
    BACKLOG = 1.0

    def __init__(self):
        self.now = 0.0
        self.free = {}
        self.flying = []
        self.waiting = []
        self.started = []
        self.count = 0

    def launch(self, item, step):
        link, size = item.steps[step]
        begin = max(self.now, self.free.get(link, 0.0))
        self.free[link] = begin + size / self.RATE
        copy = item.send(step)
        self.started.append(copy)
        self.count += 1
        self.flying.append((self.free[link] + self.HOP, self.count, item, step, copy))

    def release(self):
        kept = []
        for item in self.waiting:
            link = item.steps[0][0]
            if self.free.get(link, 0.0) - self.now < self.BACKLOG:
                self.launch(item, 0)
            else:
                kept.append(item)
        self.waiting = kept

    def post(self, *items):
        self.waiting += items
        self.release()

    def run_until(self, time):
        while self.flying or self.waiting:
            if not self.flying:
                self.now = max(self.now, min(self.free[i.steps[0][0]] for i in self.waiting))
                self.release()
                continue
            first = min(self.flying, key=lambda f: f[:2])
            if first[0] > time:
                break
            self.flying.remove(first)
            self.now = max(self.now, first[0])
            _, _, item, step, copy = first
            item.take(step, copy)
            if step + 1 < len(item.steps):
                self.launch(item, step + 1)
            elif item.follow is not None:
                self.launch(item.follow, 0)
            self.release()
        if time != math.inf:
            self.now = max(self.now, time)
        self.release()

    def finish(self):
        self.run_until(math.inf)
        for copy in self.started:
            copy.wait_send()


class Chunk:
    def __init__(self, steps, send, take):
        self.steps, self.send, self.take, self.follow = steps, send, take, None


class Several:
    def __init__(self, copies):
        self.copies = copies

    def wait_recv(self):
        for copy in self.copies:
            copy.wait_recv()

    def wait_send(self):
        for copy in self.copies:
            copy.wait_send()


def decoder_kernel(
    names,
    vocab_here,
    part_cols,
    table_rows,
    n_dp,
    bits,
    low_bits,
    *refs,
):
    r = SimpleNamespace(**dict(zip(names, refs)))
    acoustic, memory, table = r.acoustic, r.memory, r.table
    targets, glance = r.targets, r.glance
    gain_1, bias_1 = r.gain_one[...], r.bias_one[...]
    gain_2, bias_2 = r.gain_two[...], r.bias_two[...]
    kernel_rows, rate_table = r.kernel_rows, r.rate_table
    token_lengths, memory_lengths, rate_groups = r.token_lengths, r.memory_lengths, r.rate_groups
    w_query, w_kv, w_out, w_in, w_back, w_vocab = r.w_query, r.w_kv, r.w_out, r.w_in, r.w_back, r.w_vocab
    mem_low, kv, padded, spare = r.mem_low, r.kv, r.padded, r.spare
    stream_in, stream_one, stream_two, stream_three = r.stream_in, r.stream_one, r.stream_two, r.stream_three
    one_low, queries, probs, mixed = r.one_low, r.queries, r.probs, r.mixed
    norm_low, hidden, gelu_slope, top = r.norm_low, r.hidden, r.gelu_slope, r.top
    logits, grad_logits, grad_others = r.logits, r.grad_logits, r.grad_others
    taken_mine, taken_theirs = r.grad_three, r.taken_theirs
    grad_three, grad_two, branch_low = r.grad_three, r.grad_two, r.branch_low
    grad_pre, att_low, grad_queries = r.grad_pre, r.att_low, r.grad_queries
    mem_arrived, meta, stats, stats_arrived = r.mem_arrived, r.meta, r.stats, r.stats_arrived
    sent, arrived, gathered = r.sent, r.arrived, r.gathered
    small_sent, small_arrived = r.small_sent, r.small_arrived
    terms, term_blocks, term_arrived = grad_three, r.term_blocks, r.term_arrived
    onehot_lo, table_theirs, whole_table = r.onehot_lo, r.table_theirs, r.whole_table
    swap_send, swap_recv, load_sem = r.swap_send, r.swap_recv, r.load_sem

    utterances, slots = targets.shape
    width = acoustic.shape[1]
    frames = memory.shape[0] // utterances
    half = w_query.shape[1]
    heads = half // HD
    tokens = utterances * slots
    me, core = lax.axis_index("dp"), lax.axis_index("mp")
    sibling = {"mp": 1 - core}
    quarter = lax.rem(me, 4)
    flips = [1 - 2 * lax.rem(me, 2), 2 - 4 * lax.rem(me // 2, 2)]
    mate = [me + flips[0] * (j % 2) + flips[1] * (j // 2) for j in range(4)]
    bit_of = {b: lax.rem(me // (1 << b), 2) for b in low_bits + bits}
    peer_of = {b: {"dp": me + (1 - 2 * bit_of[b]) * (1 << b)} for b in low_bits + bits}
    score_scale = 1.0 / math.sqrt(HD)

    loads = []

    def load(source, target):
        copy = pltpu.make_async_copy(source, target, load_sem.at[len(loads)])
        copy.start()
        loads.append(copy)
        return copy

    load_memory = load(memory, mem_low)
    load_kv = [
        load(r.w_key_hbm, w_kv.at[:, pl.ds(0, half)]),
        load(r.w_value_hbm, w_kv.at[:, pl.ds(half, half)]),
    ]
    load_query = load(r.w_query_hbm, w_query)
    load_out = load(r.w_out_hbm, w_out)

    barrier = pltpu.get_barrier_semaphore()

    def greet(k, carry):
        pl.semaphore_signal(
            barrier, inc=1, device_id={"dp": lax.rem(me + k, n_dp)}, device_id_type=MESH
        )
        return carry

    lax.fori_loop(1, n_dp, greet, 0)
    pl.semaphore_signal(barrier, inc=1, device_id=sibling, device_id_type=MESH)

    load_in = load(r.w_in_hbm, w_in)
    load_back = load(r.w_back_hbm, w_back)
    block = 1024
    per_core = table_rows // (2 * block)
    mains = 2 * per_core * block

    def load_table(k):
        at = pl.ds(pl.multiple_of((core * per_core + k) * block, block), block)
        return load(table.at[at, :], spare.at[pl.ds(k % 2 * block, block), :])

    table_loads = [load_table(0), load_table(1)]
    main = 4 * part_cols
    load_vocab = load(r.w_vocab_hbm, w_vocab)
    w_rest = r.w_rest
    w_rest[...] = jnp.zeros(w_rest.shape, BF16)
    rest_rows = (table_rows - mains) // 16 * 16
    r.table_rest[...] = jnp.zeros(r.table_rest.shape, BF16)
    load_rest = load(table.at[pl.ds(mains, rest_rows), :], r.table_rest.at[pl.ds(0, rest_rows), :])
    r.table_rest[pl.ds(rest_rows, table_rows - mains - rest_rows), :] = r.table_tail[...]

    stores = []

    def store(source, target):
        copy = pltpu.make_async_copy(source, target, r.store_sem.at[len(stores)])
        copy.start()
        stores.append(copy)

    swaps = []

    def swap(source, target, device):
        k = len(swaps)
        copy = pltpu.make_async_remote_copy(
            src_ref=source,
            dst_ref=target,
            send_sem=swap_send.at[k],
            recv_sem=swap_recv.at[k],
            device_id=device,
            device_id_type=MESH,
        )
        copy.start()
        swaps.append(copy)
        return copy

    lane = lax.broadcasted_iota(jnp.int32, (1, slots), 1)
    row_of = lax.broadcasted_iota(jnp.int32, (8, slots), 0)
    for u in range(utterances):
        target_row = targets[pl.ds(u, 1), :].astype(F32)
        glance_row = glance[pl.ds(u, 1), :].astype(F32)
        valid_row = (lane < token_lengths[u]).astype(F32)
        meta[0, :, pl.ds(u * slots, slots)] = jnp.where(
            row_of == 0, target_row, jnp.where(row_of == 1, valid_row, glance_row)
        )
    own_columns = to_columns(meta[0])
    own_target = own_columns[:, 0:1]
    own_valid = own_columns[:, 1:2]

    def rows(u):
        return pl.ds(u * slots, slots)

    edge = jnp.zeros((8, width), F32)
    for u in range(utterances):
        padded[u, pl.ds(0, 8), :] = edge
        padded[u, pl.ds(8 + slots, 8), :] = edge

    step_rows = 256
    row_chunks = frames // step_rows

    def key_of(u, h):
        return kv[pl.ds(u * frames, frames), pl.ds(h * HD, HD)]

    def value_of(u, h):
        return kv[pl.ds(u * frames, frames), pl.ds(half + h * HD, HD)]

    frame_lane = lax.broadcasted_iota(jnp.int32, (1, frames), 1)

    def look_up(first_row, count, allowed, source):
        ids = first_row + lax.broadcasted_iota(jnp.int32, (1, count), 1)
        local = jnp.where(allowed, own_target.astype(jnp.int32), -1)
        onehot = jnp.where(ids == local, 1.0, 0.0).astype(BF16)
        return dot_nn(onehot, source)

    def look_up_block(k):
        table_loads[k].wait()
        part = look_up(
            (core * per_core + k) * block, block, True, spare[pl.ds(k % 2 * block, block), :]
        )
        for u in range(utterances):
            piece = part[u * slots : (u + 1) * slots]
            taken_mine[u] = piece if k == 0 else taken_mine[u] + piece
        if k + 2 < per_core:
            table_loads.append(load_table(k + 2))

    def look_up_rest():
        load_rest.wait()
        part = look_up(mains, r.table_rest.shape[0], core == 0, r.table_rest[...])
        for u in range(utterances):
            taken_mine[u] = taken_mine[u] + part[u * slots : (u + 1) * slots]

    def local_targets(target_column):
        local = target_column.astype(jnp.int32) - core * vocab_here
        return jnp.where((local >= 0) & (local < vocab_here), local, -1)

    def vocab_stats(target, keep=False):
        tiles = main // 128
        step_tiles = 4

        ids = main + lax.broadcasted_iota(jnp.int32, (1, 128), 1)
        last = jnp.where(ids < vocab_here, dot_nt(top[0], w_rest[...]), NEG)
        logits[tiles] = last
        top_m, picked = last, jnp.where(ids == target, last, 0.0)
        for j in range(tiles // step_tiles):
            col = j * step_tiles * 128
            product = dot_nt(top[0], w_vocab[pl.ds(col, step_tiles * 128), :])
            for i in range(step_tiles):
                tile = product[:, i * 128 : (i + 1) * 128]
                ids = col + i * 128 + lax.broadcasted_iota(jnp.int32, (1, 128), 1)
                logits[j * step_tiles + i] = tile
                top_m = jnp.maximum(top_m, tile)
                picked = picked + jnp.where(ids == target, tile, 0.0)
        top_row = jnp.max(top_m, axis=1, keepdims=True)

        def add(j, total):
            for i in range(3):
                raised = jnp.exp(logits[3 * j + i] - top_row)
                if keep:
                    logits[3 * j + i] = raised
                total = total + raised
            return total

        total = lax.fori_loop(0, (tiles + 1) // 3, add, jnp.zeros((tokens, 128), F32))
        return (
            top_row,
            jnp.sum(total, axis=1, keepdims=True),
            jnp.sum(picked, axis=1, keepdims=True),
        )

    def join(mine, theirs):
        top_value = jnp.maximum(mine[0], theirs[0])
        total = mine[1] * jnp.exp(mine[0] - top_value) + theirs[1] * jnp.exp(theirs[0] - top_value)
        return top_value + jnp.log(total), mine[2] + theirs[2]

    def memory_block(u):
        at = rows(u)
        valid = own_valid[u * slots : (u + 1) * slots]
        hat, _ = normalise(stream_in[at, :])
        padded[u, pl.ds(8, slots), :] = (hat * gain_1 + bias_1) * valid
        for j in range(width // 128):
            cols = pl.ds(j * 128, 128)
            total = jnp.zeros((slots, 128), F32)
            for k in range(kernel_rows.shape[0]):
                shift = 8 + k - kernel_rows.shape[0] // 2
                total = total + kernel_rows[pl.ds(k, 1), cols] * padded[u, pl.ds(shift, slots), cols]
            stream_one[at, cols] = stream_in[at, cols] + total * valid
        low = stream_one[at, :].astype(BF16)
        one_low[at, :] = low
        queries[at, :] = dot_nn(low, w_query[...]).astype(BF16)

    def forward(second, beside_one=None, beside_two=None):
        copies = []
        for u in range(utterances):
            at = rows(u)
            if second:
                memory_block(u)
            frame_ok = frame_lane < memory_lengths[u]
            for h in range(heads):
                cols = pl.ds(h * HD, HD)
                scores = dot_nt(queries[at, cols], key_of(u, h)) * score_scale
                scores = jnp.where(frame_ok, scores, NEG)
                raised = jnp.exp(scores - jnp.max(scores, axis=-1, keepdims=True))
                prob = raised * (1.0 / jnp.sum(raised, axis=-1, keepdims=True))
                if second:
                    probs[u, h] = prob
                mixed[at, cols] = dot_nn(prob.astype(BF16), value_of(u, h)).astype(BF16)
            sent[u] = dot_nn(mixed[at, :], w_out[...])
            copies.append(swap(sent.at[u], arrived.at[u], sibling))
        if not second:
            beside_one()
            load_in.wait()
            load_back.wait()
        ff_copies = []
        for u in range(utterances):
            at = rows(u)
            copies[u].wait()
            two = stream_one[at, :] + (sent[u] + arrived[u])
            stream_two[at, :] = two
            hat, _ = normalise(two)
            low = (hat * gain_2 + bias_2).astype(BF16)
            norm_low[at, :] = low
            pre = dot_nn(low, w_in[...])
            phi = 0.5 * (1.0 + lax.erf(pre * math.sqrt(0.5)))
            hidden[at, :] = (pre * phi).astype(BF16)
            if second:
                gelu_slope[at, :] = phi + pre * (
                    jnp.exp(-0.5 * pre * pre) * (1.0 / math.sqrt(2.0 * math.pi))
                )
            sent[utterances + u] = dot_nn(hidden[at, :], w_back[...])
            ff_copies.append(swap(sent.at[utterances + u], arrived.at[utterances + u], sibling))
        if not second:
            beside_two()
        for u in range(utterances):
            at = rows(u)
            ff_copies[u].wait()
            three = stream_two[at, :] + (sent[utterances + u] + arrived[utterances + u])
            stream_three[u] = three
            top[0, at, :] = three.astype(BF16)

    stream_in[...] = acoustic[...].astype(F32)

    def beside_one():
        look_up_block(0)
        look_up_block(1)

    def beside_two():
        for k in range(2, per_core):
            look_up_block(k)
        look_up_rest()

    load_query.wait()
    for u in range(utterances):
        memory_block(u)
    load_memory.wait()
    for copy in load_kv:
        copy.wait()
    kv_rows = 512
    kv_chunks = frames // kv_rows

    def kv_step(i, carry):
        at = pl.ds(pl.multiple_of(i * kv_rows, kv_rows), kv_rows)
        group = jnp.zeros((1, width), jnp.int32) + rate_groups[i // kv_chunks]
        rate_row = jnp.where(group == 1, rate_table[pl.ds(1, 1), :], rate_table[pl.ds(0, 1), :])
        low = (mem_low[at, :].astype(F32) + rate_row).astype(BF16)
        mem_low[at, :] = low
        kv[at, :] = dot_nn(low, w_kv[...]).astype(BF16)
        return carry

    lax.fori_loop(0, utterances * kv_chunks, kv_step, 0)

    pl.semaphore_wait(barrier, n_dp)
    load_out.wait()
    forward(False, beside_one, beside_two)
    table_swap = swap(taken_mine, taken_theirs, sibling)
    load_vocab.wait()
    w_rest[pl.ds(0, vocab_here - main), :] = w_vocab[pl.ds(main, vocab_here - main), :]
    own_local = local_targets(own_target)
    mine = vocab_stats(own_local)
    stats[0] = side_by_side(mine)
    first_swap = swap(stats.at[0], stats_arrived.at[0], sibling)
    table_swap.wait()
    first_swap.wait()
    log_total, picked = join(mine, [stats_arrived[0, :, i : i + 1] for i in range(3)])
    first_loss = (log_total - picked) * own_valid
    blend = own_columns[:, 2:3] * own_valid / (1.0 + jnp.exp(math.log(V) - first_loss))
    for u in range(utterances):
        at = rows(u)
        wide_acoustic = acoustic[at, :].astype(F32)
        taken = taken_mine[u] + taken_theirs[u]
        stream_in[at, :] = wide_acoustic + blend[u * slots : (u + 1) * slots] * (taken - wide_acoustic)

    forward(True)
    token_swaps = [
        swap(stream_three.at[core], gathered.at[j - 1, 0], {"dp": mate[j]}) for j in (1, 2)
    ]
    mine = vocab_stats(own_local, keep=True)
    stats[1] = side_by_side(mine)
    stat_swap = swap(stats.at[1], stats_arrived.at[1], sibling)
    stat_swap.wait()
    log_column, picked = join(mine, [stats_arrived[1, :, i : i + 1] for i in range(3)])

    factor = jnp.exp(mine[0] - log_column) * own_valid
    valid_local = jnp.where(own_valid > 0.0, own_local, -1)

    def slope(j, carry):
        col = pl.multiple_of(j * 128, 128)
        ids = col + lax.broadcasted_iota(jnp.int32, (1, 128), 1)
        grad = logits[j] * factor - jnp.where(ids == valid_local, 1.0, 0.0)
        grad_logits[:, pl.ds(col, 128)] = grad.astype(BF16)
        return carry

    lax.fori_loop(0, main // 128 + 1, slope, 0, unroll=3)
    three_copies = []
    for u in range(utterances):
        sent[u] = dot_nn(grad_logits[rows(u), pl.ds(0, main)], w_vocab[pl.ds(0, main), :]) + dot_nn(
            grad_logits[rows(u), pl.ds(main, 128)], w_rest[...]
        )
        three_copies.append(swap(sent.at[u], arrived.at[u], sibling))
    for copy in token_swaps:
        copy.wait()
    part = slots // 2
    relays = [
        swap(gathered.at[0, 0, pl.ds(0, part)], gathered.at[2, 0, pl.ds(0, part)], {"dp": mate[2]}),
        swap(gathered.at[1, 0, pl.ds(part, part)], gathered.at[2, 0, pl.ds(part, part)], {"dp": mate[1]}),
    ]
    share_swaps = [swap(gathered.at[j, 0], gathered.at[j, 1], sibling) for j in range(2)]
    meta[0] = to_rows([own_target, own_valid, log_column, (log_column - picked) * own_valid])
    meta_swaps = [swap(meta.at[0], meta.at[j], {"dp": mate[j]}) for j in range(1, 4)]
    for u in range(utterances):
        r.loss_sum[pl.ds(u, 1), :] = meta[0, 3:4, u * slots : (u + 1) * slots]
    store(r.loss_sum, r.loss_out)

    plan = Planner()
    steps_all = len(bits)
    scatter_send, scatter_recv = r.scatter_send, r.scatter_recv

    vocab_parts = []

    def vocab_done():
        vocab_parts.append(1)
        if len(vocab_parts) == 1 + part_cols // 512:
            store(r.vocab_whole, r.vocab_out)

    def make_chunk(index):
        name, start, cols, order = chunk_list(part_cols, width, bits, low_bits, r)[index]
        source, landing = getattr(r, "src_" + name), r.landing[index]
        out_start = start
        if name == "kv":
            out, final = ((r.key_sum, r.key_out), (r.value_sum, r.value_out))[start // cols]
            out_start = 0
        else:
            out, final = getattr(r, name + "_sum"), getattr(r, name + "_out")
        rows_here = source.shape[-2]

        def pick(step, which):
            rest = sorted([b for b in bits if b not in order[:step]], reverse=True)
            where = tuple(which if b == order[step] else slice(None) for b in rest)
            if step == 0:
                return source, where + (slice(None), pl.ds(start, cols))
            return landing[step - 1], where + (slice(None), slice(None))

        def send(step):
            b = order[step]
            ref, where = pick(step, 1 - bit_of[b])
            copy = pltpu.make_async_remote_copy(
                src_ref=ref.at[where],
                dst_ref=landing[step],
                send_sem=scatter_send.at[index, step],
                recv_sem=scatter_recv.at[index, step],
                device_id=peer_of[b],
                device_id_type=MESH,
            )
            copy.start()
            return copy

        def take(step, copy):
            copy.wait_recv()
            ref, where = pick(step, bit_of[order[step]])
            got = landing[step]
            at = pl.ds(out_start, cols)
            if step < len(order) - 1:
                got[...] = got[...] + ref[where]
                return
            out[..., at] = got[...] + ref[where]
            if low_bits or name not in ("vocab", "rest"):
                store(out.at[..., at], final.at[..., at])
            elif name == "rest":
                rest = vocab_here - main
                r.vocab_whole[:, pl.ds(main, rest)] = out[...][:, :rest]
                vocab_done()

        steps = [
            (link_of(b, bits), rows_here * cols * 4 * 2 ** (steps_all - 1 - s))
            for s, b in enumerate(order)
        ]
        return Chunk(steps, send, take)

    def make_trade(start, cols):
        summed, traded = r.vocab_sum, r.vocab_traded
        at = pl.ds(start, cols)

        def send(step):
            copies = []
            for j in range(1, 4):
                to = lax.rem(mate[j], 4)
                copies.append(
                    pltpu.make_async_remote_copy(
                        src_ref=summed.at[to // 2, lax.rem(to, 2), :, at],
                        dst_ref=traded.at[j - 1, :, at],
                        send_sem=r.trade_send.at[start // 128, j - 1],
                        recv_sem=r.trade_recv.at[start // 128, j - 1],
                        device_id={"dp": mate[j]},
                        device_id_type=MESH,
                    )
                )
                copies[-1].start()
            return Several(copies)

        def take(step, copies):
            copies.wait_recv()
            for j in range(1, 4):
                there = pl.multiple_of(lax.rem(mate[j], 4) * part_cols + start, 128)
                r.vocab_whole[:, pl.ds(there, cols)] = traded[j - 1, :, at]
            here = pl.multiple_of(base + start, 128)
            r.vocab_whole[:, pl.ds(here, cols)] = summed[quarter // 2, lax.rem(quarter, 2), :, at]
            vocab_done()

        return Chunk([(0, 2 * r.src_vocab.shape[-2] * cols * 4)], send, take)

    chunks = {}
    for index, (name, start, cols, _) in enumerate(chunk_list(part_cols, width, bits, low_bits, r)):
        chunks[name, start] = make_chunk(index)
        if name == "vocab" and not low_bits:
            chunks[name, start].follow = make_trade(start, cols)

    def put(name, at, product):
        source = getattr(r, "src_" + name)
        source[..., at] = product.reshape(source.shape[:-1] + (product.shape[1],))

    copies = []
    for u in range(utterances):
        at = rows(u)
        three_copies[u].wait()
        three = sent[u] + arrived[u]
        grad_three[u] = three
        low = three.astype(BF16)
        branch_low[at, :] = low
        pre = (dot_nt(low, w_back[...]) * gelu_slope[at, :]).astype(BF16)
        grad_pre[at, :] = pre
        sent[utterances + u] = dot_nt(pre, w_in[...])
        copies.append(swap(sent.at[utterances + u], arrived.at[utterances + u], sibling))
    plan.run_until(plan.now + 8.0)
    for name, left, right in (("back", branch_low, hidden), ("in", norm_low, grad_pre)):
        left_turned = left[...].T
        for start in sorted(s for n, s in chunks if n == name):
            at = pl.ds(start, 512)
            put(name, at, dot_nn(left_turned, right[:, at]))
            plan.run_until(plan.now + 0.5)
            plan.post(chunks[name, start])

    at_core = pl.ds(pl.multiple_of(core * slots, slots), slots)
    at_other = pl.ds(pl.multiple_of((1 - core) * slots, slots), slots)
    base = pl.multiple_of(quarter * part_cols, part_cols)
    pieces = [(c, 256) for c in range(0, part_cols, 256)]
    for j in range(1, 4):
        if j == 2:
            for copy in relays:
                copy.wait()
            share_swaps.append(swap(gathered.at[2, 0], gathered.at[2, 1], sibling))
        meta_swaps[j - 1].wait()
        columns = to_columns(meta[j])
        valid = columns[:, 1:2] > 0.0
        target = jnp.where(valid, local_targets(columns[:, 0:1]), -1)
        log_total = jnp.where(valid, columns[:, 2:3], -NEG)
        top[j, at_core, :] = gathered[j - 1, 0].astype(BF16)
        share_swaps[j - 1].wait()
        top[j, at_other, :] = gathered[j - 1, 1].astype(BF16)
        for col, cols in pieces:
            ids = base + col + lax.broadcasted_iota(jnp.int32, (1, cols), 1)
            tile = dot_nt(top[j], w_vocab[pl.ds(base + col, cols), :])
            grad = jnp.exp(tile - log_total) - jnp.where(ids == target, 1.0, 0.0)
            grad_others[pl.ds((j - 1) * tokens, tokens), pl.ds(col, cols)] = grad.astype(BF16)
    top_turned = r.top_turned
    for j in range(4):
        top_turned[:, pl.ds(j * tokens, tokens)] = top[j].T
    plan.run_until(plan.now + 4.0)
    put("rest", slice(None), dot_nn(top_turned[:, pl.ds(0, tokens)], grad_logits[:, pl.ds(main, 128)]))
    starts = sorted(start for name, start in chunks if name == "vocab")
    for start, stop in zip(starts, starts[1:] + [part_cols]):
        for col in range(start, stop, 256):
            cols = min(256, stop - col)
            product = dot_nn(top_turned[:, pl.ds(0, tokens)], grad_logits[:, pl.ds(base + col, cols)])
            product = product + dot_nn(
                top_turned[:, pl.ds(tokens, 3 * tokens)], grad_others[:, pl.ds(col, cols)]
            )
            put("vocab", pl.ds(col, cols), product)
        plan.run_until(plan.now + 0.7)
        plan.post(chunks["vocab", start])
    plan.post(chunks["rest", 0])

    one_copies = []
    gain_2_total, bias_2_total = 0.0, 0.0
    for u in range(utterances):
        at = rows(u)
        copies[u].wait()
        grad_norm = sent[utterances + u] + arrived[utterances + u]
        hat, scale = normalise(stream_two[at, :])
        gain_2_total = gain_2_total + jnp.sum(grad_norm * hat, axis=0, keepdims=True)
        bias_2_total = bias_2_total + jnp.sum(grad_norm, axis=0, keepdims=True)
        two = grad_three[u] + normalise_back(grad_norm * gain_2, hat, scale)
        grad_two[at, :] = two
        low = two.astype(BF16)
        att_low[at, :] = low
        grad_mixed = dot_nt(low, w_out[...]).astype(BF16)
        for h in range(heads):
            cols = pl.ds(h * HD, HD)
            grad_head = grad_mixed[:, h * HD : (h + 1) * HD]
            prob = probs[u, h]
            grad_prob = dot_nt(grad_head, value_of(u, h))
            spare[pl.ds(u * frames, frames), pl.ds(half + h * HD, HD)] = dot_tn(
                prob.astype(BF16), grad_head
            ).astype(BF16)
            inner = jnp.sum(prob * grad_prob, axis=-1, keepdims=True)
            grad_score = (prob * (grad_prob - inner)).astype(BF16)
            grad_queries[at, cols] = (dot_nn(grad_score, key_of(u, h)) * score_scale).astype(BF16)
            spare[pl.ds(u * frames, frames), cols] = (
                dot_tn(grad_score, queries[at, cols]) * score_scale
            ).astype(BF16)
            plan.run_until(plan.now + 1.5)
        sent[u] = dot_nt(grad_queries[at, :], w_query[...])
        one_copies.append(swap(sent.at[u], arrived.at[u], sibling))
    every = slice(None)
    put("out", every, dot_tn(att_low[...], mixed[...]))
    plan.post(chunks["out", 0])
    put("query", every, dot_tn(one_low[...], grad_queries[...]))
    plan.post(chunks["query", 0])
    plan.run_until(plan.now + 1.0)

    mem_copies = []
    rate_sums = [0.0, 0.0]
    for u in range(utterances):
        total = jnp.zeros((1, width), F32)
        for i in range(row_chunks):
            at = pl.ds(u * frames + i * step_rows, step_rows)
            part = dot_nt(spare[at, :], w_kv[...])
            for j in range(width // 128):
                side_of, tile = j // (width // 256), j % (width // 256)
                index = ((side_of * utterances + u) * row_chunks + i) * (width // 256) + tile
                logits[index] = part[:, j * 128 : (j + 1) * 128]
            total = total + jnp.sum(part, axis=0, keepdims=True)
        tiles = row_chunks * (width // 256)
        mem_copies.append(
            swap(
                logits.at[pl.ds(((1 - core) * utterances + u) * tiles, tiles)],
                mem_arrived.at[pl.ds(u * tiles, tiles)],
                sibling,
            )
        )
        group = jnp.zeros((1, width), jnp.int32) + rate_groups[u]
        for k in range(2):
            rate_sums[k] = rate_sums[k] + jnp.where((group == 1) == (k == 1), total, 0.0)
        plan.run_until(plan.now + 1.2)
    span = frames // 2
    for k in range(2 * utterances):
        at = pl.ds(k * span, span)
        product = dot_tn(mem_low[at, :], spare[at, :])
        product = product.reshape(r.src_kv.shape)
        r.src_kv[...] = product if k == 0 else r.src_kv[...] + product
    plan.run_until(plan.now + 2.0)
    plan.post(*[chunks["kv", start] for start in sorted(s for n, s in chunks if n == "kv")])

    gain_1_total, bias_1_total = 0.0, 0.0
    for u in range(utterances):
        at = rows(u)
        valid = own_valid[u * slots : (u + 1) * slots]
        one_copies[u].wait()
        one = grad_two[at, :] + (sent[u] + arrived[u])
        grad_two[at, :] = one
        masked = one * valid
        for k in range(kernel_rows.shape[0]):
            shift = 8 + k - kernel_rows.shape[0] // 2
            row = jnp.sum(masked * padded[u, pl.ds(shift, slots), :], axis=0, keepdims=True)
            if u == 0:
                small_sent[0, pl.ds(k, 1), :] = row
            else:
                small_sent[0, pl.ds(k, 1), :] = small_sent[0, pl.ds(k, 1), :] + row
        padded[u, pl.ds(8, slots), :] = masked
        for j in range(width // 128):
            cols = pl.ds(j * 128, 128)
            total = jnp.zeros((slots, 128), F32)
            for k in range(kernel_rows.shape[0]):
                shift = 8 - k + kernel_rows.shape[0] // 2
                total = total + kernel_rows[pl.ds(k, 1), cols] * padded[u, pl.ds(shift, slots), cols]
            stream_one[at, cols] = total * valid
        grad_norm = stream_one[at, :]
        hat, scale = normalise(stream_in[at, :])
        gain_1_total = gain_1_total + jnp.sum(grad_norm * hat, axis=0, keepdims=True)
        bias_1_total = bias_1_total + jnp.sum(grad_norm, axis=0, keepdims=True)
        zero = grad_two[at, :] + normalise_back(grad_norm * gain_1, hat, scale)
        terms[u] = blend[u * slots : (u + 1) * slots] * zero
        stream_one[at, :] = zero - terms[u]
        plan.run_until(plan.now + 1.5)

    last_taps = kernel_rows.shape[0]
    small_sent[0, pl.ds(last_taps, 12 - last_taps), :] = jnp.zeros((12 - last_taps, width), F32)
    for i, row in enumerate((gain_1_total, bias_1_total, gain_2_total, bias_2_total)):
        small_sent[0, pl.ds(12 + i, 1), :] = row
    for k in range(2):
        small_sent[0, pl.ds(16 + k, 1), :] = rate_sums[k]
    small_sent[0, pl.ds(18, 6), :] = jnp.zeros((6, width), F32)
    small_peers = [peer_of[b] for b in low_bits + bits] + [sibling]

    def small_send(step):
        copy = pltpu.make_async_remote_copy(
            src_ref=small_sent.at[step],
            dst_ref=small_arrived.at[step],
            send_sem=r.small_send.at[step],
            recv_sem=r.small_recv.at[step],
            device_id=small_peers[step],
            device_id_type=MESH,
        )
        copy.start()
        return copy

    def small_take(step, copy):
        copy.wait_recv()
        if step + 1 == len(small_peers):
            copy.wait_send()
            plan.started = [c for c in plan.started if c is not copy]
        if step + 1 < len(small_peers):
            small_sent[step + 1] = small_sent[step] + small_arrived[step]
        else:
            small_sent[step, pl.ds(16, 8), :] = (
                small_sent[step, pl.ds(16, 8), :] + small_arrived[step, pl.ds(16, 8), :]
            )
            store(small_sent.at[step], r.small_out)

    small_links = [link_of(b, bits) for b in low_bits + bits] + ["core"]
    plan.post(Chunk([(l, 24 * width * 4) for l in small_links], small_send, small_take))

    features = width // n_dp
    feature_rows = max(features, 8)
    block_rows = term_blocks.shape[1]
    turned = terms[core].T
    id_row = targets[pl.ds(core, 1), :].astype(F32)
    rest = block_rows - features - 1
    for p in range(n_dp):
        term_blocks[p, pl.ds(0, features), :] = turned[p * features : (p + 1) * features]
        term_blocks[p, pl.ds(features, 1), :] = id_row
        term_blocks[p, pl.ds(features + 1, rest), :] = jnp.zeros((rest, slots), F32)

    def term_copy(k):
        there = lax.rem(me + k, n_dp)
        return pltpu.make_async_remote_copy(
            src_ref=term_blocks.at[there],
            dst_ref=term_arrived.at[me],
            send_sem=r.term_send.at[k],
            recv_sem=r.term_recv.at[k],
            device_id={"dp": there},
            device_id_type=MESH,
        )

    def term_start(k, carry):
        term_copy(k).start()
        return carry

    def term_wait(k, carry):
        term_copy(k).wait()
        return carry

    term_arrived[me] = term_blocks[me]
    lax.fori_loop(1, n_dp, term_start, 0)
    store(stream_one, r.acoustic_out)
    for u in range(utterances):
        mem_copies[u].wait()
        for i in range(row_chunks):
            for j in range(width // 256):
                index = (u * row_chunks + i) * (width // 256) + j
                first_tile = (core * utterances) * row_chunks * (width // 256)
                mem_arrived[index] = logits[first_tile + index] + mem_arrived[index]
                at = pl.ds(u * frames + i * step_rows, step_rows)
                store(mem_arrived.at[index], r.memory_out.at[at, pl.ds(j * 128, 128)])
    plan.run_until(plan.now + 8.0)
    lax.fori_loop(1, n_dp, term_wait, 0)
    per_piece = 512 // slots
    blocks_hi = (table_rows + 255) // 256
    batch = 4

    def table_piece(p, fresh):
        found = [term_arrived[p * per_piece + i] for i in range(per_piece)]
        values = jnp.concatenate([f[:feature_rows] for f in found], axis=1)
        ids = jnp.concatenate([f[features : features + 1] for f in found], axis=1).astype(jnp.int32)
        low_ids, high_ids = ids & 255, ids >> 8
        onehot_lo[...] = jnp.where(
            lax.broadcasted_iota(jnp.int32, (256, 512), 0) == low_ids, 1.0, 0.0
        ).astype(BF16)
        coarse = values.astype(BF16).astype(F32)
        both = jnp.concatenate([coarse, values - coarse], axis=0)
        for first_hi in range(0, blocks_hi, batch):
            here = range(first_hi, min(first_hi + batch, blocks_hi))
            masked = jnp.concatenate([jnp.where(high_ids == hi, both, 0.0) for hi in here], axis=0)
            product = dot_nt(masked.astype(BF16), onehot_lo[...])
            for i, hi in enumerate(here):
                top_part = product[2 * i * feature_rows : (2 * i + 1) * feature_rows]
                low_part = product[(2 * i + 1) * feature_rows : (2 * i + 2) * feature_rows]
                cols = min(256, table_rows - hi * 256)
                at = pl.ds(hi * 256, cols)
                found = (top_part + low_part)[:features, :cols]
                whole_table[:, at] = found if fresh else whole_table[:, at] + found

    pieces = n_dp // per_piece
    table_piece(0, True)
    if pieces <= 4:
        for p in range(1, pieces):
            plan.run_until(plan.now + 1.5)
            table_piece(p, False)
    else:
        lax.fori_loop(1, pieces, lambda p, c: (table_piece(p, False), c)[1], 0)
    table_swap = swap(whole_table, table_theirs, sibling)
    plan.run_until(plan.now + 8.0)
    table_swap.wait()
    whole_table[...] = whole_table[...] + table_theirs[...]
    store(whole_table, r.table_out)
    plan.finish()
    for copy in stores:
        copy.wait()


def link_of(bit, bits):
    if bit == bits[-1]:
        return bits[-2]
    return bit


def chunk_list(part_cols, width, bits, low_bits, sizes):
    turned = [bits[1], bits[0]] + bits[2:]
    listing = []
    for start in range(0, part_cols, 512):
        listing.append(("vocab", start, 512, [b for b in bits if b > 1]))
    listing.append(("rest", 0, 128, bits))
    for name, order in (("back", turned), ("in", bits)):
        for start in range(0, sizes.units, 512):
            if name == "in" and start:
                order = [bits[2], bits[0], bits[1]] + bits[3:]
            listing.append((name, start, 512, order))
    listing.append(("out", 0, sizes.half, turned))
    listing.append(("query", 0, sizes.half, bits))
    for k, start in enumerate(range(0, 2 * sizes.half, 256)):
        listing.append(("kv", start, 256, [bits, turned][k % 2]))
    return listing


def decoder_call(
    acoustic, memory, embedding, w_query, w_key, w_value, w_out, w_in, w_back, w_vocab, norms,
    fsmn_kernel, rate_table, token_lengths, memory_lengths, rate_groups, glance, targets, n_dp,
):
    utterances = token_lengths.shape[0]
    tokens, width = acoustic.shape
    slots = tokens // utterances
    mem_rows = memory.shape[0]
    half = w_query.shape[1]
    heads = half // HD
    frames = mem_rows // utterances
    units = w_in.shape[1]
    vocab_here = w_vocab.shape[1]
    table_rows = embedding.shape[0]
    part_cols = vocab_here // 512 * 128
    all_cols = 4 * part_cols + 128
    w_turned = w_vocab.T
    mains = table_rows // 2048 * 2048
    nbits = n_dp.bit_length() - 1
    steps = nbits
    while width >> steps < 8:
        steps -= 1
    low_bits, bits = list(range(nbits - steps)), list(range(nbits - steps, nbits))
    rows = width >> steps
    features = width // n_dp
    feature_rows = max(features, 8)
    block_rows = feature_rows + 8 if features >= 8 else 8
    blocks_hi = (table_rows + 255) // 256
    sizes = SimpleNamespace(units=units, half=half)
    plane = [b for b in bits if b < 2]
    listing = chunk_list(part_cols, width, bits, low_bits, sizes)
    most = max(len(c[3]) for c in listing)

    f32 = lambda *shape: jax.ShapeDtypeStruct(shape, F32)
    v32 = lambda *shape: pltpu.VMEM(shape, F32)
    v16 = lambda *shape: pltpu.VMEM(shape, BF16)
    dma = lambda *shape: pltpu.SemaphoreType.DMA(shape)
    inputs = dict(
        acoustic=(VMEM, acoustic),
        table_tail=(VMEM, embedding[mains + (table_rows - mains) // 16 * 16 :]),
        memory=(ANY, memory),
        table=(ANY, embedding),
        w_query_hbm=(ANY, w_query),
        w_key_hbm=(ANY, w_key),
        w_value_hbm=(ANY, w_value),
        w_out_hbm=(ANY, w_out),
        w_in_hbm=(ANY, w_in),
        w_back_hbm=(ANY, w_back),
        w_vocab_hbm=(ANY, w_turned),
        gain_one=(VMEM, norms[0][None]),
        bias_one=(VMEM, norms[1][None]),
        gain_two=(VMEM, norms[2][None]),
        bias_two=(VMEM, norms[3][None]),
        kernel_rows=(VMEM, fsmn_kernel),
        rate_table=(VMEM, rate_table),
        token_lengths=(SMEM, token_lengths),
        memory_lengths=(SMEM, memory_lengths),
        rate_groups=(SMEM, rate_groups),
        glance=(VMEM, glance.reshape(utterances, slots)),
        targets=(VMEM, targets.reshape(utterances, slots)),
    )
    outputs = dict(
        loss_out=f32(utterances, slots),
        small_out=f32(24, width),
        vocab_out=f32(2, rows, part_cols) if low_bits else f32(rows, vocab_here),
        rest_out=f32(rows, 128),
        in_out=f32(rows, units),
        back_out=f32(rows, units),
        query_out=f32(rows, half),
        out_out=f32(rows, half),
        key_out=f32(rows, half),
        value_out=f32(rows, half),
        acoustic_out=f32(tokens, width),
        memory_out=f32(mem_rows, width // 2),
        table_out=f32(features, table_rows),
    )
    shape = (2,) * steps + (rows,)
    scratch = dict(
        w_query=v16(width, half),
        w_kv=v16(width, 2 * half),
        w_out=v16(half, width),
        w_in=v16(width, units),
        w_back=v16(units, width),
        w_vocab=v16(vocab_here, width),
        w_rest=v16(128, width),
        mem_low=v16(mem_rows, width),
        kv=v16(mem_rows, 2 * half),
        spare=v16(mem_rows, 2 * half),
        padded=v32(utterances, slots + 16, width),
        stream_in=v32(tokens, width),
        stream_one=v32(tokens, width),
        stream_two=v32(tokens, width),
        stream_three=v32(utterances, slots, width),
        one_low=v16(tokens, width),
        queries=v16(tokens, half),
        probs=v32(utterances, heads, slots, frames),
        mixed=v16(tokens, half),
        norm_low=v16(tokens, width),
        hidden=v16(tokens, units),
        gelu_slope=v32(tokens, units),
        top=v16(4, tokens, width),
        logits=v32(all_cols // 128, tokens, 128),
        grad_logits=v16(tokens, all_cols),
        grad_others=v16(3 * tokens, part_cols),
        top_turned=v16(width, 4 * tokens),
        taken_theirs=v32(utterances, slots, width),
        grad_three=v32(utterances, slots, width),
        grad_two=v32(tokens, width),
        branch_low=v16(tokens, width),
        grad_pre=v16(tokens, units),
        att_low=v16(tokens, width),
        grad_queries=v16(tokens, half),
        mem_arrived=v32(mem_rows // 256 * (width // 256), 256, 128),
        meta=v32(4, 8, tokens),
        stats=v32(2, tokens, 128),
        stats_arrived=v32(2, tokens, 128),
        sent=v32(2 * utterances, slots, width),
        arrived=v32(2 * utterances, slots, width),
        gathered=v32(3, 2, slots, width),
        small_sent=v32(nbits + 1, 24, width),
        small_arrived=v32(nbits + 1, 24, width),
        term_blocks=v32(n_dp, block_rows, slots),
        term_arrived=v32(n_dp, block_rows, slots),
        onehot_lo=v16(256, 512),
        table_rest=v16((table_rows - mains + 127) // 128 * 128, width),
        table_theirs=v32(features, table_rows),
        src_vocab=v32(*shape, part_cols),
        src_rest=v32(*shape, 128),
        whole_table=v32(features, table_rows),
        src_back=v32(*shape, units),
        vocab_sum=v32(*(2,) * len(plane), rows, part_cols),
        rest_sum=v32(rows, 128),
        vocab_whole=v32(rows, vocab_here),
        in_sum=v32(rows, units),
        back_sum=v32(rows, units),
        query_sum=v32(rows, half),
        out_sum=v32(rows, half),
        key_sum=v32(rows, half),
        value_sum=v32(rows, half),
        loss_sum=v32(utterances, slots),
        vocab_traded=v32(3, rows, part_cols),
        src_in=v32(*shape, units),
        src_out=v32(*shape, half),
        src_query=v32(*shape, half),
        src_kv=v32(*shape, 2 * half),
        load_sem=dma(24),
        store_sem=dma(48),
        trade_send=dma(part_cols // 128, 3),
        trade_recv=dma(part_cols // 128, 3),
        swap_send=dma(40),
        swap_recv=dma(40),
        scatter_send=dma(len(listing), most),
        scatter_recv=dma(len(listing), most),
        small_send=dma(nbits + 1),
        small_recv=dma(nbits + 1),
        term_send=dma(n_dp),
        term_recv=dma(n_dp),
    )
    landing = [
        [v32(*(2,) * (steps - 1 - s), rows, cols) for s in range(len(order))]
        for _, _, cols, order in listing
    ]
    names = list(inputs) + list(outputs) + list(scratch)
    flat = [ref for chunk in landing for ref in chunk]

    def kernel(*refs):
        named, rest = refs[: len(names)], list(refs[len(names) :])
        lands = [[rest.pop(0) for _ in chunk] for chunk in landing]
        decoder_kernel(
            names + ["landing", "units", "half"], vocab_here, part_cols, table_rows, n_dp, bits,
            low_bits, *named, lands, units, half,
        )

    out = pl.pallas_call(
        kernel,
        out_shape=list(outputs.values()),
        in_specs=[spec for spec, _ in inputs.values()],
        out_specs=[ANY] * len(outputs),
        scratch_shapes=list(scratch.values()) + flat,
        compiler_params=pltpu.CompilerParams(
            collective_id=1, has_side_effects=True, vmem_limit_bytes=64 << 20
        ),
    )(*[value for _, value in inputs.values()])
    return SimpleNamespace(**dict(zip(outputs, out))), low_bits


def deliver_kernel(n_dp, n_passed, *refs):
    n = n_passed + 2
    sources, targets, held = refs[:n], refs[n : 2 * n + 5], refs[2 * n + 5 : 3 * n + 5]
    shaped, (sem_in, sem_out) = refs[3 * n + 5 : 3 * n + 12], refs[3 * n + 12 :]
    reads, writes = [], []
    for i, (source, buffer) in enumerate(zip(sources, held)):
        reads.append(pltpu.make_async_copy(source, buffer, sem_in.at[i]))
        reads[-1].start()
    for i in range(n_passed):
        reads[i].wait()
        writes.append(pltpu.make_async_copy(held[i], targets[i], sem_out.at[i]))
        writes[-1].start()
    reads[n_passed].wait()
    reads[n_passed + 1].wait()
    loss, small = held[n_passed:]
    loss_at, gain_one_at, bias_one_at, gain_two_at, bias_two_at, taps_at, rate_at = shaped
    slots = loss.shape[1]
    for u in range(loss.shape[0]):
        loss_at[:, pl.ds(u * slots, slots)] = loss[pl.ds(u, 1), :]
    me = lax.axis_index("dp")
    own = small.shape[1] // n_dp
    mine = jnp.zeros((16, own), F32)
    for p in range(n_dp):
        mine = jnp.where(me == p, small[pl.ds(0, 16), p * own : (p + 1) * own], mine)
    taps_at[...] = mine[: taps_at.shape[0]]
    for i, target in enumerate((gain_one_at, bias_one_at, gain_two_at, bias_two_at)):
        target[...] = mine[12 + i : 13 + i]
    rate_at[...] = small[pl.ds(16, 2), :]
    for i, source in enumerate(shaped):
        writes.append(pltpu.make_async_copy(source, targets[n_passed + i], sem_out.at[n_passed + i]))
        writes[-1].start()
    for copy in writes:
        copy.wait()


def per_device(
    acoustic,
    memory,
    embedding,
    w_query,
    w_key,
    w_value,
    w_out,
    w_in,
    w_back,
    w_vocab,
    gain_one,
    bias_one,
    gain_two,
    bias_two,
    fsmn_kernel,
    rate_table,
    token_lengths,
    memory_lengths,
    rate_groups,
    glance_mask,
    targets,
):
    tok_rows, model_width = acoustic.shape
    half = w_query.shape[1]
    n_dp = lax.axis_size("dp")
    result, low_bits = decoder_call(
        acoustic, memory, embedding, w_query, w_key, w_value, w_out, w_in, w_back, w_vocab,
        (gain_one, bias_one, gain_two, bias_two), fsmn_kernel, rate_table,
        token_lengths, memory_lengths, rate_groups, glance_mask, targets, n_dp,
    )
    vocab = result.vocab_out
    summed = [
        result.query_out, result.key_out, result.value_out, result.out_out, result.in_out,
        result.back_out,
    ]
    if low_bits:
        size = 1 << len(low_bits)
        groups = [list(range(g * size, (g + 1) * size)) for g in range(n_dp // size)]
        planes = [list(range(4 * g, 4 * g + 4)) for g in range(n_dp // 4)]
        vocab = lax.all_to_all(
            vocab.reshape(4, model_width // n_dp, -1), "dp", 0, 0, axis_index_groups=planes, tiled=True
        )
        *summed, rest = [
            lax.psum_scatter(s, "dp", scatter_dimension=0, axis_index_groups=groups, tiled=True)
            for s in (*summed, result.rest_out)
        ]
        vocab = jnp.concatenate([*vocab, rest], axis=1)[:, : w_vocab.shape[1]]
    own = model_width // n_dp
    f32 = lambda *shape: jax.ShapeDtypeStruct(shape, F32)
    like = lambda x: jax.ShapeDtypeStruct(x.shape, F32)
    passed = (result.memory_out, result.table_out, result.acoustic_out, vocab, *summed)
    handed = (*passed, result.loss_out, result.small_out)
    small_shapes = [
        f32(1, tok_rows), *[f32(1, own)] * 4, f32(fsmn_kernel.shape[0], own), f32(2, model_width)
    ]
    (
        grad_memory, grad_table, grad_acoustic, grad_vocab, grad_query, grad_key, grad_value,
        grad_out, grad_in, grad_back, token_loss, gain_1, bias_1, gain_2, bias_2, grad_taps, grad_rate,
    ) = pl.pallas_call(
        partial(deliver_kernel, n_dp, len(passed)),
        out_shape=[*[like(x) for x in passed], *small_shapes],
        in_specs=[ANY] * len(handed),
        out_specs=[ANY] * (len(passed) + 7),
        scratch_shapes=[pltpu.VMEM(x.shape, F32) for x in (*handed, *small_shapes)]
        + [pltpu.SemaphoreType.DMA((len(handed),)), pltpu.SemaphoreType.DMA((len(passed) + 7,))],
        compiler_params=pltpu.CompilerParams(vmem_limit_bytes=60 << 20),
    )(*handed)
    return (
        token_loss.reshape(tok_rows),
        grad_acoustic,
        grad_memory,
        grad_table.T,
        grad_query,
        grad_key,
        grad_value,
        grad_out.T,
        grad_in,
        grad_back.T,
        grad_vocab,
        gain_1.reshape(own),
        bias_1.reshape(own),
        gain_2.reshape(own),
        bias_2.reshape(own),
        grad_taps,
        grad_rate,
    )


def solution(mesh):
    return jax.shard_map(
        per_device,
        mesh=mesh,
        in_specs=(
            P("dp", None),
            P("dp", None),
            P(),
            P(None, "mp"),
            P(None, "mp"),
            P(None, "mp"),
            P("mp", None),
            P(None, "mp"),
            P("mp", None),
            P(None, "mp"),
            P(),
            P(),
            P(),
            P(),
            P(),
            P(),
            P("dp"),
            P("dp"),
            P("dp"),
            P("dp"),
            P("dp"),
        ),
        out_specs=(
            P("dp"),
            P("dp", None),
            P("dp", "mp"),
            P(None, "dp"),
            P("dp", "mp"),
            P("dp", "mp"),
            P("dp", "mp"),
            P("mp", "dp"),
            P("dp", "mp"),
            P("mp", "dp"),
            P("dp", "mp"),
            P("dp"),
            P("dp"),
            P("dp"),
            P("dp"),
            P(None, "dp"),
            P(),
        ),
        check_vma=False,
    )
```
